32 devices in a mesh: dp: 8 (over y, x, core), fsdp: 4 (over z).
Axes of the slice: x: 2, y: 2, z: 4, core: 2. Of those that a mesh axis runs over, the one named last changes fastest.
Arguments:
- tokens: bfloat16 [32768, 768], P(('dp', 'fsdp')), may hold values from -6 to 6
- lengths: int32 [32], P(('dp', 'fsdp')), may hold values from 1 to 1024, 24576 in all
- cotangent: bfloat16 [32768, 768], P(('dp', 'fsdp')), may hold values from -6 to 6
- project_weight: bfloat16 [768, 2304], P('dp', 'fsdp'), may hold values from -0.21875 to 0.21875
- project_bias: bfloat16 [1536], P('dp'), may hold values from -1.1953125 to 1.1953125
- output_weight: bfloat16 [768, 768], P('dp', 'fsdp'), may hold values from -3.5 to 3.5
- output_bias: bfloat16 [768], P('dp'), may hold values from -1.1953125 to 1.1953125
- expand_weight: bfloat16 [768, 3072], P('dp', 'fsdp'), may hold values from -0.21875 to 0.21875
- expand_bias: bfloat16 [3072], P('dp'), may hold values from -1.1953125 to 1.1953125
- contract_weight: bfloat16 [3072, 768], P('dp', 'fsdp'), may hold values from -0.109375 to 0.109375
- contract_bias: bfloat16 [768], P('dp'), may hold values from -1.1953125 to 1.1953125
- first_gain: bfloat16 [768], P('dp'), may hold values from 0.25 to 1.75
- first_shift: bfloat16 [768], P('dp'), may hold values from -1.1953125 to 1.1953125
- second_gain: bfloat16 [768], P('dp'), may hold values from 0.25 to 1.75
- second_shift: bfloat16 [768], P('dp'), may hold values from -1.1953125 to 1.1953125
Outputs:
- block_out: bfloat16 [32768, 768], P(('dp', 'fsdp'))
- tokens_grad: bfloat16 [32768, 768], P(('dp', 'fsdp'))
- project_weight_grad: float32 [768, 2304], P('dp', 'fsdp')
- project_bias_grad: float32 [1536], P('dp')
- output_weight_grad: float32 [768, 768], P('dp', 'fsdp')
- output_bias_grad: float32 [768], P('dp')
- expand_weight_grad: float32 [768, 3072], P('dp', 'fsdp')
- expand_bias_grad: float32 [3072], P('dp')
- contract_weight_grad: float32 [3072, 768], P('dp', 'fsdp')
- contract_bias_grad: float32 [768], P('dp')
- first_gain_grad: float32 [768], P('dp')
- first_shift_grad: float32 [768], P('dp')
- second_gain_grad: float32 [768], P('dp')
- second_shift_grad: float32 [768], P('dp')
The draws below stay inside these ranges and needn't reach their ends.
Inputs may be any that keep to these rules, and one draw needn't show every extreme that they name: `lengths`: each cell's number of live tokens; some cell has exactly 1024.
All inputs are finite; a program needn't handle non-finite values. No bound on the sum of `lengths` on one device may be relied on, other than what follows from the above.
Results may differ from the reference program's by a relative error of at most 0.013.
Values may be sent and summed in bfloat16 or wider, within the bound.
A program may use at most 256 MiB of HBM per device.

```python
import math
import jax
import jax.numpy as jnp
import numpy as np
from jax import lax

D = 768
H = 12
HD = 64
FF = 3072
SLOT = 1024
CELLS = 32
TOKENS = 32768


def shard_levels(stream_key, dims, cuts, least, largest):
    level, own = 1.0, jax.random.fold_in(stream_key, 6)
    for axis_at, blocks in cuts:
        draws = jnp.exp(jax.random.uniform(jax.random.fold_in(own, axis_at), (blocks,), jnp.float32, least / len(cuts), largest / len(cuts)))
        level = level * jnp.repeat(draws, dims[axis_at] // blocks).reshape([-1 if axis == axis_at else 1 for axis in range(len(dims))])
    return level


def split_up(number_of, total, most, slope):
    portions = [(1 << 20) // math.isqrt(standing ** slope) + 1 for standing in range(2, number_of + 1)]
    spare, given = total - most - (number_of - 1), [1] * (number_of - 1)
    while spare > 0:
        candidates = [i for i in range(number_of - 1) if given[i] < most]
        whole, budget = sum([portions[i] for i in candidates]), spare
        for i in candidates:
            addition = min(most - given[i], max(1, budget * portions[i] // whole), spare)
            given[i] = given[i] + addition
            spare = spare - addition
    return np.array([most] + given)


def uneven(key, count, total, bound, lean):
    if count == 2:
        one = jax.random.randint(key, (), max(1, total - bound), min(bound, total - 1) + 1)
        return jnp.stack([one, total - one])
    sizes = jnp.asarray(split_up(count, total, bound, lean), jnp.int32)
    couples = (count - 1) // 2
    giver, taker = sizes[1:1 + 2 * couples:2], sizes[2:2 + 2 * couples:2]
    slack = jnp.minimum(giver - 1, bound - taker)
    shifted = jax.random.randint(jax.random.fold_in(key, 1), (couples,), 0, 1 << 20) % (slack + 1)
    sizes = sizes.at[1:1 + 2 * couples:2].set(giver - shifted).at[2:2 + 2 * couples:2].set(taker + shifted)
    return sizes[jax.random.permutation(jax.random.fold_in(key, 2), count)]


def normal_values(key, shape, deviation, limit, pieces=(), kind=jnp.bfloat16):
    entries = jax.random.normal(key, shape, jnp.float32) * deviation
    if len(pieces) > 0:
        entries = shard_levels(key, shape, pieces, -0.22, 0.18) * entries
    return jnp.clip(entries, min=-limit, max=limit).astype(kind)


def setup_inputs(seed: int = 0) -> dict:
    key_of = jax.random.split(jax.random.key(seed), 16)
    tokens = normal_values(key_of[0], (TOKENS, D), 1.0, 6.0, ((0, 32),))
    lengths = uneven(key_of[1], CELLS, CELLS * SLOT * 3 // 4, SLOT, 2).astype(jnp.int32)
    cotangent = normal_values(key_of[2], (TOKENS, D), 1.0, 6.0, ((0, 32),))
    project_weight = normal_values(key_of[3], (D, 3 * D), D ** -0.5, 0.21875, ((0, 8), (1, 4)))
    project_bias = normal_values(key_of[4], (2 * D,), 0.2, 1.1953125, ((0, 8),))
    output_weight = normal_values(key_of[5], (D, D), (max(4 * D // SLOT, 1)) ** -0.5, 3.5, ((0, 8), (1, 4)))
    output_bias = normal_values(key_of[6], (D,), 0.2, 1.1953125, ((0, 8),))
    expand_weight = normal_values(key_of[7], (D, FF), D ** -0.5, 0.21875, ((0, 8), (1, 4)))
    expand_bias = normal_values(key_of[8], (FF,), 0.2, 1.1953125, ((0, 8),))
    contract_weight = normal_values(key_of[9], (FF, D), FF ** -0.5, 0.109375, ((0, 8), (1, 4)))
    contract_bias = normal_values(key_of[10], (D,), 0.2, 1.1953125, ((0, 8),))
    first_gain = jnp.clip(1.0 + 0.15 * jax.random.normal(key_of[11], (D,), jnp.float32), 0.25, 1.75).astype(jnp.bfloat16)
    first_shift = normal_values(key_of[12], (D,), 0.2, 1.1953125, ((0, 8),))
    second_gain = jnp.clip(1.0 + 0.15 * jax.random.normal(key_of[13], (D,), jnp.float32), 0.25, 1.75).astype(jnp.bfloat16)
    second_shift = normal_values(key_of[14], (D,), 0.2, 1.1953125, ((0, 8),))
    return {"tokens": tokens, "lengths": lengths, "cotangent": cotangent, "project_weight": project_weight, "project_bias": project_bias, "output_weight": output_weight, "output_bias": output_bias, "expand_weight": expand_weight, "expand_bias": expand_bias, "contract_weight": contract_weight, "contract_bias": contract_bias, "first_gain": first_gain, "first_shift": first_shift, "second_gain": second_gain, "second_shift": second_shift}


@jax.custom_vjp
def low(v):
    return lax.optimization_barrier(v.astype(jnp.bfloat16)).astype(jnp.float32)

@jax.custom_vjp
def low_back(v):
    return v

def low_keep(v):
    return (low(v), None)

def low_pass(kept, grad):
    return (grad,)

def back_keep(v):
    return (v, None)

def back_low(kept, grad):
    return (low(grad),)
low.defvjp(low_keep, low_pass)
low_back.defvjp(back_keep, back_low)
eps_norm = 1e-05
neg_fill = -1000000000.0
highest = lax.Precision.HIGHEST

def layer_norm(values, gain_row, shift_row):
    centre = lax.optimization_barrier(jnp.mean(values, axis=-1, keepdims=True))
    centred = values - centre
    spread = lax.optimization_barrier(jnp.mean(centred * centred, axis=-1, keepdims=True))
    return centred * lax.rsqrt(spread + eps_norm) * gain_row + shift_row

def cell_forward(params, rows_in, length):
    project_weight, project_bias, output_weight, output_bias, expand_weight, expand_bias, contract_weight, contract_bias, first_gain, first_shift, second_gain, second_shift = params
    positions = jnp.arange(SLOT, dtype=jnp.int32)
    live_rows = positions < length
    normed_one = low(layer_norm(rows_in, first_gain, first_shift))
    bias_full = jnp.concatenate([project_bias[:D], jnp.zeros((D,), jnp.float32), project_bias[D:]])
    projected = low(low_back(jnp.dot(normed_one, project_weight, precision=highest) + bias_full))
    queries = projected[:, :D].reshape(SLOT, H, HD)
    keys_all = projected[:, D:2 * D].reshape(SLOT, H, HD)
    values_all = projected[:, 2 * D:].reshape(SLOT, H, HD)
    scores = jnp.einsum('qhe,khe->hqk', queries, keys_all, precision=highest) * HD ** (-0.5)
    scores = low_back(scores)
    scores = jnp.where(live_rows[None, None, :], scores, neg_fill)
    weights = jax.nn.softmax(scores, axis=-1)
    mixed_rows = jnp.einsum('hqk,khe->qhe', low(weights), values_all, precision=highest).reshape(SLOT, D)
    mixed_rows = low(low_back(mixed_rows))
    branch = low_back(jnp.dot(mixed_rows, output_weight, precision=highest) + output_bias)
    middle = rows_in + branch
    normed_two = low(layer_norm(middle, second_gain, second_shift))
    hidden = low_back(jnp.dot(normed_two, expand_weight, precision=highest) + expand_bias)
    active = low(jax.nn.gelu(hidden, approximate=False))
    result = middle + (jnp.dot(active, contract_weight, precision=highest) + contract_bias)
    return jnp.where(live_rows[:, None], result, 0.0)

def reference(tokens, lengths, cotangent, project_weight, project_bias, output_weight, output_bias, expand_weight, expand_bias, contract_weight, contract_bias, first_gain, first_shift, second_gain, second_shift):
    params = tuple((item.astype(jnp.float32) for item in (project_weight, project_bias, output_weight, output_bias, expand_weight, expand_bias, contract_weight, contract_bias, first_gain, first_shift, second_gain, second_shift)))
    cells_in = tokens.astype(jnp.float32).reshape(CELLS, SLOT, D)
    cells_grad = cotangent.astype(jnp.float32).reshape(CELLS, SLOT, D)
    zeros_init = tuple((jnp.zeros_like(item) for item in params))

    def visit_cell(carried, inputs):
        cell_rows, cell_grad, length = inputs
        result, pull_back = jax.vjp(lambda weight_set, rows_in: cell_forward(weight_set, rows_in, length), params, cell_rows)
        grad_params, grad_rows = pull_back(cell_grad)
        carried = tuple((prior + extra for prior, extra in zip(carried, grad_params)))
        return (carried, (result.astype(jnp.bfloat16), grad_rows.astype(jnp.bfloat16)))
    totals, (outputs, grad_cells) = lax.scan(visit_cell, zeros_init, (cells_in, cells_grad, lengths))
    return (outputs.reshape(CELLS * SLOT, D), grad_cells.reshape(CELLS * SLOT, D), totals[0], totals[1], totals[2], totals[3], totals[4], totals[5], totals[6], totals[7], totals[8], totals[9], totals[10], totals[11])
```

```python
import functools
import jax
import jax.numpy as jnp
from jax import lax
from jax.experimental import pallas as pl
from jax.experimental.pallas import tpu as pltpu
from jax.sharding import PartitionSpec as P

H = 12
HD = 64
F32 = jnp.float32
BF = jnp.bfloat16
MESH = pl.DeviceIdType.MESH
eps_norm = 1e-05
neg_fill = -1000000000.0


def dot(first, second):
    return jnp.dot(first, second, preferred_element_type=F32)


def dot_nt(first, second):
    return lax.dot_general(first, second, (((1,), (1,)), ((), ())), preferred_element_type=F32)


def dot_tn(first, second):
    return lax.dot_general(first, second, (((0,), (0,)), ((), ())), preferred_element_type=F32)


def mo(value, multiple):
    return pl.multiple_of(value, multiple)


class Place:
    def __init__(self):
        self.d = lax.axis_index("dp")
        self.z = lax.axis_index("fsdp")
        core = lax.rem(self.d, 2)
        across = lax.rem(lax.div(self.d, 2), 2)
        up = lax.div(self.d, 4)
        self.dc = self.d + 1 - 2 * core
        self.dx = self.d + 2 - 4 * across
        self.dy = self.d + 4 - 8 * up
        self.dd = self.dx + 4 - 8 * up
        self.odd = lax.rem(self.z, 2)

    def zt(self, step):
        return lax.rem(self.z + step, 4)

    def zf(self, step):
        return lax.rem(self.z + 4 - step, 4)

    def id(self, to):
        if to == "x":
            return (self.dx, self.z)
        if to == "y":
            return (self.dy, self.z)
        if to == "c":
            return (self.dc, self.z)
        return (self.d, self.zt(to))


def enter(place):
    barrier = pltpu.get_barrier_semaphore()
    for to in ("x", "y", "c", 1, 2, 3):
        pl.semaphore_signal(barrier, inc=1, device_id=place.id(to), device_id_type=MESH)
    pl.semaphore_wait(barrier, 6)


class Link:
    def __init__(self, place, send_sem, recv_sem):
        self.place, self.send_sem, self.recv_sem = place, send_sem, recv_sem
        self.count = 0
        self.copies = []

    def slot(self):
        self.count += 1
        return self.count - 1

    def copy(self, slot, source, target, to):
        return pltpu.make_async_remote_copy(
            src_ref=source, dst_ref=target, send_sem=self.send_sem.at[slot],
            recv_sem=self.recv_sem.at[slot], device_id=self.place.id(to), device_id_type=MESH)

    def send(self, slot, source, target, to, like):
        self.copy(slot, source, target, to).start()
        self.copies.append((slot, like))

    def got(self, slot, target):
        self.copy(slot, target, target, "x").wait_recv()

    def finish(self):
        for slot, like in self.copies:
            view = like()
            self.copy(slot, view, view, "x").wait_send()


def gather_events(link, place, block):
    p = place
    zs = [link.slot() for _ in range(4)]
    xs = [link.slot() for _ in range(4)]
    ys = [link.slot() for _ in range(4)]
    fx = [link.slot() for _ in range(4)]
    cs = [[link.slot() for _ in range(4)] for _ in range(4)]
    got = link.got
    send = functools.partial(link.send, like=lambda: block(0, 0))

    def begin():
        own = block(p.z, p.d)
        for step in (1, 3, 2):
            send(zs[step], own, own, step)
        for slots, to in ((xs, "x"), (ys, "y")):
            send(slots[0], own, own, to)
        send(cs[0][0], own, own, "c")

    def onward(step):
        def run():
            here = block(p.zf(step), p.d)
            got(zs[step], here)
            for slots, to in ((xs, "x"), (ys, "y")):
                send(slots[step], here, here, to)
            send(cs[0][step], here, here, "c")
        return run

    def turn(step):
        def run():
            z = p.zf(step)
            bx, by = block(z, p.dx), block(z, p.dy)
            got(xs[step], bx)
            got(ys[step], by)
            if step in (0, 1):
                send(fx[step], bx, bx, "y")
            else:
                send(fx[step], by, by, "x")
            send(cs[1][step], bx, bx, "c")
            send(cs[2][step], by, by, "c")
        return run

    def corner(step):
        def run():
            z = p.zf(step)
            bd = block(z, p.dd)
            got(fx[step], bd)
            send(cs[3][step], bd, bd, "c")
        return run

    def close():
        dc = p.dc
        core = lax.rem(dc, 2)
        across = lax.rem(lax.div(dc, 2), 2)
        up = lax.div(dc, 4)
        cx = dc + 2 - 4 * across
        cy = dc + 4 - 8 * up
        cd = cx + 4 - 8 * up
        for which, d in enumerate((dc, cx, cy, cd)):
            for step in range(4):
                got(cs[which][step], block(p.zf(step), d))

    return ([begin, onward(1), onward(3), turn(0), onward(2), turn(1), turn(3), turn(2)]
            + [corner(0), corner(1), corner(3), corner(2), close])


def window(value, odd, wide):
    rows, k = value.shape
    fill = jnp.zeros((rows, wide - k), F32)
    value = value.astype(F32)
    left = jnp.concatenate([value, fill], axis=1)
    right = jnp.concatenate([fill, value], axis=1)
    return jnp.where(odd == 0, left, right).astype(BF)


def merge_windows(blocks, full, tiles, rows_step):
    rows = full.shape[0]
    half = tiles // 2

    def body(i, _):
        r = pl.ds(mo(i * rows_step, rows_step), rows_step)
        for pair in range(2):
            even, odd = blocks.at[2 * pair], blocks.at[2 * pair + 1]
            base = pair * tiles * 128
            full[r, base:base + half * 128] = even[r, 0:half * 128]
            full[r, base + half * 128:base + (half + 1) * 128] = (
                even[r, half * 128:(half + 1) * 128] + odd[r, 0:128])
            full[r, base + (half + 1) * 128:base + tiles * 128] = odd[r, 128:(half + 1) * 128]
        return 0

    lax.fori_loop(0, rows // rows_step, body, 0)


def split3(value):
    high = value.astype(BF)
    rest = value - high.astype(F32)
    mid = rest.astype(BF)
    low = (rest - mid.astype(F32)).astype(BF)
    return high.astype(F32), mid.astype(F32), low.astype(F32)


def extend(head, pair, lane, one, two, three, four):
    base = 64 * (1 - head)
    extra = jnp.where(lane == base, one, jnp.where(lane == base + 1, two, jnp.where(
        lane == base + 2, three, jnp.where(lane == base + 3, four, 0.0))))
    keep = (lane < 64) if head == 0 else (lane >= 64)
    return jnp.where(keep, pair, extra).astype(BF)


def iota(shape, axis):
    return lax.broadcasted_iota(jnp.int32, shape, axis)


QB = 512


def first_kernel(length_ref, x_ref, wp_ref, wo_ref, we_ref, vec_ref,
                 n1_out, proj_out, mixed_out, qa_out, wp_out, wo_out, we_out, v_out,
                 wp_blk, wo_blk, we, wp, wo, vb, n1, proj, mixed, qa, ka, va, vrow,
                 send_sem, recv_sem, out_sem):
    p = Place()
    T, D = x_ref.shape
    R = wp_ref.shape[0]
    FF = we.shape[1]
    link = Link(p, send_sem, recv_sem)
    rows_of = lambda d: pl.ds(mo(d * R, 16), R)
    bp = lambda z, d: wp_blk.at[z, rows_of(d), :]
    bo = lambda z, d: wo_blk.at[z, rows_of(d), :]
    be = lambda z, d: we.at[rows_of(d), pl.ds(mo(z * (FF // 4), 128), FF // 4)]
    ev_p, ev_o, ev_e = (gather_events(link, p, b) for b in (bp, bo, be))
    vs = [link.slot() for _ in range(7)]

    wp_blk[p.z, rows_of(p.d), :] = window(wp_ref[...], p.odd, wp_blk.shape[2])
    wo_blk[p.z, rows_of(p.d), :] = window(wo_ref[...], p.odd, wo_blk.shape[2])
    we[rows_of(p.d), pl.ds(mo(p.z * (FF // 4), 128), FF // 4)] = we_ref[...]
    vb[p.d] = vec_ref[...]

    outs = []

    def out(source, target):
        made = pltpu.make_async_copy(source, target, out_sem.at[len(outs)])
        made.start()
        outs.append(made)

    enter(p)
    send_v = lambda slot, d, to: link.send(vs[slot], vb.at[d], vb.at[d], to, lambda: vb.at[0])
    for slot, to in ((0, "x"), (1, "y"), (3, "c")):
        send_v(slot, p.d, to)
    ev_p[0]()
    link.got(vs[0], vb.at[p.dx])
    link.got(vs[1], vb.at[p.dy])
    send_v(2, p.dx, "y")
    send_v(4, p.dx, "c")
    send_v(5, p.dy, "c")
    ev_p[1]()
    ev_p[2]()
    link.got(vs[2], vb.at[p.dd])
    send_v(6, p.dd, "c")
    ev_p[3]()
    ev_p[4]()
    dc = p.dc
    link.got(vs[3], vb.at[dc])
    cx = p.dx + p.dc - p.d
    cy = p.dy + p.dc - p.d
    cd = p.dd + p.dc - p.d
    link.got(vs[4], vb.at[cx])
    link.got(vs[5], vb.at[cy])
    link.got(vs[6], vb.at[cd])
    got = vb[...].astype(F32)
    side = lambda row, wide: jnp.concatenate([got[i, row:row + 1, 0:wide] for i in range(8)], axis=1)
    bias = side(0, 2 * R)
    vrow[0:1, 0:D] = bias[:, 0:D]
    vrow[0:1, D:2 * D] = jnp.zeros((1, D), F32)
    vrow[0:1, 2 * D:3 * D] = bias[:, D:]
    vrow[1:2, :] = side(2, FF // 8)
    for row, at in ((2, 1), (3, 3), (4, 4), (5, 5), (6, 6), (7, 7)):
        vrow[row:row + 1, 0:D] = side(at, R)
    out(vrow, v_out)
    ev_p[5]()

    LR = 128
    gain, shift = vrow[4:5, 0:D], vrow[5:6, 0:D]

    def norm_body(i, _):
        r = pl.ds(mo(i * LR, LR), LR)
        value = x_ref[r, :].astype(F32)
        u = value - jnp.mean(value, axis=-1, keepdims=True)
        spread = jnp.mean(u * u, axis=-1, keepdims=True)
        n1[r, :] = (u * lax.rsqrt(spread + eps_norm) * gain + shift).astype(BF)
        return 0

    lax.fori_loop(0, T // LR, norm_body, 0)
    out(n1, n1_out)
    for event in ev_p[6:]:
        event()
    ev_o[0]()
    merge_windows(wp_blk, wp, 9, 96)
    out(wp, wp_out)
    ev_o[1]()
    ev_o[2]()

    def project_body(i, _):
        r = pl.ds(mo(i * 256, 256), 256)
        left = n1[r, :]
        for j in range(3):
            cols = slice(j * D, (j + 1) * D)
            value = dot(left, wp[:, cols]) + vrow[0:1, cols]
            proj[r, cols] = value.astype(BF)
        return 0

    lax.fori_loop(0, T // 256, project_body, 0)
    out(proj, proj_out)

    length = length_ref[0]
    nq = T // QB

    def attend_steps(events):
        def body(step, _):
            for at, event in events:
                pl.when(step == at)(event)
            pair = lax.div(step, nq)
            part = lax.rem(step, nq)
            cols = lambda off: pl.ds(mo(off + pair * 128, 128), 128)

            @pl.when(part == 0)
            def _():
                lane, row = iota((T, 128), 1), iota((T, 128), 0)
                q = proj[:, cols(0)].astype(F32) * (HD ** -0.5)
                k = proj[:, cols(D)].astype(F32)
                v = proj[:, cols(2 * D)].astype(F32)
                dead = jnp.where(row < length, 0.0, neg_fill)
                for head in range(2):
                    ka[head] = extend(head, k, lane, 1.0, 1.0, 1.0, dead)
                    qa[pair * 2 + head] = extend(head, q, lane, 0.0, 0.0, 0.0, 1.0)
                    keep = (lane < 64) if head == 0 else (lane >= 64)
                    va[head] = jnp.where(keep, v, 1.0).astype(BF)

            r = pl.ds(mo(part * QB, QB), QB)
            lane = iota((QB, 128), 1)
            halves = []
            for head in range(2):
                query = qa[pair * 2 + head, r, :]
                scores = dot_nt(query, ka[head])
                top = jnp.max(scores, axis=-1, keepdims=True)
                powers = jnp.exp(scores - top).astype(BF)
                value = dot(powers, va[head])
                total = value[:, 64:65] if head == 0 else value[:, 0:1]
                one, two, three = split3(-(top + jnp.log(total)))
                qa[pair * 2 + head, r, :] = extend(head, query.astype(F32), lane, one, two, three, 1.0)
                halves.append(value * (1.0 / total))
            mixed[r, cols(0)] = jnp.where(lane < 64, halves[0], halves[1]).astype(BF)
            return 0

        lax.fori_loop(0, (H // 2) * nq, body, 0)

    rest = ev_o[3:] + ev_e
    spots = [0, 0, 0, 0, 1, 1, 1, 1, 1, 1] + [2, 3, 3, 4, 4, 5, 5, 6, 7, 8, 8, 9, 10]
    assert len(rest) == len(spots)
    attend_steps(list(zip(spots, rest)))
    merge_windows(wo_blk, wo, 3, 96)
    out(wo, wo_out)
    out(we, we_out)
    out(mixed, mixed_out)
    out(qa, qa_out)
    link.finish()
    for made in outs:
        made.wait()


def first_call(length, x, wp, wo, we, vec):
    T, D = x.shape
    FF = we.shape[1] * 4
    ANY = pl.BlockSpec(memory_space=pl.ANY)
    V = pl.BlockSpec(memory_space=pltpu.VMEM)
    S = pl.BlockSpec(memory_space=pltpu.SMEM)
    sds = jax.ShapeDtypeStruct
    n = 3 * 32 + 7
    return pl.pallas_call(
        first_kernel,
        in_specs=[S, V, V, V, V, V],
        out_specs=[ANY] * 8,
        out_shape=[sds((T, D), BF), sds((T, 3 * D), BF), sds((T, D), BF), sds((H, T, 128), BF),
                   sds((D, 3 * D), BF), sds((D, D), BF), sds((D, FF), BF), sds((8, FF), F32)],
        scratch_shapes=[
            pltpu.VMEM((4, D, 640), BF), pltpu.VMEM((4, D, 256), BF), pltpu.VMEM((D, FF), BF),
            pltpu.VMEM((D, 3 * D), BF), pltpu.VMEM((D, D), BF), pltpu.VMEM((8,) + vec.shape, BF),
            pltpu.VMEM((T, D), BF), pltpu.VMEM((T, 3 * D), BF), pltpu.VMEM((T, D), BF),
            pltpu.VMEM((H, T, 128), BF), pltpu.VMEM((2, T, 128), BF), pltpu.VMEM((2, T, 128), BF),
            pltpu.VMEM((8, FF), F32),
            pltpu.SemaphoreType.DMA((n,)), pltpu.SemaphoreType.DMA((n,)), pltpu.SemaphoreType.DMA((8,)),
        ],
        compiler_params=pltpu.CompilerParams(
            collective_id=0, has_side_effects=True, vmem_limit_bytes=60 << 20),
        name="first_part",
    )(length, x, wp, wo, we, vec)


def pack_vectors(project_bias, output_bias, expand_bias, contract_bias, g1, s1, g2, s2):
    wide = expand_bias.shape[0]
    rows = [jnp.pad(v, (0, wide - v.shape[0])) for v in
            (project_bias, output_bias, expand_bias, contract_bias, g1, s1, g2, s2)]
    return jnp.pad(jnp.stack(rows), ((0, 8), (0, 0)))


def layer_norm(values, gain_row, shift_row):
    centre = jnp.mean(values, axis=-1, keepdims=True)
    centred = values - centre
    spread = jnp.mean(centred * centred, axis=-1, keepdims=True)
    return centred * lax.rsqrt(spread + eps_norm) * gain_row + shift_row


def gelu_exact(values):
    return jax.nn.gelu(values, approximate=False)


def matmul(first, second):
    return jnp.dot(first, second, preferred_element_type=jnp.float32)


def over_rows(first, second):
    return lax.dot_general(
        first, second, (((0,), (0,)), ((), ())), preferred_element_type=jnp.float32
    )


def over_columns(first, second):
    return lax.dot_general(
        first, second, (((1,), (1,)), ((), ())), preferred_element_type=jnp.float32
    )


def fetch_forward(
    project_weight,
    output_weight,
    expand_weight,
    contract_weight,
    project_bias,
    output_bias,
    expand_bias,
    contract_bias,
    first_gain,
    first_shift,
    second_gain,
    second_shift,
):
    wide_project, wide_output, wide_expand, wide_contract = (
        lax.all_gather(project_weight, "fsdp", axis=1, tiled=True),
        lax.all_gather(output_weight, "fsdp", axis=1, tiled=True),
        lax.all_gather(expand_weight, "fsdp", axis=1, tiled=True),
        lax.all_gather(contract_weight, "fsdp", axis=1, tiled=True),
    )
    return (
        lax.all_gather(wide_project, "dp", axis=0, tiled=True),
        lax.all_gather(wide_output, "dp", axis=0, tiled=True),
        lax.all_gather(wide_expand, "dp", axis=0, tiled=True),
        lax.all_gather(wide_contract, "dp", axis=0, tiled=True),
        lax.all_gather(project_bias, "dp", axis=0, tiled=True),
        lax.all_gather(output_bias, "dp", axis=0, tiled=True),
        lax.all_gather(expand_bias, "dp", axis=0, tiled=True),
        lax.all_gather(contract_bias, "dp", axis=0, tiled=True),
        lax.all_gather(first_gain, "dp", axis=0, tiled=True),
        lax.all_gather(first_shift, "dp", axis=0, tiled=True),
        lax.all_gather(second_gain, "dp", axis=0, tiled=True),
        lax.all_gather(second_shift, "dp", axis=0, tiled=True),
    )


def fetch_backward(
    project_weight,
    output_weight,
    expand_weight,
    contract_weight,
    project_bias,
    output_bias,
    expand_bias,
    contract_bias,
    first_gain,
    first_shift,
    second_gain,
    second_shift,
):
    wide_project, wide_output, wide_expand, wide_contract = (
        lax.all_gather(project_weight, "fsdp", axis=1, tiled=True),
        lax.all_gather(output_weight, "fsdp", axis=1, tiled=True),
        lax.all_gather(expand_weight, "fsdp", axis=1, tiled=True),
        lax.all_gather(contract_weight, "fsdp", axis=1, tiled=True),
    )
    return (
        lax.all_gather(wide_project, "dp", axis=0, tiled=True),
        lax.all_gather(wide_output, "dp", axis=0, tiled=True),
        lax.all_gather(wide_expand, "dp", axis=0, tiled=True),
        lax.all_gather(wide_contract, "dp", axis=0, tiled=True),
        lax.all_gather(project_bias, "dp", axis=0, tiled=True),
        lax.all_gather(output_bias, "dp", axis=0, tiled=True),
        lax.all_gather(expand_bias, "dp", axis=0, tiled=True),
        lax.all_gather(contract_bias, "dp", axis=0, tiled=True),
        lax.all_gather(first_gain, "dp", axis=0, tiled=True),
        lax.all_gather(first_shift, "dp", axis=0, tiled=True),
        lax.all_gather(second_gain, "dp", axis=0, tiled=True),
        lax.all_gather(second_shift, "dp", axis=0, tiled=True),
    )


def split_heads(cell_rows, block_rows):
    slot_count = cell_rows.shape[0]
    width = cell_rows.shape[1] // 3
    query_blocks = cell_rows[:, :width].reshape(slot_count // block_rows, block_rows, H, HD)
    keys_all = cell_rows[:, width : 2 * width].reshape(slot_count, H, HD)
    values_all = cell_rows[:, 2 * width :].reshape(slot_count, H, HD)
    return (query_blocks, keys_all, values_all)


def block_scores(query_block, keys_all, key_live):
    scores = jnp.einsum(
        "qhe,khe->hqk", query_block, keys_all, preferred_element_type=jnp.float32
    ) * HD ** (-0.5)
    return jnp.where(key_live[None, None, :], scores, neg_fill)


def attend_forward(query_block, keys_all, values_all, key_live):
    scores = block_scores(query_block, keys_all, key_live)
    row_max = jnp.max(scores, axis=-1, keepdims=True)
    powers = jnp.exp(scores - row_max)
    row_total = jnp.sum(powers, axis=-1, keepdims=True)
    weights = (powers / row_total).astype(jnp.bfloat16)
    mixed_block = jnp.einsum(
        "hqk,khe->qhe", weights, values_all, preferred_element_type=jnp.float32
    )
    return (mixed_block, (row_max + jnp.log(row_total))[:, :, 0])


def attend_backward(query_block, grad_block, log_block, keys_all, values_all, key_live):
    scores = block_scores(query_block, keys_all, key_live)
    weights = jnp.exp(scores - log_block[:, :, None])
    grad_weights = jnp.einsum(
        "qhe,khe->hqk", grad_block, values_all, preferred_element_type=jnp.float32
    )
    row_inner = jnp.sum(grad_weights * weights, axis=-1, keepdims=True)
    grad_scores = (weights * (grad_weights - row_inner)).astype(jnp.bfloat16)
    grad_query = jnp.einsum(
        "hqk,khe->qhe", grad_scores, keys_all, preferred_element_type=jnp.float32
    ) * HD ** (-0.5)
    grad_key = jnp.einsum(
        "hqk,qhe->khe", grad_scores, query_block, preferred_element_type=jnp.float32
    ) * HD ** (-0.5)
    grad_value = jnp.einsum(
        "hqk,qhe->khe", weights.astype(jnp.bfloat16), grad_block, preferred_element_type=jnp.float32
    )
    return (grad_query, grad_key, grad_value)


def per_device(
    tokens,
    lengths,
    cotangent,
    project_weight,
    project_bias,
    output_weight,
    output_bias,
    expand_weight,
    expand_bias,
    contract_weight,
    contract_bias,
    first_gain,
    first_shift,
    second_gain,
    second_shift,
):
    fetched = fetch_forward(
        project_weight,
        output_weight,
        expand_weight,
        contract_weight,
        project_bias,
        output_bias,
        expand_bias,
        contract_bias,
        first_gain,
        first_shift,
        second_gain,
        second_shift,
    )
    full_project, full_output, full_expand, full_contract = (
        fetched[0],
        fetched[1],
        fetched[2],
        fetched[3],
    )
    vectors = [item.astype(jnp.float32) for item in fetched[4:]]
    bias_project, bias_output, bias_expand, bias_contract = (
        vectors[0],
        vectors[1],
        vectors[2],
        vectors[3],
    )
    gain_one, shift_one, gain_two, shift_two = (vectors[4], vectors[5], vectors[6], vectors[7])
    cell_count = lengths.shape[0]
    slot_count = tokens.shape[0] // cell_count
    width = tokens.shape[1]
    block_rows = min(512, slot_count)
    positions = jnp.arange(slot_count, dtype=jnp.int32)
    live_keys = positions[None, :] < lengths[:, None]
    live_rows = live_keys.reshape(-1)
    rows_in = tokens.astype(jnp.float32)
    normed_one = layer_norm(rows_in, gain_one, shift_one).astype(jnp.bfloat16)
    bias_full = jnp.concatenate(
        [bias_project[:width], jnp.zeros((width,), jnp.float32), bias_project[width:]]
    )
    projected = (matmul(normed_one, full_project) + bias_full).astype(jnp.bfloat16)
    cell_index = 0
    query_blocks, keys_all, values_all = split_heads(projected, block_rows)
    key_live = live_keys[cell_index]
    mixed_blocks, log_blocks = lax.map(
        lambda query_block: attend_forward(query_block, keys_all, values_all, key_live),
        query_blocks,
    )
    mixed_list = mixed_blocks.reshape(slot_count, width)
    log_list = [log_blocks]
    mixed_low = mixed_list.astype(jnp.bfloat16)
    middle = rows_in + (matmul(mixed_low, full_output) + bias_output)
    normed_two = layer_norm(middle, gain_two, shift_two).astype(jnp.bfloat16)
    hidden = matmul(normed_two, full_expand) + bias_expand
    active = gelu_exact(hidden).astype(jnp.bfloat16)
    result = middle + (matmul(active, full_contract) + bias_contract)
    block_out = jnp.where(live_rows[:, None], result, 0.0).astype(jnp.bfloat16)
    again = fetch_backward(
        project_weight,
        output_weight,
        expand_weight,
        contract_weight,
        project_bias,
        output_bias,
        expand_bias,
        contract_bias,
        first_gain,
        first_shift,
        second_gain,
        second_shift,
    )
    back_project, back_output, back_expand, back_contract = (again[0], again[1], again[2], again[3])
    grad_out = jnp.where(live_rows[:, None], cotangent.astype(jnp.float32), 0.0)
    grad_out_low = grad_out.astype(jnp.bfloat16)
    grad_contract = over_rows(active, grad_out_low)
    grad_contract_bias = jnp.sum(grad_out, axis=0)
    grad_active = over_columns(grad_out_low, back_contract)
    gelu_value, gelu_pull = jax.vjp(gelu_exact, hidden)
    grad_hidden = gelu_pull(grad_active)[0].astype(jnp.bfloat16)
    grad_expand = over_rows(normed_two, grad_hidden)
    grad_expand_bias = jnp.sum(grad_hidden.astype(jnp.float32), axis=0)
    grad_normed_two = over_columns(grad_hidden, back_expand)
    norm_value, second_pull = jax.vjp(layer_norm, middle, gain_two, shift_two)
    grad_middle, grad_gain_two, grad_shift_two = second_pull(grad_normed_two)
    grad_middle = grad_middle + grad_out
    grad_branch = grad_middle.astype(jnp.bfloat16)
    grad_output = over_rows(mixed_low, grad_branch)
    grad_output_bias = jnp.sum(grad_branch.astype(jnp.float32), axis=0)
    grad_mixed = over_columns(grad_branch, back_output).astype(jnp.bfloat16)
    cell_index = 0
    query_blocks, keys_all, values_all = split_heads(projected, block_rows)
    key_live = live_keys[cell_index]
    grad_blocks = grad_mixed.reshape(slot_count // block_rows, block_rows, H, HD)

    def visit_block(carried, inputs):
        query_block, grad_block, log_block = inputs
        grad_query, grad_key, grad_value = attend_backward(
            query_block, grad_block, log_block, keys_all, values_all, key_live
        )
        return ((carried[0] + grad_key, carried[1] + grad_value), grad_query)

    initial = (
        jnp.zeros((slot_count, H, HD), jnp.float32),
        jnp.zeros((slot_count, H, HD), jnp.float32),
    )
    (key_sums, value_sums), query_grads = lax.scan(
        visit_block, initial, (query_blocks, grad_blocks, log_list[cell_index])
    )
    grad_cells = jnp.concatenate(
        [
            query_grads.reshape(slot_count, width),
            key_sums.reshape(slot_count, width),
            value_sums.reshape(slot_count, width),
        ],
        axis=1,
    )
    grad_projected = grad_cells.astype(jnp.bfloat16)
    grad_project = over_rows(normed_one, grad_projected)
    column_sums = jnp.sum(grad_projected.astype(jnp.float32), axis=0)
    grad_project_bias = jnp.concatenate([column_sums[:width], column_sums[2 * width :]])
    grad_normed_one = over_columns(grad_projected, back_project)
    first_value, first_pull = jax.vjp(layer_norm, rows_in, gain_one, shift_one)
    grad_rows_in, grad_gain_one, grad_shift_one = first_pull(grad_normed_one)
    tokens_grad = (grad_rows_in + grad_middle).astype(jnp.bfloat16)
    reduced = (
        lax.psum_scatter(grad_project, "dp", scatter_dimension=0, tiled=True),
        lax.psum_scatter(grad_output, "dp", scatter_dimension=0, tiled=True),
        lax.psum_scatter(grad_expand, "dp", scatter_dimension=0, tiled=True),
        lax.psum_scatter(grad_contract, "dp", scatter_dimension=0, tiled=True),
        lax.psum_scatter(grad_project_bias, "dp", scatter_dimension=0, tiled=True),
        lax.psum_scatter(grad_output_bias, "dp", scatter_dimension=0, tiled=True),
        lax.psum_scatter(grad_expand_bias, "dp", scatter_dimension=0, tiled=True),
        lax.psum_scatter(grad_contract_bias, "dp", scatter_dimension=0, tiled=True),
        lax.psum_scatter(grad_gain_one, "dp", scatter_dimension=0, tiled=True),
        lax.psum_scatter(grad_shift_one, "dp", scatter_dimension=0, tiled=True),
        lax.psum_scatter(grad_gain_two, "dp", scatter_dimension=0, tiled=True),
        lax.psum_scatter(grad_shift_two, "dp", scatter_dimension=0, tiled=True),
    )
    shard_project, shard_output, shard_expand, shard_contract = (
        lax.psum_scatter(
            reduced[0].astype(jnp.bfloat16), "fsdp", scatter_dimension=1, tiled=True
        ).astype(jnp.float32),
        lax.psum_scatter(
            reduced[1].astype(jnp.bfloat16), "fsdp", scatter_dimension=1, tiled=True
        ).astype(jnp.float32),
        lax.psum_scatter(
            reduced[2].astype(jnp.bfloat16), "fsdp", scatter_dimension=1, tiled=True
        ).astype(jnp.float32),
        lax.psum_scatter(
            reduced[3].astype(jnp.bfloat16), "fsdp", scatter_dimension=1, tiled=True
        ).astype(jnp.float32),
    )
    summed = lax.psum(
        (
            reduced[4],
            reduced[5],
            reduced[6],
            reduced[7],
            reduced[8],
            reduced[9],
            reduced[10],
            reduced[11],
        ),
        "fsdp",
    )
    return (
        block_out,
        tokens_grad,
        shard_project,
        summed[0],
        shard_output,
        summed[1],
        shard_expand,
        summed[2],
        shard_contract,
        summed[3],
        summed[4],
        summed[5],
        summed[6],
        summed[7],
    )


def back_kernel(length_ref, proj_ref, mixed_ref, qa_ref, dm_ref, dproj_ref, ka_ref, da_ref, dq_ref, va_ref, kT_ref):
    length = length_ref[0]
    T, D = mixed_ref.shape
    KB = 256

    def pair_body(p, _):
        lane, row = iota((T, 128), 1), iota((T, 128), 0)
        ps = lambda off: pl.ds(mo(off + p * 128, 128), 128)
        k = proj_ref[:, ps(D)].astype(F32)
        v = proj_ref[:, ps(2 * D)].astype(F32)
        do = dm_ref[:, ps(0)].astype(F32)
        pr = do * mixed_ref[:, ps(0)].astype(F32)
        dead = jnp.where(row < length, 0.0, neg_fill)
        for head in range(2):
            keep = (lane < 64) if head == 0 else (lane >= 64)
            delta = jnp.sum(jnp.where(keep, pr, 0.0), axis=-1, keepdims=True)
            one, two, three = split3(-delta)
            da_ref[head] = extend(head, do, lane, one, two, three, 0.0)
            ka_ref[head] = extend(head, k, lane, 1.0, 1.0, 1.0, dead)
            va_ref[head] = extend(head, v, lane, 1.0, 1.0, 1.0, 0.0)
            kT_ref[head] = jnp.where(keep, k, 0.0).astype(BF).T
        dq_ref[...] = jnp.zeros_like(dq_ref)

        def kblk(i, _):
            rows = pl.ds(mo(i * KB, KB), KB)
            lk = iota((KB, 128), 1)
            dks, dvs = [], []
            for head in range(2):
                weights = jnp.exp(dot_nt(ka_ref[head, rows, :], qa_ref[p * 2 + head]))
                low = weights.astype(BF)
                ds = (weights * dot_nt(va_ref[head, rows, :], da_ref[head])).astype(BF)
                dvs.append(dot(low, da_ref[head]))
                dks.append(dot(ds, qa_ref[p * 2 + head]))
                dq_ref[head] += dot(kT_ref[head, :, rows], ds)
            dproj_ref[rows, ps(D)] = jnp.where(lk < 64, dks[0], dks[1]).astype(BF)
            dproj_ref[rows, ps(2 * D)] = jnp.where(lk < 64, dvs[0], dvs[1]).astype(BF)
            return 0

        lax.fori_loop(0, T // KB, kblk, 0)
        dproj_ref[:, ps(0)] = ((dq_ref[0] + dq_ref[1]) * (HD ** -0.5)).T.astype(BF)
        return 0

    lax.fori_loop(0, H // 2, pair_body, 0)


def back_call(length, proj, mixed, qa, dm):
    T, D = mixed.shape
    V = pl.BlockSpec(memory_space=pltpu.VMEM)
    return pl.pallas_call(
        back_kernel, in_specs=[pl.BlockSpec(memory_space=pltpu.SMEM), V, V, V, V], out_specs=V,
        out_shape=jax.ShapeDtypeStruct((T, 3 * D), BF),
        scratch_shapes=[pltpu.VMEM((2, T, 128), BF), pltpu.VMEM((2, T, 128), BF), pltpu.VMEM((2, 128, T), F32),
                        pltpu.VMEM((2, T, 128), BF), pltpu.VMEM((2, 128, T), BF)],
        compiler_params=pltpu.CompilerParams(vmem_limit_bytes=60 << 20), name="back_part")(
            length, proj, mixed, qa, dm)


def per_device_fast(tokens, lengths, cotangent, project_weight, project_bias, output_weight, output_bias,
                    expand_weight, expand_bias, contract_weight, contract_bias, first_gain, first_shift,
                    second_gain, second_shift):
    T, D = tokens.shape
    wide = lax.all_gather(contract_weight, "fsdp", axis=1, tiled=True)
    full_contract = lax.all_gather(wide, "dp", axis=0, tiled=True)
    vec = pack_vectors(project_bias, output_bias, expand_bias, contract_bias,
                       first_gain, first_shift, second_gain, second_shift)
    normed_one, projected, mixed_low, qa, full_project, full_output, full_expand, v = first_call(
        lengths, tokens, project_weight, output_weight, expand_weight, vec)
    bias_expand = v[1]
    bias_output, bias_contract, gain_one, shift_one, gain_two, shift_two = [v[i, :D] for i in range(2, 8)]
    live = (jnp.arange(T) < lengths[0])[:, None]
    rows_in = tokens.astype(F32)
    middle = rows_in + (matmul(mixed_low, full_output) + bias_output)
    normed_two = layer_norm(middle, gain_two, shift_two).astype(BF)
    hidden = matmul(normed_two, full_expand) + bias_expand
    active = gelu_exact(hidden).astype(BF)
    result = middle + (matmul(active, full_contract) + bias_contract)
    block_out = jnp.where(live, result, 0.0).astype(BF)
    grad_out = jnp.where(live, cotangent.astype(F32), 0.0)
    grad_out_low = grad_out.astype(BF)
    grad_contract = over_rows(active, grad_out_low)
    grad_contract_bias = jnp.sum(grad_out, axis=0)
    grad_active = over_columns(grad_out_low, full_contract)
    gelu_value, gelu_pull = jax.vjp(gelu_exact, hidden)
    grad_hidden = gelu_pull(grad_active)[0].astype(BF)
    grad_expand = over_rows(normed_two, grad_hidden)
    grad_expand_bias = jnp.sum(grad_hidden.astype(F32), axis=0)
    grad_normed_two = over_columns(grad_hidden, full_expand)
    norm_value, second_pull = jax.vjp(layer_norm, middle, gain_two, shift_two)
    grad_middle, grad_gain_two, grad_shift_two = second_pull(grad_normed_two)
    grad_middle = grad_middle + grad_out
    grad_branch = grad_middle.astype(BF)
    grad_output = over_rows(mixed_low, grad_branch)
    grad_output_bias = jnp.sum(grad_branch.astype(F32), axis=0)
    grad_mixed = over_columns(grad_branch, full_output).astype(BF)
    grad_projected = back_call(lengths, projected, mixed_low, qa, grad_mixed)
    grad_project = over_rows(normed_one, grad_projected)
    column_sums = jnp.sum(grad_projected.astype(F32), axis=0)
    grad_project_bias = jnp.concatenate([column_sums[:D], column_sums[2 * D:]])
    grad_normed_one = over_columns(grad_projected, full_project)
    first_value, first_pull = jax.vjp(layer_norm, rows_in, gain_one, shift_one)
    grad_rows_in, grad_gain_one, grad_shift_one = first_pull(grad_normed_one)
    tokens_grad = (grad_rows_in + grad_middle).astype(BF)

    def scatter(g):
        g = lax.psum_scatter(g.astype(BF), "dp", scatter_dimension=0, tiled=True)
        return lax.psum_scatter(g, "fsdp", scatter_dimension=1, tiled=True).astype(F32)

    small = (grad_project_bias, grad_output_bias, grad_expand_bias, grad_contract_bias,
             grad_gain_one, grad_shift_one, grad_gain_two, grad_shift_two)
    total = lax.psum(jnp.concatenate(small), ("dp", "fsdp"))
    d = lax.axis_index("dp")
    picked, at = [], 0
    for item in small:
        n = item.shape[0]
        picked.append(lax.dynamic_slice(total, (at + d * (n // 8),), (n // 8,)))
        at += n
    return (block_out, tokens_grad, scatter(grad_project), picked[0], scatter(grad_output), picked[1],
            scatter(grad_expand), picked[2], scatter(grad_contract), picked[3],
            picked[4], picked[5], picked[6], picked[7])


def solution(mesh):
    both, rows, grid = P(("dp", "fsdp"), None), P("dp"), P("dp", "fsdp")
    weights = (grid, rows, grid, rows, grid, rows, grid, rows)
    fast = mesh.shape["dp"] == 8 and mesh.shape["fsdp"] == 4
    return jax.shard_map(
        per_device_fast if fast else per_device,
        mesh=mesh,
        in_specs=(both, P(("dp", "fsdp")), both) + weights + (rows,) * 4,
        out_specs=(both, both) + weights + (rows,) * 4,
        check_vma=False,
    )
```

```python
import functools
import jax
import jax.numpy as jnp
from jax import lax
from jax.experimental import pallas as pl
from jax.experimental.pallas import tpu as pltpu
from jax.sharding import PartitionSpec as P

H = 12
HD = 64
F32 = jnp.float32
BF = jnp.bfloat16
MESH = pl.DeviceIdType.MESH
eps_norm = 1e-05
neg_fill = -1000000000.0


def dot(first, second):
    return jnp.dot(first, second, preferred_element_type=F32)


def dot_nt(first, second):
    return lax.dot_general(first, second, (((1,), (1,)), ((), ())), preferred_element_type=F32)


def dot_tn(first, second):
    return lax.dot_general(first, second, (((0,), (0,)), ((), ())), preferred_element_type=F32)


def mo(value, multiple):
    return pl.multiple_of(value, multiple)


class Place:
    def __init__(self):
        self.d = lax.axis_index("dp")
        self.z = lax.axis_index("fsdp")
        core = lax.rem(self.d, 2)
        across = lax.rem(lax.div(self.d, 2), 2)
        up = lax.div(self.d, 4)
        self.dc = self.d + 1 - 2 * core
        self.dx = self.d + 2 - 4 * across
        self.dy = self.d + 4 - 8 * up
        self.dd = self.dx + 4 - 8 * up
        self.odd = lax.rem(self.z, 2)

    def zt(self, step):
        return lax.rem(self.z + step, 4)

    def zf(self, step):
        return lax.rem(self.z + 4 - step, 4)

    def id(self, to):
        if to == "x":
            return (self.dx, self.z)
        if to == "y":
            return (self.dy, self.z)
        if to == "c":
            return (self.dc, self.z)
        if isinstance(to, tuple):
            return (self.d, to[1])
        return (self.d, self.zt(to))


def enter(place):
    barrier = pltpu.get_barrier_semaphore()
    for to in ("x", "y", "c", 1, 2, 3):
        pl.semaphore_signal(barrier, inc=1, device_id=place.id(to), device_id_type=MESH)
    pl.semaphore_wait(barrier, 6)


class Link:
    def __init__(self, place, send_sem, recv_sem):
        self.place, self.send_sem, self.recv_sem = place, send_sem, recv_sem
        self.count = 0
        self.copies = []

    def slot(self):
        self.count += 1
        return self.count - 1

    def copy(self, slot, source, target, to):
        return pltpu.make_async_remote_copy(
            src_ref=source, dst_ref=target, send_sem=self.send_sem.at[slot],
            recv_sem=self.recv_sem.at[slot], device_id=self.place.id(to), device_id_type=MESH)

    def send(self, slot, source, target, to, like):
        self.copy(slot, source, target, to).start()
        self.copies.append((slot, like))

    def got(self, slot, target):
        self.copy(slot, target, target, "x").wait_recv()

    def finish(self):
        for slot, like in self.copies:
            view = like()
            self.copy(slot, view, view, "x").wait_send()


def gather_events(link, place, block):
    p = place
    zs = [link.slot() for _ in range(4)]
    xs = [link.slot() for _ in range(4)]
    ys = [link.slot() for _ in range(4)]
    fx = [link.slot() for _ in range(4)]
    cs = [[link.slot() for _ in range(4)] for _ in range(4)]
    got = link.got
    send = functools.partial(link.send, like=lambda: block(0, 0))

    def begin():
        own = block(p.z, p.d)
        for step in (1, 3, 2):
            send(zs[step], own, own, step)
        for slots, to in ((xs, "x"), (ys, "y")):
            send(slots[0], own, own, to)
        send(cs[0][0], own, own, "c")

    def onward(step):
        def run():
            here = block(p.zf(step), p.d)
            got(zs[step], here)
            for slots, to in ((xs, "x"), (ys, "y")):
                send(slots[step], here, here, to)
            send(cs[0][step], here, here, "c")
        return run

    def turn(step):
        def run():
            z = p.zf(step)
            bx, by = block(z, p.dx), block(z, p.dy)
            got(xs[step], bx)
            got(ys[step], by)
            if step in (0, 1):
                send(fx[step], bx, bx, "y")
            else:
                send(fx[step], by, by, "x")
            send(cs[1][step], bx, bx, "c")
            send(cs[2][step], by, by, "c")
        return run

    def corner(step):
        def run():
            z = p.zf(step)
            bd = block(z, p.dd)
            got(fx[step], bd)
            send(cs[3][step], bd, bd, "c")
        return run

    def close():
        dc = p.dc
        core = lax.rem(dc, 2)
        across = lax.rem(lax.div(dc, 2), 2)
        up = lax.div(dc, 4)
        cx = dc + 2 - 4 * across
        cy = dc + 4 - 8 * up
        cd = cx + 4 - 8 * up
        for which, d in enumerate((dc, cx, cy, cd)):
            for step in range(4):
                got(cs[which][step], block(p.zf(step), d))

    return ([begin, onward(1), onward(3), turn(0), onward(2), turn(1), turn(3), turn(2)]
            + [corner(0), corner(1), corner(3), corner(2), close])


def window(value, odd, wide):
    rows, k = value.shape
    fill = jnp.zeros((rows, wide - k), F32)
    value = value.astype(F32)
    left = jnp.concatenate([value, fill], axis=1)
    right = jnp.concatenate([fill, value], axis=1)
    return jnp.where(odd == 0, left, right).astype(BF)


def merge_windows(blocks, full, tiles, rows_step):
    rows = full.shape[0]
    half = tiles // 2

    def body(i, _):
        r = pl.ds(mo(i * rows_step, rows_step), rows_step)
        for pair in range(2):
            even, odd = blocks.at[2 * pair], blocks.at[2 * pair + 1]
            base = pair * tiles * 128
            full[r, base:base + half * 128] = even[r, 0:half * 128]
            full[r, base + half * 128:base + (half + 1) * 128] = (
                even[r, half * 128:(half + 1) * 128] + odd[r, 0:128])
            full[r, base + (half + 1) * 128:base + tiles * 128] = odd[r, 128:(half + 1) * 128]
        return 0

    lax.fori_loop(0, rows // rows_step, body, 0)


def split3(value):
    high = value.astype(BF)
    rest = value - high.astype(F32)
    mid = rest.astype(BF)
    low = (rest - mid.astype(F32)).astype(BF)
    return high.astype(F32), mid.astype(F32), low.astype(F32)


def extend(head, pair, lane, one, two, three, four):
    base = 64 * (1 - head)
    extra = jnp.where(lane == base, one, jnp.where(lane == base + 1, two, jnp.where(
        lane == base + 2, three, jnp.where(lane == base + 3, four, 0.0))))
    keep = (lane < 64) if head == 0 else (lane >= 64)
    return jnp.where(keep, pair, extra).astype(BF)


def iota(shape, axis):
    return lax.broadcasted_iota(jnp.int32, shape, axis)


QB = 512


def first_kernel(length_ref, x_ref, wp_ref, wo_ref, we_ref, vec_ref,
                 n1_out, proj_out, mixed_out, qa_out, wp_out, wo_out, we_out, v_out,
                 wp_blk, wo_blk, we, wp, wo, vb, n1, proj, mixed, qa, ka, va, vrow,
                 send_sem, recv_sem, out_sem):
    p = Place()
    T, D = x_ref.shape
    R = wp_ref.shape[0]
    FF = we.shape[1]
    link = Link(p, send_sem, recv_sem)
    rows_of = lambda d: pl.ds(mo(d * R, 16), R)
    bp = lambda z, d: wp_blk.at[z, rows_of(d), :]
    bo = lambda z, d: wo_blk.at[z, rows_of(d), :]
    be = lambda z, d: we.at[rows_of(d), pl.ds(mo(z * (FF // 4), 128), FF // 4)]
    ev_p, ev_o, ev_e = (gather_events(link, p, b) for b in (bp, bo, be))
    vs = [link.slot() for _ in range(7)]

    wp_blk[p.z, rows_of(p.d), :] = window(wp_ref[...], p.odd, wp_blk.shape[2])
    wo_blk[p.z, rows_of(p.d), :] = window(wo_ref[...], p.odd, wo_blk.shape[2])
    we[rows_of(p.d), pl.ds(mo(p.z * (FF // 4), 128), FF // 4)] = we_ref[...]
    vb[p.d] = vec_ref[...]

    outs = []

    def out(source, target):
        made = pltpu.make_async_copy(source, target, out_sem.at[len(outs)])
        made.start()
        outs.append(made)

    enter(p)
    send_v = lambda slot, d, to: link.send(vs[slot], vb.at[d], vb.at[d], to, lambda: vb.at[0])
    for slot, to in ((0, "x"), (1, "y"), (3, "c")):
        send_v(slot, p.d, to)
    ev_p[0]()
    link.got(vs[0], vb.at[p.dx])
    link.got(vs[1], vb.at[p.dy])
    send_v(2, p.dx, "y")
    send_v(4, p.dx, "c")
    send_v(5, p.dy, "c")
    ev_p[1]()
    ev_p[2]()
    link.got(vs[2], vb.at[p.dd])
    send_v(6, p.dd, "c")
    ev_p[3]()
    ev_p[4]()
    dc = p.dc
    link.got(vs[3], vb.at[dc])
    cx = p.dx + p.dc - p.d
    cy = p.dy + p.dc - p.d
    cd = p.dd + p.dc - p.d
    link.got(vs[4], vb.at[cx])
    link.got(vs[5], vb.at[cy])
    link.got(vs[6], vb.at[cd])
    got = vb[...].astype(F32)
    side = lambda row, wide: jnp.concatenate([got[i, row:row + 1, 0:wide] for i in range(8)], axis=1)
    bias = side(0, 2 * R)
    vrow[0:1, 0:D] = bias[:, 0:D]
    vrow[0:1, D:2 * D] = jnp.zeros((1, D), F32)
    vrow[0:1, 2 * D:3 * D] = bias[:, D:]
    vrow[1:2, :] = side(2, FF // 8)
    for row, at in ((2, 1), (3, 3), (4, 4), (5, 5), (6, 6), (7, 7)):
        vrow[row:row + 1, 0:D] = side(at, R)
    out(vrow, v_out)
    ev_p[5]()

    LR = 128
    gain, shift = vrow[4:5, 0:D], vrow[5:6, 0:D]

    def norm_body(i, _):
        r = pl.ds(mo(i * LR, LR), LR)
        value = x_ref[r, :].astype(F32)
        u = value - jnp.mean(value, axis=-1, keepdims=True)
        spread = jnp.mean(u * u, axis=-1, keepdims=True)
        n1[r, :] = (u * lax.rsqrt(spread + eps_norm) * gain + shift).astype(BF)
        return 0

    lax.fori_loop(0, T // LR, norm_body, 0)
    out(n1, n1_out)
    for event in ev_p[6:]:
        event()
    ev_o[0]()
    merge_windows(wp_blk, wp, 9, 96)
    out(wp, wp_out)
    ev_o[1]()
    ev_o[2]()

    def project_body(i, _):
        r = pl.ds(mo(i * 256, 256), 256)
        left = n1[r, :]
        for j in range(3):
            cols = slice(j * D, (j + 1) * D)
            value = dot(left, wp[:, cols]) + vrow[0:1, cols]
            proj[r, cols] = value.astype(BF)
        return 0

    lax.fori_loop(0, T // 256, project_body, 0)
    out(proj, proj_out)

    length = length_ref[0]
    nq = T // QB

    def attend_steps(events):
        def body(step, _):
            for at, event in events:
                pl.when(step == at)(event)
            pair = lax.div(step, nq)
            part = lax.rem(step, nq)
            cols = lambda off: pl.ds(mo(off + pair * 128, 128), 128)

            @pl.when(part == 0)
            def _():
                lane, row = iota((T, 128), 1), iota((T, 128), 0)
                q = proj[:, cols(0)].astype(F32) * (HD ** -0.5)
                k = proj[:, cols(D)].astype(F32)
                v = proj[:, cols(2 * D)].astype(F32)
                dead = jnp.where(row < length, 0.0, neg_fill)
                for head in range(2):
                    ka[head] = extend(head, k, lane, 1.0, 1.0, 1.0, dead)
                    qa[pair * 2 + head] = extend(head, q, lane, 0.0, 0.0, 0.0, 1.0)
                    keep = (lane < 64) if head == 0 else (lane >= 64)
                    va[head] = jnp.where(keep, v, 1.0).astype(BF)

            r = pl.ds(mo(part * QB, QB), QB)
            lane = iota((QB, 128), 1)
            halves = []
            for head in range(2):
                query = qa[pair * 2 + head, r, :]
                scores = dot_nt(query, ka[head])
                top = jnp.max(scores, axis=-1, keepdims=True)
                powers = jnp.exp(scores - top).astype(BF)
                value = dot(powers, va[head])
                total = value[:, 64:65] if head == 0 else value[:, 0:1]
                one, two, three = split3(-(top + jnp.log(total)))
                qa[pair * 2 + head, r, :] = extend(head, query.astype(F32), lane, one, two, three, 1.0)
                halves.append(value * (1.0 / total))
            mixed[r, cols(0)] = jnp.where(lane < 64, halves[0], halves[1]).astype(BF)
            return 0

        lax.fori_loop(0, (H // 2) * nq, body, 0)

    rest = ev_o[3:] + ev_e
    spots = [0, 0, 0, 0, 1, 1, 1, 1, 1, 1] + [2, 3, 3, 4, 4, 5, 5, 6, 7, 8, 8, 9, 10]
    assert len(rest) == len(spots)
    attend_steps(list(zip(spots, rest)))
    merge_windows(wo_blk, wo, 3, 96)
    out(wo, wo_out)
    out(we, we_out)
    out(mixed, mixed_out)
    out(qa, qa_out)
    link.finish()
    for made in outs:
        made.wait()


def first_call(length, x, wp, wo, we, vec):
    T, D = x.shape
    FF = we.shape[1] * 4
    ANY = pl.BlockSpec(memory_space=pl.ANY)
    V = pl.BlockSpec(memory_space=pltpu.VMEM)
    S = pl.BlockSpec(memory_space=pltpu.SMEM)
    sds = jax.ShapeDtypeStruct
    n = 3 * 32 + 7
    return pl.pallas_call(
        first_kernel,
        in_specs=[S, V, V, V, V, V],
        out_specs=[ANY] * 8,
        out_shape=[sds((T, D), BF), sds((T, 3 * D), BF), sds((T, D), BF), sds((H, T, 128), BF),
                   sds((D, 3 * D), BF), sds((D, D), BF), sds((D, FF), BF), sds((8, FF), F32)],
        scratch_shapes=[
            pltpu.VMEM((4, D, 640), BF), pltpu.VMEM((4, D, 256), BF), pltpu.VMEM((D, FF), BF),
            pltpu.VMEM((D, 3 * D), BF), pltpu.VMEM((D, D), BF), pltpu.VMEM((8,) + vec.shape, BF),
            pltpu.VMEM((T, D), BF), pltpu.VMEM((T, 3 * D), BF), pltpu.VMEM((T, D), BF),
            pltpu.VMEM((H, T, 128), BF), pltpu.VMEM((2, T, 128), BF), pltpu.VMEM((2, T, 128), BF),
            pltpu.VMEM((8, FF), F32),
            pltpu.SemaphoreType.DMA((n,)), pltpu.SemaphoreType.DMA((n,)), pltpu.SemaphoreType.DMA((8,)),
        ],
        compiler_params=pltpu.CompilerParams(
            collective_id=0, has_side_effects=True, vmem_limit_bytes=60 << 20),
        name="first_part",
    )(length, x, wp, wo, we, vec)


def pack_vectors(project_bias, output_bias, expand_bias, contract_bias, g1, s1, g2, s2):
    wide = expand_bias.shape[0]
    rows = [jnp.pad(v, (0, wide - v.shape[0])) for v in
            (project_bias, output_bias, expand_bias, contract_bias, g1, s1, g2, s2)]
    return jnp.pad(jnp.stack(rows), ((0, 8), (0, 0)))


def layer_norm(values, gain_row, shift_row):
    centre = jnp.mean(values, axis=-1, keepdims=True)
    centred = values - centre
    spread = jnp.mean(centred * centred, axis=-1, keepdims=True)
    return centred * lax.rsqrt(spread + eps_norm) * gain_row + shift_row


def gelu_exact(values):
    return jax.nn.gelu(values, approximate=False)


def matmul(first, second):
    return jnp.dot(first, second, preferred_element_type=jnp.float32)


def over_rows(first, second):
    return lax.dot_general(
        first, second, (((0,), (0,)), ((), ())), preferred_element_type=jnp.float32
    )


def over_columns(first, second):
    return lax.dot_general(
        first, second, (((1,), (1,)), ((), ())), preferred_element_type=jnp.float32
    )


def fetch_forward(
    project_weight,
    output_weight,
    expand_weight,
    contract_weight,
    project_bias,
    output_bias,
    expand_bias,
    contract_bias,
    first_gain,
    first_shift,
    second_gain,
    second_shift,
):
    wide_project, wide_output, wide_expand, wide_contract = (
        lax.all_gather(project_weight, "fsdp", axis=1, tiled=True),
        lax.all_gather(output_weight, "fsdp", axis=1, tiled=True),
        lax.all_gather(expand_weight, "fsdp", axis=1, tiled=True),
        lax.all_gather(contract_weight, "fsdp", axis=1, tiled=True),
    )
    return (
        lax.all_gather(wide_project, "dp", axis=0, tiled=True),
        lax.all_gather(wide_output, "dp", axis=0, tiled=True),
        lax.all_gather(wide_expand, "dp", axis=0, tiled=True),
        lax.all_gather(wide_contract, "dp", axis=0, tiled=True),
        lax.all_gather(project_bias, "dp", axis=0, tiled=True),
        lax.all_gather(output_bias, "dp", axis=0, tiled=True),
        lax.all_gather(expand_bias, "dp", axis=0, tiled=True),
        lax.all_gather(contract_bias, "dp", axis=0, tiled=True),
        lax.all_gather(first_gain, "dp", axis=0, tiled=True),
        lax.all_gather(first_shift, "dp", axis=0, tiled=True),
        lax.all_gather(second_gain, "dp", axis=0, tiled=True),
        lax.all_gather(second_shift, "dp", axis=0, tiled=True),
    )


def fetch_backward(
    project_weight,
    output_weight,
    expand_weight,
    contract_weight,
    project_bias,
    output_bias,
    expand_bias,
    contract_bias,
    first_gain,
    first_shift,
    second_gain,
    second_shift,
):
    wide_project, wide_output, wide_expand, wide_contract = (
        lax.all_gather(project_weight, "fsdp", axis=1, tiled=True),
        lax.all_gather(output_weight, "fsdp", axis=1, tiled=True),
        lax.all_gather(expand_weight, "fsdp", axis=1, tiled=True),
        lax.all_gather(contract_weight, "fsdp", axis=1, tiled=True),
    )
    return (
        lax.all_gather(wide_project, "dp", axis=0, tiled=True),
        lax.all_gather(wide_output, "dp", axis=0, tiled=True),
        lax.all_gather(wide_expand, "dp", axis=0, tiled=True),
        lax.all_gather(wide_contract, "dp", axis=0, tiled=True),
        lax.all_gather(project_bias, "dp", axis=0, tiled=True),
        lax.all_gather(output_bias, "dp", axis=0, tiled=True),
        lax.all_gather(expand_bias, "dp", axis=0, tiled=True),
        lax.all_gather(contract_bias, "dp", axis=0, tiled=True),
        lax.all_gather(first_gain, "dp", axis=0, tiled=True),
        lax.all_gather(first_shift, "dp", axis=0, tiled=True),
        lax.all_gather(second_gain, "dp", axis=0, tiled=True),
        lax.all_gather(second_shift, "dp", axis=0, tiled=True),
    )


def split_heads(cell_rows, block_rows):
    slot_count = cell_rows.shape[0]
    width = cell_rows.shape[1] // 3
    query_blocks = cell_rows[:, :width].reshape(slot_count // block_rows, block_rows, H, HD)
    keys_all = cell_rows[:, width : 2 * width].reshape(slot_count, H, HD)
    values_all = cell_rows[:, 2 * width :].reshape(slot_count, H, HD)
    return (query_blocks, keys_all, values_all)


def block_scores(query_block, keys_all, key_live):
    scores = jnp.einsum(
        "qhe,khe->hqk", query_block, keys_all, preferred_element_type=jnp.float32
    ) * HD ** (-0.5)
    return jnp.where(key_live[None, None, :], scores, neg_fill)


def attend_forward(query_block, keys_all, values_all, key_live):
    scores = block_scores(query_block, keys_all, key_live)
    row_max = jnp.max(scores, axis=-1, keepdims=True)
    powers = jnp.exp(scores - row_max)
    row_total = jnp.sum(powers, axis=-1, keepdims=True)
    weights = (powers / row_total).astype(jnp.bfloat16)
    mixed_block = jnp.einsum(
        "hqk,khe->qhe", weights, values_all, preferred_element_type=jnp.float32
    )
    return (mixed_block, (row_max + jnp.log(row_total))[:, :, 0])


def attend_backward(query_block, grad_block, log_block, keys_all, values_all, key_live):
    scores = block_scores(query_block, keys_all, key_live)
    weights = jnp.exp(scores - log_block[:, :, None])
    grad_weights = jnp.einsum(
        "qhe,khe->hqk", grad_block, values_all, preferred_element_type=jnp.float32
    )
    row_inner = jnp.sum(grad_weights * weights, axis=-1, keepdims=True)
    grad_scores = (weights * (grad_weights - row_inner)).astype(jnp.bfloat16)
    grad_query = jnp.einsum(
        "hqk,khe->qhe", grad_scores, keys_all, preferred_element_type=jnp.float32
    ) * HD ** (-0.5)
    grad_key = jnp.einsum(
        "hqk,qhe->khe", grad_scores, query_block, preferred_element_type=jnp.float32
    ) * HD ** (-0.5)
    grad_value = jnp.einsum(
        "hqk,qhe->khe", weights.astype(jnp.bfloat16), grad_block, preferred_element_type=jnp.float32
    )
    return (grad_query, grad_key, grad_value)


def per_device(
    tokens,
    lengths,
    cotangent,
    project_weight,
    project_bias,
    output_weight,
    output_bias,
    expand_weight,
    expand_bias,
    contract_weight,
    contract_bias,
    first_gain,
    first_shift,
    second_gain,
    second_shift,
):
    fetched = fetch_forward(
        project_weight,
        output_weight,
        expand_weight,
        contract_weight,
        project_bias,
        output_bias,
        expand_bias,
        contract_bias,
        first_gain,
        first_shift,
        second_gain,
        second_shift,
    )
    full_project, full_output, full_expand, full_contract = (
        fetched[0],
        fetched[1],
        fetched[2],
        fetched[3],
    )
    vectors = [item.astype(jnp.float32) for item in fetched[4:]]
    bias_project, bias_output, bias_expand, bias_contract = (
        vectors[0],
        vectors[1],
        vectors[2],
        vectors[3],
    )
    gain_one, shift_one, gain_two, shift_two = (vectors[4], vectors[5], vectors[6], vectors[7])
    cell_count = lengths.shape[0]
    slot_count = tokens.shape[0] // cell_count
    width = tokens.shape[1]
    block_rows = min(512, slot_count)
    positions = jnp.arange(slot_count, dtype=jnp.int32)
    live_keys = positions[None, :] < lengths[:, None]
    live_rows = live_keys.reshape(-1)
    rows_in = tokens.astype(jnp.float32)
    normed_one = layer_norm(rows_in, gain_one, shift_one).astype(jnp.bfloat16)
    bias_full = jnp.concatenate(
        [bias_project[:width], jnp.zeros((width,), jnp.float32), bias_project[width:]]
    )
    projected = (matmul(normed_one, full_project) + bias_full).astype(jnp.bfloat16)
    cell_index = 0
    query_blocks, keys_all, values_all = split_heads(projected, block_rows)
    key_live = live_keys[cell_index]
    mixed_blocks, log_blocks = lax.map(
        lambda query_block: attend_forward(query_block, keys_all, values_all, key_live),
        query_blocks,
    )
    mixed_list = mixed_blocks.reshape(slot_count, width)
    log_list = [log_blocks]
    mixed_low = mixed_list.astype(jnp.bfloat16)
    middle = rows_in + (matmul(mixed_low, full_output) + bias_output)
    normed_two = layer_norm(middle, gain_two, shift_two).astype(jnp.bfloat16)
    hidden = matmul(normed_two, full_expand) + bias_expand
    active = gelu_exact(hidden).astype(jnp.bfloat16)
    result = middle + (matmul(active, full_contract) + bias_contract)
    block_out = jnp.where(live_rows[:, None], result, 0.0).astype(jnp.bfloat16)
    again = fetch_backward(
        project_weight,
        output_weight,
        expand_weight,
        contract_weight,
        project_bias,
        output_bias,
        expand_bias,
        contract_bias,
        first_gain,
        first_shift,
        second_gain,
        second_shift,
    )
    back_project, back_output, back_expand, back_contract = (again[0], again[1], again[2], again[3])
    grad_out = jnp.where(live_rows[:, None], cotangent.astype(jnp.float32), 0.0)
    grad_out_low = grad_out.astype(jnp.bfloat16)
    grad_contract = over_rows(active, grad_out_low)
    grad_contract_bias = jnp.sum(grad_out, axis=0)
    grad_active = over_columns(grad_out_low, back_contract)
    gelu_value, gelu_pull = jax.vjp(gelu_exact, hidden)
    grad_hidden = gelu_pull(grad_active)[0].astype(jnp.bfloat16)
    grad_expand = over_rows(normed_two, grad_hidden)
    grad_expand_bias = jnp.sum(grad_hidden.astype(jnp.float32), axis=0)
    grad_normed_two = over_columns(grad_hidden, back_expand)
    norm_value, second_pull = jax.vjp(layer_norm, middle, gain_two, shift_two)
    grad_middle, grad_gain_two, grad_shift_two = second_pull(grad_normed_two)
    grad_middle = grad_middle + grad_out
    grad_branch = grad_middle.astype(jnp.bfloat16)
    grad_output = over_rows(mixed_low, grad_branch)
    grad_output_bias = jnp.sum(grad_branch.astype(jnp.float32), axis=0)
    grad_mixed = over_columns(grad_branch, back_output).astype(jnp.bfloat16)
    cell_index = 0
    query_blocks, keys_all, values_all = split_heads(projected, block_rows)
    key_live = live_keys[cell_index]
    grad_blocks = grad_mixed.reshape(slot_count // block_rows, block_rows, H, HD)

    def visit_block(carried, inputs):
        query_block, grad_block, log_block = inputs
        grad_query, grad_key, grad_value = attend_backward(
            query_block, grad_block, log_block, keys_all, values_all, key_live
        )
        return ((carried[0] + grad_key, carried[1] + grad_value), grad_query)

    initial = (
        jnp.zeros((slot_count, H, HD), jnp.float32),
        jnp.zeros((slot_count, H, HD), jnp.float32),
    )
    (key_sums, value_sums), query_grads = lax.scan(
        visit_block, initial, (query_blocks, grad_blocks, log_list[cell_index])
    )
    grad_cells = jnp.concatenate(
        [
            query_grads.reshape(slot_count, width),
            key_sums.reshape(slot_count, width),
            value_sums.reshape(slot_count, width),
        ],
        axis=1,
    )
    grad_projected = grad_cells.astype(jnp.bfloat16)
    grad_project = over_rows(normed_one, grad_projected)
    column_sums = jnp.sum(grad_projected.astype(jnp.float32), axis=0)
    grad_project_bias = jnp.concatenate([column_sums[:width], column_sums[2 * width :]])
    grad_normed_one = over_columns(grad_projected, back_project)
    first_value, first_pull = jax.vjp(layer_norm, rows_in, gain_one, shift_one)
    grad_rows_in, grad_gain_one, grad_shift_one = first_pull(grad_normed_one)
    tokens_grad = (grad_rows_in + grad_middle).astype(jnp.bfloat16)
    reduced = (
        lax.psum_scatter(grad_project, "dp", scatter_dimension=0, tiled=True),
        lax.psum_scatter(grad_output, "dp", scatter_dimension=0, tiled=True),
        lax.psum_scatter(grad_expand, "dp", scatter_dimension=0, tiled=True),
        lax.psum_scatter(grad_contract, "dp", scatter_dimension=0, tiled=True),
        lax.psum_scatter(grad_project_bias, "dp", scatter_dimension=0, tiled=True),
        lax.psum_scatter(grad_output_bias, "dp", scatter_dimension=0, tiled=True),
        lax.psum_scatter(grad_expand_bias, "dp", scatter_dimension=0, tiled=True),
        lax.psum_scatter(grad_contract_bias, "dp", scatter_dimension=0, tiled=True),
        lax.psum_scatter(grad_gain_one, "dp", scatter_dimension=0, tiled=True),
        lax.psum_scatter(grad_shift_one, "dp", scatter_dimension=0, tiled=True),
        lax.psum_scatter(grad_gain_two, "dp", scatter_dimension=0, tiled=True),
        lax.psum_scatter(grad_shift_two, "dp", scatter_dimension=0, tiled=True),
    )
    shard_project, shard_output, shard_expand, shard_contract = (
        lax.psum_scatter(
            reduced[0].astype(jnp.bfloat16), "fsdp", scatter_dimension=1, tiled=True
        ).astype(jnp.float32),
        lax.psum_scatter(
            reduced[1].astype(jnp.bfloat16), "fsdp", scatter_dimension=1, tiled=True
        ).astype(jnp.float32),
        lax.psum_scatter(
            reduced[2].astype(jnp.bfloat16), "fsdp", scatter_dimension=1, tiled=True
        ).astype(jnp.float32),
        lax.psum_scatter(
            reduced[3].astype(jnp.bfloat16), "fsdp", scatter_dimension=1, tiled=True
        ).astype(jnp.float32),
    )
    summed = lax.psum(
        (
            reduced[4],
            reduced[5],
            reduced[6],
            reduced[7],
            reduced[8],
            reduced[9],
            reduced[10],
            reduced[11],
        ),
        "fsdp",
    )
    return (
        block_out,
        tokens_grad,
        shard_project,
        summed[0],
        shard_output,
        summed[1],
        shard_expand,
        summed[2],
        shard_contract,
        summed[3],
        summed[4],
        summed[5],
        summed[6],
        summed[7],
    )


def scatter_events(link, place, col, pair_of, block_of, lc, lxh, lyh, lx, ly, lz, finish):
    p = place
    family = (p.dc, p.dx + p.dc - p.d, p.dy + p.dc - p.d, p.dd + p.dc - p.d)
    cs = [link.slot() for _ in range(4)]
    hx, hy, fx, fy = (link.slot() for _ in range(4))
    zs = [link.slot() for _ in range(4)]
    got = link.got

    def add(target, *terms):
        total = target[...].astype(F32)
        for term in terms:
            total = total + term[...].astype(F32)
        target[...] = total.astype(BF)

    def to_sibling(which):
        link.send(cs[which], col(family[which]), lc.at[which], "c", lambda: col(0))

    def halves():
        got(cs[3], lc.at[3])
        add(col(p.dd), lc.at[3])
        link.send(hx, pair_of(col(p.dd), 0), lxh, "x", lambda: lxh)
        link.send(hy, pair_of(col(p.dd), 1), lyh, "y", lambda: lyh)

    def near():
        got(cs[1], lc.at[1])
        got(cs[2], lc.at[2])
        add(col(p.dx), lc.at[1])
        add(col(p.dy), lc.at[2])

    def pass_y():
        got(hx, lxh)
        add(pair_of(col(p.dy), 0), lxh)
        link.send(fy, col(p.dy), ly, "y", lambda: ly)

    def pass_x():
        got(hy, lyh)
        add(pair_of(col(p.dx), 1), lyh)
        link.send(fx, col(p.dx), lx, "x", lambda: lx)

    def own():
        got(cs[0], lc.at[0])

    def along_z():
        got(fx, lx)
        got(fy, ly)
        add(col(p.d), lc.at[0], lx, ly)
        for step in (1, 3, 2) if lz is not None else ():
            link.send(zs[step], block_of(col(p.d), p.zt(step)), lz.at[step], step, lambda: lz.at[0])

    def last():
        total = block_of(col(p.d), p.z)[...].astype(F32)
        for step in (1, 3, 2):
            got(zs[step], lz.at[step])
            total = total + lz[step].astype(F32)
        finish(total)

    return to_sibling, [halves, near, pass_y, pass_x, own, along_z, last]


def gelu_pair(value):
    lift = 0.5 * (1.0 + lax.erf(value * 0.7071067811865476))
    bell = jnp.exp(value * value * -0.5) * 0.3989422804014327
    return value * lift, lift + value * bell


def second_kernel(length_ref, x_ref, cot_ref, mixed_ref, wo_ref, we_hbm, wc_ref, v_ref,
                  block_out, dmixed_out, dmiddle_out, ge_out, go_out, gc_out, vg_out,
                  we, wct, act, slope, middle, n2t, dot_t, mixed_t, dbranch, dout, gc, go, dmixed, bout, vg,
                  lc, lxh, lyh, lx, ly, lz, send_sem, recv_sem, out_sem):
    p = Place()
    T, D = x_ref.shape
    FF = we.shape[1]
    R = D // 8
    Q = FF // 4
    C8 = FF // 8
    link = Link(p, send_sem, recv_sem)
    bc = lambda z, d: wct.at[pl.ds(mo(z * (D // 4), 16), D // 4), pl.ds(mo(d * C8, 128), C8)]
    gather = gather_events(link, p, bc)

    def finish(total):
        gc_out[...] = total.T

    to_sibling, scatter = scatter_events(
        link, p, lambda d: gc.at[d], lambda ref, h: ref.at[pl.ds(2 * h, 2)], lambda ref, z: ref.at[z],
        lc, lxh, lyh, lx, ly, lz, finish)
    load = pltpu.make_async_copy(we_hbm, we, out_sem.at[0])
    load.start()
    wct[pl.ds(mo(p.z * (D // 4), 16), D // 4), pl.ds(mo(p.d * C8, 128), C8)] = wc_ref[...].astype(F32).T.astype(BF)
    enter(p)
    gather[0]()
    length = length_ref[0]
    LR = 256
    rows = lambda i: pl.ds(mo(i * LR, LR), LR)
    vec = lambda i: v_ref[i:i + 1, 0:D]
    vg[...] = jnp.zeros_like(vg)

    def at(i, spots):
        for where, event in spots:
            pl.when(i == where)(event)

    def norm(value):
        u = value - jnp.mean(value, axis=-1, keepdims=True)
        r = lax.rsqrt(jnp.mean(u * u, axis=-1, keepdims=True) + eps_norm)
        return u * r, r

    def middle_body(i, _):
        at(i, [(1, gather[1]), (3, gather[2])])
        r = rows(i)
        value = x_ref[r, :].astype(F32) + (dot(mixed_ref[r, :], wo_ref[...]) + vec(2))
        middle[r, :] = value
        xhat, _ = norm(value)
        n2 = (xhat * vec(6) + vec(7)).astype(BF)
        dmixed[r, :] = n2
        n2t[:, r] = n2.T
        live = iota((LR, D), 0) + i * LR < length
        grad = jnp.where(live, cot_ref[r, :].astype(F32), 0.0)
        vg[7:8, :] += jnp.sum(grad, axis=0, keepdims=True)
        dout[r, :] = grad.astype(BF)
        dot_t[:, r] = grad.astype(BF).T
        mixed_t[:, r] = mixed_ref[r, :].T
        return 0

    lax.fori_loop(0, T // LR, middle_body, 0)
    load.wait()

    def hidden_body(i, _):
        at(i, [(0, gather[3]), (1, gather[4]), (1, gather[5]), (2, gather[6]), (2, gather[7]), (3, gather[8]),
               (3, gather[9])])
        r = rows(i)
        left = dmixed[r, :]
        for j in range(4):
            cols = slice(j * Q, (j + 1) * Q)
            first, second = gelu_pair(dot(left, we[:, cols]) + v_ref[1:2, cols])
            act[r, cols] = first.astype(BF)
            slope[r, cols] = second.astype(BF)
        return 0

    lax.fori_loop(0, T // LR, hidden_body, 0)
    gather[10]()

    def column(d):
        value = dot(dot_t[...], act[:, pl.ds(mo(d * C8, 128), C8)])
        gc[d] = value.reshape(4, D // 4, C8).astype(BF)

    sib = p.dc - p.d
    column(p.dd + sib)
    to_sibling(3)
    column(p.dd)
    gather[11]()
    column(p.dx + sib)
    to_sibling(1)
    column(p.dy + sib)
    to_sibling(2)
    scatter[0]()
    column(p.dx)
    column(p.dy)
    scatter[1]()
    column(p.d + sib)
    to_sibling(0)
    column(p.d)
    gather[12]()

    def back_body(i, _):
        at(i, [(0, scatter[2]), (0, scatter[3]), (1, scatter[4]), (3, scatter[5])])
        r = rows(i)
        grad_low = dout[r, :]
        result = middle[r, :] + vec(3)
        dn = jnp.zeros((LR, D), F32)
        for j in range(4):
            cols = slice(j * Q, (j + 1) * Q)
            dh = dot(grad_low, wct[:, cols]) * slope[r, cols].astype(F32)
            low = dh.astype(BF)
            slope[r, cols] = low
            vg[3 + j:4 + j, :] += jnp.sum(low.astype(F32), axis=0, keepdims=True)
            result = result + dot_nt(act[r, cols], wct[:, cols])
            dn = dn + dot_nt(low, we[:, cols])
        live = iota((LR, D), 0) + i * LR < length
        bout[r, :] = jnp.where(live, result, 0.0).astype(BF)
        xhat, spread = norm(middle[r, :])
        vg[10:11, :] += jnp.sum(dn * xhat, axis=0, keepdims=True)
        vg[11:12, :] += jnp.sum(dn, axis=0, keepdims=True)
        gx = dn * vec(6)
        back = spread * (gx - jnp.mean(gx, axis=-1, keepdims=True)
                         - xhat * jnp.mean(gx * xhat, axis=-1, keepdims=True))
        total = dout[r, :].astype(F32) + back
        middle[r, :] = total
        branch = total.astype(BF)
        dbranch[r, :] = branch
        vg[2:3, :] += jnp.sum(branch.astype(F32), axis=0, keepdims=True)
        dmixed[r, :] = dot_nt(branch, wo_ref[...]).astype(BF)
        return 0

    lax.fori_loop(0, T // LR, back_body, 0)
    outs = []

    def out(source, target):
        made = pltpu.make_async_copy(source, target, out_sem.at[1 + len(outs)])
        made.start()
        outs.append(made)

    out(bout, block_out)
    out(dmixed, dmixed_out)
    out(middle, dmiddle_out)
    for z in range(4):
        act[0:D, z * Q:(z + 1) * Q] = dot(n2t[...], slope[:, z * Q:(z + 1) * Q]).astype(BF)
    out(act.at[0:D, :], ge_out)
    for z in range(4):
        cols = slice(3 * z // 2 * 128, 3 * z // 2 * 128 + 256)
        go[:, z] = dot(mixed_t[...], dbranch[:, cols]).reshape(8, R, 256).astype(BF)
    out(go, go_out)
    vg_out[...] = vg[...]
    scatter[6]()
    link.finish()
    for made in outs:
        made.wait()


ANY = pl.BlockSpec(memory_space=pl.ANY)
VM = pl.BlockSpec(memory_space=pltpu.VMEM)
SM = pl.BlockSpec(memory_space=pltpu.SMEM)
sds = jax.ShapeDtypeStruct


def second_call(length, x, cot, mixed, wo, we, wc, v):
    T, D = x.shape
    FF = we.shape[1]
    n = 32 + 12
    R, C8, Z = D // 8, FF // 8, D // 4
    vm = pltpu.VMEM
    return pl.pallas_call(
        second_kernel,
        in_specs=[SM, VM, VM, VM, VM, ANY, VM, VM],
        out_specs=[ANY] * 5 + [VM] * 2,
        out_shape=[sds((T, D), BF), sds((T, D), BF), sds((T, D), F32), sds((D, FF), BF), sds((8, 4, R, 256), BF),
                   sds((C8, Z), F32), sds((16, D), F32)],
        scratch_shapes=[
            vm((D, FF), BF), vm((D, FF), BF), vm((T, FF), BF), vm((T, FF), BF), vm((T, D), F32),
            vm((D, T), BF), vm((D, T), BF), vm((D, T), BF), vm((T, D), BF), vm((T, D), BF),
            vm((8, 4, Z, C8), BF), vm((8, 4, R, 256), BF), vm((T, D), BF), vm((T, D), BF), vm((16, D), F32),
            vm((4, 4, Z, C8), BF), vm((2, Z, C8), BF), vm((2, Z, C8), BF), vm((4, Z, C8), BF), vm((4, Z, C8), BF),
            vm((4, Z, C8), BF),
            pltpu.SemaphoreType.DMA((n,)), pltpu.SemaphoreType.DMA((n,)), pltpu.SemaphoreType.DMA((6,)),
        ],
        compiler_params=pltpu.CompilerParams(
            collective_id=1, has_side_effects=True, vmem_limit_bytes=62 << 20),
        name="second_part",
    )(length, x, cot, mixed, wo, we, wc, v)


def third_kernel(length_ref, proj_hbm, qa_hbm, mixed_hbm, dm_hbm, n1_hbm, wp_hbm, x_hbm, dmiddle_hbm, ge_hbm, go_hbm,
                 vg_ref, v_ref,
                 tokens_out, gp_out, go_out, ge_out, vec_out,
                 proj, qa, mixed, dm, n1, n1t, wpp, x, dmiddle, ge, go, dproj, tg, gp,
                 ka, da, dq, va, kt, vs, vl,
                 lce, lxhe, lyhe, lxe, lye, lze, lco, lxho, lyho, lxo, lyo, lzo,
                 lcp, lxhp, lyhp, lxp, lyp, lzp, gpw,
                 send_sem, recv_sem, load_sem):
    p = Place()
    T, D = x.shape
    FF = ge.shape[1]
    R = D // 8
    Q = FF // 4
    pairs = H // 2
    KB = 256
    parts = T // KB
    link = Link(p, send_sem, recv_sem)
    loads = []

    def load(source, target):
        made = pltpu.make_async_copy(source, target, load_sem.at[len(loads)])
        made.start()
        loads.append(made)
        return made

    first_loads = [load(a, b) for a, b in ((proj_hbm, proj), (qa_hbm, qa), (mixed_hbm, mixed), (dm_hbm, dm))]
    ge_load, go_load, n1_load = load(ge_hbm, ge), load(go_hbm, go), load(n1_hbm, n1)
    late = [load(x_hbm, x), load(dmiddle_hbm, dmiddle)]
    for i in range(pairs):
        for s in range(3):
            late.append(load(wp_hbm.at[:, pl.ds((s * pairs + i) * 128, 128)],
                             wpp.at[:, pl.ds((i * 3 + s) * 128, 128)]))

    def finish_e(total):
        ge_out[...] = total

    def finish_o(total):
        go_out[...] = jnp.where(p.odd == 0, total[:, 0:192], total[:, 64:256])

    rows_of = lambda d: pl.ds(mo(d * R, 16), R)
    e_sib, ev_e = scatter_events(
        link, p, lambda d: ge.at[rows_of(d), :], lambda ref, h: ref.at[:, pl.ds(h * (FF // 2), FF // 2)],
        lambda ref, z: ref.at[:, pl.ds(mo(z * Q, 128), Q)], lce, lxhe, lyhe, lxe, lye, lze, finish_e)
    o_sib, ev_o = scatter_events(
        link, p, lambda d: go.at[d], lambda ref, h: ref.at[pl.ds(2 * h, 2)], lambda ref, z: ref.at[z],
        lco, lxho, lyho, lxo, lyo, lzo, finish_o)
    ended = []
    combos = []
    for i in range(pairs):
        for s in range(3):
            tile = s * pairs + i
            for owner in range(4):
                left = 9 * owner // 2
                if left <= tile < left + 5:
                    combos.append((i, s, owner, tile - left))
    assert len(combos) == 20
    z_slots = [[link.slot() for _ in range(3)] for _ in combos]

    def pair_scatter(i):
        column = lambda d: gp.at[i, d]
        sib, events = scatter_events(
            link, p, column, lambda ref, h: ref.at[pl.ds(h * (R // 2), R // 2)], None,
            lcp.at[i], lxhp.at[i], lyhp.at[i], lxp.at[i], lyp.at[i], None, None)
        mine = [(at, c) for at, c in enumerate(combos) if c[0] == i]

        def along(add_own):
            def run():
                add_own()
                for at, (_, s, owner, _) in mine:
                    @pl.when(p.z != owner)
                    def _():
                        step = lax.rem(owner - p.z + 4, 4)
                        part = column(p.d).at[:, pl.ds(s * 128, 128)]
                        link.copy(z_slots[at][0] + step - 1, part, lzp.at[at, step - 1], ("z", owner)).start()
            return run

        def last():
            for at, (_, s, owner, place) in mine:
                @pl.when(p.z == owner)
                def _():
                    total = gp[i, p.d, :, s * 128:(s + 1) * 128].astype(F32)
                    for step in range(1, 4):
                        link.got(z_slots[at][step - 1], lzp.at[at, step - 1])
                        total = total + lzp[at, step - 1].astype(F32)
                    gpw[:, place * 128:(place + 1) * 128] = total

        def ending():
            for at, (_, s, owner, _) in mine:
                @pl.when(p.z != owner)
                def _():
                    step = lax.rem(owner - p.z + 4, 4)
                    view = lzp.at[at, 0]
                    link.copy(z_slots[at][0] + step - 1, view, view, "x").wait_send()

        ended.append(ending)

        def start():
            for k in (3, 1, 2, 0):
                sib(k)

        return [start] + events[:5] + [along(events[5]), last]

    ev_p = [pair_scatter(i) for i in range(pairs)]

    enter(p)
    for made in first_loads:
        made.wait()
    length = length_ref[0]

    def start_e():
        ge_load.wait()
        for k in (3, 1, 2, 0):
            e_sib(k)

    def start_o():
        go_load.wait()
        for k in (3, 1, 2, 0):
            o_sib(k)

    def turn_n1():
        n1_load.wait()
        for i in range(T // 256):
            n1t[:, i * 256:(i + 1) * 256] = n1[i * 256:(i + 1) * 256, :].T

    timeline = [(0, start_e), (1, turn_n1), (3, ev_e[0]), (3, ev_e[1]), (7, ev_e[2]), (7, ev_e[3]), (8, ev_e[4]),
                (9, start_o), (10, ev_o[0]), (10, ev_o[1]),
                (14, ev_e[5]), (15, ev_o[2]), (15, ev_o[3]), (15, ev_o[4]), (17, ev_o[5]), (20, ev_o[6]), (21, ev_e[6])]
    for i in range(pairs - 1):
        base = max(4 * (i + 1), 9)
        for k, event in enumerate(ev_p[i]):
            spot = {0: base, 1: base + 2, 2: base + 2, 3: base + 4, 4: base + 4, 5: base + 4, 6: base + 6, 7: base + 9}[k]
            timeline.append((spot, event))
    timeline.sort(key=lambda e: e[0])

    def body(step, _):
        for at, event in timeline:
            if at < pairs * parts:
                pl.when(step == at)(event)
        pair = lax.div(step, parts)
        part = lax.rem(step, parts)
        ps = lambda off: pl.ds(mo(off + pair * 128, 128), 128)
        own = lambda s: pl.ds(mo(pair * 384 + s * 128, 128), 128)

        @pl.when(part == 0)
        def _():
            lane, row = iota((T, 128), 1), iota((T, 128), 0)
            k = proj[:, ps(D)].astype(F32)
            v = proj[:, ps(2 * D)].astype(F32)
            do = dm[:, ps(0)].astype(F32)
            pr = do * mixed[:, ps(0)].astype(F32)
            dead = jnp.where(row < length, 0.0, neg_fill)
            for head in range(2):
                keep = (lane < 64) if head == 0 else (lane >= 64)
                delta = jnp.sum(jnp.where(keep, pr, 0.0), axis=-1, keepdims=True)
                one, two, three = split3(-delta)
                da[head] = extend(head, do, lane, one, two, three, 0.0)
                ka[head] = extend(head, k, lane, 1.0, 1.0, 1.0, dead)
                va[head] = extend(head, v, lane, 1.0, 1.0, 1.0, 0.0)
                kt[head] = jnp.where(keep, k, 0.0).astype(BF).T
            dq[...] = jnp.zeros_like(dq)

        r = pl.ds(mo(part * KB, KB), KB)
        lk = iota((KB, 128), 1)
        dks, dvs = [], []
        for head in range(2):
            weights = jnp.exp(dot_nt(ka[head, r, :], qa[pair * 2 + head]))
            low = weights.astype(BF)
            ds = (weights * dot_nt(va[head, r, :], da[head])).astype(BF)
            dvs.append(dot(low, da[head]))
            dks.append(dot(ds, qa[pair * 2 + head]))
            dq[head] += dot(kt[head, :, r], ds)
        dproj[r, own(1)] = jnp.where(lk < 64, dks[0], dks[1]).astype(BF)
        dproj[r, own(2)] = jnp.where(lk < 64, dvs[0], dvs[1]).astype(BF)

        @pl.when(part == parts - 1)
        def _():
            dproj[:, own(0)] = ((dq[0] + dq[1]) * (HD ** -0.5)).T.astype(BF)
            value = dot(n1t[...], dproj[:, pl.ds(mo(pair * 384, 128), 384)])
            gp[pair] = value.reshape(8, R, 384).astype(BF)

        return 0

    lax.fori_loop(0, pairs * parts, body, 0)
    tail = [e for at, e in timeline if at >= pairs * parts]
    ev_p[pairs - 1][0]()
    for made in late:
        made.wait()
    vs[...] = vg_ref[...]
    LR = 256

    def norm_body(i, _):
        def spot(where, events):
            @pl.when(i == where)
            def _():
                for event in events:
                    event()

        spot(1, ev_p[pairs - 1][1:3])
        spot(2, ev_p[pairs - 1][3:6])
        r = pl.ds(mo(i * LR, LR), LR)
        left = dproj[r, :]
        dn = dot_nt(left, wpp[...])
        sums = jnp.sum(left.astype(F32), axis=0, keepdims=True)
        for j in range(pairs):
            vs[0:1, j * 128:(j + 1) * 128] += sums[:, j * 384:j * 384 + 128]
            vs[1:2, j * 128:(j + 1) * 128] += sums[:, j * 384 + 256:j * 384 + 384]
        value = x[r, :].astype(F32)
        u = value - jnp.mean(value, axis=-1, keepdims=True)
        spread = lax.rsqrt(jnp.mean(u * u, axis=-1, keepdims=True) + eps_norm)
        xhat = u * spread
        vs[8:9, :] += jnp.sum(dn * xhat, axis=0, keepdims=True)
        vs[9:10, :] += jnp.sum(dn, axis=0, keepdims=True)
        gx = dn * v_ref[4:5, 0:D]
        back = spread * (gx - jnp.mean(gx, axis=-1, keepdims=True)
                         - xhat * jnp.mean(gx * xhat, axis=-1, keepdims=True))
        tg[r, :] = (back + dmiddle[r, :]).astype(BF)
        return 0

    lax.fori_loop(0, T // LR, norm_body, 0)
    out = load(tg, tokens_out)
    v_slots = [link.slot() for _ in range(6)]
    link.send(v_slots[0], vs, vl.at[0], "c", lambda: vl.at[0])
    for event in tail:
        event()
    ev_p[pairs - 1][6]()
    link.got(v_slots[0], vl.at[0])
    vl[6] = vs[...] + vl[0]
    link.send(v_slots[1], vl.at[6], vl.at[1], "x", lambda: vl.at[0])
    link.got(v_slots[1], vl.at[1])
    vl[7] = vl[6] + vl[1]
    link.send(v_slots[2], vl.at[7], vl.at[2], "y", lambda: vl.at[0])
    link.got(v_slots[2], vl.at[2])
    vl[8] = vl[7] + vl[2]
    for step in (1, 3, 2):
        link.send(v_slots[2 + step], vl.at[8], vl.at[2 + step], step, lambda: vl.at[0])
    ev_p[pairs - 1][7]()
    gp_out[...] = jnp.where(p.odd == 0, gpw[:, 0:576], gpw[:, 64:640])
    for step in (1, 3, 2):
        link.got(v_slots[2 + step], vl.at[2 + step])
    total = vl[8] + vl[3] + vl[4] + vl[5]
    quarter, half = lax.div(p.d, 4), lax.div(p.d, 2)
    pb = jnp.where(quarter == 0, total[0:1], total[1:2])
    eb = jnp.where(half < 2, jnp.where(half == 0, total[3:4], total[4:5]), jnp.where(half == 2, total[5:6], total[6:7]))
    plain = jnp.concatenate([total[2:3], total[7:12], total[2:4]], axis=0)
    turn = lambda value, by: pltpu.roll(value, lax.rem(D - by, D), 1)
    wide8 = lambda value: jnp.broadcast_to(value, (8, D))
    vec_out[0] = turn(plain, p.d * R)[:, 0:384]
    vec_out[1] = turn(wide8(pb), lax.rem(p.d, 4) * 2 * R)[:, 0:384]
    vec_out[2] = turn(wide8(eb), lax.rem(p.d, 2) * 4 * R)[:, 0:384]
    link.finish()
    for ending in ended:
        ending()
    out.wait()


def third_call(length, proj, qa, mixed, dm, n1, wp, x, dmiddle, ge, go, vg, v):
    T, D = x.shape
    FF = ge.shape[1]
    R, Q, pairs = D // 8, FF // 4, H // 2
    vm = pltpu.VMEM
    n = 12 + 12 + 6 * 12 + 60 + 6
    return pl.pallas_call(
        third_kernel,
        in_specs=[SM] + [ANY] * 10 + [VM] * 2,
        out_specs=[ANY] + [VM] * 4,
        out_shape=[sds((T, D), BF), sds((R, 3 * D // 4), F32), sds((R, D // 4), F32), sds((R, Q), F32),
                   sds((3, 8, 384), F32)],
        scratch_shapes=[
            vm((T, 3 * D), BF), vm((H, T, 128), BF), vm((T, D), BF), vm((T, D), BF), vm((T, D), BF), vm((D, T), BF),
            vm((D, 3 * D), BF), vm((T, D), BF), vm((T, D), F32), vm((D, FF), BF), vm((8, 4, R, 256), BF),
            vm((T, 3 * D), BF), vm((T, D), BF), vm((pairs, 8, R, 384), BF),
            vm((2, T, 128), BF), vm((2, T, 128), BF), vm((2, 128, T), F32), vm((2, T, 128), BF), vm((2, 128, T), BF),
            vm((16, D), F32), vm((9, 16, D), F32),
            vm((4, R, FF), BF), vm((R, FF // 2), BF), vm((R, FF // 2), BF), vm((R, FF), BF), vm((R, FF), BF), vm((4, R, Q), BF),
            vm((4, 4, R, 256), BF), vm((2, R, 256), BF), vm((2, R, 256), BF), vm((4, R, 256), BF), vm((4, R, 256), BF),
            vm((4, R, 256), BF),
            vm((pairs, 4, R, 384), BF), vm((pairs, R // 2, 384), BF), vm((pairs, R // 2, 384), BF),
            vm((pairs, R, 384), BF), vm((pairs, R, 384), BF), vm((20, 3, R, 128), BF), vm((R, 640), F32),
            pltpu.SemaphoreType.DMA((n,)), pltpu.SemaphoreType.DMA((n,)), pltpu.SemaphoreType.DMA((28,)),
        ],
        compiler_params=pltpu.CompilerParams(
            collective_id=2, has_side_effects=True, vmem_limit_bytes=63 << 20),
        name="third_part",
    )(length, proj, qa, mixed, dm, n1, wp, x, dmiddle, ge, go, vg, v)


def per_device_fast(tokens, lengths, cotangent, project_weight, project_bias, output_weight, output_bias,
                    expand_weight, expand_bias, contract_weight, contract_bias, first_gain, first_shift,
                    second_gain, second_shift):
    vec = pack_vectors(project_bias, output_bias, expand_bias, contract_bias,
                       first_gain, first_shift, second_gain, second_shift)
    normed_one, projected, mixed, qa, full_project, full_output, full_expand, v = first_call(
        lengths, tokens, project_weight, output_weight, expand_weight, vec)
    block_out, grad_mixed, grad_middle, ge, go, grad_contract, vg = second_call(
        lengths, tokens, cotangent, mixed, full_output, full_expand, contract_weight, v)
    tokens_grad, grad_project, grad_output, grad_expand, vo = third_call(
        lengths, projected, qa, mixed, grad_mixed, normed_one, full_project, tokens, grad_middle, ge, go, vg, v)
    r = output_bias.shape[0]
    return (block_out, tokens_grad, grad_project, vo[1, 0, :2 * r], grad_output, vo[0, 0, :r],
            grad_expand, vo[2, 0, :4 * r], grad_contract, vo[0, 1, :r],
            vo[0, 2, :r], vo[0, 3, :r], vo[0, 4, :r], vo[0, 5, :r])


def solution(mesh):
    both, rows, grid = P(("dp", "fsdp"), None), P("dp"), P("dp", "fsdp")
    weights = (grid, rows, grid, rows, grid, rows, grid, rows)
    fast = mesh.shape["dp"] == 8 and mesh.shape["fsdp"] == 4
    return jax.shard_map(
        per_device_fast if fast else per_device,
        mesh=mesh,
        in_specs=(both, P(("dp", "fsdp")), both) + weights + (rows,) * 4,
        out_specs=(both, both) + weights + (rows,) * 4,
        check_vma=False,
    )
```

```python
import functools
import jax
import jax.numpy as jnp
from jax import lax
from jax.experimental import pallas as pl
from jax.experimental.pallas import tpu as pltpu
from jax.sharding import PartitionSpec as P

H = 12
HD = 64
F32 = jnp.float32
BF = jnp.bfloat16
MESH = pl.DeviceIdType.MESH
eps_norm = 1e-05
neg_fill = -1000000000.0


def dot(first, second):
    return jnp.dot(first, second, preferred_element_type=F32)


def dot_nt(first, second):
    return lax.dot_general(first, second, (((1,), (1,)), ((), ())), preferred_element_type=F32)


def dot_tn(first, second):
    return lax.dot_general(first, second, (((0,), (0,)), ((), ())), preferred_element_type=F32)


def mo(value, multiple):
    return pl.multiple_of(value, multiple)


class Place:
    def __init__(self):
        self.d = lax.axis_index("dp")
        self.z = lax.axis_index("fsdp")
        core = lax.rem(self.d, 2)
        across = lax.rem(lax.div(self.d, 2), 2)
        up = lax.div(self.d, 4)
        self.dc = self.d + 1 - 2 * core
        self.dx = self.d + 2 - 4 * across
        self.dy = self.d + 4 - 8 * up
        self.dd = self.dx + 4 - 8 * up
        self.odd = lax.rem(self.z, 2)
        z = self.z
        pick = lambda a, b, c, d: jnp.where(z < 2, jnp.where(z == 0, a, b), jnp.where(z == 2, c, d))
        self.order = [z, pick(1, 0, 3, 2), pick(2, 2, 1, 1), pick(3, 3, 0, 0)]

    def zt(self, step):
        return lax.rem(self.z + step, 4)

    def zf(self, step):
        return lax.rem(self.z + 4 - step, 4)

    def id(self, to):
        if to == "x":
            return (self.dx, self.z)
        if to == "y":
            return (self.dy, self.z)
        if to == "c":
            return (self.dc, self.z)
        if isinstance(to, tuple):
            return (self.d, to[1])
        return (self.d, self.zt(to))


def enter(place):
    barrier = pltpu.get_barrier_semaphore()
    for to in ("x", "y", "c", 1, 2, 3):
        pl.semaphore_signal(barrier, inc=1, device_id=place.id(to), device_id_type=MESH)
    pl.semaphore_wait(barrier, 6)


class Link:
    def __init__(self, place, send_sem, recv_sem):
        self.place, self.send_sem, self.recv_sem = place, send_sem, recv_sem
        self.count = 0
        self.copies = []

    def slot(self, many=1):
        self.count += many
        return self.count - many

    def copy(self, slot, source, target, to, land=None):
        return pltpu.make_async_remote_copy(
            src_ref=source, dst_ref=target, send_sem=self.send_sem.at[slot],
            recv_sem=self.recv_sem.at[slot if land is None else land], device_id=self.place.id(to),
            device_id_type=MESH)

    def send(self, slot, source, target, to, like, land=None, when=None):
        def start():
            self.copy(slot, source, target, to, land).start()

        if when is None:
            start()
        else:
            pl.when(when())(start)
        self.copies.append((slot, like, when))

    def got(self, slot, target):
        self.copy(slot, target, target, "x").wait_recv()

    def finish(self):
        for slot, like, when in self.copies:
            def done(slot=slot, like=like):
                view = like()
                self.copy(slot, view, view, "x").wait_send()

            if when is None:
                done()
            else:
                pl.when(when())(done)


class Gather:
    def __init__(self, link, place, block):
        p = place
        zr, zs = link.slot(4), link.slot(5)
        xs, ys, fx = link.slot(4), link.slot(4), link.slot(4)
        cs = link.slot(16)
        got = link.got
        send = functools.partial(link.send, like=lambda: block(0, 0))
        inner = lambda: (p.z == 1) | (p.z == 2)

        def z_step(a):
            def run():
                b = p.order[a]
                here = block(b, p.d)
                if a == 0:
                    send(zs, here, here, ("z", p.z + 1), land=zr + p.z, when=lambda: p.z < 3)
                    send(zs + 1, here, here, ("z", p.z - 1), land=zr + p.z, when=lambda: p.z > 0)
                else:
                    got(zr + b, here)
                    to = jnp.where(b < p.z, p.z + 1, p.z - 1)
                    send(zs + 1 + a, here, here, ("z", to), land=zr + b, when=inner)
            return run

        def x_step(a):
            def run():
                here = block(p.order[a], p.d)
                send(xs + a, here, here, "x")
                send(ys + a, here, here, "y")
                send(cs + a, here, here, "c")
            return run

        def turn(a):
            def run():
                b = p.order[a]
                bx, by = block(b, p.dx), block(b, p.dy)
                got(xs + a, bx)
                got(ys + a, by)
                if a in (0, 1):
                    send(fx + a, bx, bx, "y")
                else:
                    send(fx + a, by, by, "x")
                send(cs + 4 + a, bx, bx, "c")
                send(cs + 8 + a, by, by, "c")
            return run

        def corner(a):
            def run():
                bd = block(p.order[a], p.dd)
                got(fx + a, bd)
                send(cs + 12 + a, bd, bd, "c")
            return run

        def close():
            sib = p.dc - p.d
            for which, d in enumerate((p.d, p.dx, p.dy, p.dd)):
                for a in range(4):
                    got(cs + 4 * which + a, block(p.order[a], d + sib))

        self.z, self.x, self.t, self.q = ([make(a) for a in range(4)] for make in (z_step, x_step, turn, corner))
        self.close = close


def spread_z(link, place, ref):
    p = place
    zs, zr = link.slot(3), link.slot(4)

    def send():
        for step in (1, 3, 2):
            link.send(zs + step - 1, ref.at[p.z], ref.at[p.z], step, lambda: ref.at[0], land=zr + p.z)

    def wait():
        for step in range(1, 4):
            b = p.zf(step)
            link.got(zr + b, ref.at[b])

    return send, wait


def run(*events):
    def together():
        for event in events:
            event()
    return together


def window(value, odd, wide):
    rows, k = value.shape
    fill = jnp.zeros((rows, wide - k), F32)
    value = value.astype(F32)
    left = jnp.concatenate([value, fill], axis=1)
    right = jnp.concatenate([fill, value], axis=1)
    return jnp.where(odd == 0, left, right).astype(BF)


def merge_windows(blocks, full, tiles, rows_step):
    rows = full.shape[0]
    half = tiles // 2

    def body(i, _):
        r = pl.ds(mo(i * rows_step, rows_step), rows_step)
        for pair in range(2):
            even, odd = blocks.at[2 * pair], blocks.at[2 * pair + 1]
            base = pair * tiles * 128
            full[r, base:base + half * 128] = even[r, 0:half * 128]
            full[r, base + half * 128:base + (half + 1) * 128] = (
                even[r, half * 128:(half + 1) * 128] + odd[r, 0:128])
            full[r, base + (half + 1) * 128:base + tiles * 128] = odd[r, 128:(half + 1) * 128]
        return 0

    lax.fori_loop(0, rows // rows_step, body, 0)


def split3(value):
    high = value.astype(BF)
    rest = value - high.astype(F32)
    mid = rest.astype(BF)
    low = (rest - mid.astype(F32)).astype(BF)
    return high.astype(F32), mid.astype(F32), low.astype(F32)


def extend(head, pair, lane, one, two, three, four):
    base = 64 * (1 - head)
    extra = jnp.where(lane == base, one, jnp.where(lane == base + 1, two, jnp.where(
        lane == base + 2, three, jnp.where(lane == base + 3, four, 0.0))))
    keep = (lane < 64) if head == 0 else (lane >= 64)
    return jnp.where(keep, pair, extra).astype(BF)


def iota(shape, axis):
    return lax.broadcasted_iota(jnp.int32, shape, axis)


QB = 512


def first_kernel(length_ref, x_ref, wp_ref, wo_ref, we_ref, wc_ref, *refs):
    vec_refs, refs = refs[:8], refs[8:]
    first_body(length_ref, x_ref, wp_ref, wo_ref, we_ref, wc_ref, vec_refs, *refs)


def first_body(length_ref, x_ref, wp_ref, wo_ref, we_ref, wc_ref, vec_refs,
                 n1_out, proj_out, mixed_out, qa_out, wp_out, wo_out, we_out, c_out, v_out,
                 wp_blk, wo_blk, we, wp, wo, vb, n1, proj, mixed, qa, ka, va, vrow, cc,
                 send_sem, recv_sem, out_sem):
    p = Place()
    T, D = x_ref.shape
    R = wp_ref.shape[0]
    FF = we.shape[1]
    link = Link(p, send_sem, recv_sem)
    rows_of = lambda d: pl.ds(mo(d * R, 16), R)
    bp = lambda z, d: wp_blk.at[z, rows_of(d), :]
    bo = lambda z, d: wo_blk.at[z, rows_of(d), :]
    be = lambda z, d: we.at[rows_of(d), pl.ds(mo(z * (FF // 4), 128), FF // 4)]
    gp, go, ge = (Gather(link, p, b) for b in (bp, bo, be))
    c_send, c_wait = spread_z(link, p, cc)
    vs = [link.slot() for _ in range(7)]

    wp_blk[p.z, rows_of(p.d), :] = window(wp_ref[...], p.odd, wp_blk.shape[2])
    wo_blk[p.z, rows_of(p.d), :] = window(wo_ref[...], p.odd, wo_blk.shape[2])
    we[rows_of(p.d), pl.ds(mo(p.z * (FF // 4), 128), FF // 4)] = we_ref[...]
    cc[p.z] = wc_ref[...]
    for i, ref in enumerate(vec_refs):
        vb[p.d, i:i + 1, 0:ref.shape[0]] = ref[...].astype(F32).reshape(1, ref.shape[0]).astype(BF)

    outs = []

    def out(source, target):
        made = pltpu.make_async_copy(source, target, out_sem.at[len(outs)])
        made.start()
        outs.append(made)

    enter(p)
    send_v = lambda slot, d, to: link.send(vs[slot], vb.at[d], vb.at[d], to, lambda: vb.at[0])
    for slot, to in ((0, "x"), (1, "y"), (3, "c")):
        send_v(slot, p.d, to)
    run(gp.z[0], gp.x[0])()
    link.got(vs[0], vb.at[p.dx])
    link.got(vs[1], vb.at[p.dy])
    send_v(2, p.dx, "y")
    send_v(4, p.dx, "c")
    send_v(5, p.dy, "c")
    run(gp.z[1], gp.x[1], gp.t[0], gp.z[2], gp.x[2])()
    link.got(vs[2], vb.at[p.dd])
    send_v(6, p.dd, "c")
    sib = p.dc - p.d
    for slot, d in ((3, p.d), (4, p.dx), (5, p.dy), (6, p.dd)):
        link.got(vs[slot], vb.at[d + sib])
    got = vb[...].astype(F32)
    side = lambda row, wide: jnp.concatenate([got[i, row:row + 1, 0:wide] for i in range(8)], axis=1)
    bias = side(0, 2 * R)
    vrow[0:1, 0:D] = bias[:, 0:D]
    vrow[0:1, D:2 * D] = jnp.zeros((1, D), F32)
    vrow[0:1, 2 * D:3 * D] = bias[:, D:]
    vrow[1:2, :] = side(2, FF // 8)
    for row, at in ((2, 1), (3, 3), (4, 4), (5, 5), (6, 6), (7, 7)):
        vrow[row:row + 1, 0:D] = side(at, R)
    out(vrow, v_out)
    run(gp.t[1], gp.z[3], gp.x[3], ge.z[0], go.z[0])()

    LR = 128
    gain, shift = vrow[4:5, 0:D], vrow[5:6, 0:D]

    def norm_body(i, _):
        r = pl.ds(mo(i * LR, LR), LR)
        value = x_ref[r, :].astype(F32)
        u = value - jnp.mean(value, axis=-1, keepdims=True)
        spread = jnp.mean(u * u, axis=-1, keepdims=True)
        n1[r, :] = (u * lax.rsqrt(spread + eps_norm) * gain + shift).astype(BF)
        return 0

    norm_part = lambda k: lax.fori_loop(k * (T // LR // 4), (k + 1) * (T // LR // 4), norm_body, 0)
    norm_part(0)
    gp.t[2]()
    norm_part(1)
    gp.t[3]()
    norm_part(2)
    run(ge.x[0], go.x[0], gp.q[0])()
    norm_part(3)
    out(n1, n1_out)
    run(gp.q[1], gp.q[2], ge.z[1], ge.x[1], gp.q[3], gp.close, go.z[1], go.x[1])()
    merge_windows(wp_blk, wp, 9, 96)
    out(wp, wp_out)

    def project_body(i, _):
        for at, event in ((1, run(ge.z[2], ge.x[2])), (2, run(ge.t[0], go.t[0])), (3, run(go.z[2], go.x[2]))):
            pl.when(i == at)(event)
        r = pl.ds(mo(i * 256, 256), 256)
        left = n1[r, :]
        for j in range(3):
            cols = slice(j * D, (j + 1) * D)
            value = dot(left, wp[:, cols]) + vrow[0:1, cols]
            proj[r, cols] = value.astype(BF)
        return 0

    lax.fori_loop(0, T // 256, project_body, 0)
    out(proj, proj_out)

    length = length_ref[0]
    nq = T // QB

    def attend_steps(events):
        def body(step, _):
            for at, event in events:
                pl.when(step == at)(event)
            pair = lax.div(step, nq)
            part = lax.rem(step, nq)
            cols = lambda off: pl.ds(mo(off + pair * 128, 128), 128)

            @pl.when(part == 0)
            def _():
                lane, row = iota((T, 128), 1), iota((T, 128), 0)
                q = proj[:, cols(0)].astype(F32) * (HD ** -0.5)
                k = proj[:, cols(D)].astype(F32)
                v = proj[:, cols(2 * D)].astype(F32)
                dead = jnp.where(row < length, 0.0, neg_fill)
                for head in range(2):
                    ka[head] = extend(head, k, lane, 1.0, 1.0, 1.0, dead)
                    qa[pair * 2 + head] = extend(head, q, lane, 0.0, 0.0, 0.0, 1.0)
                    keep = (lane < 64) if head == 0 else (lane >= 64)
                    va[head] = jnp.where(keep, v, 1.0).astype(BF)

            r = pl.ds(mo(part * QB, QB), QB)
            lane = iota((QB, 128), 1)
            halves = []
            for head in range(2):
                query = qa[pair * 2 + head, r, :]
                scores = dot_nt(query, ka[head])
                top = jnp.max(scores, axis=-1, keepdims=True)
                powers = jnp.exp(scores - top).astype(BF)
                value = dot(powers, va[head])
                total = value[:, 64:65] if head == 0 else value[:, 0:1]
                one, two, three = split3(-(top + jnp.log(total)))
                qa[pair * 2 + head, r, :] = extend(head, query.astype(F32), lane, one, two, three, 1.0)
                halves.append(value * (1.0 / total))
            mixed[r, cols(0)] = jnp.where(lane < 64, halves[0], halves[1]).astype(BF)
            return 0

        lax.fori_loop(0, (H // 2) * nq, body, 0)

    attend_steps([(1, run(ge.t[1], go.t[1])), (2, run(ge.z[3], ge.x[3], go.z[3], go.x[3], c_send)),
                  (3, run(ge.t[2], ge.q[0])), (4, run(go.t[2], go.q[0])), (6, run(ge.q[1], go.q[1])), (7, ge.q[2]),
                  (8, run(ge.t[3], go.t[3], go.q[2])), (11, ge.q[3])])
    run(go.q[3], c_wait, ge.close, go.close)()
    out(cc, c_out)
    merge_windows(wo_blk, wo, 3, 96)
    out(wo, wo_out)
    out(we, we_out)
    out(mixed, mixed_out)
    out(qa, qa_out)
    link.finish()
    for made in outs:
        made.wait()


def first_call(length, x, wp, wo, we, wc, vectors):
    T, D = x.shape
    FF = we.shape[1] * 4
    ANY = pl.BlockSpec(memory_space=pl.ANY)
    V = pl.BlockSpec(memory_space=pltpu.VMEM)
    S = pl.BlockSpec(memory_space=pltpu.SMEM)
    sds = jax.ShapeDtypeStruct
    n = 3 * 37 + 7 + 7
    return pl.pallas_call(
        first_kernel,
        in_specs=[S] + [V] * 13,
        out_specs=[ANY] * 9,
        out_shape=[sds((T, D), BF), sds((T, 3 * D), BF), sds((T, D), BF), sds((H, T, 128), BF),
                   sds((D, 3 * D), BF), sds((D, D), BF), sds((D, FF), BF), sds((4,) + wc.shape, BF), sds((8, FF), F32)],
        scratch_shapes=[
            pltpu.VMEM((4, D, 640), BF), pltpu.VMEM((4, D, 256), BF), pltpu.VMEM((D, FF), BF),
            pltpu.VMEM((D, 3 * D), BF), pltpu.VMEM((D, D), BF), pltpu.VMEM((8, 16, FF // 8), BF),
            pltpu.VMEM((T, D), BF), pltpu.VMEM((T, 3 * D), BF), pltpu.VMEM((T, D), BF),
            pltpu.VMEM((H, T, 128), BF), pltpu.VMEM((2, T, 128), BF), pltpu.VMEM((2, T, 128), BF),
            pltpu.VMEM((8, FF), F32), pltpu.VMEM((4,) + wc.shape, BF),
            pltpu.SemaphoreType.DMA((n,)), pltpu.SemaphoreType.DMA((n,)), pltpu.SemaphoreType.DMA((9,)),
        ],
        compiler_params=pltpu.CompilerParams(
            collective_id=0, has_side_effects=True, vmem_limit_bytes=60 << 20),
        name="first_part",
    )(length, x, wp, wo, we, wc, *vectors)


def layer_norm(values, gain_row, shift_row):
    centre = jnp.mean(values, axis=-1, keepdims=True)
    centred = values - centre
    spread = jnp.mean(centred * centred, axis=-1, keepdims=True)
    return centred * lax.rsqrt(spread + eps_norm) * gain_row + shift_row


def gelu_exact(values):
    return jax.nn.gelu(values, approximate=False)


def matmul(first, second):
    return jnp.dot(first, second, preferred_element_type=jnp.float32)


def over_rows(first, second):
    return lax.dot_general(
        first, second, (((0,), (0,)), ((), ())), preferred_element_type=jnp.float32
    )


def over_columns(first, second):
    return lax.dot_general(
        first, second, (((1,), (1,)), ((), ())), preferred_element_type=jnp.float32
    )


def fetch_forward(
    project_weight,
    output_weight,
    expand_weight,
    contract_weight,
    project_bias,
    output_bias,
    expand_bias,
    contract_bias,
    first_gain,
    first_shift,
    second_gain,
    second_shift,
):
    wide_project, wide_output, wide_expand, wide_contract = (
        lax.all_gather(project_weight, "fsdp", axis=1, tiled=True),
        lax.all_gather(output_weight, "fsdp", axis=1, tiled=True),
        lax.all_gather(expand_weight, "fsdp", axis=1, tiled=True),
        lax.all_gather(contract_weight, "fsdp", axis=1, tiled=True),
    )
    return (
        lax.all_gather(wide_project, "dp", axis=0, tiled=True),
        lax.all_gather(wide_output, "dp", axis=0, tiled=True),
        lax.all_gather(wide_expand, "dp", axis=0, tiled=True),
        lax.all_gather(wide_contract, "dp", axis=0, tiled=True),
        lax.all_gather(project_bias, "dp", axis=0, tiled=True),
        lax.all_gather(output_bias, "dp", axis=0, tiled=True),
        lax.all_gather(expand_bias, "dp", axis=0, tiled=True),
        lax.all_gather(contract_bias, "dp", axis=0, tiled=True),
        lax.all_gather(first_gain, "dp", axis=0, tiled=True),
        lax.all_gather(first_shift, "dp", axis=0, tiled=True),
        lax.all_gather(second_gain, "dp", axis=0, tiled=True),
        lax.all_gather(second_shift, "dp", axis=0, tiled=True),
    )


def fetch_backward(
    project_weight,
    output_weight,
    expand_weight,
    contract_weight,
    project_bias,
    output_bias,
    expand_bias,
    contract_bias,
    first_gain,
    first_shift,
    second_gain,
    second_shift,
):
    wide_project, wide_output, wide_expand, wide_contract = (
        lax.all_gather(project_weight, "fsdp", axis=1, tiled=True),
        lax.all_gather(output_weight, "fsdp", axis=1, tiled=True),
        lax.all_gather(expand_weight, "fsdp", axis=1, tiled=True),
        lax.all_gather(contract_weight, "fsdp", axis=1, tiled=True),
    )
    return (
        lax.all_gather(wide_project, "dp", axis=0, tiled=True),
        lax.all_gather(wide_output, "dp", axis=0, tiled=True),
        lax.all_gather(wide_expand, "dp", axis=0, tiled=True),
        lax.all_gather(wide_contract, "dp", axis=0, tiled=True),
        lax.all_gather(project_bias, "dp", axis=0, tiled=True),
        lax.all_gather(output_bias, "dp", axis=0, tiled=True),
        lax.all_gather(expand_bias, "dp", axis=0, tiled=True),
        lax.all_gather(contract_bias, "dp", axis=0, tiled=True),
        lax.all_gather(first_gain, "dp", axis=0, tiled=True),
        lax.all_gather(first_shift, "dp", axis=0, tiled=True),
        lax.all_gather(second_gain, "dp", axis=0, tiled=True),
        lax.all_gather(second_shift, "dp", axis=0, tiled=True),
    )


def split_heads(cell_rows, block_rows):
    slot_count = cell_rows.shape[0]
    width = cell_rows.shape[1] // 3
    query_blocks = cell_rows[:, :width].reshape(slot_count // block_rows, block_rows, H, HD)
    keys_all = cell_rows[:, width : 2 * width].reshape(slot_count, H, HD)
    values_all = cell_rows[:, 2 * width :].reshape(slot_count, H, HD)
    return (query_blocks, keys_all, values_all)


def block_scores(query_block, keys_all, key_live):
    scores = jnp.einsum(
        "qhe,khe->hqk", query_block, keys_all, preferred_element_type=jnp.float32
    ) * HD ** (-0.5)
    return jnp.where(key_live[None, None, :], scores, neg_fill)


def attend_forward(query_block, keys_all, values_all, key_live):
    scores = block_scores(query_block, keys_all, key_live)
    row_max = jnp.max(scores, axis=-1, keepdims=True)
    powers = jnp.exp(scores - row_max)
    row_total = jnp.sum(powers, axis=-1, keepdims=True)
    weights = (powers / row_total).astype(jnp.bfloat16)
    mixed_block = jnp.einsum(
        "hqk,khe->qhe", weights, values_all, preferred_element_type=jnp.float32
    )
    return (mixed_block, (row_max + jnp.log(row_total))[:, :, 0])


def attend_backward(query_block, grad_block, log_block, keys_all, values_all, key_live):
    scores = block_scores(query_block, keys_all, key_live)
    weights = jnp.exp(scores - log_block[:, :, None])
    grad_weights = jnp.einsum(
        "qhe,khe->hqk", grad_block, values_all, preferred_element_type=jnp.float32
    )
    row_inner = jnp.sum(grad_weights * weights, axis=-1, keepdims=True)
    grad_scores = (weights * (grad_weights - row_inner)).astype(jnp.bfloat16)
    grad_query = jnp.einsum(
        "hqk,khe->qhe", grad_scores, keys_all, preferred_element_type=jnp.float32
    ) * HD ** (-0.5)
    grad_key = jnp.einsum(
        "hqk,qhe->khe", grad_scores, query_block, preferred_element_type=jnp.float32
    ) * HD ** (-0.5)
    grad_value = jnp.einsum(
        "hqk,qhe->khe", weights.astype(jnp.bfloat16), grad_block, preferred_element_type=jnp.float32
    )
    return (grad_query, grad_key, grad_value)


def per_device(
    tokens,
    lengths,
    cotangent,
    project_weight,
    project_bias,
    output_weight,
    output_bias,
    expand_weight,
    expand_bias,
    contract_weight,
    contract_bias,
    first_gain,
    first_shift,
    second_gain,
    second_shift,
):
    fetched = fetch_forward(
        project_weight,
        output_weight,
        expand_weight,
        contract_weight,
        project_bias,
        output_bias,
        expand_bias,
        contract_bias,
        first_gain,
        first_shift,
        second_gain,
        second_shift,
    )
    full_project, full_output, full_expand, full_contract = (
        fetched[0],
        fetched[1],
        fetched[2],
        fetched[3],
    )
    vectors = [item.astype(jnp.float32) for item in fetched[4:]]
    bias_project, bias_output, bias_expand, bias_contract = (
        vectors[0],
        vectors[1],
        vectors[2],
        vectors[3],
    )
    gain_one, shift_one, gain_two, shift_two = (vectors[4], vectors[5], vectors[6], vectors[7])
    cell_count = lengths.shape[0]
    slot_count = tokens.shape[0] // cell_count
    width = tokens.shape[1]
    block_rows = min(512, slot_count)
    positions = jnp.arange(slot_count, dtype=jnp.int32)
    live_keys = positions[None, :] < lengths[:, None]
    live_rows = live_keys.reshape(-1)
    rows_in = tokens.astype(jnp.float32)
    normed_one = layer_norm(rows_in, gain_one, shift_one).astype(jnp.bfloat16)
    bias_full = jnp.concatenate(
        [bias_project[:width], jnp.zeros((width,), jnp.float32), bias_project[width:]]
    )
    projected = (matmul(normed_one, full_project) + bias_full).astype(jnp.bfloat16)
    cell_index = 0
    query_blocks, keys_all, values_all = split_heads(projected, block_rows)
    key_live = live_keys[cell_index]
    mixed_blocks, log_blocks = lax.map(
        lambda query_block: attend_forward(query_block, keys_all, values_all, key_live),
        query_blocks,
    )
    mixed_list = mixed_blocks.reshape(slot_count, width)
    log_list = [log_blocks]
    mixed_low = mixed_list.astype(jnp.bfloat16)
    middle = rows_in + (matmul(mixed_low, full_output) + bias_output)
    normed_two = layer_norm(middle, gain_two, shift_two).astype(jnp.bfloat16)
    hidden = matmul(normed_two, full_expand) + bias_expand
    active = gelu_exact(hidden).astype(jnp.bfloat16)
    result = middle + (matmul(active, full_contract) + bias_contract)
    block_out = jnp.where(live_rows[:, None], result, 0.0).astype(jnp.bfloat16)
    again = fetch_backward(
        project_weight,
        output_weight,
        expand_weight,
        contract_weight,
        project_bias,
        output_bias,
        expand_bias,
        contract_bias,
        first_gain,
        first_shift,
        second_gain,
        second_shift,
    )
    back_project, back_output, back_expand, back_contract = (again[0], again[1], again[2], again[3])
    grad_out = jnp.where(live_rows[:, None], cotangent.astype(jnp.float32), 0.0)
    grad_out_low = grad_out.astype(jnp.bfloat16)
    grad_contract = over_rows(active, grad_out_low)
    grad_contract_bias = jnp.sum(grad_out, axis=0)
    grad_active = over_columns(grad_out_low, back_contract)
    gelu_value, gelu_pull = jax.vjp(gelu_exact, hidden)
    grad_hidden = gelu_pull(grad_active)[0].astype(jnp.bfloat16)
    grad_expand = over_rows(normed_two, grad_hidden)
    grad_expand_bias = jnp.sum(grad_hidden.astype(jnp.float32), axis=0)
    grad_normed_two = over_columns(grad_hidden, back_expand)
    norm_value, second_pull = jax.vjp(layer_norm, middle, gain_two, shift_two)
    grad_middle, grad_gain_two, grad_shift_two = second_pull(grad_normed_two)
    grad_middle = grad_middle + grad_out
    grad_branch = grad_middle.astype(jnp.bfloat16)
    grad_output = over_rows(mixed_low, grad_branch)
    grad_output_bias = jnp.sum(grad_branch.astype(jnp.float32), axis=0)
    grad_mixed = over_columns(grad_branch, back_output).astype(jnp.bfloat16)
    cell_index = 0
    query_blocks, keys_all, values_all = split_heads(projected, block_rows)
    key_live = live_keys[cell_index]
    grad_blocks = grad_mixed.reshape(slot_count // block_rows, block_rows, H, HD)

    def visit_block(carried, inputs):
        query_block, grad_block, log_block = inputs
        grad_query, grad_key, grad_value = attend_backward(
            query_block, grad_block, log_block, keys_all, values_all, key_live
        )
        return ((carried[0] + grad_key, carried[1] + grad_value), grad_query)

    initial = (
        jnp.zeros((slot_count, H, HD), jnp.float32),
        jnp.zeros((slot_count, H, HD), jnp.float32),
    )
    (key_sums, value_sums), query_grads = lax.scan(
        visit_block, initial, (query_blocks, grad_blocks, log_list[cell_index])
    )
    grad_cells = jnp.concatenate(
        [
            query_grads.reshape(slot_count, width),
            key_sums.reshape(slot_count, width),
            value_sums.reshape(slot_count, width),
        ],
        axis=1,
    )
    grad_projected = grad_cells.astype(jnp.bfloat16)
    grad_project = over_rows(normed_one, grad_projected)
    column_sums = jnp.sum(grad_projected.astype(jnp.float32), axis=0)
    grad_project_bias = jnp.concatenate([column_sums[:width], column_sums[2 * width :]])
    grad_normed_one = over_columns(grad_projected, back_project)
    first_value, first_pull = jax.vjp(layer_norm, rows_in, gain_one, shift_one)
    grad_rows_in, grad_gain_one, grad_shift_one = first_pull(grad_normed_one)
    tokens_grad = (grad_rows_in + grad_middle).astype(jnp.bfloat16)
    reduced = (
        lax.psum_scatter(grad_project, "dp", scatter_dimension=0, tiled=True),
        lax.psum_scatter(grad_output, "dp", scatter_dimension=0, tiled=True),
        lax.psum_scatter(grad_expand, "dp", scatter_dimension=0, tiled=True),
        lax.psum_scatter(grad_contract, "dp", scatter_dimension=0, tiled=True),
        lax.psum_scatter(grad_project_bias, "dp", scatter_dimension=0, tiled=True),
        lax.psum_scatter(grad_output_bias, "dp", scatter_dimension=0, tiled=True),
        lax.psum_scatter(grad_expand_bias, "dp", scatter_dimension=0, tiled=True),
        lax.psum_scatter(grad_contract_bias, "dp", scatter_dimension=0, tiled=True),
        lax.psum_scatter(grad_gain_one, "dp", scatter_dimension=0, tiled=True),
        lax.psum_scatter(grad_shift_one, "dp", scatter_dimension=0, tiled=True),
        lax.psum_scatter(grad_gain_two, "dp", scatter_dimension=0, tiled=True),
        lax.psum_scatter(grad_shift_two, "dp", scatter_dimension=0, tiled=True),
    )
    shard_project, shard_output, shard_expand, shard_contract = (
        lax.psum_scatter(
            reduced[0].astype(jnp.bfloat16), "fsdp", scatter_dimension=1, tiled=True
        ).astype(jnp.float32),
        lax.psum_scatter(
            reduced[1].astype(jnp.bfloat16), "fsdp", scatter_dimension=1, tiled=True
        ).astype(jnp.float32),
        lax.psum_scatter(
            reduced[2].astype(jnp.bfloat16), "fsdp", scatter_dimension=1, tiled=True
        ).astype(jnp.float32),
        lax.psum_scatter(
            reduced[3].astype(jnp.bfloat16), "fsdp", scatter_dimension=1, tiled=True
        ).astype(jnp.float32),
    )
    summed = lax.psum(
        (
            reduced[4],
            reduced[5],
            reduced[6],
            reduced[7],
            reduced[8],
            reduced[9],
            reduced[10],
            reduced[11],
        ),
        "fsdp",
    )
    return (
        block_out,
        tokens_grad,
        shard_project,
        summed[0],
        shard_output,
        summed[1],
        shard_expand,
        summed[2],
        shard_contract,
        summed[3],
        summed[4],
        summed[5],
        summed[6],
        summed[7],
    )


def scatter_events(link, place, col, pair_of, lc, lxh, lyh, lx, ly):
    p = place
    family = (p.dc, p.dx + p.dc - p.d, p.dy + p.dc - p.d, p.dd + p.dc - p.d)
    cs = [link.slot() for _ in range(4)]
    hx, hy, fx, fy = (link.slot() for _ in range(4))
    got = link.got

    def add(target, *terms):
        total = target[...].astype(F32)
        for term in terms:
            total = total + term[...].astype(F32)
        target[...] = total.astype(BF)

    def to_sibling(which):
        link.send(cs[which], col(family[which]), lc.at[which], "c", lambda: col(0))

    def halves():
        got(cs[3], lc.at[3])
        add(col(p.dd), lc.at[3])
        link.send(hx, pair_of(col(p.dd), 0), lxh, "x", lambda: lxh)
        link.send(hy, pair_of(col(p.dd), 1), lyh, "y", lambda: lyh)

    def near():
        got(cs[1], lc.at[1])
        got(cs[2], lc.at[2])
        add(col(p.dx), lc.at[1])
        add(col(p.dy), lc.at[2])

    def pass_y():
        got(hx, lxh)
        add(pair_of(col(p.dy), 0), lxh)
        link.send(fy, col(p.dy), ly, "y", lambda: ly)

    def pass_x():
        got(hy, lyh)
        add(pair_of(col(p.dx), 1), lyh)
        link.send(fx, col(p.dx), lx, "x", lambda: lx)

    def own():
        got(cs[0], lc.at[0])

    def total():
        got(fx, lx)
        got(fy, ly)
        add(col(p.d), lc.at[0], lx, ly)

    return to_sibling, [halves, near, pass_y, pass_x, own, total]


def z_sum(link, place, block, lz, finish):
    p = place
    zs = link.slot(4)

    def send():
        for step in (1, 3, 2):
            link.send(zs + step, block(p.zt(step)), lz.at[step], step, lambda: lz.at[0])

    def last():
        total = block(p.z)[...].astype(F32)
        for step in (1, 3, 2):
            link.got(zs + step, lz.at[step])
            total = total + lz[step].astype(F32)
        finish(total)

    return send, last


def gelu_pair(value):
    lift = 0.5 * (1.0 + lax.erf(value * 0.7071067811865476))
    bell = jnp.exp(value * value * -0.5) * 0.3989422804014327
    return value * lift, lift + value * bell


def second_kernel(length_ref, x_ref, cot_ref, mixed_ref, wo_ref, we_hbm, c_hbm, v_ref,
                  block_out, dmixed_out, dmiddle_out, ge_out, go_out, gc_out, vg_out,
                  we, wct, act, slope, middle, n2t, dot_t, mixed_t, dbranch, dout, gc, go, dmixed, bout, vg,
                  lc, lxh, lyh, lx, ly, send_sem, recv_sem, out_sem):
    p = Place()
    T, D = x_ref.shape
    FF = we.shape[1]
    R = D // 8
    Q = FF // 4
    C8 = FF // 8
    link = Link(p, send_sem, recv_sem)
    bc = lambda z, d: wct.at[pl.ds(mo(z * (D // 4), 16), D // 4), pl.ds(mo(d * C8, 128), C8)]
    gather = Gather(link, p, bc)

    to_sibling, scatter = scatter_events(
        link, p, lambda d: gc.at[d], lambda ref, h: ref.at[pl.ds(2 * h, 2)], lc, lxh, lyh, lx, ly)
    load = pltpu.make_async_copy(we_hbm, we, out_sem.at[0])
    columns = [pltpu.make_async_copy(c_hbm.at[z], bc(z, p.d), out_sem.at[8 + z]) for z in range(4)]
    for made in columns:
        made.start()
    load.start()
    enter(p)
    for made in columns:
        made.wait()
    run(*gather.x)()
    length = length_ref[0]
    LR = 256
    rows = lambda i: pl.ds(mo(i * LR, LR), LR)
    vec = lambda i: v_ref[i:i + 1, 0:D]
    vg[...] = jnp.zeros_like(vg)

    def at(i, spots):
        for where, event in spots:
            pl.when(i == where)(event)

    def norm(value):
        u = value - jnp.mean(value, axis=-1, keepdims=True)
        r = lax.rsqrt(jnp.mean(u * u, axis=-1, keepdims=True) + eps_norm)
        return u * r, r

    def middle_body(i, _):
        at(i, [(3, gather.t[0])])
        r = rows(i)
        value = x_ref[r, :].astype(F32) + (dot(mixed_ref[r, :], wo_ref[...]) + vec(2))
        middle[r, :] = value
        xhat, _ = norm(value)
        n2 = (xhat * vec(6) + vec(7)).astype(BF)
        dmixed[r, :] = n2
        n2t[:, r] = n2.T
        live = iota((LR, D), 0) + i * LR < length
        grad = jnp.where(live, cot_ref[r, :].astype(F32), 0.0)
        vg[7:8, :] += jnp.sum(grad, axis=0, keepdims=True)
        dout[r, :] = grad.astype(BF)
        dot_t[:, r] = grad.astype(BF).T
        mixed_t[:, r] = mixed_ref[r, :].T
        return 0

    lax.fori_loop(0, T // LR, middle_body, 0)
    load.wait()

    def hidden_body(i, _):
        at(i, [(1, gather.t[1]), (2, gather.t[2]), (3, run(gather.t[3], gather.q[0]))])
        r = rows(i)
        left = dmixed[r, :]
        for j in range(4):
            cols = slice(j * Q, (j + 1) * Q)
            first, second = gelu_pair(dot(left, we[:, cols]) + v_ref[1:2, cols])
            act[r, cols] = first.astype(BF)
            slope[r, cols] = second.astype(BF)
        return 0

    lax.fori_loop(0, T // LR, hidden_body, 0)

    def column(d):
        value = dot(dot_t[...], act[:, pl.ds(mo(d * C8, 128), C8)])
        gc[d] = value.reshape(4, D // 4, C8).astype(BF)

    sib = p.dc - p.d
    column(p.dd + sib)
    to_sibling(3)
    column(p.dd)
    gather.q[1]()
    column(p.dx + sib)
    to_sibling(1)
    column(p.dy + sib)
    to_sibling(2)
    gather.q[2]()
    column(p.dx)
    scatter[0]()
    column(p.dy)
    gather.q[3]()
    column(p.d + sib)
    to_sibling(0)
    column(p.d)
    run(scatter[1], gather.close)()

    def back_body(i, _):
        at(i, [(1, run(scatter[2], scatter[3], scatter[4]))])
        r = rows(i)
        grad_low = dout[r, :]
        result = middle[r, :] + vec(3)
        dn = jnp.zeros((LR, D), F32)
        for j in range(4):
            cols = slice(j * Q, (j + 1) * Q)
            dh = dot(grad_low, wct[:, cols]) * slope[r, cols].astype(F32)
            low = dh.astype(BF)
            slope[r, cols] = low
            vg[3 + j:4 + j, :] += jnp.sum(low.astype(F32), axis=0, keepdims=True)
            result = result + dot_nt(act[r, cols], wct[:, cols])
            dn = dn + dot_nt(low, we[:, cols])
        live = iota((LR, D), 0) + i * LR < length
        bout[r, :] = jnp.where(live, result, 0.0).astype(BF)
        xhat, spread = norm(middle[r, :])
        vg[10:11, :] += jnp.sum(dn * xhat, axis=0, keepdims=True)
        vg[11:12, :] += jnp.sum(dn, axis=0, keepdims=True)
        gx = dn * vec(6)
        back = spread * (gx - jnp.mean(gx, axis=-1, keepdims=True)
                         - xhat * jnp.mean(gx * xhat, axis=-1, keepdims=True))
        total = dout[r, :].astype(F32) + back
        middle[r, :] = total
        branch = total.astype(BF)
        dbranch[r, :] = branch
        vg[2:3, :] += jnp.sum(branch.astype(F32), axis=0, keepdims=True)
        dmixed[r, :] = dot_nt(branch, wo_ref[...]).astype(BF)
        return 0

    lax.fori_loop(0, T // LR, back_body, 0)
    outs = []

    def out(source, target):
        made = pltpu.make_async_copy(source, target, out_sem.at[1 + len(outs)])
        made.start()
        outs.append(made)

    out(bout, block_out)
    out(dmixed, dmixed_out)
    out(middle, dmiddle_out)
    for z in range(4):
        act[0:D, z * Q:(z + 1) * Q] = dot(n2t[...], slope[:, z * Q:(z + 1) * Q]).astype(BF)
    out(act.at[0:D, :], ge_out)
    scatter[5]()
    out(gc.at[p.d], gc_out)
    for z in range(4):
        cols = slice(3 * z // 2 * 128, 3 * z // 2 * 128 + 256)
        go[:, z] = dot(mixed_t[...], dbranch[:, cols]).reshape(8, R, 256).astype(BF)
    out(go, go_out)
    vg_out[...] = vg[...]
    link.finish()
    for made in outs:
        made.wait()


ANY = pl.BlockSpec(memory_space=pl.ANY)
VM = pl.BlockSpec(memory_space=pltpu.VMEM)
SM = pl.BlockSpec(memory_space=pltpu.SMEM)
sds = jax.ShapeDtypeStruct


def second_call(length, x, cot, mixed, wo, we, wc, v):
    T, D = x.shape
    FF = we.shape[1]
    n = 37 + 8
    R, C8, Z = D // 8, FF // 8, D // 4
    vm = pltpu.VMEM
    return pl.pallas_call(
        second_kernel,
        in_specs=[SM, VM, VM, VM, VM, ANY, ANY, VM],
        out_specs=[ANY] * 6 + [VM],
        out_shape=[sds((T, D), BF), sds((T, D), BF), sds((T, D), F32), sds((D, FF), BF), sds((8, 4, R, 256), BF),
                   sds((4, Z, C8), BF), sds((16, D), F32)],
        scratch_shapes=[
            vm((D, FF), BF), vm((D, FF), BF), vm((T, FF), BF), vm((T, FF), BF), vm((T, D), F32),
            vm((D, T), BF), vm((D, T), BF), vm((D, T), BF), vm((T, D), BF), vm((T, D), BF),
            vm((8, 4, Z, C8), BF), vm((8, 4, R, 256), BF), vm((T, D), BF), vm((T, D), BF), vm((16, D), F32),
            vm((4, 4, Z, C8), BF), vm((2, Z, C8), BF), vm((2, Z, C8), BF), vm((4, Z, C8), BF), vm((4, Z, C8), BF),
            pltpu.SemaphoreType.DMA((n,)), pltpu.SemaphoreType.DMA((n,)), pltpu.SemaphoreType.DMA((12,)),
        ],
        compiler_params=pltpu.CompilerParams(
            collective_id=1, has_side_effects=True, vmem_limit_bytes=62 << 20),
        name="second_part",
    )(length, x, cot, mixed, wo, we, wc, v)


def third_kernel(length_ref, proj_hbm, qa_hbm, mixed_hbm, dm_hbm, n1_hbm, wp_hbm, x_hbm, dmiddle_hbm, ge_hbm, go_hbm,
                 gc_hbm, vg_ref, v_ref,
                 tokens_out, gp_out, go_out, ge_out, gc_out, vec_out,
                 proj, qa, mixed, dm, n1, n1t, wpp, x, dmiddle, ge, go, dproj, tg, gp,
                 ka, da, dq, va, kt, vs, vl,
                 lce, lxhe, lyhe, lxe, lye, lze, lco, lxho, lyho, lxo, lyo, lzo,
                 lcp, lxhp, lyhp, lxp, lyp, lzp, gpw, gcol, lzc,
                 send_sem, recv_sem, load_sem):
    p = Place()
    T, D = x.shape
    FF = ge.shape[1]
    R = D // 8
    Q = FF // 4
    pairs = H // 2
    KB = 256
    parts = T // KB
    link = Link(p, send_sem, recv_sem)
    loads = []

    def load(source, target):
        made = pltpu.make_async_copy(source, target, load_sem.at[len(loads)])
        made.start()
        loads.append(made)
        return made

    first_loads = [load(a, b) for a, b in ((proj_hbm, proj), (qa_hbm, qa), (mixed_hbm, mixed), (dm_hbm, dm))]
    ge_load, gc_load, go_load, n1_load = load(ge_hbm, ge), load(gc_hbm, gcol), load(go_hbm, go), load(n1_hbm, n1)
    late = [load(x_hbm, x), load(dmiddle_hbm, dmiddle)]
    for i in range(pairs):
        for s in range(3):
            late.append(load(wp_hbm.at[:, pl.ds((s * pairs + i) * 128, 128)],
                             wpp.at[:, pl.ds((i * 3 + s) * 128, 128)]))

    def finish_e(total):
        ge_out[...] = total

    def finish_o(total):
        go_out[...] = jnp.where(p.odd == 0, total[:, 0:192], total[:, 64:256])

    rows_of = lambda d: pl.ds(mo(d * R, 16), R)
    def finish_c(total):
        gc_out[...] = total

    e_col, o_col = (lambda d: ge.at[rows_of(d), :]), (lambda d: go.at[d])
    e_sib, ev_e = scatter_events(
        link, p, e_col, lambda ref, h: ref.at[:, pl.ds(h * (FF // 2), FF // 2)], lce, lxhe, lyhe, lxe, lye)
    o_sib, ev_o = scatter_events(
        link, p, o_col, lambda ref, h: ref.at[pl.ds(2 * h, 2)], lco, lxho, lyho, lxo, lyo)
    e_send, e_last = z_sum(link, p, lambda z: e_col(p.d).at[:, pl.ds(mo(z * Q, 128), Q)], lze, finish_e)
    o_send, o_last = z_sum(link, p, lambda z: o_col(p.d).at[z], lzo, finish_o)
    c_send, c_last = z_sum(link, p, lambda z: gcol.at[z], lzc, finish_c)
    ended = []
    combos = []
    for i in range(pairs):
        for s in range(3):
            tile = s * pairs + i
            for owner in range(4):
                left = 9 * owner // 2
                if left <= tile < left + 5:
                    combos.append((i, s, owner, tile - left))
    assert len(combos) == 20
    z_slots = [[link.slot() for _ in range(3)] for _ in combos]

    def pair_scatter(i):
        column = lambda d: gp.at[i, d]
        sib, events = scatter_events(
            link, p, column, lambda ref, h: ref.at[pl.ds(h * (R // 2), R // 2)],
            lcp.at[i], lxhp.at[i], lyhp.at[i], lxp.at[i], lyp.at[i])
        mine = [(at, c) for at, c in enumerate(combos) if c[0] == i]

        def along(add_own):
            def run():
                add_own()
                for at, (_, s, owner, _) in mine:
                    @pl.when(p.z != owner)
                    def _():
                        step = lax.rem(owner - p.z + 4, 4)
                        part = column(p.d).at[:, pl.ds(s * 128, 128)]
                        link.copy(z_slots[at][0] + step - 1, part, lzp.at[at, step - 1], ("z", owner)).start()
            return run

        def last():
            for at, (_, s, owner, place) in mine:
                @pl.when(p.z == owner)
                def _():
                    total = gp[i, p.d, :, s * 128:(s + 1) * 128].astype(F32)
                    for step in range(1, 4):
                        link.got(z_slots[at][step - 1], lzp.at[at, step - 1])
                        total = total + lzp[at, step - 1].astype(F32)
                    gpw[:, place * 128:(place + 1) * 128] = total

        def ending():
            for at, (_, s, owner, _) in mine:
                @pl.when(p.z != owner)
                def _():
                    step = lax.rem(owner - p.z + 4, 4)
                    view = lzp.at[at, 0]
                    link.copy(z_slots[at][0] + step - 1, view, view, "x").wait_send()

        ended.append(ending)

        def start():
            for k in (3, 1, 2, 0):
                sib(k)

        return [start] + events[:5] + [along(events[5]), last]

    ev_p = [pair_scatter(i) for i in range(pairs)]

    enter(p)
    for made in first_loads:
        made.wait()
    length = length_ref[0]

    def start_e():
        ge_load.wait()
        for k in (3, 1, 2, 0):
            e_sib(k)

    def start_o():
        go_load.wait()
        for k in (3, 1, 2, 0):
            o_sib(k)

    def turn_n1():
        n1_load.wait()
        for i in range(T // 256):
            n1t[:, i * 256:(i + 1) * 256] = n1[i * 256:(i + 1) * 256, :].T

    def start_c():
        gc_load.wait()
        c_send()

    e, o = ev_e, ev_o
    q = ev_p
    timeline = [
        (0, start_c), (0, start_e), (1, start_o), (1, turn_n1), (2, e[0]), (3, e[1]), (3, e[4]), (4, q[0][0]), (4, o[0]), (4, o[1]), (4, o[4]),
        (5, q[0][1]), (5, q[0][2]), (6, q[0][5]), (7, e[2]), (7, e[3]), (8, c_last), (8, o[2]), (8, o[3]), (8, q[1][0]),
        (9, q[0][3]), (9, q[0][4]), (9, q[1][1]), (9, q[1][2]), (10, q[1][5]), (12, q[2][0]), (13, q[2][1]), (13, q[2][2]),
        (14, e[5]), (14, e_send), (14, q[2][5]), (16, o[5]), (16, o_send), (16, q[3][0]), (16, q[2][3]), (16, q[2][4]),
        (16, q[1][3]), (16, q[1][4]), (17, q[0][6]), (17, q[3][1]), (17, q[3][2]), (18, q[3][5]), (19, q[2][6]),
        (20, q[4][0]), (20, q[3][3]), (20, q[3][4]), (20, q[1][6]), (21, e_last), (21, q[4][1]), (21, q[4][2]),
        (22, q[4][5]), (22, q[0][7]), (22, q[3][6]), (22, o_last), (23, q[4][3]), (23, q[4][4]), (23, q[1][7]), (23, q[2][7])]
    timeline.sort(key=lambda e: e[0])

    def body(step, _):
        for at, event in timeline:
            if at < pairs * parts:
                pl.when(step == at)(event)
        pair = lax.div(step, parts)
        part = lax.rem(step, parts)
        ps = lambda off: pl.ds(mo(off + pair * 128, 128), 128)
        own = lambda s: pl.ds(mo(pair * 384 + s * 128, 128), 128)

        @pl.when(part == 0)
        def _():
            lane, row = iota((T, 128), 1), iota((T, 128), 0)
            k = proj[:, ps(D)].astype(F32)
            v = proj[:, ps(2 * D)].astype(F32)
            do = dm[:, ps(0)].astype(F32)
            pr = do * mixed[:, ps(0)].astype(F32)
            dead = jnp.where(row < length, 0.0, neg_fill)
            for head in range(2):
                keep = (lane < 64) if head == 0 else (lane >= 64)
                delta = jnp.sum(jnp.where(keep, pr, 0.0), axis=-1, keepdims=True)
                one, two, three = split3(-delta)
                da[head] = extend(head, do, lane, one, two, three, 0.0)
                ka[head] = extend(head, k, lane, 1.0, 1.0, 1.0, dead)
                va[head] = extend(head, v, lane, 1.0, 1.0, 1.0, 0.0)
                kt[head] = jnp.where(keep, k, 0.0).astype(BF).T
            dq[...] = jnp.zeros_like(dq)

        r = pl.ds(mo(part * KB, KB), KB)
        lk = iota((KB, 128), 1)
        dks, dvs = [], []
        for head in range(2):
            weights = jnp.exp(dot_nt(ka[head, r, :], qa[pair * 2 + head]))
            low = weights.astype(BF)
            ds = (weights * dot_nt(va[head, r, :], da[head])).astype(BF)
            dvs.append(dot(low, da[head]))
            dks.append(dot(ds, qa[pair * 2 + head]))
            dq[head] += dot(kt[head, :, r], ds)
        dproj[r, own(1)] = jnp.where(lk < 64, dks[0], dks[1]).astype(BF)
        dproj[r, own(2)] = jnp.where(lk < 64, dvs[0], dvs[1]).astype(BF)

        @pl.when(part == parts - 1)
        def _():
            dproj[:, own(0)] = ((dq[0] + dq[1]) * (HD ** -0.5)).T.astype(BF)
            value = dot(n1t[...], dproj[:, pl.ds(mo(pair * 384, 128), 384)])
            gp[pair] = value.reshape(8, R, 384).astype(BF)

        return 0

    lax.fori_loop(0, pairs * parts, body, 0)
    ev_p[pairs - 1][0]()
    for made in late:
        made.wait()
    vs[...] = vg_ref[...]
    LR = 256

    def norm_body(i, _):
        def spot(where, events):
            @pl.when(i == where)
            def _():
                for event in events:
                    event()

        spot(0, q[3][7:8])
        spot(1, q[5][1:3] + q[5][5:6] + q[4][6:7])
        spot(3, q[5][3:5] + q[4][7:8])
        r = pl.ds(mo(i * LR, LR), LR)
        left = dproj[r, :]
        dn = dot_nt(left, wpp[...])
        sums = jnp.sum(left.astype(F32), axis=0, keepdims=True)
        for j in range(pairs):
            vs[0:1, j * 128:(j + 1) * 128] += sums[:, j * 384:j * 384 + 128]
            vs[1:2, j * 128:(j + 1) * 128] += sums[:, j * 384 + 256:j * 384 + 384]
        value = x[r, :].astype(F32)
        u = value - jnp.mean(value, axis=-1, keepdims=True)
        spread = lax.rsqrt(jnp.mean(u * u, axis=-1, keepdims=True) + eps_norm)
        xhat = u * spread
        vs[8:9, :] += jnp.sum(dn * xhat, axis=0, keepdims=True)
        vs[9:10, :] += jnp.sum(dn, axis=0, keepdims=True)
        gx = dn * v_ref[4:5, 0:D]
        back = spread * (gx - jnp.mean(gx, axis=-1, keepdims=True)
                         - xhat * jnp.mean(gx * xhat, axis=-1, keepdims=True))
        tg[r, :] = (back + dmiddle[r, :]).astype(BF)
        return 0

    lax.fori_loop(0, T // LR, norm_body, 0)
    out = load(tg, tokens_out)
    v_slots = [link.slot() for _ in range(6)]
    link.send(v_slots[0], vs, vl.at[0], "c", lambda: vl.at[0])
    ev_p[pairs - 1][6]()
    link.got(v_slots[0], vl.at[0])
    vl[6] = vs[...] + vl[0]
    link.send(v_slots[1], vl.at[6], vl.at[1], "x", lambda: vl.at[0])
    link.got(v_slots[1], vl.at[1])
    vl[7] = vl[6] + vl[1]
    link.send(v_slots[2], vl.at[7], vl.at[2], "y", lambda: vl.at[0])
    link.got(v_slots[2], vl.at[2])
    vl[8] = vl[7] + vl[2]
    for step in (1, 3, 2):
        link.send(v_slots[2 + step], vl.at[8], vl.at[2 + step], step, lambda: vl.at[0])
    ev_p[pairs - 1][7]()
    gp_out[...] = jnp.where(p.odd == 0, gpw[:, 0:576], gpw[:, 64:640])
    for step in (1, 3, 2):
        link.got(v_slots[2 + step], vl.at[2 + step])
    total = vl[8] + vl[3] + vl[4] + vl[5]
    quarter, half = lax.div(p.d, 4), lax.div(p.d, 2)
    pb = jnp.where(quarter == 0, total[0:1], total[1:2])
    eb = jnp.where(half < 2, jnp.where(half == 0, total[3:4], total[4:5]), jnp.where(half == 2, total[5:6], total[6:7]))
    plain = jnp.concatenate([total[2:3], total[7:12], total[2:4]], axis=0)
    turn = lambda value, by: pltpu.roll(value, lax.rem(D - by, D), 1)
    wide8 = lambda value: jnp.broadcast_to(value, (8, D))
    vec_out[0] = turn(plain, p.d * R)[:, 0:384]
    vec_out[1] = turn(wide8(pb), lax.rem(p.d, 4) * 2 * R)[:, 0:384]
    vec_out[2] = turn(wide8(eb), lax.rem(p.d, 2) * 4 * R)[:, 0:384]
    link.finish()
    for ending in ended:
        ending()
    out.wait()


def third_call(length, proj, qa, mixed, dm, n1, wp, x, dmiddle, ge, go, gc, vg, v):
    T, D = x.shape
    FF = ge.shape[1]
    R, Q, pairs = D // 8, FF // 4, H // 2
    vm = pltpu.VMEM
    n = 8 * 8 + 12 + 60 + 6
    return pl.pallas_call(
        third_kernel,
        in_specs=[SM] + [ANY] * 11 + [VM] * 2,
        out_specs=[ANY] + [VM] * 5,
        out_shape=[sds((T, D), BF), sds((R, 3 * D // 4), F32), sds((R, D // 4), F32), sds((R, Q), F32), sds((D // 4, FF // 8), F32),
                   sds((3, 8, 384), F32)],
        scratch_shapes=[
            vm((T, 3 * D), BF), vm((H, T, 128), BF), vm((T, D), BF), vm((T, D), BF), vm((T, D), BF), vm((D, T), BF),
            vm((D, 3 * D), BF), vm((T, D), BF), vm((T, D), F32), vm((D, FF), BF), vm((8, 4, R, 256), BF),
            vm((T, 3 * D), BF), vm((T, D), BF), vm((pairs, 8, R, 384), BF),
            vm((2, T, 128), BF), vm((2, T, 128), BF), vm((2, 128, T), F32), vm((2, T, 128), BF), vm((2, 128, T), BF),
            vm((16, D), F32), vm((9, 16, D), F32),
            vm((4, R, FF), BF), vm((R, FF // 2), BF), vm((R, FF // 2), BF), vm((R, FF), BF), vm((R, FF), BF), vm((4, R, Q), BF),
            vm((4, 4, R, 256), BF), vm((2, R, 256), BF), vm((2, R, 256), BF), vm((4, R, 256), BF), vm((4, R, 256), BF),
            vm((4, R, 256), BF),
            vm((pairs, 4, R, 384), BF), vm((pairs, R // 2, 384), BF), vm((pairs, R // 2, 384), BF),
            vm((pairs, R, 384), BF), vm((pairs, R, 384), BF), vm((20, 3, R, 128), BF), vm((R, 640), F32),
            vm((4, D // 4, FF // 8), BF), vm((4, D // 4, FF // 8), BF),
            pltpu.SemaphoreType.DMA((n,)), pltpu.SemaphoreType.DMA((n,)), pltpu.SemaphoreType.DMA((29,)),
        ],
        compiler_params=pltpu.CompilerParams(
            collective_id=2, has_side_effects=True, vmem_limit_bytes=63 << 20),
        name="third_part",
    )(length, proj, qa, mixed, dm, n1, wp, x, dmiddle, ge, go, gc, vg, v)


def last_kernel(block_in, tokens_in, p_in, o_in, e_in, c_in, vec_in,
                block_out, tokens_out, p_out, o_out, e_out, c_out, *rest):
    vectors, held, vec, sem = rest[:8], rest[8:14], rest[14], rest[15]
    parts = 2
    rows = block_in.shape[0] // parts
    whole = lambda ref: ref
    legs = []
    for i in range(parts):
        part = lambda ref, i=i: ref.at[pl.ds(i * rows, rows)]
        legs += [(part, block_in, held[0], block_out), (part, tokens_in, held[1], tokens_out)]
    legs += [(whole, a, b, c) for a, b, c in zip((p_in, o_in, e_in, c_in), held[2:], (p_out, o_out, e_out, c_out))]
    first = pltpu.make_async_copy(vec_in, vec, sem.at[2 * len(legs)])
    first.start()
    ins = [pltpu.make_async_copy(part(a), part(b), sem.at[k]) for k, (part, a, b, _) in enumerate(legs)]
    outs = [pltpu.make_async_copy(part(b), part(c), sem.at[len(legs) + k]) for k, (part, _, b, c) in enumerate(legs)]
    for made in ins:
        made.start()
    for came, goes in zip(ins, outs):
        came.wait()
        goes.start()
    first.wait()
    for at, (i, j) in enumerate(((1, 0), (0, 0), (2, 0), (0, 1), (0, 2), (0, 3), (0, 4), (0, 5))):
        n = vectors[at].shape[0]
        vectors[at][...] = vec[i, j:j + 1, 0:n].reshape(n)
    for goes in outs:
        goes.wait()


def last_call(sizes, *arrays):
    return pl.pallas_call(
        last_kernel,
        in_specs=[ANY] * 7,
        out_specs=[ANY] * 6 + [VM] * 8,
        out_shape=[sds(item.shape, item.dtype) for item in arrays[:6]] + [sds((n,), F32) for n in sizes],
        scratch_shapes=[pltpu.VMEM(item.shape, item.dtype) for item in arrays] + [pltpu.SemaphoreType.DMA((17,))],
        compiler_params=pltpu.CompilerParams(vmem_limit_bytes=63 << 20),
        name="last_part",
    )(*arrays)


def per_device_fast(tokens, lengths, cotangent, project_weight, project_bias, output_weight, output_bias,
                    expand_weight, expand_bias, contract_weight, contract_bias, first_gain, first_shift,
                    second_gain, second_shift):
    vectors = (project_bias, output_bias, expand_bias, contract_bias, first_gain, first_shift, second_gain, second_shift)
    normed_one, projected, mixed, qa, full_project, full_output, full_expand, cc, v = first_call(
        lengths, tokens, project_weight, output_weight, expand_weight, contract_weight.T, vectors)
    block_out, grad_mixed, grad_middle, ge, go, gc, vg = second_call(
        lengths, tokens, cotangent, mixed, full_output, full_expand, cc, v)
    third = third_call(
        lengths, projected, qa, mixed, grad_mixed, normed_one, full_project, tokens, grad_middle, ge, go, gc, vg, v)
    out = last_call([item.shape[0] for item in vectors], block_out, *third)
    return (out[0], out[1], out[2], out[6], out[3], out[7], out[4], out[8], out[5].T, *out[9:])


def solution(mesh):
    both, rows, grid = P(("dp", "fsdp"), None), P("dp"), P("dp", "fsdp")
    weights = (grid, rows, grid, rows, grid, rows, grid, rows)
    fast = mesh.shape["dp"] == 8 and mesh.shape["fsdp"] == 4
    return jax.shard_map(
        per_device_fast if fast else per_device,
        mesh=mesh,
        in_specs=(both, P(("dp", "fsdp")), both) + weights + (rows,) * 4,
        out_specs=(both, both) + weights + (rows,) * 4,
        check_vma=False,
    )
```

```python
import functools
import jax
import jax.numpy as jnp
from jax import lax
from jax.experimental import pallas as pl
from jax.experimental.pallas import tpu as pltpu
from jax.sharding import PartitionSpec as P

H = 12
HD = 64
F32 = jnp.float32
BF = jnp.bfloat16
MESH = pl.DeviceIdType.MESH
eps_norm = 1e-05
neg_fill = -1000000000.0


def dot(first, second):
    return jnp.dot(first, second, preferred_element_type=F32)


def dot_nt(first, second):
    return lax.dot_general(first, second, (((1,), (1,)), ((), ())), preferred_element_type=F32)


def dot_tn(first, second):
    return lax.dot_general(first, second, (((0,), (0,)), ((), ())), preferred_element_type=F32)


def mo(value, multiple):
    return pl.multiple_of(value, multiple)


class Place:
    def __init__(self):
        self.d = lax.axis_index("dp")
        self.z = lax.axis_index("fsdp")
        core = lax.rem(self.d, 2)
        across = lax.rem(lax.div(self.d, 2), 2)
        up = lax.div(self.d, 4)
        self.dc = self.d + 1 - 2 * core
        self.dx = self.d + 2 - 4 * across
        self.dy = self.d + 4 - 8 * up
        self.dd = self.dx + 4 - 8 * up
        self.odd = lax.rem(self.z, 2)
        z = self.z
        pick = lambda a, b, c, d: jnp.where(z < 2, jnp.where(z == 0, a, b), jnp.where(z == 2, c, d))
        self.order = [z, pick(1, 0, 3, 2), pick(2, 2, 1, 1), pick(3, 3, 0, 0)]

    def zt(self, step):
        return lax.rem(self.z + step, 4)

    def zf(self, step):
        return lax.rem(self.z + 4 - step, 4)

    def id(self, to):
        if to == "x":
            return (self.dx, self.z)
        if to == "y":
            return (self.dy, self.z)
        if to == "c":
            return (self.dc, self.z)
        if isinstance(to, tuple):
            return (to[1], self.z) if to[0] == "d" else (self.d, to[1])
        return (self.d, self.zt(to))


def enter(place, wide=False):
    barrier = pltpu.get_barrier_semaphore()
    sib = place.dc - place.d
    others = [("d", d + sib) for d in (place.dx, place.dy, place.dd)] + [("d", place.dd)] if wide else []
    partners = ["x", "y", "c", 1, 2, 3] + others
    for to in partners:
        pl.semaphore_signal(barrier, inc=1, device_id=place.id(to), device_id_type=MESH)
    pl.semaphore_wait(barrier, len(partners))


class Link:
    def __init__(self, place, send_sem, recv_sem):
        self.place, self.send_sem, self.recv_sem = place, send_sem, recv_sem
        self.count = 0
        self.copies = []

    def slot(self, many=1):
        self.count += many
        return self.count - many

    def copy(self, slot, source, target, to, land=None):
        return pltpu.make_async_remote_copy(
            src_ref=source, dst_ref=target, send_sem=self.send_sem.at[slot],
            recv_sem=self.recv_sem.at[slot if land is None else land], device_id=self.place.id(to),
            device_id_type=MESH)

    def send(self, slot, source, target, to, like, land=None, when=None):
        def start():
            self.copy(slot, source, target, to, land).start()

        if when is None:
            start()
        else:
            pl.when(when())(start)
        self.copies.append((slot, like, when))

    def got(self, slot, target):
        self.copy(slot, target, target, "x").wait_recv()

    def finish(self):
        for slot, like, when in self.copies:
            def done(slot=slot, like=like):
                view = like()
                self.copy(slot, view, view, "x").wait_send()

            if when is None:
                done()
            else:
                pl.when(when())(done)


class Gather:
    def __init__(self, link, place, block):
        p = place
        zr, zs = link.slot(4), link.slot(4)
        xs, ys, fx = link.slot(4), link.slot(4), link.slot(4)
        cs = link.slot(16)
        got = link.got
        send = functools.partial(link.send, like=lambda: block(0, 0))

        def z_step(a):
            def run():
                if a == 0:
                    own = block(p.z, p.d)
                    for k in (1, 2, 3):
                        send(zs + k, own, own, ("z", p.order[k]), land=zr + p.z)
                else:
                    got(zr + p.order[a], block(p.order[a], p.d))
            return run

        def x_step(a):
            def run():
                here = block(p.order[a], p.d)
                send(xs + a, here, here, "x")
                send(ys + a, here, here, "y")
                send(cs + a, here, here, "c")
            return run

        def turn(a):
            def run():
                b = p.order[a]
                bx, by = block(b, p.dx), block(b, p.dy)
                got(xs + a, bx)
                got(ys + a, by)
                if a in (0, 1):
                    send(fx + a, bx, bx, "y")
                else:
                    send(fx + a, by, by, "x")
                send(cs + 4 + a, bx, bx, "c")
                send(cs + 8 + a, by, by, "c")
            return run

        def corner(a):
            def run():
                bd = block(p.order[a], p.dd)
                got(fx + a, bd)
                send(cs + 12 + a, bd, bd, "c")
            return run

        def close():
            sib = p.dc - p.d
            for which, d in enumerate((p.d, p.dx, p.dy, p.dd)):
                for a in range(4):
                    got(cs + 4 * which + a, block(p.order[a], d + sib))

        self.z, self.x, self.t, self.q = ([make(a) for a in range(4)] for make in (z_step, x_step, turn, corner))
        self.close = close


def spread_z(link, place, ref):
    p = place
    zs, zr = link.slot(3), link.slot(4)

    def send():
        for k in (1, 2, 3):
            link.send(zs + k - 1, ref.at[p.z], ref.at[p.z], ("z", p.order[k]), lambda: ref.at[0], land=zr + p.z)

    def wait():
        for k in (1, 2, 3):
            b = p.order[k]
            link.got(zr + b, ref.at[b])

    return send, wait


def run(*events):
    def together():
        for event in events:
            event()
    return together


def window(value, odd, wide):
    rows, k = value.shape
    fill = jnp.zeros((rows, wide - k), F32)
    value = value.astype(F32)
    left = jnp.concatenate([value, fill], axis=1)
    right = jnp.concatenate([fill, value], axis=1)
    return jnp.where(odd == 0, left, right).astype(BF)


def merge_windows(blocks, full, tiles, rows_step):
    rows = full.shape[0]
    half = tiles // 2

    def body(i, _):
        r = pl.ds(mo(i * rows_step, rows_step), rows_step)
        for pair in range(2):
            even, odd = blocks.at[2 * pair], blocks.at[2 * pair + 1]
            base = pair * tiles * 128
            full[r, base:base + half * 128] = even[r, 0:half * 128]
            full[r, base + half * 128:base + (half + 1) * 128] = (
                even[r, half * 128:(half + 1) * 128] + odd[r, 0:128])
            full[r, base + (half + 1) * 128:base + tiles * 128] = odd[r, 128:(half + 1) * 128]
        return 0

    lax.fori_loop(0, rows // rows_step, body, 0)


def split3(value):
    high = value.astype(BF)
    rest = value - high.astype(F32)
    mid = rest.astype(BF)
    low = (rest - mid.astype(F32)).astype(BF)
    return high.astype(F32), mid.astype(F32), low.astype(F32)


def extend(head, pair, lane, one, two, three, four):
    base = 64 * (1 - head)
    extra = jnp.where(lane == base, one, jnp.where(lane == base + 1, two, jnp.where(
        lane == base + 2, three, jnp.where(lane == base + 3, four, 0.0))))
    keep = (lane < 64) if head == 0 else (lane >= 64)
    return jnp.where(keep, pair, extra).astype(BF)


def iota(shape, axis):
    return lax.broadcasted_iota(jnp.int32, shape, axis)


QB = 256


def first_kernel(length_ref, x_ref, wp_ref, wo_ref, we_ref, wc_ref, *refs):
    vec_refs, refs = refs[:8], refs[8:]
    first_body(length_ref, x_ref, wp_ref, wo_ref, we_ref, wc_ref, vec_refs, *refs)


def first_body(length_ref, x_ref, wp_ref, wo_ref, we_ref, wc_ref, vec_refs,
                 n1_out, proj_out, mixed_out, qa_out, wp_out, wo_out, we_out, c_out, v_out,
                 wp_blk, wo_blk, we, wp, wo, vb, n1, proj, mixed, qa, ka, va, vrow, cc,
                 send_sem, recv_sem, out_sem, pair_sem):
    p = Place()
    T, D = x_ref.shape
    R = wp_ref.shape[0]
    FF = we.shape[1]
    link = Link(p, send_sem, recv_sem)
    rows_of = lambda d: pl.ds(mo(d * R, 16), R)
    half = R // 2
    bpa = lambda z, d: wp_blk.at[z, pl.ds(mo(d * R, 16), half), :]
    bpb = lambda z, d: wp_blk.at[z, pl.ds(mo(d * R + half, 16), half), :]
    bo = lambda z, d: wo_blk.at[z, rows_of(d), :]
    be = lambda z, d: we.at[rows_of(d), pl.ds(mo(z * (FF // 4), 128), FF // 4)]
    g0, g1, go, ge = (Gather(link, p, b) for b in (bpa, bpb, bo, be))
    c_send, c_wait = spread_z(link, p, cc)
    vs = [link.slot() for _ in range(7)]

    wp_blk[p.z, rows_of(p.d), :] = window(wp_ref[...], p.odd, wp_blk.shape[2])
    wo_blk[p.z, rows_of(p.d), :] = window(wo_ref[...], p.odd, wo_blk.shape[2])
    we[rows_of(p.d), pl.ds(mo(p.z * (FF // 4), 128), FF // 4)] = we_ref[...]
    cc[p.z] = wc_ref[...]
    for i, ref in enumerate(vec_refs):
        vb[p.d, i:i + 1, 0:ref.shape[0]] = ref[...].astype(F32).reshape(1, ref.shape[0]).astype(BF)

    outs = []

    def out(source, target):
        made = pltpu.make_async_copy(source, target, out_sem.at[len(outs)])
        made.start()
        outs.append(made)

    enter(p)
    send_v = lambda slot, d, to: link.send(vs[slot], vb.at[d], vb.at[d], to, lambda: vb.at[0])
    for slot, to in ((0, "x"), (1, "y"), (3, "c")):
        send_v(slot, p.d, to)
    run(g0.z[0], g0.x[0], g1.z[0], g1.x[0])()
    link.got(vs[0], vb.at[p.dx])
    link.got(vs[1], vb.at[p.dy])
    send_v(2, p.dx, "y")
    send_v(4, p.dx, "c")
    send_v(5, p.dy, "c")
    run(g0.z[1], g0.x[1], g0.t[0], g1.t[0], g0.z[2], g0.x[2])()
    link.got(vs[2], vb.at[p.dd])
    send_v(6, p.dd, "c")
    sib = p.dc - p.d
    for slot, d in ((3, p.d), (4, p.dx), (5, p.dy), (6, p.dd)):
        link.got(vs[slot], vb.at[d + sib])
    got = vb[...].astype(F32)
    side = lambda row, wide: jnp.concatenate([got[i, row:row + 1, 0:wide] for i in range(8)], axis=1)
    bias = side(0, 2 * R)
    vrow[0:1, 0:D] = bias[:, 0:D]
    vrow[0:1, D:2 * D] = jnp.zeros((1, D), F32)
    vrow[0:1, 2 * D:3 * D] = bias[:, D:]
    vrow[1:2, :] = side(2, FF // 8)
    for row, at in ((2, 1), (3, 3), (4, 4), (5, 5), (6, 6), (7, 7)):
        vrow[row:row + 1, 0:D] = side(at, R)
    out(vrow, v_out)
    run(g0.t[1], g0.z[3], g0.x[3], g0.q[0], g1.z[1], g1.x[1], g1.q[0])()

    LR = 128
    gain, shift = vrow[4:5, 0:D], vrow[5:6, 0:D]

    def norm_body(i, _):
        r = pl.ds(mo(i * LR, LR), LR)
        value = x_ref[r, :].astype(F32)
        u = value - jnp.mean(value, axis=-1, keepdims=True)
        spread = jnp.mean(u * u, axis=-1, keepdims=True)
        n1[r, :] = (u * lax.rsqrt(spread + eps_norm) * gain + shift).astype(BF)
        return 0

    norm_part = lambda k: lax.fori_loop(k * (T // LR // 4), (k + 1) * (T // LR // 4), norm_body, 0)
    g0.t[2]()
    norm_part(0)
    run(g1.z[2], g1.x[2], g0.q[1])()
    norm_part(1)
    run(g1.z[3], g1.x[3], ge.z[0], go.z[0], g0.t[3])()
    norm_part(2)
    run(g0.q[2], g1.t[1])()
    norm_part(3)
    run(g1.t[2], g1.t[3], ge.x[0], g0.q[3], g1.q[1], g1.q[2], g1.q[3], go.x[0])()
    out(n1, n1_out)
    run(g0.close, g1.close)()
    merge_windows(wp_blk, wp, 9, 96)
    out(wp, wp_out)
    run(ge.z[1], ge.x[1])()

    def project_body(i, _):
        for at, event in ((2, run(ge.z[2], ge.x[2], ge.t[0])), (3, go.t[0])):
            pl.when(i == at)(event)
        r = pl.ds(mo(i * 256, 256), 256)
        left = n1[r, :]
        for j in range(3):
            cols = slice(j * D, (j + 1) * D)
            value = dot(left, wp[:, cols]) + vrow[0:1, cols]
            proj[r, cols] = value.astype(BF)
        return 0

    lax.fori_loop(0, T // 256, project_body, 0)
    out(proj, proj_out)

    length = length_ref[0]
    subs = T // QB

    def pair_outs(pair):
        heads = pl.ds(2 * pair, 2)
        cols = pl.ds(mo(pair * 128, 128), 128)
        return (pltpu.make_async_copy(qa.at[heads], qa_out.at[heads], pair_sem.at[pair, 0]),
                pltpu.make_async_copy(mixed.at[:, cols], mixed_out.at[:, cols], pair_sem.at[pair, 1]))

    def attend_steps(events):
        def body(pair, _):
            for at, event in events:
                pl.when(pair == at)(event)
            cols = lambda off: pl.ds(mo(off + pair * 128, 128), 128)
            lane, row = iota((T, 128), 1), iota((T, 128), 0)
            q = proj[:, cols(0)].astype(F32) * (HD ** -0.5)
            k = proj[:, cols(D)].astype(F32)
            v = proj[:, cols(2 * D)].astype(F32)
            dead = jnp.where(row < length, 0.0, neg_fill)
            for head in range(2):
                ka[head] = extend(head, k, lane, 1.0, 1.0, 1.0, dead)
                qa[pair * 2 + head] = extend(head, q, lane, 0.0, 0.0, 0.0, 1.0)
                keep = (lane < 64) if head == 0 else (lane >= 64)
                va[head] = jnp.where(keep, v, 1.0).astype(BF)
            sub_lane = iota((QB, 128), 1)
            items = [(head, pl.ds(i * QB, QB)) for i in range(subs) for head in range(2)]
            halves = {}

            def scores(n):
                head, r = items[n]
                return dot_nt(qa[pair * 2 + head, r, :], ka[head])

            def soften(value):
                top = jnp.max(value, axis=-1, keepdims=True)
                return top, jnp.exp(value - top).astype(BF)

            def finish(n, top, powers):
                head, r = items[n]
                value = dot(powers, va[head])
                total = value[:, 64:65] if head == 0 else value[:, 0:1]
                one, two, three = split3(-(top + jnp.log(total)))
                query = qa[pair * 2 + head, r, :].astype(F32)
                qa[pair * 2 + head, r, :] = extend(head, query, sub_lane, one, two, three, 1.0)
                halves[n] = value * (1.0 / total)
                if head == 1:
                    mixed[r, cols(0)] = jnp.where(sub_lane < 64, halves[n - 1], halves[n]).astype(BF)

            value, waiting = scores(0), None
            for n in range(len(items)):
                following = scores(n + 1) if n + 1 < len(items) else None
                soft = soften(value)
                if waiting is not None:
                    finish(n - 1, *waiting)
                value, waiting = following, soft
            finish(len(items) - 1, *waiting)
            for made in pair_outs(pair):
                made.start()
            return 0

        lax.fori_loop(0, H // 2, body, 0)

    attend_steps([(1, run(go.z[1], go.x[1], ge.z[3], ge.x[3], go.z[2], go.x[2], ge.t[1])),
                  (2, run(go.z[3], go.x[3], ge.t[2], c_send)), (3, run(ge.q[0], go.t[1], go.q[0])),
                  (4, run(ge.t[3], go.t[2])), (5, run(ge.q[1], ge.q[2], go.t[3]))])
    run(ge.q[3], go.q[1], go.q[2], go.q[3], go.close)()
    merge_windows(wo_blk, wo, 3, 96)
    out(wo, wo_out)
    ge.close()
    out(we, we_out)
    c_wait()
    out(cc, c_out)
    link.finish()
    for made in outs:
        made.wait()
    for pair in range(H // 2):
        for made in pair_outs(pair):
            made.wait()


def first_call(length, x, wp, wo, we, wc, vectors):
    T, D = x.shape
    FF = we.shape[1] * 4
    ANY = pl.BlockSpec(memory_space=pl.ANY)
    V = pl.BlockSpec(memory_space=pltpu.VMEM)
    S = pl.BlockSpec(memory_space=pltpu.SMEM)
    sds = jax.ShapeDtypeStruct
    n = 4 * 36 + 7 + 7
    return pl.pallas_call(
        first_kernel,
        in_specs=[S] + [V] * 13,
        out_specs=[ANY] * 9,
        out_shape=[sds((T, D), BF), sds((T, 3 * D), BF), sds((T, D), BF), sds((H, T, 128), BF),
                   sds((D, 3 * D), BF), sds((D, D), BF), sds((D, FF), BF), sds((4,) + wc.shape, BF), sds((8, FF), F32)],
        scratch_shapes=[
            pltpu.VMEM((4, D, 640), BF), pltpu.VMEM((4, D, 256), BF), pltpu.VMEM((D, FF), BF),
            pltpu.VMEM((D, 3 * D), BF), pltpu.VMEM((D, D), BF), pltpu.VMEM((8, 16, FF // 8), BF),
            pltpu.VMEM((T, D), BF), pltpu.VMEM((T, 3 * D), BF), pltpu.VMEM((T, D), BF),
            pltpu.VMEM((H, T, 128), BF), pltpu.VMEM((2, T, 128), BF), pltpu.VMEM((2, T, 128), BF),
            pltpu.VMEM((8, FF), F32), pltpu.VMEM((4,) + wc.shape, BF),
            pltpu.SemaphoreType.DMA((n,)), pltpu.SemaphoreType.DMA((n,)), pltpu.SemaphoreType.DMA((9,)), pltpu.SemaphoreType.DMA((H // 2, 2)),
        ],
        compiler_params=pltpu.CompilerParams(
            collective_id=0, has_side_effects=True, vmem_limit_bytes=60 << 20),
        name="first_part",
    )(length, x, wp, wo, we, wc, *vectors)


def layer_norm(values, gain_row, shift_row):
    centre = jnp.mean(values, axis=-1, keepdims=True)
    centred = values - centre
    spread = jnp.mean(centred * centred, axis=-1, keepdims=True)
    return centred * lax.rsqrt(spread + eps_norm) * gain_row + shift_row


def gelu_exact(values):
    return jax.nn.gelu(values, approximate=False)


def matmul(first, second):
    return jnp.dot(first, second, preferred_element_type=jnp.float32)


def over_rows(first, second):
    return lax.dot_general(
        first, second, (((0,), (0,)), ((), ())), preferred_element_type=jnp.float32
    )


def over_columns(first, second):
    return lax.dot_general(
        first, second, (((1,), (1,)), ((), ())), preferred_element_type=jnp.float32
    )


def fetch_forward(
    project_weight,
    output_weight,
    expand_weight,
    contract_weight,
    project_bias,
    output_bias,
    expand_bias,
    contract_bias,
    first_gain,
    first_shift,
    second_gain,
    second_shift,
):
    wide_project, wide_output, wide_expand, wide_contract = (
        lax.all_gather(project_weight, "fsdp", axis=1, tiled=True),
        lax.all_gather(output_weight, "fsdp", axis=1, tiled=True),
        lax.all_gather(expand_weight, "fsdp", axis=1, tiled=True),
        lax.all_gather(contract_weight, "fsdp", axis=1, tiled=True),
    )
    return (
        lax.all_gather(wide_project, "dp", axis=0, tiled=True),
        lax.all_gather(wide_output, "dp", axis=0, tiled=True),
        lax.all_gather(wide_expand, "dp", axis=0, tiled=True),
        lax.all_gather(wide_contract, "dp", axis=0, tiled=True),
        lax.all_gather(project_bias, "dp", axis=0, tiled=True),
        lax.all_gather(output_bias, "dp", axis=0, tiled=True),
        lax.all_gather(expand_bias, "dp", axis=0, tiled=True),
        lax.all_gather(contract_bias, "dp", axis=0, tiled=True),
        lax.all_gather(first_gain, "dp", axis=0, tiled=True),
        lax.all_gather(first_shift, "dp", axis=0, tiled=True),
        lax.all_gather(second_gain, "dp", axis=0, tiled=True),
        lax.all_gather(second_shift, "dp", axis=0, tiled=True),
    )


def fetch_backward(
    project_weight,
    output_weight,
    expand_weight,
    contract_weight,
    project_bias,
    output_bias,
    expand_bias,
    contract_bias,
    first_gain,
    first_shift,
    second_gain,
    second_shift,
):
    wide_project, wide_output, wide_expand, wide_contract = (
        lax.all_gather(project_weight, "fsdp", axis=1, tiled=True),
        lax.all_gather(output_weight, "fsdp", axis=1, tiled=True),
        lax.all_gather(expand_weight, "fsdp", axis=1, tiled=True),
        lax.all_gather(contract_weight, "fsdp", axis=1, tiled=True),
    )
    return (
        lax.all_gather(wide_project, "dp", axis=0, tiled=True),
        lax.all_gather(wide_output, "dp", axis=0, tiled=True),
        lax.all_gather(wide_expand, "dp", axis=0, tiled=True),
        lax.all_gather(wide_contract, "dp", axis=0, tiled=True),
        lax.all_gather(project_bias, "dp", axis=0, tiled=True),
        lax.all_gather(output_bias, "dp", axis=0, tiled=True),
        lax.all_gather(expand_bias, "dp", axis=0, tiled=True),
        lax.all_gather(contract_bias, "dp", axis=0, tiled=True),
        lax.all_gather(first_gain, "dp", axis=0, tiled=True),
        lax.all_gather(first_shift, "dp", axis=0, tiled=True),
        lax.all_gather(second_gain, "dp", axis=0, tiled=True),
        lax.all_gather(second_shift, "dp", axis=0, tiled=True),
    )


def split_heads(cell_rows, block_rows):
    slot_count = cell_rows.shape[0]
    width = cell_rows.shape[1] // 3
    query_blocks = cell_rows[:, :width].reshape(slot_count // block_rows, block_rows, H, HD)
    keys_all = cell_rows[:, width : 2 * width].reshape(slot_count, H, HD)
    values_all = cell_rows[:, 2 * width :].reshape(slot_count, H, HD)
    return (query_blocks, keys_all, values_all)


def block_scores(query_block, keys_all, key_live):
    scores = jnp.einsum(
        "qhe,khe->hqk", query_block, keys_all, preferred_element_type=jnp.float32
    ) * HD ** (-0.5)
    return jnp.where(key_live[None, None, :], scores, neg_fill)


def attend_forward(query_block, keys_all, values_all, key_live):
    scores = block_scores(query_block, keys_all, key_live)
    row_max = jnp.max(scores, axis=-1, keepdims=True)
    powers = jnp.exp(scores - row_max)
    row_total = jnp.sum(powers, axis=-1, keepdims=True)
    weights = (powers / row_total).astype(jnp.bfloat16)
    mixed_block = jnp.einsum(
        "hqk,khe->qhe", weights, values_all, preferred_element_type=jnp.float32
    )
    return (mixed_block, (row_max + jnp.log(row_total))[:, :, 0])


def attend_backward(query_block, grad_block, log_block, keys_all, values_all, key_live):
    scores = block_scores(query_block, keys_all, key_live)
    weights = jnp.exp(scores - log_block[:, :, None])
    grad_weights = jnp.einsum(
        "qhe,khe->hqk", grad_block, values_all, preferred_element_type=jnp.float32
    )
    row_inner = jnp.sum(grad_weights * weights, axis=-1, keepdims=True)
    grad_scores = (weights * (grad_weights - row_inner)).astype(jnp.bfloat16)
    grad_query = jnp.einsum(
        "hqk,khe->qhe", grad_scores, keys_all, preferred_element_type=jnp.float32
    ) * HD ** (-0.5)
    grad_key = jnp.einsum(
        "hqk,qhe->khe", grad_scores, query_block, preferred_element_type=jnp.float32
    ) * HD ** (-0.5)
    grad_value = jnp.einsum(
        "hqk,qhe->khe", weights.astype(jnp.bfloat16), grad_block, preferred_element_type=jnp.float32
    )
    return (grad_query, grad_key, grad_value)


def per_device(
    tokens,
    lengths,
    cotangent,
    project_weight,
    project_bias,
    output_weight,
    output_bias,
    expand_weight,
    expand_bias,
    contract_weight,
    contract_bias,
    first_gain,
    first_shift,
    second_gain,
    second_shift,
):
    fetched = fetch_forward(
        project_weight,
        output_weight,
        expand_weight,
        contract_weight,
        project_bias,
        output_bias,
        expand_bias,
        contract_bias,
        first_gain,
        first_shift,
        second_gain,
        second_shift,
    )
    full_project, full_output, full_expand, full_contract = (
        fetched[0],
        fetched[1],
        fetched[2],
        fetched[3],
    )
    vectors = [item.astype(jnp.float32) for item in fetched[4:]]
    bias_project, bias_output, bias_expand, bias_contract = (
        vectors[0],
        vectors[1],
        vectors[2],
        vectors[3],
    )
    gain_one, shift_one, gain_two, shift_two = (vectors[4], vectors[5], vectors[6], vectors[7])
    cell_count = lengths.shape[0]
    slot_count = tokens.shape[0] // cell_count
    width = tokens.shape[1]
    block_rows = min(512, slot_count)
    positions = jnp.arange(slot_count, dtype=jnp.int32)
    live_keys = positions[None, :] < lengths[:, None]
    live_rows = live_keys.reshape(-1)
    rows_in = tokens.astype(jnp.float32)
    normed_one = layer_norm(rows_in, gain_one, shift_one).astype(jnp.bfloat16)
    bias_full = jnp.concatenate(
        [bias_project[:width], jnp.zeros((width,), jnp.float32), bias_project[width:]]
    )
    projected = (matmul(normed_one, full_project) + bias_full).astype(jnp.bfloat16)
    cell_index = 0
    query_blocks, keys_all, values_all = split_heads(projected, block_rows)
    key_live = live_keys[cell_index]
    mixed_blocks, log_blocks = lax.map(
        lambda query_block: attend_forward(query_block, keys_all, values_all, key_live),
        query_blocks,
    )
    mixed_list = mixed_blocks.reshape(slot_count, width)
    log_list = [log_blocks]
    mixed_low = mixed_list.astype(jnp.bfloat16)
    middle = rows_in + (matmul(mixed_low, full_output) + bias_output)
    normed_two = layer_norm(middle, gain_two, shift_two).astype(jnp.bfloat16)
    hidden = matmul(normed_two, full_expand) + bias_expand
    active = gelu_exact(hidden).astype(jnp.bfloat16)
    result = middle + (matmul(active, full_contract) + bias_contract)
    block_out = jnp.where(live_rows[:, None], result, 0.0).astype(jnp.bfloat16)
    again = fetch_backward(
        project_weight,
        output_weight,
        expand_weight,
        contract_weight,
        project_bias,
        output_bias,
        expand_bias,
        contract_bias,
        first_gain,
        first_shift,
        second_gain,
        second_shift,
    )
    back_project, back_output, back_expand, back_contract = (again[0], again[1], again[2], again[3])
    grad_out = jnp.where(live_rows[:, None], cotangent.astype(jnp.float32), 0.0)
    grad_out_low = grad_out.astype(jnp.bfloat16)
    grad_contract = over_rows(active, grad_out_low)
    grad_contract_bias = jnp.sum(grad_out, axis=0)
    grad_active = over_columns(grad_out_low, back_contract)
    gelu_value, gelu_pull = jax.vjp(gelu_exact, hidden)
    grad_hidden = gelu_pull(grad_active)[0].astype(jnp.bfloat16)
    grad_expand = over_rows(normed_two, grad_hidden)
    grad_expand_bias = jnp.sum(grad_hidden.astype(jnp.float32), axis=0)
    grad_normed_two = over_columns(grad_hidden, back_expand)
    norm_value, second_pull = jax.vjp(layer_norm, middle, gain_two, shift_two)
    grad_middle, grad_gain_two, grad_shift_two = second_pull(grad_normed_two)
    grad_middle = grad_middle + grad_out
    grad_branch = grad_middle.astype(jnp.bfloat16)
    grad_output = over_rows(mixed_low, grad_branch)
    grad_output_bias = jnp.sum(grad_branch.astype(jnp.float32), axis=0)
    grad_mixed = over_columns(grad_branch, back_output).astype(jnp.bfloat16)
    cell_index = 0
    query_blocks, keys_all, values_all = split_heads(projected, block_rows)
    key_live = live_keys[cell_index]
    grad_blocks = grad_mixed.reshape(slot_count // block_rows, block_rows, H, HD)

    def visit_block(carried, inputs):
        query_block, grad_block, log_block = inputs
        grad_query, grad_key, grad_value = attend_backward(
            query_block, grad_block, log_block, keys_all, values_all, key_live
        )
        return ((carried[0] + grad_key, carried[1] + grad_value), grad_query)

    initial = (
        jnp.zeros((slot_count, H, HD), jnp.float32),
        jnp.zeros((slot_count, H, HD), jnp.float32),
    )
    (key_sums, value_sums), query_grads = lax.scan(
        visit_block, initial, (query_blocks, grad_blocks, log_list[cell_index])
    )
    grad_cells = jnp.concatenate(
        [
            query_grads.reshape(slot_count, width),
            key_sums.reshape(slot_count, width),
            value_sums.reshape(slot_count, width),
        ],
        axis=1,
    )
    grad_projected = grad_cells.astype(jnp.bfloat16)
    grad_project = over_rows(normed_one, grad_projected)
    column_sums = jnp.sum(grad_projected.astype(jnp.float32), axis=0)
    grad_project_bias = jnp.concatenate([column_sums[:width], column_sums[2 * width :]])
    grad_normed_one = over_columns(grad_projected, back_project)
    first_value, first_pull = jax.vjp(layer_norm, rows_in, gain_one, shift_one)
    grad_rows_in, grad_gain_one, grad_shift_one = first_pull(grad_normed_one)
    tokens_grad = (grad_rows_in + grad_middle).astype(jnp.bfloat16)
    reduced = (
        lax.psum_scatter(grad_project, "dp", scatter_dimension=0, tiled=True),
        lax.psum_scatter(grad_output, "dp", scatter_dimension=0, tiled=True),
        lax.psum_scatter(grad_expand, "dp", scatter_dimension=0, tiled=True),
        lax.psum_scatter(grad_contract, "dp", scatter_dimension=0, tiled=True),
        lax.psum_scatter(grad_project_bias, "dp", scatter_dimension=0, tiled=True),
        lax.psum_scatter(grad_output_bias, "dp", scatter_dimension=0, tiled=True),
        lax.psum_scatter(grad_expand_bias, "dp", scatter_dimension=0, tiled=True),
        lax.psum_scatter(grad_contract_bias, "dp", scatter_dimension=0, tiled=True),
        lax.psum_scatter(grad_gain_one, "dp", scatter_dimension=0, tiled=True),
        lax.psum_scatter(grad_shift_one, "dp", scatter_dimension=0, tiled=True),
        lax.psum_scatter(grad_gain_two, "dp", scatter_dimension=0, tiled=True),
        lax.psum_scatter(grad_shift_two, "dp", scatter_dimension=0, tiled=True),
    )
    shard_project, shard_output, shard_expand, shard_contract = (
        lax.psum_scatter(
            reduced[0].astype(jnp.bfloat16), "fsdp", scatter_dimension=1, tiled=True
        ).astype(jnp.float32),
        lax.psum_scatter(
            reduced[1].astype(jnp.bfloat16), "fsdp", scatter_dimension=1, tiled=True
        ).astype(jnp.float32),
        lax.psum_scatter(
            reduced[2].astype(jnp.bfloat16), "fsdp", scatter_dimension=1, tiled=True
        ).astype(jnp.float32),
        lax.psum_scatter(
            reduced[3].astype(jnp.bfloat16), "fsdp", scatter_dimension=1, tiled=True
        ).astype(jnp.float32),
    )
    summed = lax.psum(
        (
            reduced[4],
            reduced[5],
            reduced[6],
            reduced[7],
            reduced[8],
            reduced[9],
            reduced[10],
            reduced[11],
        ),
        "fsdp",
    )
    return (
        block_out,
        tokens_grad,
        shard_project,
        summed[0],
        shard_output,
        summed[1],
        shard_expand,
        summed[2],
        shard_contract,
        summed[3],
        summed[4],
        summed[5],
        summed[6],
        summed[7],
    )


def scatter_events(link, place, col, pair_of, lc, lxh, lyh, lx, ly):
    p = place
    family = (p.dc, p.dx + p.dc - p.d, p.dy + p.dc - p.d, p.dd + p.dc - p.d)
    cs = [link.slot() for _ in range(4)]
    hx, hy, fx, fy = (link.slot() for _ in range(4))
    got = link.got

    def add(target, *terms):
        total = target[...].astype(F32)
        for term in terms:
            total = total + term[...].astype(F32)
        target[...] = total.astype(BF)

    def to_sibling(which):
        link.send(cs[which], col(family[which]), lc.at[which], "c", lambda: col(0))

    def halves():
        got(cs[3], lc.at[3])
        add(col(p.dd), lc.at[3])
        link.send(hx, pair_of(col(p.dd), 0), lxh, "x", lambda: lxh)
        link.send(hy, pair_of(col(p.dd), 1), lyh, "y", lambda: lyh)

    def near():
        got(cs[1], lc.at[1])
        got(cs[2], lc.at[2])
        add(col(p.dx), lc.at[1])
        add(col(p.dy), lc.at[2])

    def pass_y():
        got(hx, lxh)
        add(pair_of(col(p.dy), 0), lxh)
        link.send(fy, col(p.dy), ly, "y", lambda: ly)

    def pass_x():
        got(hy, lyh)
        add(pair_of(col(p.dx), 1), lyh)
        link.send(fx, col(p.dx), lx, "x", lambda: lx)

    def own():
        got(cs[0], lc.at[0])

    def total():
        got(fx, lx)
        got(fy, ly)
        add(col(p.d), lc.at[0], lx, ly)

    return to_sibling, [halves, near, pass_y, pass_x, own, total]


def z_sum(link, place, block, lz, finish):
    p = place
    zs = link.slot(4)

    def send():
        for step in (1, 3, 2):
            link.send(zs + step, block(p.zt(step)), lz.at[step], step, lambda: lz.at[0])

    def last():
        total = block(p.z)[...].astype(F32)
        for step in (1, 3, 2):
            link.got(zs + step, lz.at[step])
            total = total + lz[step].astype(F32)
        finish(total)

    return send, last


def gelu_pair(value):
    lift = 0.5 * (1.0 + lax.erf(value * 0.7071067811865476))
    bell = jnp.exp(value * value * -0.5) * 0.3989422804014327
    return value * lift, lift + value * bell


def second_kernel(length_ref, x_hbm, cot_hbm, mixed_hbm, wo_hbm, we_hbm, c_hbm, v_ref,
                  block_out, dmixed_out, dmiddle_out, ge_out, go_out, gc_out, vg_out,
                  x_ref, cot_ref, mixed_ref, wo_ref, we, wct, act, slope, middle, n2t, dot_t, mixed_t, dbranch, dout, gc, go, dmixed, bout, vg,
                  lc, lxh, lyh, lx, ly, send_sem, recv_sem, out_sem):
    p = Place()
    T, D = x_ref.shape
    FF = we.shape[1]
    R = D // 8
    Q = FF // 4
    C8 = FF // 8
    link = Link(p, send_sem, recv_sem)
    bc = lambda z, d: wct.at[pl.ds(mo(z * (D // 4), 16), D // 4), pl.ds(mo(d * C8, 128), C8)]
    gather = Gather(link, p, bc)

    to_sibling, scatter = scatter_events(
        link, p, lambda d: gc.at[d], lambda ref, h: ref.at[pl.ds(2 * h, 2)], lc, lxh, lyh, lx, ly)
    load = pltpu.make_async_copy(we_hbm, we, out_sem.at[0])
    columns = [pltpu.make_async_copy(c_hbm.at[z], bc(z, p.d), out_sem.at[19 + z]) for z in range(4)]
    for made in columns:
        made.start()
    halves = [pl.ds(i * (T // 2), T // 2) for i in range(2)]
    early = [[pltpu.make_async_copy(wo_hbm, wo_ref, out_sem.at[12])], []]
    for i, r in enumerate(halves):
        for at, (a, b) in enumerate(((mixed_hbm, mixed_ref), (x_hbm, x_ref), (cot_hbm, cot_ref))):
            early[i].append(pltpu.make_async_copy(a.at[r], b.at[r], out_sem.at[13 + 3 * i + at]))
    for made in early[0] + early[1]:
        made.start()
    load.start()
    enter(p)
    for made in columns:
        made.wait()
    run(*gather.x)()
    for made in early[0] + early[1]:
        made.wait()
    length = length_ref[0]
    LR = 256
    rows = lambda i: pl.ds(mo(i * LR, LR), LR)
    vec = lambda i: v_ref[i:i + 1, 0:D]
    vg[...] = jnp.zeros_like(vg)

    def at(i, spots):
        for where, event in spots:
            pl.when(i == where)(event)

    def norm(value):
        u = value - jnp.mean(value, axis=-1, keepdims=True)
        r = lax.rsqrt(jnp.mean(u * u, axis=-1, keepdims=True) + eps_norm)
        return u * r, r

    def middle_body(i, _):
        at(i, [(3, gather.t[0])])
        r = rows(i)
        value = x_ref[r, :].astype(F32) + (dot(mixed_ref[r, :], wo_ref[...]) + vec(2))
        middle[r, :] = value
        xhat, _ = norm(value)
        n2 = (xhat * vec(6) + vec(7)).astype(BF)
        dmixed[r, :] = n2
        n2t[:, r] = n2.T
        live = iota((LR, D), 0) + i * LR < length
        grad = jnp.where(live, cot_ref[r, :].astype(F32), 0.0)
        vg[7:8, :] += jnp.sum(grad, axis=0, keepdims=True)
        dout[r, :] = grad.astype(BF)
        dot_t[:, r] = grad.astype(BF).T
        mixed_t[:, r] = mixed_ref[r, :].T
        return 0

    lax.fori_loop(0, T // LR, middle_body, 0)
    load.wait()

    def hidden_body(i, _):
        at(i, [(1, gather.t[1]), (2, gather.t[2]), (3, run(gather.t[3], gather.q[0]))])
        r = rows(i)
        left = dmixed[r, :]
        for j in range(4):
            cols = slice(j * Q, (j + 1) * Q)
            first, second = gelu_pair(dot(left, we[:, cols]) + v_ref[1:2, cols])
            act[r, cols] = first.astype(BF)
            slope[r, cols] = second.astype(BF)
        return 0

    lax.fori_loop(0, T // LR, hidden_body, 0)

    def column(d):
        value = dot(dot_t[...], act[:, pl.ds(mo(d * C8, 128), C8)])
        gc[d] = value.reshape(4, D // 4, C8).astype(BF)

    sib = p.dc - p.d
    column(p.dd + sib)
    to_sibling(3)
    column(p.dd)
    gather.q[1]()
    column(p.dx + sib)
    to_sibling(1)
    column(p.dy + sib)
    to_sibling(2)
    gather.q[2]()
    column(p.dx)
    scatter[0]()
    column(p.dy)
    gather.q[3]()
    column(p.d + sib)
    to_sibling(0)
    column(p.d)
    run(scatter[1], gather.close)()

    def back_body(i, _):
        at(i, [(1, run(scatter[2], scatter[3], scatter[4]))])
        r = rows(i)
        grad_low = dout[r, :]
        result = middle[r, :] + vec(3)
        dn = jnp.zeros((LR, D), F32)
        for j in range(4):
            cols = slice(j * Q, (j + 1) * Q)
            dh = dot(grad_low, wct[:, cols]) * slope[r, cols].astype(F32)
            low = dh.astype(BF)
            slope[r, cols] = low
            vg[3 + j:4 + j, :] += jnp.sum(low.astype(F32), axis=0, keepdims=True)
            result = result + dot_nt(act[r, cols], wct[:, cols])
            dn = dn + dot_nt(low, we[:, cols])
        live = iota((LR, D), 0) + i * LR < length
        bout[r, :] = jnp.where(live, result, 0.0).astype(BF)
        xhat, spread = norm(middle[r, :])
        vg[10:11, :] += jnp.sum(dn * xhat, axis=0, keepdims=True)
        vg[11:12, :] += jnp.sum(dn, axis=0, keepdims=True)
        gx = dn * vec(6)
        back = spread * (gx - jnp.mean(gx, axis=-1, keepdims=True)
                         - xhat * jnp.mean(gx * xhat, axis=-1, keepdims=True))
        total = dout[r, :].astype(F32) + back
        middle[r, :] = total
        branch = total.astype(BF)
        dbranch[r, :] = branch
        vg[2:3, :] += jnp.sum(branch.astype(F32), axis=0, keepdims=True)
        dmixed[r, :] = dot_nt(branch, wo_ref[...]).astype(BF)
        return 0

    lax.fori_loop(0, T // LR, back_body, 0)
    outs = []

    def out(source, target):
        made = pltpu.make_async_copy(source, target, out_sem.at[1 + len(outs)])
        made.start()
        outs.append(made)

    out(bout, block_out)
    out(dmixed, dmixed_out)
    out(middle, dmiddle_out)
    for z in range(4):
        cols = slice(3 * z // 2 * 128, 3 * z // 2 * 128 + 256)
        go[:, z] = dot(mixed_t[...], dbranch[:, cols]).reshape(8, R, 256).astype(BF)
    out(go, go_out)
    for z in range(4):
        act[0:D, z * Q:(z + 1) * Q] = dot(n2t[...], slope[:, z * Q:(z + 1) * Q]).astype(BF)
        out(act.at[0:D, z * Q:(z + 1) * Q], ge_out.at[:, z * Q:(z + 1) * Q])
        if z == 2:
            scatter[5]()
            out(gc.at[p.d], gc_out)
    vg_out[...] = vg[...]
    link.finish()
    for made in outs:
        made.wait()


ANY = pl.BlockSpec(memory_space=pl.ANY)
VM = pl.BlockSpec(memory_space=pltpu.VMEM)
SM = pl.BlockSpec(memory_space=pltpu.SMEM)
sds = jax.ShapeDtypeStruct


def second_call(length, x, cot, mixed, wo, we, wc, v):
    T, D = x.shape
    FF = we.shape[1]
    n = 36 + 8
    R, C8, Z = D // 8, FF // 8, D // 4
    vm = pltpu.VMEM
    return pl.pallas_call(
        second_kernel,
        in_specs=[SM] + [ANY] * 6 + [VM],
        out_specs=[ANY] * 6 + [VM],
        out_shape=[sds((T, D), BF), sds((T, D), BF), sds((T, D), F32), sds((D, FF), BF), sds((8, 4, R, 256), BF),
                   sds((4, Z, C8), BF), sds((16, D), F32)],
        scratch_shapes=[
            vm((T, D), BF), vm((T, D), BF), vm((T, D), BF), vm((D, D), BF), vm((D, FF), BF), vm((D, FF), BF), vm((T, FF), BF), vm((T, FF), BF), vm((T, D), F32),
            vm((D, T), BF), vm((D, T), BF), vm((D, T), BF), vm((T, D), BF), vm((T, D), BF),
            vm((8, 4, Z, C8), BF), vm((8, 4, R, 256), BF), vm((T, D), BF), vm((T, D), BF), vm((16, D), F32),
            vm((4, 4, Z, C8), BF), vm((2, Z, C8), BF), vm((2, Z, C8), BF), vm((4, Z, C8), BF), vm((4, Z, C8), BF),
            pltpu.SemaphoreType.DMA((n,)), pltpu.SemaphoreType.DMA((n,)), pltpu.SemaphoreType.DMA((23,)),
        ],
        compiler_params=pltpu.CompilerParams(
            collective_id=1, has_side_effects=True, vmem_limit_bytes=62 << 20),
        name="second_part",
    )(length, x, cot, mixed, wo, we, wc, v)


def third_kernel(length_ref, proj_hbm, qa_hbm, mixed_hbm, dm_hbm, n1_hbm, wp_hbm, x_hbm, dmiddle_hbm, ge_hbm, go_hbm,
                 gc_hbm, vg_ref, v_ref,
                 tokens_out, gp_out, go_out, ge_out, gc_out, vec_out,
                 proj, qa, mixed, dm, n1, n1t, wpp, x, dmiddle, ge, go, dproj, tg, gp,
                 ka, da, dq, va, kt, vs, vo, vl, vz,
                 lce, lxhe, lyhe, lxe, lye, lze, lco, lxho, lyho, lxo, lyo, lzo,
                 lcp, lxhp, lyhp, lxp, lyp, lzp, gpw, gcol, lzc,
                 send_sem, recv_sem, load_sem):
    p = Place()
    T, D = x.shape
    FF = ge.shape[1]
    R = D // 8
    Q = FF // 4
    pairs = H // 2
    KB = 256
    parts = 2
    link = Link(p, send_sem, recv_sem)
    loads = []

    def load(source, target):
        made = pltpu.make_async_copy(source, target, load_sem.at[len(loads)])
        made.start()
        loads.append(made)
        return made

    first_loads = [load(a, b) for a, b in ((proj_hbm, proj), (qa_hbm, qa), (mixed_hbm, mixed), (dm_hbm, dm))]
    ge_load, gc_load, go_load, n1_load = load(ge_hbm, ge), load(gc_hbm, gcol), load(go_hbm, go), load(n1_hbm, n1)
    late = [load(x_hbm, x), load(dmiddle_hbm, dmiddle)]
    for i in range(pairs):
        for s in range(3):
            late.append(load(wp_hbm.at[:, pl.ds((s * pairs + i) * 128, 128)],
                             wpp.at[:, pl.ds((i * 3 + s) * 128, 128)]))

    def finish_e(total):
        ge_out[...] = total

    def finish_o(total):
        go_out[...] = jnp.where(p.odd == 0, total[:, 0:192], total[:, 64:256])

    rows_of = lambda d: pl.ds(mo(d * R, 16), R)
    def finish_c(total):
        gc_out[...] = total

    e_col, o_col = (lambda d: ge.at[rows_of(d), :]), (lambda d: go.at[d])
    e_sib, ev_e = scatter_events(
        link, p, e_col, lambda ref, h: ref.at[:, pl.ds(h * (FF // 2), FF // 2)], lce, lxhe, lyhe, lxe, lye)
    o_sib, ev_o = scatter_events(
        link, p, o_col, lambda ref, h: ref.at[pl.ds(2 * h, 2)], lco, lxho, lyho, lxo, lyo)
    e_send, e_last = z_sum(link, p, lambda z: e_col(p.d).at[:, pl.ds(mo(z * Q, 128), Q)], lze, finish_e)
    o_send, o_last = z_sum(link, p, lambda z: o_col(p.d).at[z], lzo, finish_o)
    c_send, c_last = z_sum(link, p, lambda z: gcol.at[z], lzc, finish_c)
    ended = []
    combos = []
    for i in range(pairs):
        for s in range(3):
            tile = s * pairs + i
            for owner in range(4):
                left = 9 * owner // 2
                if left <= tile < left + 5:
                    combos.append((i, s, owner, tile - left))
    assert len(combos) == 20
    z_slots = [[link.slot() for _ in range(3)] for _ in combos]

    def pair_scatter(i):
        column = lambda d: gp.at[i, d]
        sib, events = scatter_events(
            link, p, column, lambda ref, h: ref.at[pl.ds(h * (R // 2), R // 2)],
            lcp.at[i], lxhp.at[i], lyhp.at[i], lxp.at[i], lyp.at[i])
        mine = [(at, c) for at, c in enumerate(combos) if c[0] == i]

        def along(add_own):
            def run():
                add_own()
                for at, (_, s, owner, _) in mine:
                    @pl.when(p.z != owner)
                    def _():
                        step = lax.rem(owner - p.z + 4, 4)
                        part = column(p.d).at[:, pl.ds(s * 128, 128)]
                        link.copy(z_slots[at][0] + step - 1, part, lzp.at[at, step - 1], ("z", owner)).start()
            return run

        def last():
            for at, (_, s, owner, place) in mine:
                @pl.when(p.z == owner)
                def _():
                    total = gp[i, p.d, :, s * 128:(s + 1) * 128].astype(F32)
                    for step in range(1, 4):
                        link.got(z_slots[at][step - 1], lzp.at[at, step - 1])
                        total = total + lzp[at, step - 1].astype(F32)
                    gpw[:, place * 128:(place + 1) * 128] = total

        def ending():
            for at, (_, s, owner, _) in mine:
                @pl.when(p.z != owner)
                def _():
                    step = lax.rem(owner - p.z + 4, 4)
                    view = lzp.at[at, 0]
                    link.copy(z_slots[at][0] + step - 1, view, view, "x").wait_send()

        ended.append(ending)

        def start():
            for k in (3, 1, 2, 0):
                sib(k)

        return [start] + events[:5] + [along(events[5]), last]

    ev_p = [pair_scatter(i) for i in range(pairs)]

    enter(p, wide=True)
    for made in first_loads:
        made.wait()
    length = length_ref[0]

    def start_e():
        ge_load.wait()
        for k in (3, 1, 2, 0):
            e_sib(k)

    def start_o():
        go_load.wait()
        for k in (3, 1, 2, 0):
            o_sib(k)

    def turn_n1():
        n1_load.wait()
        for i in range(T // 256):
            n1t[:, i * 256:(i + 1) * 256] = n1[i * 256:(i + 1) * 256, :].T

    def start_c():
        gc_load.wait()
        c_send()

    e, o = ev_e, ev_o
    q = ev_p
    timeline = [
        (0, start_c), (0, start_e), (0, start_o), (0, turn_n1), (1, e[0]), (2, e[1]), (2, e[4]), (2, o[0]), (2, o[1]), (2, o[4]),
        (2, q[0][0]), (3, q[0][1]), (3, q[0][2]), (3, q[0][5]), (4, e[2]), (4, e[3]), (4, c_last), (4, o[2]), (4, o[3]),
        (4, q[0][3]), (4, q[0][4]), (4, q[1][0]), (5, q[1][1]), (5, q[1][2]), (5, q[1][5]), (6, q[2][0]),
        (7, q[2][1]), (7, q[2][2]), (7, q[2][5]), (8, e[5]), (8, e_send), (8, q[3][0]), (9, o[5]), (9, o_send),
        (9, q[3][1]), (9, q[3][2]), (9, q[3][5]), (10, q[0][6]), (10, q[1][3]), (10, q[1][4]), (10, q[2][3]), (10, q[2][4]),
        (10, q[3][3]), (10, q[3][4]), (10, q[4][0]), (11, q[4][1]), (11, q[4][2]), (11, q[4][5])]
    timeline.sort(key=lambda e: e[0])

    def body(step, _):
        for at, event in timeline:
            if at < pairs * parts:
                pl.when(step == at)(event)
        pair = lax.div(step, parts)
        part = lax.rem(step, parts)
        ps = lambda off: pl.ds(mo(off + pair * 128, 128), 128)
        own = lambda s: pl.ds(mo(pair * 384 + s * 128, 128), 128)

        @pl.when(part == 0)
        def _():
            lane, row = iota((T, 128), 1), iota((T, 128), 0)
            k = proj[:, ps(D)].astype(F32)
            v = proj[:, ps(2 * D)].astype(F32)
            do = dm[:, ps(0)].astype(F32)
            pr = do * mixed[:, ps(0)].astype(F32)
            dead = jnp.where(row < length, 0.0, neg_fill)
            for head in range(2):
                keep = (lane < 64) if head == 0 else (lane >= 64)
                delta = jnp.sum(jnp.where(keep, pr, 0.0), axis=-1, keepdims=True)
                one, two, three = split3(-delta)
                da[head] = extend(head, do, lane, one, two, three, 0.0)
                ka[head] = extend(head, k, lane, 1.0, 1.0, 1.0, dead)
                va[head] = extend(head, v, lane, 1.0, 1.0, 1.0, 0.0)
                kt[head] = jnp.where(keep, k, 0.0).astype(BF).T
            dq[...] = jnp.zeros_like(dq)

        lk = iota((KB, 128), 1)
        spans = [pl.ds(mo(part * (T // parts) + i * KB, KB), KB) for i in range(T // parts // KB)]
        items = [(head, r) for r in spans for head in range(2)]
        kept = {}

        def products(n):
            head, r = items[n]
            return dot_nt(ka[head, r, :], qa[pair * 2 + head]), dot_nt(va[head, r, :], da[head])

        def weigh(scores, grads):
            weights = jnp.exp(scores)
            return weights.astype(BF), (weights * grads).astype(BF)

        def finish(n, low, ds):
            head, r = items[n]
            kept[n] = dot(ds, qa[pair * 2 + head]), dot(low, da[head])
            dq[head] += dot(kt[head, :, r], ds)
            if head == 1:
                dproj[r, own(1)] = jnp.where(lk < 64, kept[n - 1][0], kept[n][0]).astype(BF)
                dproj[r, own(2)] = jnp.where(lk < 64, kept[n - 1][1], kept[n][1]).astype(BF)

        value, waiting = products(0), None
        for n in range(len(items)):
            following = products(n + 1) if n + 1 < len(items) else None
            done = weigh(*value)
            if waiting is not None:
                finish(n - 1, *waiting)
            value, waiting = following, done
        finish(len(items) - 1, *waiting)

        @pl.when(part == parts - 1)
        def _():
            dproj[:, own(0)] = ((dq[0] + dq[1]) * (HD ** -0.5)).T.astype(BF)
            value = dot(n1t[...], dproj[:, pl.ds(mo(pair * 384, 128), 384)])
            gp[pair] = value.reshape(8, R, 384).astype(BF)

        return 0

    lax.fori_loop(0, pairs * parts, body, 0)
    ev_p[pairs - 1][0]()
    for made in late:
        made.wait()
    vs[...] = vg_ref[...]
    LR = 256

    def norm_body(i, _):
        def spot(where, events):
            @pl.when(i == where)
            def _():
                for event in events:
                    event()

        spot(0, [e_last, q[1][6], q[2][6], q[3][6], q[4][3], q[4][4]])
        spot(1, q[5][1:3] + q[5][5:6])
        spot(2, [o_last, q[0][7], q[1][7], q[4][6], q[2][7]])
        spot(3, q[5][3:5] + q[3][7:8])
        r = pl.ds(mo(i * LR, LR), LR)
        left = dproj[r, :]
        dn = dot_nt(left, wpp[...])
        sums = jnp.sum(left.astype(F32), axis=0, keepdims=True)
        for j in range(pairs):
            vs[0:1, j * 128:(j + 1) * 128] += sums[:, j * 384:j * 384 + 128]
            vs[1:2, j * 128:(j + 1) * 128] += sums[:, j * 384 + 256:j * 384 + 384]
        value = x[r, :].astype(F32)
        u = value - jnp.mean(value, axis=-1, keepdims=True)
        spread = lax.rsqrt(jnp.mean(u * u, axis=-1, keepdims=True) + eps_norm)
        xhat = u * spread
        vs[8:9, :] += jnp.sum(dn * xhat, axis=0, keepdims=True)
        vs[9:10, :] += jnp.sum(dn, axis=0, keepdims=True)
        gx = dn * v_ref[4:5, 0:D]
        back = spread * (gx - jnp.mean(gx, axis=-1, keepdims=True)
                         - xhat * jnp.mean(gx * xhat, axis=-1, keepdims=True))
        tg[r, :] = (back + dmiddle[r, :]).astype(BF)
        return 0

    lax.fori_loop(0, T // LR, norm_body, 0)
    out = load(tg, tokens_out)
    v_slots = link.slot(16)
    for d in range(8):
        line = lambda row, at, n: jnp.concatenate(
            [vs[row:row + 1, at:at + n], jnp.zeros((1, 384 - n), F32)], axis=1) if n < 384 else vs[row:row + 1, at:at + n]
        vo[d] = jnp.concatenate(
            [line(d // 4, d % 4 * 2 * R, 2 * R), line(2, d * R, R), line(3 + d // 2, d % 2 * 4 * R, 4 * R)]
            + [line(row, d * R, R) for row in (7, 8, 9, 10, 11)], axis=0)
    for d in range(8):
        @pl.when(p.d != d)
        def _():
            link.copy(v_slots + d, vo.at[d], vl.at[p.d], ("d", d), land=v_slots + p.d).start()
    for event in (q[4][7], q[5][6]):
        event()
    vl[p.d] = vo[p.d]
    for d in range(8):
        @pl.when(p.d != d)
        def _():
            link.got(v_slots + d, vl.at[d])
    own = vl[0]
    for d in range(1, 8):
        own = own + vl[d]
    vz[p.z] = own
    for k in (1, 2, 3):
        link.send(v_slots + 8 + k, vz.at[p.z], vz.at[p.z], ("z", p.order[k]), lambda: vz.at[0], land=v_slots + 12 + p.z)
    q[5][7]()
    gp_out[...] = jnp.where(p.odd == 0, gpw[:, 0:576], gpw[:, 64:640])
    for k in (1, 2, 3):
        link.got(v_slots + 12 + p.order[k], vz.at[p.order[k]])
    vec_out[...] = vz[0] + vz[1] + vz[2] + vz[3]
    for d in range(8):
        @pl.when(p.d != d)
        def _():
            link.copy(v_slots + d, vo.at[d], vo.at[d], "x").wait_send()
    link.finish()
    for ending in ended:
        ending()
    out.wait()


def third_call(length, proj, qa, mixed, dm, n1, wp, x, dmiddle, ge, go, gc, vg, v):
    T, D = x.shape
    FF = ge.shape[1]
    R, Q, pairs = D // 8, FF // 4, H // 2
    vm = pltpu.VMEM
    n = 8 * 8 + 12 + 60 + 16
    return pl.pallas_call(
        third_kernel,
        in_specs=[SM] + [ANY] * 11 + [VM] * 2,
        out_specs=[ANY] + [VM] * 5,
        out_shape=[sds((T, D), BF), sds((R, 3 * D // 4), F32), sds((R, D // 4), F32), sds((R, Q), F32), sds((D // 4, FF // 8), F32),
                   sds((8, 384), F32)],
        scratch_shapes=[
            vm((T, 3 * D), BF), vm((H, T, 128), BF), vm((T, D), BF), vm((T, D), BF), vm((T, D), BF), vm((D, T), BF),
            vm((D, 3 * D), BF), vm((T, D), BF), vm((T, D), F32), vm((D, FF), BF), vm((8, 4, R, 256), BF),
            vm((T, 3 * D), BF), vm((T, D), BF), vm((pairs, 8, R, 384), BF),
            vm((2, T, 128), BF), vm((2, T, 128), BF), vm((2, 128, T), F32), vm((2, T, 128), BF), vm((2, 128, T), BF),
            vm((16, D), F32), vm((8, 8, 384), F32), vm((8, 8, 384), F32), vm((4, 8, 384), F32),
            vm((4, R, FF), BF), vm((R, FF // 2), BF), vm((R, FF // 2), BF), vm((R, FF), BF), vm((R, FF), BF), vm((4, R, Q), BF),
            vm((4, 4, R, 256), BF), vm((2, R, 256), BF), vm((2, R, 256), BF), vm((4, R, 256), BF), vm((4, R, 256), BF),
            vm((4, R, 256), BF),
            vm((pairs, 4, R, 384), BF), vm((pairs, R // 2, 384), BF), vm((pairs, R // 2, 384), BF),
            vm((pairs, R, 384), BF), vm((pairs, R, 384), BF), vm((20, 3, R, 128), BF), vm((R, 640), F32),
            vm((4, D // 4, FF // 8), BF), vm((4, D // 4, FF // 8), BF),
            pltpu.SemaphoreType.DMA((n,)), pltpu.SemaphoreType.DMA((n,)), pltpu.SemaphoreType.DMA((29,)),
        ],
        compiler_params=pltpu.CompilerParams(
            collective_id=2, has_side_effects=True, vmem_limit_bytes=63 << 20),
        name="third_part",
    )(length, proj, qa, mixed, dm, n1, wp, x, dmiddle, ge, go, gc, vg, v)


def last_kernel(block_in, tokens_in, p_in, o_in, e_in, c_in, vec_in,
                block_out, tokens_out, p_out, o_out, e_out, c_out, *rest):
    vectors, held, vec, sem = rest[:8], rest[8:14], rest[14], rest[15]
    parts = 2
    rows = block_in.shape[0] // parts
    whole = lambda ref: ref
    legs = []
    for i in range(parts):
        part = lambda ref, i=i: ref.at[pl.ds(i * rows, rows)]
        legs += [(part, block_in, held[0], block_out), (part, tokens_in, held[1], tokens_out)]
    legs += [(whole, a, b, c) for a, b, c in zip((p_in, o_in, e_in, c_in), held[2:], (p_out, o_out, e_out, c_out))]
    first = pltpu.make_async_copy(vec_in, vec, sem.at[2 * len(legs)])
    first.start()
    ins = [pltpu.make_async_copy(part(a), part(b), sem.at[k]) for k, (part, a, b, _) in enumerate(legs)]
    outs = [pltpu.make_async_copy(part(b), part(c), sem.at[len(legs) + k]) for k, (part, _, b, c) in enumerate(legs)]
    for made in ins:
        made.start()
    for came, goes in zip(ins, outs):
        came.wait()
        goes.start()
    first.wait()
    for at, target in enumerate(vectors):
        n = target.shape[0]
        target[...] = vec[at:at + 1, 0:n].reshape(n)
    for goes in outs:
        goes.wait()


def last_call(sizes, *arrays):
    return pl.pallas_call(
        last_kernel,
        in_specs=[ANY] * 7,
        out_specs=[ANY] * 6 + [VM] * 8,
        out_shape=[sds(item.shape, item.dtype) for item in arrays[:6]] + [sds((n,), F32) for n in sizes],
        scratch_shapes=[pltpu.VMEM(item.shape, item.dtype) for item in arrays] + [pltpu.SemaphoreType.DMA((17,))],
        compiler_params=pltpu.CompilerParams(vmem_limit_bytes=63 << 20),
        name="last_part",
    )(*arrays)


def per_device_fast(tokens, lengths, cotangent, project_weight, project_bias, output_weight, output_bias,
                    expand_weight, expand_bias, contract_weight, contract_bias, first_gain, first_shift,
                    second_gain, second_shift):
    vectors = (project_bias, output_bias, expand_bias, contract_bias, first_gain, first_shift, second_gain, second_shift)
    normed_one, projected, mixed, qa, full_project, full_output, full_expand, cc, v = first_call(
        lengths, tokens, project_weight, output_weight, expand_weight, contract_weight.T, vectors)
    block_out, grad_mixed, grad_middle, ge, go, gc, vg = second_call(
        lengths, tokens, cotangent, mixed, full_output, full_expand, cc, v)
    third = third_call(
        lengths, projected, qa, mixed, grad_mixed, normed_one, full_project, tokens, grad_middle, ge, go, gc, vg, v)
    out = last_call([item.shape[0] for item in vectors], block_out, *third)
    return (out[0], out[1], out[2], out[6], out[3], out[7], out[4], out[8], out[5].T, *out[9:])


def solution(mesh):
    both, rows, grid = P(("dp", "fsdp"), None), P("dp"), P("dp", "fsdp")
    weights = (grid, rows, grid, rows, grid, rows, grid, rows)
    fast = mesh.shape["dp"] == 8 and mesh.shape["fsdp"] == 4
    return jax.shard_map(
        per_device_fast if fast else per_device,
        mesh=mesh,
        in_specs=(both, P(("dp", "fsdp")), both) + weights + (rows,) * 4,
        out_specs=(both, both) + weights + (rows,) * 4,
        check_vma=False,
    )
```

```python
import functools
import jax
import jax.numpy as jnp
from jax import lax
from jax.experimental import pallas as pl
from jax.experimental.pallas import tpu as pltpu
from jax.sharding import PartitionSpec as P

H = 12
HD = 64
F32 = jnp.float32
BF = jnp.bfloat16
MESH = pl.DeviceIdType.MESH
eps_norm = 1e-05
neg_fill = -1000000000.0


def dot(first, second):
    return jnp.dot(first, second, preferred_element_type=F32)


def dot_nt(first, second):
    return lax.dot_general(first, second, (((1,), (1,)), ((), ())), preferred_element_type=F32)


def dot_tn(first, second):
    return lax.dot_general(first, second, (((0,), (0,)), ((), ())), preferred_element_type=F32)


def mo(value, multiple):
    return pl.multiple_of(value, multiple)


class Place:
    def __init__(self):
        self.d = lax.axis_index("dp")
        self.z = lax.axis_index("fsdp")
        core = lax.rem(self.d, 2)
        across = lax.rem(lax.div(self.d, 2), 2)
        up = lax.div(self.d, 4)
        self.dc = self.d + 1 - 2 * core
        self.dx = self.d + 2 - 4 * across
        self.dy = self.d + 4 - 8 * up
        self.dd = self.dx + 4 - 8 * up
        self.odd = lax.rem(self.z, 2)
        z = self.z
        pick = lambda a, b, c, d: jnp.where(z < 2, jnp.where(z == 0, a, b), jnp.where(z == 2, c, d))
        self.order = [z, pick(1, 0, 3, 2), pick(2, 2, 1, 1), pick(3, 3, 0, 0)]

    def zt(self, step):
        return lax.rem(self.z + step, 4)

    def zf(self, step):
        return lax.rem(self.z + 4 - step, 4)

    def id(self, to):
        if to == "x":
            return (self.dx, self.z)
        if to == "y":
            return (self.dy, self.z)
        if to == "c":
            return (self.dc, self.z)
        if isinstance(to, tuple):
            return (to[1], self.z) if to[0] == "d" else (self.d, to[1])
        return (self.d, self.zt(to))


def enter(place, wide=False):
    barrier = pltpu.get_barrier_semaphore()
    sib = place.dc - place.d
    others = [("d", d + sib) for d in (place.dx, place.dy, place.dd)] + [("d", place.dd)] if wide else []
    partners = ["x", "y", "c", 1, 2, 3] + others
    for to in partners:
        pl.semaphore_signal(barrier, inc=1, device_id=place.id(to), device_id_type=MESH)
    pl.semaphore_wait(barrier, len(partners))


class Link:
    def __init__(self, place, send_sem, recv_sem):
        self.place, self.send_sem, self.recv_sem = place, send_sem, recv_sem
        self.count = 0
        self.copies = []

    def slot(self, many=1):
        self.count += many
        return self.count - many

    def copy(self, slot, source, target, to, land=None):
        return pltpu.make_async_remote_copy(
            src_ref=source, dst_ref=target, send_sem=self.send_sem.at[slot],
            recv_sem=self.recv_sem.at[slot if land is None else land], device_id=self.place.id(to),
            device_id_type=MESH)

    def send(self, slot, source, target, to, like, land=None, when=None):
        def start():
            self.copy(slot, source, target, to, land).start()

        if when is None:
            start()
        else:
            pl.when(when())(start)
        self.copies.append((slot, like, when))

    def got(self, slot, target):
        self.copy(slot, target, target, "x").wait_recv()

    def finish(self):
        for slot, like, when in self.copies:
            def done(slot=slot, like=like):
                view = like()
                self.copy(slot, view, view, "x").wait_send()

            if when is None:
                done()
            else:
                pl.when(when())(done)


class Gather:
    def __init__(self, link, place, block):
        p = place
        zr, zs = link.slot(4), link.slot(4)
        xs, ys, fx = link.slot(4), link.slot(4), link.slot(4)
        cs = link.slot(16)
        got = link.got
        send = functools.partial(link.send, like=lambda: block(0, 0))

        def z_step(a):
            def run():
                if a == 0:
                    own = block(p.z, p.d)
                    for k in (1, 2, 3):
                        send(zs + k, own, own, ("z", p.order[k]), land=zr + p.z)
                else:
                    got(zr + p.order[a], block(p.order[a], p.d))
            return run

        def x_step(a):
            def run():
                here = block(p.order[a], p.d)
                send(xs + a, here, here, "x")
                send(ys + a, here, here, "y")
                send(cs + a, here, here, "c")
            return run

        def turn(a):
            def run():
                b = p.order[a]
                bx, by = block(b, p.dx), block(b, p.dy)
                got(xs + a, bx)
                got(ys + a, by)
                if a in (0, 1):
                    send(fx + a, bx, bx, "y")
                else:
                    send(fx + a, by, by, "x")
                send(cs + 4 + a, bx, bx, "c")
                send(cs + 8 + a, by, by, "c")
            return run

        def corner(a):
            def run():
                bd = block(p.order[a], p.dd)
                got(fx + a, bd)
                send(cs + 12 + a, bd, bd, "c")
            return run

        def close():
            sib = p.dc - p.d
            for which, d in enumerate((p.d, p.dx, p.dy, p.dd)):
                for a in range(4):
                    got(cs + 4 * which + a, block(p.order[a], d + sib))

        self.z, self.x, self.t, self.q = ([make(a) for a in range(4)] for make in (z_step, x_step, turn, corner))
        self.close = close


def spread_z(link, place, ref):
    p = place
    zs, zr = link.slot(3), link.slot(4)

    def send():
        for k in (1, 2, 3):
            link.send(zs + k - 1, ref.at[p.z], ref.at[p.z], ("z", p.order[k]), lambda: ref.at[0], land=zr + p.z)

    def wait():
        for k in (1, 2, 3):
            b = p.order[k]
            link.got(zr + b, ref.at[b])

    return send, wait


def run(*events):
    def together():
        for event in events:
            event()
    return together


def window(value, odd, wide):
    rows, k = value.shape
    fill = jnp.zeros((rows, wide - k), F32)
    value = value.astype(F32)
    left = jnp.concatenate([value, fill], axis=1)
    right = jnp.concatenate([fill, value], axis=1)
    return jnp.where(odd == 0, left, right).astype(BF)


def merge_windows(blocks, full, tiles, rows_step):
    rows = full.shape[0]
    half = tiles // 2

    def body(i, _):
        r = pl.ds(mo(i * rows_step, rows_step), rows_step)
        for pair in range(2):
            even, odd = blocks.at[2 * pair], blocks.at[2 * pair + 1]
            base = pair * tiles * 128
            full[r, base:base + half * 128] = even[r, 0:half * 128]
            full[r, base + half * 128:base + (half + 1) * 128] = (
                even[r, half * 128:(half + 1) * 128] + odd[r, 0:128])
            full[r, base + (half + 1) * 128:base + tiles * 128] = odd[r, 128:(half + 1) * 128]
        return 0

    lax.fori_loop(0, rows // rows_step, body, 0)


def split3(value):
    high = value.astype(BF)
    rest = value - high.astype(F32)
    mid = rest.astype(BF)
    low = (rest - mid.astype(F32)).astype(BF)
    return high.astype(F32), mid.astype(F32), low.astype(F32)


def extend(head, pair, lane, one, two, three, four):
    base = 64 * (1 - head)
    extra = jnp.where(lane == base, one, jnp.where(lane == base + 1, two, jnp.where(
        lane == base + 2, three, jnp.where(lane == base + 3, four, 0.0))))
    keep = (lane < 64) if head == 0 else (lane >= 64)
    return jnp.where(keep, pair, extra).astype(BF)


def iota(shape, axis):
    return lax.broadcasted_iota(jnp.int32, shape, axis)


QB = 256


def first_kernel(length_ref, x_ref, wp_ref, wo_ref, we_ref, wc_ref, *refs):
    vec_refs, refs = refs[:8], refs[8:]
    first_body(length_ref, x_ref, wp_ref, wo_ref, we_ref, wc_ref, vec_refs, *refs)


def first_body(length_ref, x_ref, wp_ref, wo_ref, we_ref, wc_ref, vec_refs,
                 n1_out, proj_out, mixed_out, qa_out, wp_out, wo_out, we_out, c_out, v_out,
                 wp_blk, wo_blk, we, wp, wo, vb, n1, proj, mixed, qa, ka, va, vrow, cc,
                 send_sem, recv_sem, out_sem, pair_sem):
    p = Place()
    T, D = x_ref.shape
    R = wp_ref.shape[0]
    FF = we.shape[1]
    link = Link(p, send_sem, recv_sem)
    rows_of = lambda d: pl.ds(mo(d * R, 16), R)
    half = R // 2
    bpa = lambda z, d: wp_blk.at[z, pl.ds(mo(d * R, 16), half), :]
    bpb = lambda z, d: wp_blk.at[z, pl.ds(mo(d * R + half, 16), half), :]
    bo = lambda z, d: wo_blk.at[z, rows_of(d), :]
    be = lambda z, d: we.at[rows_of(d), pl.ds(mo(z * (FF // 4), 128), FF // 4)]
    g0, g1, go, ge = (Gather(link, p, b) for b in (bpa, bpb, bo, be))
    c_send, c_wait = spread_z(link, p, cc)
    vs = [link.slot() for _ in range(7)]

    wp_blk[p.z, rows_of(p.d), :] = window(wp_ref[...], p.odd, wp_blk.shape[2])
    wo_blk[p.z, rows_of(p.d), :] = window(wo_ref[...], p.odd, wo_blk.shape[2])
    we[rows_of(p.d), pl.ds(mo(p.z * (FF // 4), 128), FF // 4)] = we_ref[...]
    cc[p.z] = wc_ref[...]
    for i, ref in enumerate(vec_refs):
        vb[p.d, i:i + 1, 0:ref.shape[0]] = ref[...].astype(F32).reshape(1, ref.shape[0]).astype(BF)

    outs = []

    def out(source, target):
        made = pltpu.make_async_copy(source, target, out_sem.at[len(outs)])
        made.start()
        outs.append(made)

    enter(p)
    send_v = lambda slot, d, to: link.send(vs[slot], vb.at[d], vb.at[d], to, lambda: vb.at[0])
    for slot, to in ((0, "x"), (1, "y"), (3, "c")):
        send_v(slot, p.d, to)
    run(g0.z[0], g0.x[0], g1.z[0], g1.x[0])()
    link.got(vs[0], vb.at[p.dx])
    link.got(vs[1], vb.at[p.dy])
    send_v(2, p.dx, "y")
    send_v(4, p.dx, "c")
    send_v(5, p.dy, "c")
    run(g0.z[1], g0.x[1], g0.t[0], g1.t[0], g0.z[2], g0.x[2])()
    link.got(vs[2], vb.at[p.dd])
    send_v(6, p.dd, "c")
    sib = p.dc - p.d
    for slot, d in ((3, p.d), (4, p.dx), (5, p.dy), (6, p.dd)):
        link.got(vs[slot], vb.at[d + sib])
    got = vb[...].astype(F32)
    side = lambda row, wide: jnp.concatenate([got[i, row:row + 1, 0:wide] for i in range(8)], axis=1)
    bias = side(0, 2 * R)
    vrow[0:1, 0:D] = bias[:, 0:D]
    vrow[0:1, D:2 * D] = jnp.zeros((1, D), F32)
    vrow[0:1, 2 * D:3 * D] = bias[:, D:]
    vrow[1:2, :] = side(2, FF // 8)
    for row, at in ((2, 1), (3, 3), (4, 4), (5, 5), (6, 6), (7, 7)):
        vrow[row:row + 1, 0:D] = side(at, R)
    out(vrow, v_out)
    run(g0.t[1], g0.z[3], g0.x[3], g0.q[0], g1.z[1], g1.x[1], g1.q[0])()

    LR = 128
    gain, shift = vrow[4:5, 0:D], vrow[5:6, 0:D]

    def norm_body(i, _):
        r = pl.ds(mo(i * LR, LR), LR)
        value = x_ref[r, :].astype(F32)
        u = value - jnp.mean(value, axis=-1, keepdims=True)
        spread = jnp.mean(u * u, axis=-1, keepdims=True)
        n1[r, :] = (u * lax.rsqrt(spread + eps_norm) * gain + shift).astype(BF)
        return 0

    norm_part = lambda k: lax.fori_loop(k * (T // LR // 4), (k + 1) * (T // LR // 4), norm_body, 0)
    g0.t[2]()
    norm_part(0)
    run(g1.z[2], g1.x[2], g0.q[1])()
    norm_part(1)
    run(g1.z[3], g1.x[3], ge.z[0], go.z[0], g0.t[3])()
    norm_part(2)
    run(g0.q[2], g1.t[1])()
    norm_part(3)
    run(g1.t[2], g1.t[3], ge.x[0], g0.q[3], g1.q[1], g1.q[2], g1.q[3], go.x[0])()
    out(n1, n1_out)
    run(g0.close, g1.close)()
    merge_windows(wp_blk, wp, 9, 96)
    out(wp, wp_out)
    run(ge.z[1], ge.x[1])()

    def project_body(i, _):
        for at, event in ((2, run(ge.z[2], ge.x[2], ge.t[0])), (3, go.t[0])):
            pl.when(i == at)(event)
        r = pl.ds(mo(i * 256, 256), 256)
        left = n1[r, :]
        for j in range(3):
            cols = slice(j * D, (j + 1) * D)
            value = dot(left, wp[:, cols]) + vrow[0:1, cols]
            proj[r, cols] = value.astype(BF)
        return 0

    lax.fori_loop(0, T // 256, project_body, 0)
    out(proj, proj_out)

    length = length_ref[0]
    subs = T // QB

    def pair_outs(pair):
        heads = pl.ds(2 * pair, 2)
        cols = pl.ds(mo(pair * 128, 128), 128)
        return (pltpu.make_async_copy(qa.at[heads], qa_out.at[heads], pair_sem.at[pair, 0]),
                pltpu.make_async_copy(mixed.at[:, cols], mixed_out.at[:, cols], pair_sem.at[pair, 1]))

    def attend_steps(events):
        def body(pair, _):
            for at, event in events:
                pl.when(pair == at)(event)
            cols = lambda off: pl.ds(mo(off + pair * 128, 128), 128)
            lane, row = iota((T, 128), 1), iota((T, 128), 0)
            q = proj[:, cols(0)].astype(F32) * (HD ** -0.5)
            k = proj[:, cols(D)].astype(F32)
            v = proj[:, cols(2 * D)].astype(F32)
            dead = jnp.where(row < length, 0.0, neg_fill)
            for head in range(2):
                ka[head] = extend(head, k, lane, 1.0, 1.0, 1.0, dead)
                qa[pair * 2 + head] = extend(head, q, lane, 0.0, 0.0, 0.0, 1.0)
                keep = (lane < 64) if head == 0 else (lane >= 64)
                va[head] = jnp.where(keep, v, 1.0).astype(BF)
            sub_lane = iota((QB, 128), 1)
            items = [(head, pl.ds(i * QB, QB)) for i in range(subs) for head in range(2)]
            halves = {}

            def scores(n):
                head, r = items[n]
                return dot_nt(qa[pair * 2 + head, r, :], ka[head])

            def soften(value):
                top = jnp.max(value, axis=-1, keepdims=True)
                return top, jnp.exp(value - top).astype(BF)

            def finish(n, top, powers):
                head, r = items[n]
                value = dot(powers, va[head])
                total = value[:, 64:65] if head == 0 else value[:, 0:1]
                one, two, three = split3(-(top + jnp.log(total)))
                query = qa[pair * 2 + head, r, :].astype(F32)
                qa[pair * 2 + head, r, :] = extend(head, query, sub_lane, one, two, three, 1.0)
                halves[n] = value * (1.0 / total)
                if head == 1:
                    mixed[r, cols(0)] = jnp.where(sub_lane < 64, halves[n - 1], halves[n]).astype(BF)

            value, waiting = scores(0), None
            for n in range(len(items)):
                following = scores(n + 1) if n + 1 < len(items) else None
                soft = soften(value)
                if waiting is not None:
                    finish(n - 1, *waiting)
                value, waiting = following, soft
            finish(len(items) - 1, *waiting)
            for made in pair_outs(pair):
                made.start()
            return 0

        lax.fori_loop(0, H // 2, body, 0)

    attend_steps([(1, run(go.z[1], go.x[1], ge.z[3], ge.x[3], go.z[2], go.x[2], ge.t[1])),
                  (2, run(go.z[3], go.x[3], ge.t[2], c_send)), (3, run(ge.q[0], go.t[1], go.q[0])),
                  (4, run(ge.t[3], go.t[2])), (5, run(ge.q[1], ge.q[2], go.t[3]))])
    run(ge.q[3], go.q[1], go.q[2], go.q[3], go.close)()
    merge_windows(wo_blk, wo, 3, 96)
    out(wo, wo_out)
    ge.close()
    out(we, we_out)
    c_wait()
    out(cc, c_out)
    link.finish()
    for made in outs:
        made.wait()
    for pair in range(H // 2):
        for made in pair_outs(pair):
            made.wait()


def first_call(length, x, wp, wo, we, wc, vectors):
    T, D = x.shape
    FF = we.shape[1] * 4
    ANY = pl.BlockSpec(memory_space=pl.ANY)
    V = pl.BlockSpec(memory_space=pltpu.VMEM)
    S = pl.BlockSpec(memory_space=pltpu.SMEM)
    sds = jax.ShapeDtypeStruct
    n = 4 * 36 + 7 + 7
    return pl.pallas_call(
        first_kernel,
        in_specs=[S] + [V] * 13,
        out_specs=[ANY] * 9,
        out_shape=[sds((T, D), BF), sds((T, 3 * D), BF), sds((T, D), BF), sds((H, T, 128), BF),
                   sds((D, 3 * D), BF), sds((D, D), BF), sds((D, FF), BF), sds((4,) + wc.shape, BF), sds((8, FF), F32)],
        scratch_shapes=[
            pltpu.VMEM((4, D, 640), BF), pltpu.VMEM((4, D, 256), BF), pltpu.VMEM((D, FF), BF),
            pltpu.VMEM((D, 3 * D), BF), pltpu.VMEM((D, D), BF), pltpu.VMEM((8, 16, FF // 8), BF),
            pltpu.VMEM((T, D), BF), pltpu.VMEM((T, 3 * D), BF), pltpu.VMEM((T, D), BF),
            pltpu.VMEM((H, T, 128), BF), pltpu.VMEM((2, T, 128), BF), pltpu.VMEM((2, T, 128), BF),
            pltpu.VMEM((8, FF), F32), pltpu.VMEM((4,) + wc.shape, BF),
            pltpu.SemaphoreType.DMA((n,)), pltpu.SemaphoreType.DMA((n,)), pltpu.SemaphoreType.DMA((9,)), pltpu.SemaphoreType.DMA((H // 2, 2)),
        ],
        compiler_params=pltpu.CompilerParams(
            collective_id=0, has_side_effects=True, vmem_limit_bytes=60 << 20),
        name="first_part",
    )(length, x, wp, wo, we, wc, *vectors)


def layer_norm(values, gain_row, shift_row):
    centre = jnp.mean(values, axis=-1, keepdims=True)
    centred = values - centre
    spread = jnp.mean(centred * centred, axis=-1, keepdims=True)
    return centred * lax.rsqrt(spread + eps_norm) * gain_row + shift_row


def gelu_exact(values):
    return jax.nn.gelu(values, approximate=False)


def matmul(first, second):
    return jnp.dot(first, second, preferred_element_type=jnp.float32)


def over_rows(first, second):
    return lax.dot_general(
        first, second, (((0,), (0,)), ((), ())), preferred_element_type=jnp.float32
    )


def over_columns(first, second):
    return lax.dot_general(
        first, second, (((1,), (1,)), ((), ())), preferred_element_type=jnp.float32
    )


def fetch_forward(
    project_weight,
    output_weight,
    expand_weight,
    contract_weight,
    project_bias,
    output_bias,
    expand_bias,
    contract_bias,
    first_gain,
    first_shift,
    second_gain,
    second_shift,
):
    wide_project, wide_output, wide_expand, wide_contract = (
        lax.all_gather(project_weight, "fsdp", axis=1, tiled=True),
        lax.all_gather(output_weight, "fsdp", axis=1, tiled=True),
        lax.all_gather(expand_weight, "fsdp", axis=1, tiled=True),
        lax.all_gather(contract_weight, "fsdp", axis=1, tiled=True),
    )
    return (
        lax.all_gather(wide_project, "dp", axis=0, tiled=True),
        lax.all_gather(wide_output, "dp", axis=0, tiled=True),
        lax.all_gather(wide_expand, "dp", axis=0, tiled=True),
        lax.all_gather(wide_contract, "dp", axis=0, tiled=True),
        lax.all_gather(project_bias, "dp", axis=0, tiled=True),
        lax.all_gather(output_bias, "dp", axis=0, tiled=True),
        lax.all_gather(expand_bias, "dp", axis=0, tiled=True),
        lax.all_gather(contract_bias, "dp", axis=0, tiled=True),
        lax.all_gather(first_gain, "dp", axis=0, tiled=True),
        lax.all_gather(first_shift, "dp", axis=0, tiled=True),
        lax.all_gather(second_gain, "dp", axis=0, tiled=True),
        lax.all_gather(second_shift, "dp", axis=0, tiled=True),
    )


def fetch_backward(
    project_weight,
    output_weight,
    expand_weight,
    contract_weight,
    project_bias,
    output_bias,
    expand_bias,
    contract_bias,
    first_gain,
    first_shift,
    second_gain,
    second_shift,
):
    wide_project, wide_output, wide_expand, wide_contract = (
        lax.all_gather(project_weight, "fsdp", axis=1, tiled=True),
        lax.all_gather(output_weight, "fsdp", axis=1, tiled=True),
        lax.all_gather(expand_weight, "fsdp", axis=1, tiled=True),
        lax.all_gather(contract_weight, "fsdp", axis=1, tiled=True),
    )
    return (
        lax.all_gather(wide_project, "dp", axis=0, tiled=True),
        lax.all_gather(wide_output, "dp", axis=0, tiled=True),
        lax.all_gather(wide_expand, "dp", axis=0, tiled=True),
        lax.all_gather(wide_contract, "dp", axis=0, tiled=True),
        lax.all_gather(project_bias, "dp", axis=0, tiled=True),
        lax.all_gather(output_bias, "dp", axis=0, tiled=True),
        lax.all_gather(expand_bias, "dp", axis=0, tiled=True),
        lax.all_gather(contract_bias, "dp", axis=0, tiled=True),
        lax.all_gather(first_gain, "dp", axis=0, tiled=True),
        lax.all_gather(first_shift, "dp", axis=0, tiled=True),
        lax.all_gather(second_gain, "dp", axis=0, tiled=True),
        lax.all_gather(second_shift, "dp", axis=0, tiled=True),
    )


def split_heads(cell_rows, block_rows):
    slot_count = cell_rows.shape[0]
    width = cell_rows.shape[1] // 3
    query_blocks = cell_rows[:, :width].reshape(slot_count // block_rows, block_rows, H, HD)
    keys_all = cell_rows[:, width : 2 * width].reshape(slot_count, H, HD)
    values_all = cell_rows[:, 2 * width :].reshape(slot_count, H, HD)
    return (query_blocks, keys_all, values_all)


def block_scores(query_block, keys_all, key_live):
    scores = jnp.einsum(
        "qhe,khe->hqk", query_block, keys_all, preferred_element_type=jnp.float32
    ) * HD ** (-0.5)
    return jnp.where(key_live[None, None, :], scores, neg_fill)


def attend_forward(query_block, keys_all, values_all, key_live):
    scores = block_scores(query_block, keys_all, key_live)
    row_max = jnp.max(scores, axis=-1, keepdims=True)
    powers = jnp.exp(scores - row_max)
    row_total = jnp.sum(powers, axis=-1, keepdims=True)
    weights = (powers / row_total).astype(jnp.bfloat16)
    mixed_block = jnp.einsum(
        "hqk,khe->qhe", weights, values_all, preferred_element_type=jnp.float32
    )
    return (mixed_block, (row_max + jnp.log(row_total))[:, :, 0])


def attend_backward(query_block, grad_block, log_block, keys_all, values_all, key_live):
    scores = block_scores(query_block, keys_all, key_live)
    weights = jnp.exp(scores - log_block[:, :, None])
    grad_weights = jnp.einsum(
        "qhe,khe->hqk", grad_block, values_all, preferred_element_type=jnp.float32
    )
    row_inner = jnp.sum(grad_weights * weights, axis=-1, keepdims=True)
    grad_scores = (weights * (grad_weights - row_inner)).astype(jnp.bfloat16)
    grad_query = jnp.einsum(
        "hqk,khe->qhe", grad_scores, keys_all, preferred_element_type=jnp.float32
    ) * HD ** (-0.5)
    grad_key = jnp.einsum(
        "hqk,qhe->khe", grad_scores, query_block, preferred_element_type=jnp.float32
    ) * HD ** (-0.5)
    grad_value = jnp.einsum(
        "hqk,qhe->khe", weights.astype(jnp.bfloat16), grad_block, preferred_element_type=jnp.float32
    )
    return (grad_query, grad_key, grad_value)


def per_device(
    tokens,
    lengths,
    cotangent,
    project_weight,
    project_bias,
    output_weight,
    output_bias,
    expand_weight,
    expand_bias,
    contract_weight,
    contract_bias,
    first_gain,
    first_shift,
    second_gain,
    second_shift,
):
    fetched = fetch_forward(
        project_weight,
        output_weight,
        expand_weight,
        contract_weight,
        project_bias,
        output_bias,
        expand_bias,
        contract_bias,
        first_gain,
        first_shift,
        second_gain,
        second_shift,
    )
    full_project, full_output, full_expand, full_contract = (
        fetched[0],
        fetched[1],
        fetched[2],
        fetched[3],
    )
    vectors = [item.astype(jnp.float32) for item in fetched[4:]]
    bias_project, bias_output, bias_expand, bias_contract = (
        vectors[0],
        vectors[1],
        vectors[2],
        vectors[3],
    )
    gain_one, shift_one, gain_two, shift_two = (vectors[4], vectors[5], vectors[6], vectors[7])
    cell_count = lengths.shape[0]
    slot_count = tokens.shape[0] // cell_count
    width = tokens.shape[1]
    block_rows = min(512, slot_count)
    positions = jnp.arange(slot_count, dtype=jnp.int32)
    live_keys = positions[None, :] < lengths[:, None]
    live_rows = live_keys.reshape(-1)
    rows_in = tokens.astype(jnp.float32)
    normed_one = layer_norm(rows_in, gain_one, shift_one).astype(jnp.bfloat16)
    bias_full = jnp.concatenate(
        [bias_project[:width], jnp.zeros((width,), jnp.float32), bias_project[width:]]
    )
    projected = (matmul(normed_one, full_project) + bias_full).astype(jnp.bfloat16)
    cell_index = 0
    query_blocks, keys_all, values_all = split_heads(projected, block_rows)
    key_live = live_keys[cell_index]
    mixed_blocks, log_blocks = lax.map(
        lambda query_block: attend_forward(query_block, keys_all, values_all, key_live),
        query_blocks,
    )
    mixed_list = mixed_blocks.reshape(slot_count, width)
    log_list = [log_blocks]
    mixed_low = mixed_list.astype(jnp.bfloat16)
    middle = rows_in + (matmul(mixed_low, full_output) + bias_output)
    normed_two = layer_norm(middle, gain_two, shift_two).astype(jnp.bfloat16)
    hidden = matmul(normed_two, full_expand) + bias_expand
    active = gelu_exact(hidden).astype(jnp.bfloat16)
    result = middle + (matmul(active, full_contract) + bias_contract)
    block_out = jnp.where(live_rows[:, None], result, 0.0).astype(jnp.bfloat16)
    again = fetch_backward(
        project_weight,
        output_weight,
        expand_weight,
        contract_weight,
        project_bias,
        output_bias,
        expand_bias,
        contract_bias,
        first_gain,
        first_shift,
        second_gain,
        second_shift,
    )
    back_project, back_output, back_expand, back_contract = (again[0], again[1], again[2], again[3])
    grad_out = jnp.where(live_rows[:, None], cotangent.astype(jnp.float32), 0.0)
    grad_out_low = grad_out.astype(jnp.bfloat16)
    grad_contract = over_rows(active, grad_out_low)
    grad_contract_bias = jnp.sum(grad_out, axis=0)
    grad_active = over_columns(grad_out_low, back_contract)
    gelu_value, gelu_pull = jax.vjp(gelu_exact, hidden)
    grad_hidden = gelu_pull(grad_active)[0].astype(jnp.bfloat16)
    grad_expand = over_rows(normed_two, grad_hidden)
    grad_expand_bias = jnp.sum(grad_hidden.astype(jnp.float32), axis=0)
    grad_normed_two = over_columns(grad_hidden, back_expand)
    norm_value, second_pull = jax.vjp(layer_norm, middle, gain_two, shift_two)
    grad_middle, grad_gain_two, grad_shift_two = second_pull(grad_normed_two)
    grad_middle = grad_middle + grad_out
    grad_branch = grad_middle.astype(jnp.bfloat16)
    grad_output = over_rows(mixed_low, grad_branch)
    grad_output_bias = jnp.sum(grad_branch.astype(jnp.float32), axis=0)
    grad_mixed = over_columns(grad_branch, back_output).astype(jnp.bfloat16)
    cell_index = 0
    query_blocks, keys_all, values_all = split_heads(projected, block_rows)
    key_live = live_keys[cell_index]
    grad_blocks = grad_mixed.reshape(slot_count // block_rows, block_rows, H, HD)

    def visit_block(carried, inputs):
        query_block, grad_block, log_block = inputs
        grad_query, grad_key, grad_value = attend_backward(
            query_block, grad_block, log_block, keys_all, values_all, key_live
        )
        return ((carried[0] + grad_key, carried[1] + grad_value), grad_query)

    initial = (
        jnp.zeros((slot_count, H, HD), jnp.float32),
        jnp.zeros((slot_count, H, HD), jnp.float32),
    )
    (key_sums, value_sums), query_grads = lax.scan(
        visit_block, initial, (query_blocks, grad_blocks, log_list[cell_index])
    )
    grad_cells = jnp.concatenate(
        [
            query_grads.reshape(slot_count, width),
            key_sums.reshape(slot_count, width),
            value_sums.reshape(slot_count, width),
        ],
        axis=1,
    )
    grad_projected = grad_cells.astype(jnp.bfloat16)
    grad_project = over_rows(normed_one, grad_projected)
    column_sums = jnp.sum(grad_projected.astype(jnp.float32), axis=0)
    grad_project_bias = jnp.concatenate([column_sums[:width], column_sums[2 * width :]])
    grad_normed_one = over_columns(grad_projected, back_project)
    first_value, first_pull = jax.vjp(layer_norm, rows_in, gain_one, shift_one)
    grad_rows_in, grad_gain_one, grad_shift_one = first_pull(grad_normed_one)
    tokens_grad = (grad_rows_in + grad_middle).astype(jnp.bfloat16)
    reduced = (
        lax.psum_scatter(grad_project, "dp", scatter_dimension=0, tiled=True),
        lax.psum_scatter(grad_output, "dp", scatter_dimension=0, tiled=True),
        lax.psum_scatter(grad_expand, "dp", scatter_dimension=0, tiled=True),
        lax.psum_scatter(grad_contract, "dp", scatter_dimension=0, tiled=True),
        lax.psum_scatter(grad_project_bias, "dp", scatter_dimension=0, tiled=True),
        lax.psum_scatter(grad_output_bias, "dp", scatter_dimension=0, tiled=True),
        lax.psum_scatter(grad_expand_bias, "dp", scatter_dimension=0, tiled=True),
        lax.psum_scatter(grad_contract_bias, "dp", scatter_dimension=0, tiled=True),
        lax.psum_scatter(grad_gain_one, "dp", scatter_dimension=0, tiled=True),
        lax.psum_scatter(grad_shift_one, "dp", scatter_dimension=0, tiled=True),
        lax.psum_scatter(grad_gain_two, "dp", scatter_dimension=0, tiled=True),
        lax.psum_scatter(grad_shift_two, "dp", scatter_dimension=0, tiled=True),
    )
    shard_project, shard_output, shard_expand, shard_contract = (
        lax.psum_scatter(
            reduced[0].astype(jnp.bfloat16), "fsdp", scatter_dimension=1, tiled=True
        ).astype(jnp.float32),
        lax.psum_scatter(
            reduced[1].astype(jnp.bfloat16), "fsdp", scatter_dimension=1, tiled=True
        ).astype(jnp.float32),
        lax.psum_scatter(
            reduced[2].astype(jnp.bfloat16), "fsdp", scatter_dimension=1, tiled=True
        ).astype(jnp.float32),
        lax.psum_scatter(
            reduced[3].astype(jnp.bfloat16), "fsdp", scatter_dimension=1, tiled=True
        ).astype(jnp.float32),
    )
    summed = lax.psum(
        (
            reduced[4],
            reduced[5],
            reduced[6],
            reduced[7],
            reduced[8],
            reduced[9],
            reduced[10],
            reduced[11],
        ),
        "fsdp",
    )
    return (
        block_out,
        tokens_grad,
        shard_project,
        summed[0],
        shard_output,
        summed[1],
        shard_expand,
        summed[2],
        shard_contract,
        summed[3],
        summed[4],
        summed[5],
        summed[6],
        summed[7],
    )


def scatter_events(link, place, col, pair_of, lc, lxh, lyh, lx, ly):
    p = place
    family = (p.dc, p.dx + p.dc - p.d, p.dy + p.dc - p.d, p.dd + p.dc - p.d)
    cs = [link.slot() for _ in range(4)]
    hx, hy, fx, fy = (link.slot() for _ in range(4))
    got = link.got

    def add(target, *terms):
        total = target[...].astype(F32)
        for term in terms:
            total = total + term[...].astype(F32)
        target[...] = total.astype(BF)

    def to_sibling(which):
        link.send(cs[which], col(family[which]), lc.at[which], "c", lambda: col(0))

    def halves():
        got(cs[3], lc.at[3])
        add(col(p.dd), lc.at[3])
        link.send(hx, pair_of(col(p.dd), 0), lxh, "x", lambda: lxh)
        link.send(hy, pair_of(col(p.dd), 1), lyh, "y", lambda: lyh)

    def near():
        got(cs[1], lc.at[1])
        got(cs[2], lc.at[2])
        add(col(p.dx), lc.at[1])
        add(col(p.dy), lc.at[2])

    def pass_y():
        got(hx, lxh)
        add(pair_of(col(p.dy), 0), lxh)
        link.send(fy, col(p.dy), ly, "y", lambda: ly)

    def pass_x():
        got(hy, lyh)
        add(pair_of(col(p.dx), 1), lyh)
        link.send(fx, col(p.dx), lx, "x", lambda: lx)

    def own():
        got(cs[0], lc.at[0])

    def total():
        got(fx, lx)
        got(fy, ly)
        add(col(p.d), lc.at[0], lx, ly)

    return to_sibling, [halves, near, pass_y, pass_x, own, total]


def z_sum(link, place, block, lz, finish):
    p = place
    zs = link.slot(4)

    def send():
        for step in (1, 3, 2):
            link.send(zs + step, block(p.zt(step)), lz.at[step], step, lambda: lz.at[0])

    def last():
        total = block(p.z)[...].astype(F32)
        for step in (1, 3, 2):
            link.got(zs + step, lz.at[step])
            total = total + lz[step].astype(F32)
        finish(total)

    return send, last


def gelu_pair(value):
    lift = 0.5 * (1.0 + lax.erf(value * 0.7071067811865476))
    bell = jnp.exp(value * value * -0.5) * 0.3989422804014327
    return value * lift, lift + value * bell


def second_kernel(length_ref, x_hbm, cot_hbm, mixed_hbm, wo_hbm, we_hbm, c_hbm, v_ref,
                  block_out, dmixed_out, dmiddle_out, ge_out, go_out, gc_out, vg_out,
                  x_ref, cot_ref, mixed_ref, wo_ref, we, wct, act, slope, middle, n2t, dot_t, mixed_t, dbranch, dout, gc, go, dmixed, bout, vg,
                  lc, lxh, lyh, lx, ly, send_sem, recv_sem, out_sem):
    p = Place()
    T, D = x_ref.shape
    FF = we.shape[1]
    R = D // 8
    Q = FF // 4
    C8 = FF // 8
    link = Link(p, send_sem, recv_sem)
    bc = lambda z, d: wct.at[pl.ds(mo(z * (D // 4), 16), D // 4), pl.ds(mo(d * C8, 128), C8)]
    gather = Gather(link, p, bc)

    to_sibling, scatter = scatter_events(
        link, p, lambda d: gc.at[d], lambda ref, h: ref.at[pl.ds(2 * h, 2)], lc, lxh, lyh, lx, ly)
    load = pltpu.make_async_copy(we_hbm, we, out_sem.at[0])
    columns = [pltpu.make_async_copy(c_hbm.at[z], bc(z, p.d), out_sem.at[19 + z]) for z in range(4)]
    for made in columns:
        made.start()
    halves = [pl.ds(i * (T // 2), T // 2) for i in range(2)]
    early = [[pltpu.make_async_copy(wo_hbm, wo_ref, out_sem.at[12])], []]
    for i, r in enumerate(halves):
        for at, (a, b) in enumerate(((mixed_hbm, mixed_ref), (x_hbm, x_ref), (cot_hbm, cot_ref))):
            early[i].append(pltpu.make_async_copy(a.at[r], b.at[r], out_sem.at[13 + 3 * i + at]))
    for made in early[0] + early[1]:
        made.start()
    load.start()
    enter(p)
    for made in columns:
        made.wait()
    run(*gather.x)()
    for made in early[0] + early[1]:
        made.wait()
    length = length_ref[0]
    LR = 256
    rows = lambda i: pl.ds(mo(i * LR, LR), LR)
    vec = lambda i: v_ref[i:i + 1, 0:D]
    vg[...] = jnp.zeros_like(vg)

    def at(i, spots):
        for where, event in spots:
            pl.when(i == where)(event)

    def norm(value):
        u = value - jnp.mean(value, axis=-1, keepdims=True)
        r = lax.rsqrt(jnp.mean(u * u, axis=-1, keepdims=True) + eps_norm)
        return u * r, r

    def middle_body(i, _):
        r = rows(i)
        value = x_ref[r, :].astype(F32) + (dot(mixed_ref[r, :], wo_ref[...]) + vec(2))
        middle[r, :] = value
        xhat, _ = norm(value)
        n2 = (xhat * vec(6) + vec(7)).astype(BF)
        dmixed[r, :] = n2
        n2t[:, r] = n2.T
        live = iota((LR, D), 0) + i * LR < length
        grad = jnp.where(live, cot_ref[r, :].astype(F32), 0.0)
        vg[7:8, :] += jnp.sum(grad, axis=0, keepdims=True)
        dout[r, :] = grad.astype(BF)
        dot_t[:, r] = grad.astype(BF).T
        mixed_t[:, r] = mixed_ref[r, :].T
        return 0

    lax.fori_loop(0, T // LR, middle_body, 0)
    load.wait()

    def hidden_body(i, _):
        at(i, [(0, gather.t[0]), (1, gather.t[1]), (2, gather.t[2]), (3, gather.t[3])])
        r = rows(i)
        left = dmixed[r, :]
        for j in range(4):
            cols = slice(j * Q, (j + 1) * Q)
            first, second = gelu_pair(dot(left, we[:, cols]) + v_ref[1:2, cols])
            act[r, cols] = first.astype(BF)
            slope[r, cols] = second.astype(BF)
        return 0

    lax.fori_loop(0, T // LR, hidden_body, 0)

    def column(d):
        value = dot(dot_t[...], act[:, pl.ds(mo(d * C8, 128), C8)])
        gc[d] = value.reshape(4, D // 4, C8).astype(BF)

    sib = p.dc - p.d
    column(p.dd + sib)
    to_sibling(3)
    column(p.dd)
    column(p.dx + sib)
    to_sibling(1)
    column(p.dy + sib)
    to_sibling(2)
    gather.q[0]()
    column(p.dx)
    column(p.dy)
    gather.q[1]()
    gather.q[2]()
    scatter[0]()
    column(p.d + sib)
    to_sibling(0)
    column(p.d)
    gather.q[3]()
    run(scatter[1], gather.close)()

    def back_body(i, _):
        at(i, [(1, run(scatter[2], scatter[3], scatter[4]))])
        r = rows(i)
        grad_low = dout[r, :]
        result = middle[r, :] + vec(3)
        for j in range(4):
            cols = slice(j * Q, (j + 1) * Q)
            dh = dot(grad_low, wct[:, cols]) * slope[r, cols].astype(F32)
            low = dh.astype(BF)
            slope[r, cols] = low
            vg[3 + j:4 + j, :] += jnp.sum(low.astype(F32), axis=0, keepdims=True)
        result = result + dot_nt(act[r, :], wct[...])
        dn = dot_nt(slope[r, :], we[...])
        live = iota((LR, D), 0) + i * LR < length
        bout[r, :] = jnp.where(live, result, 0.0).astype(BF)
        xhat, spread = norm(middle[r, :])
        vg[10:11, :] += jnp.sum(dn * xhat, axis=0, keepdims=True)
        vg[11:12, :] += jnp.sum(dn, axis=0, keepdims=True)
        gx = dn * vec(6)
        back = spread * (gx - jnp.mean(gx, axis=-1, keepdims=True)
                         - xhat * jnp.mean(gx * xhat, axis=-1, keepdims=True))
        total = dout[r, :].astype(F32) + back
        middle[r, :] = total
        branch = total.astype(BF)
        dbranch[r, :] = branch
        vg[2:3, :] += jnp.sum(branch.astype(F32), axis=0, keepdims=True)
        dmixed[r, :] = dot_nt(branch, wo_ref[...]).astype(BF)
        return 0

    lax.fori_loop(0, T // LR, back_body, 0)
    outs = []

    def out(source, target):
        made = pltpu.make_async_copy(source, target, out_sem.at[1 + len(outs)])
        made.start()
        outs.append(made)

    out(bout, block_out)
    out(dmixed, dmixed_out)
    out(middle, dmiddle_out)
    for z in range(4):
        cols = slice(3 * z // 2 * 128, 3 * z // 2 * 128 + 256)
        go[:, z] = dot(mixed_t[...], dbranch[:, cols]).reshape(8, R, 256).astype(BF)
    out(go, go_out)
    for z in range(4):
        act[0:D, z * Q:(z + 1) * Q] = dot(n2t[...], slope[:, z * Q:(z + 1) * Q]).astype(BF)
        out(act.at[0:D, z * Q:(z + 1) * Q], ge_out.at[:, z * Q:(z + 1) * Q])
        if z == 2:
            scatter[5]()
            out(gc.at[p.d], gc_out)
    vg_out[...] = vg[...]
    link.finish()
    for made in outs:
        made.wait()


ANY = pl.BlockSpec(memory_space=pl.ANY)
VM = pl.BlockSpec(memory_space=pltpu.VMEM)
SM = pl.BlockSpec(memory_space=pltpu.SMEM)
sds = jax.ShapeDtypeStruct


def second_call(length, x, cot, mixed, wo, we, wc, v):
    T, D = x.shape
    FF = we.shape[1]
    n = 36 + 8
    R, C8, Z = D // 8, FF // 8, D // 4
    vm = pltpu.VMEM
    return pl.pallas_call(
        second_kernel,
        in_specs=[SM] + [ANY] * 6 + [VM],
        out_specs=[ANY] * 6 + [VM],
        out_shape=[sds((T, D), BF), sds((T, D), BF), sds((T, D), F32), sds((D, FF), BF), sds((8, 4, R, 256), BF),
                   sds((4, Z, C8), BF), sds((16, D), F32)],
        scratch_shapes=[
            vm((T, D), BF), vm((T, D), BF), vm((T, D), BF), vm((D, D), BF), vm((D, FF), BF), vm((D, FF), BF), vm((T, FF), BF), vm((T, FF), BF), vm((T, D), F32),
            vm((D, T), BF), vm((D, T), BF), vm((D, T), BF), vm((T, D), BF), vm((T, D), BF),
            vm((8, 4, Z, C8), BF), vm((8, 4, R, 256), BF), vm((T, D), BF), vm((T, D), BF), vm((16, D), F32),
            vm((4, 4, Z, C8), BF), vm((2, Z, C8), BF), vm((2, Z, C8), BF), vm((4, Z, C8), BF), vm((4, Z, C8), BF),
            pltpu.SemaphoreType.DMA((n,)), pltpu.SemaphoreType.DMA((n,)), pltpu.SemaphoreType.DMA((23,)),
        ],
        compiler_params=pltpu.CompilerParams(
            collective_id=1, has_side_effects=True, vmem_limit_bytes=62 << 20),
        name="second_part",
    )(length, x, cot, mixed, wo, we, wc, v)


def third_kernel(length_ref, proj_hbm, qa_hbm, mixed_hbm, dm_hbm, n1_hbm, wp_hbm, x_hbm, dmiddle_hbm, ge_hbm, go_hbm,
                 gc_hbm, vg_ref, v_ref,
                 tokens_out, gp_out, go_out, ge_out, gc_out, vec_out,
                 proj, qa, mixed, dm, n1, n1t, wpp, x, dmiddle, ge, go, dproj, tg, gp,
                 ka, da, dq, va, kt, vs, vo, vl, vz,
                 lce, lxhe, lyhe, lxe, lye, lze, lco, lxho, lyho, lxo, lyo, lzo,
                 lcp, lxhp, lyhp, lxp, lyp, lzp, gpw, gcol, lzc,
                 send_sem, recv_sem, load_sem):
    p = Place()
    T, D = x.shape
    FF = ge.shape[1]
    R = D // 8
    Q = FF // 4
    pairs = H // 2
    KB = 256
    parts = 2
    link = Link(p, send_sem, recv_sem)
    loads = []

    def load(source, target):
        made = pltpu.make_async_copy(source, target, load_sem.at[len(loads)])
        made.start()
        loads.append(made)
        return made

    first_loads = [load(a, b) for a, b in ((proj_hbm, proj), (qa_hbm, qa), (mixed_hbm, mixed), (dm_hbm, dm))]
    ge_load, gc_load, go_load, n1_load = load(ge_hbm, ge), load(gc_hbm, gcol), load(go_hbm, go), load(n1_hbm, n1)
    late = [load(x_hbm, x), load(dmiddle_hbm, dmiddle)]
    for i in range(pairs):
        for s in range(3):
            late.append(load(wp_hbm.at[:, pl.ds((s * pairs + i) * 128, 128)],
                             wpp.at[:, pl.ds((i * 3 + s) * 128, 128)]))

    def finish_e(total):
        ge_out[...] = total

    def finish_o(total):
        go_out[...] = jnp.where(p.odd == 0, total[:, 0:192], total[:, 64:256])

    rows_of = lambda d: pl.ds(mo(d * R, 16), R)
    def finish_c(total):
        gc_out[...] = total

    e_col, o_col = (lambda d: ge.at[rows_of(d), :]), (lambda d: go.at[d])
    e_sib, ev_e = scatter_events(
        link, p, e_col, lambda ref, h: ref.at[:, pl.ds(h * (FF // 2), FF // 2)], lce, lxhe, lyhe, lxe, lye)
    o_sib, ev_o = scatter_events(
        link, p, o_col, lambda ref, h: ref.at[pl.ds(2 * h, 2)], lco, lxho, lyho, lxo, lyo)
    e_send, e_last = z_sum(link, p, lambda z: e_col(p.d).at[:, pl.ds(mo(z * Q, 128), Q)], lze, finish_e)
    o_send, o_last = z_sum(link, p, lambda z: o_col(p.d).at[z], lzo, finish_o)
    c_send, c_last = z_sum(link, p, lambda z: gcol.at[z], lzc, finish_c)
    ended = []
    combos = []
    for i in range(pairs):
        for s in range(3):
            tile = s * pairs + i
            for owner in range(4):
                left = 9 * owner // 2
                if left <= tile < left + 5:
                    combos.append((i, s, owner, tile - left))
    assert len(combos) == 20
    z_slots = [[link.slot() for _ in range(3)] for _ in combos]

    def pair_scatter(i):
        column = lambda d: gp.at[i, d]
        sib, events = scatter_events(
            link, p, column, lambda ref, h: ref.at[pl.ds(h * (R // 2), R // 2)],
            lcp.at[i], lxhp.at[i], lyhp.at[i], lxp.at[i], lyp.at[i])
        mine = [(at, c) for at, c in enumerate(combos) if c[0] == i]

        def along(add_own):
            def run():
                add_own()
                for at, (_, s, owner, _) in mine:
                    @pl.when(p.z != owner)
                    def _():
                        step = lax.rem(owner - p.z + 4, 4)
                        part = column(p.d).at[:, pl.ds(s * 128, 128)]
                        link.copy(z_slots[at][0] + step - 1, part, lzp.at[at, step - 1], ("z", owner)).start()
            return run

        def last():
            for at, (_, s, owner, place) in mine:
                @pl.when(p.z == owner)
                def _():
                    total = gp[i, p.d, :, s * 128:(s + 1) * 128].astype(F32)
                    for step in range(1, 4):
                        link.got(z_slots[at][step - 1], lzp.at[at, step - 1])
                        total = total + lzp[at, step - 1].astype(F32)
                    gpw[:, place * 128:(place + 1) * 128] = total

        def ending():
            for at, (_, s, owner, _) in mine:
                @pl.when(p.z != owner)
                def _():
                    step = lax.rem(owner - p.z + 4, 4)
                    view = lzp.at[at, 0]
                    link.copy(z_slots[at][0] + step - 1, view, view, "x").wait_send()

        ended.append(ending)

        def start():
            for k in (3, 1, 2, 0):
                sib(k)

        return [start] + events[:5] + [along(events[5]), last]

    ev_p = [pair_scatter(i) for i in range(pairs)]

    enter(p, wide=True)
    for made in first_loads:
        made.wait()
    length = length_ref[0]

    def start_e():
        ge_load.wait()
        for k in (3, 1, 2, 0):
            e_sib(k)

    def start_o():
        go_load.wait()
        for k in (3, 1, 2, 0):
            o_sib(k)

    def turn_n1():
        n1_load.wait()
        for i in range(T // 256):
            n1t[:, i * 256:(i + 1) * 256] = n1[i * 256:(i + 1) * 256, :].T

    def start_c():
        gc_load.wait()
        c_send()

    e, o = ev_e, ev_o
    q = ev_p
    timeline = [
        (0, start_c), (0, start_e), (0, start_o), (0, turn_n1), (1, e[0]), (2, e[1]), (2, e[4]), (2, o[0]), (2, o[1]), (2, o[4]),
        (2, q[0][0]), (3, q[0][1]), (3, q[0][2]), (3, q[0][5]), (4, e[2]), (4, e[3]), (4, c_last), (4, o[2]), (4, o[3]),
        (4, q[0][3]), (4, q[0][4]), (4, q[1][0]), (5, q[1][1]), (5, q[1][2]), (5, q[1][5]), (6, q[2][0]),
        (7, q[2][1]), (7, q[2][2]), (7, q[2][5]), (8, e[5]), (8, e_send), (8, q[3][0]), (9, o[5]), (9, o_send),
        (9, q[3][1]), (9, q[3][2]), (9, q[3][5]), (10, q[0][6]), (10, q[1][3]), (10, q[1][4]), (10, q[2][3]), (10, q[2][4]),
        (10, q[3][3]), (10, q[3][4]), (10, q[4][0]), (11, q[4][1]), (11, q[4][2]), (11, q[4][5])]
    timeline.sort(key=lambda e: e[0])

    def body(step, _):
        for at, event in timeline:
            if at < pairs * parts:
                pl.when(step == at)(event)
        pair = lax.div(step, parts)
        part = lax.rem(step, parts)
        ps = lambda off: pl.ds(mo(off + pair * 128, 128), 128)
        own = lambda s: pl.ds(mo(pair * 384 + s * 128, 128), 128)

        @pl.when(part == 0)
        def _():
            lane, row = iota((T, 128), 1), iota((T, 128), 0)
            k = proj[:, ps(D)].astype(F32)
            v = proj[:, ps(2 * D)].astype(F32)
            do = dm[:, ps(0)].astype(F32)
            pr = do * mixed[:, ps(0)].astype(F32)
            dead = jnp.where(row < length, 0.0, neg_fill)
            for head in range(2):
                keep = (lane < 64) if head == 0 else (lane >= 64)
                delta = jnp.sum(jnp.where(keep, pr, 0.0), axis=-1, keepdims=True)
                one, two, three = split3(-delta)
                da[head] = extend(head, do, lane, one, two, three, 0.0)
                ka[head] = extend(head, k, lane, 1.0, 1.0, 1.0, dead)
                va[head] = extend(head, v, lane, 1.0, 1.0, 1.0, 0.0)
                kt[head] = jnp.where(keep, k, 0.0).astype(BF).T
            dq[...] = jnp.zeros_like(dq)

        lk = iota((KB, 128), 1)
        spans = [pl.ds(mo(part * (T // parts) + i * KB, KB), KB) for i in range(T // parts // KB)]
        items = [(head, r) for r in spans for head in range(2)]
        kept = {}

        def products(n):
            head, r = items[n]
            return dot_nt(ka[head, r, :], qa[pair * 2 + head]), dot_nt(va[head, r, :], da[head])

        def weigh(scores, grads):
            weights = jnp.exp(scores)
            return weights.astype(BF), (weights * grads).astype(BF)

        def finish(n, low, ds):
            head, r = items[n]
            kept[n] = dot(ds, qa[pair * 2 + head]), dot(low, da[head])
            dq[head] += dot(kt[head, :, r], ds)
            if head == 1:
                dproj[r, own(1)] = jnp.where(lk < 64, kept[n - 1][0], kept[n][0]).astype(BF)
                dproj[r, own(2)] = jnp.where(lk < 64, kept[n - 1][1], kept[n][1]).astype(BF)

        value, waiting = products(0), None
        for n in range(len(items)):
            following = products(n + 1) if n + 1 < len(items) else None
            done = weigh(*value)
            if waiting is not None:
                finish(n - 1, *waiting)
            value, waiting = following, done
        finish(len(items) - 1, *waiting)

        @pl.when(part == parts - 1)
        def _():
            dproj[:, own(0)] = ((dq[0] + dq[1]) * (HD ** -0.5)).T.astype(BF)
            value = dot(n1t[...], dproj[:, pl.ds(mo(pair * 384, 128), 384)])
            gp[pair] = value.reshape(8, R, 384).astype(BF)

        return 0

    lax.fori_loop(0, pairs * parts, body, 0)
    ev_p[pairs - 1][0]()
    for made in late:
        made.wait()
    vs[...] = vg_ref[...]
    LR = 256

    def norm_body(i, _):
        def spot(where, events):
            @pl.when(i == where)
            def _():
                for event in events:
                    event()

        spot(0, [e_last, q[1][6], q[2][6], q[3][6], q[4][3], q[4][4]])
        spot(1, q[5][1:3] + q[5][5:6])
        spot(2, [o_last, q[0][7], q[1][7], q[4][6], q[2][7]])
        spot(3, q[5][3:5] + q[3][7:8])
        r = pl.ds(mo(i * LR, LR), LR)
        left = dproj[r, :]
        dn = dot_nt(left, wpp[...])
        sums = jnp.sum(left.astype(F32), axis=0, keepdims=True)
        for j in range(pairs):
            vs[0:1, j * 128:(j + 1) * 128] += sums[:, j * 384:j * 384 + 128]
            vs[1:2, j * 128:(j + 1) * 128] += sums[:, j * 384 + 256:j * 384 + 384]
        value = x[r, :].astype(F32)
        u = value - jnp.mean(value, axis=-1, keepdims=True)
        spread = lax.rsqrt(jnp.mean(u * u, axis=-1, keepdims=True) + eps_norm)
        xhat = u * spread
        vs[8:9, :] += jnp.sum(dn * xhat, axis=0, keepdims=True)
        vs[9:10, :] += jnp.sum(dn, axis=0, keepdims=True)
        gx = dn * v_ref[4:5, 0:D]
        back = spread * (gx - jnp.mean(gx, axis=-1, keepdims=True)
                         - xhat * jnp.mean(gx * xhat, axis=-1, keepdims=True))
        tg[r, :] = (back + dmiddle[r, :]).astype(BF)
        return 0

    lax.fori_loop(0, T // LR, norm_body, 0)
    out = load(tg, tokens_out)
    v_slots = link.slot(16)
    for d in range(8):
        line = lambda row, at, n: jnp.concatenate(
            [vs[row:row + 1, at:at + n], jnp.zeros((1, 384 - n), F32)], axis=1) if n < 384 else vs[row:row + 1, at:at + n]
        vo[d] = jnp.concatenate(
            [line(d // 4, d % 4 * 2 * R, 2 * R), line(2, d * R, R), line(3 + d // 2, d % 2 * 4 * R, 4 * R)]
            + [line(row, d * R, R) for row in (7, 8, 9, 10, 11)], axis=0)
    for d in range(8):
        @pl.when(p.d != d)
        def _():
            link.copy(v_slots + d, vo.at[d], vl.at[p.d], ("d", d), land=v_slots + p.d).start()
    for event in (q[4][7], q[5][6]):
        event()
    vl[p.d] = vo[p.d]
    for d in range(8):
        @pl.when(p.d != d)
        def _():
            link.got(v_slots + d, vl.at[d])
    own = vl[0]
    for d in range(1, 8):
        own = own + vl[d]
    vz[p.z] = own
    for k in (1, 2, 3):
        link.send(v_slots + 8 + k, vz.at[p.z], vz.at[p.z], ("z", p.order[k]), lambda: vz.at[0], land=v_slots + 12 + p.z)
    q[5][7]()
    gp_out[...] = jnp.where(p.odd == 0, gpw[:, 0:576], gpw[:, 64:640])
    for k in (1, 2, 3):
        link.got(v_slots + 12 + p.order[k], vz.at[p.order[k]])
    vec_out[...] = vz[0] + vz[1] + vz[2] + vz[3]
    for d in range(8):
        @pl.when(p.d != d)
        def _():
            link.copy(v_slots + d, vo.at[d], vo.at[d], "x").wait_send()
    link.finish()
    for ending in ended:
        ending()
    out.wait()


def third_call(length, proj, qa, mixed, dm, n1, wp, x, dmiddle, ge, go, gc, vg, v):
    T, D = x.shape
    FF = ge.shape[1]
    R, Q, pairs = D // 8, FF // 4, H // 2
    vm = pltpu.VMEM
    n = 8 * 8 + 12 + 60 + 16
    return pl.pallas_call(
        third_kernel,
        in_specs=[SM] + [ANY] * 11 + [VM] * 2,
        out_specs=[ANY] + [VM] * 5,
        out_shape=[sds((T, D), BF), sds((R, 3 * D // 4), F32), sds((R, D // 4), F32), sds((R, Q), F32), sds((D // 4, FF // 8), F32),
                   sds((8, 384), F32)],
        scratch_shapes=[
            vm((T, 3 * D), BF), vm((H, T, 128), BF), vm((T, D), BF), vm((T, D), BF), vm((T, D), BF), vm((D, T), BF),
            vm((D, 3 * D), BF), vm((T, D), BF), vm((T, D), F32), vm((D, FF), BF), vm((8, 4, R, 256), BF),
            vm((T, 3 * D), BF), vm((T, D), BF), vm((pairs, 8, R, 384), BF),
            vm((2, T, 128), BF), vm((2, T, 128), BF), vm((2, 128, T), F32), vm((2, T, 128), BF), vm((2, 128, T), BF),
            vm((16, D), F32), vm((8, 8, 384), F32), vm((8, 8, 384), F32), vm((4, 8, 384), F32),
            vm((4, R, FF), BF), vm((R, FF // 2), BF), vm((R, FF // 2), BF), vm((R, FF), BF), vm((R, FF), BF), vm((4, R, Q), BF),
            vm((4, 4, R, 256), BF), vm((2, R, 256), BF), vm((2, R, 256), BF), vm((4, R, 256), BF), vm((4, R, 256), BF),
            vm((4, R, 256), BF),
            vm((pairs, 4, R, 384), BF), vm((pairs, R // 2, 384), BF), vm((pairs, R // 2, 384), BF),
            vm((pairs, R, 384), BF), vm((pairs, R, 384), BF), vm((20, 3, R, 128), BF), vm((R, 640), F32),
            vm((4, D // 4, FF // 8), BF), vm((4, D // 4, FF // 8), BF),
            pltpu.SemaphoreType.DMA((n,)), pltpu.SemaphoreType.DMA((n,)), pltpu.SemaphoreType.DMA((29,)),
        ],
        compiler_params=pltpu.CompilerParams(
            collective_id=2, has_side_effects=True, vmem_limit_bytes=63 << 20),
        name="third_part",
    )(length, proj, qa, mixed, dm, n1, wp, x, dmiddle, ge, go, gc, vg, v)


def last_kernel(block_in, tokens_in, p_in, o_in, e_in, c_in, vec_in,
                block_out, tokens_out, p_out, o_out, e_out, c_out, *rest):
    vectors, held, vec, sem = rest[:8], rest[8:14], rest[14], rest[15]
    parts = 2
    rows = block_in.shape[0] // parts
    whole = lambda ref: ref
    legs = []
    for i in range(parts):
        part = lambda ref, i=i: ref.at[pl.ds(i * rows, rows)]
        legs += [(part, block_in, held[0], block_out), (part, tokens_in, held[1], tokens_out)]
    legs += [(whole, a, b, c) for a, b, c in zip((p_in, o_in, e_in, c_in), held[2:], (p_out, o_out, e_out, c_out))]
    first = pltpu.make_async_copy(vec_in, vec, sem.at[2 * len(legs)])
    first.start()
    ins = [pltpu.make_async_copy(part(a), part(b), sem.at[k]) for k, (part, a, b, _) in enumerate(legs)]
    outs = [pltpu.make_async_copy(part(b), part(c), sem.at[len(legs) + k]) for k, (part, _, b, c) in enumerate(legs)]
    for made in ins:
        made.start()
    for came, goes in zip(ins, outs):
        came.wait()
        goes.start()
    first.wait()
    for at, target in enumerate(vectors):
        n = target.shape[0]
        target[...] = vec[at:at + 1, 0:n].reshape(n)
    for goes in outs:
        goes.wait()


def last_call(sizes, *arrays):
    return pl.pallas_call(
        last_kernel,
        in_specs=[ANY] * 7,
        out_specs=[ANY] * 6 + [VM] * 8,
        out_shape=[sds(item.shape, item.dtype) for item in arrays[:6]] + [sds((n,), F32) for n in sizes],
        scratch_shapes=[pltpu.VMEM(item.shape, item.dtype) for item in arrays] + [pltpu.SemaphoreType.DMA((17,))],
        compiler_params=pltpu.CompilerParams(vmem_limit_bytes=63 << 20),
        name="last_part",
    )(*arrays)


def per_device_fast(tokens, lengths, cotangent, project_weight, project_bias, output_weight, output_bias,
                    expand_weight, expand_bias, contract_weight, contract_bias, first_gain, first_shift,
                    second_gain, second_shift):
    vectors = (project_bias, output_bias, expand_bias, contract_bias, first_gain, first_shift, second_gain, second_shift)
    normed_one, projected, mixed, qa, full_project, full_output, full_expand, cc, v = first_call(
        lengths, tokens, project_weight, output_weight, expand_weight, contract_weight.T, vectors)
    block_out, grad_mixed, grad_middle, ge, go, gc, vg = second_call(
        lengths, tokens, cotangent, mixed, full_output, full_expand, cc, v)
    third = third_call(
        lengths, projected, qa, mixed, grad_mixed, normed_one, full_project, tokens, grad_middle, ge, go, gc, vg, v)
    out = last_call([item.shape[0] for item in vectors], block_out, *third)
    return (out[0], out[1], out[2], out[6], out[3], out[7], out[4], out[8], out[5].T, *out[9:])


def solution(mesh):
    both, rows, grid = P(("dp", "fsdp"), None), P("dp"), P("dp", "fsdp")
    weights = (grid, rows, grid, rows, grid, rows, grid, rows)
    fast = mesh.shape["dp"] == 8 and mesh.shape["fsdp"] == 4
    return jax.shard_map(
        per_device_fast if fast else per_device,
        mesh=mesh,
        in_specs=(both, P(("dp", "fsdp")), both) + weights + (rows,) * 4,
        out_specs=(both, both) + weights + (rows,) * 4,
        check_vma=False,
    )
```

```python
import functools
import jax
import jax.numpy as jnp
from jax import lax
from jax.experimental import pallas as pl
from jax.experimental.pallas import tpu as pltpu
from jax.sharding import PartitionSpec as P

H = 12
HD = 64
F32 = jnp.float32
BF = jnp.bfloat16
MESH = pl.DeviceIdType.MESH
eps_norm = 1e-05
neg_fill = -1000000000.0


def dot(first, second):
    return jnp.dot(first, second, preferred_element_type=F32)


def dot_nt(first, second):
    return lax.dot_general(first, second, (((1,), (1,)), ((), ())), preferred_element_type=F32)


def dot_tn(first, second):
    return lax.dot_general(first, second, (((0,), (0,)), ((), ())), preferred_element_type=F32)


def mo(value, multiple):
    return pl.multiple_of(value, multiple)


class Place:
    def __init__(self):
        self.d = lax.axis_index("dp")
        self.z = lax.axis_index("fsdp")
        core = lax.rem(self.d, 2)
        across = lax.rem(lax.div(self.d, 2), 2)
        up = lax.div(self.d, 4)
        self.dc = self.d + 1 - 2 * core
        self.dx = self.d + 2 - 4 * across
        self.dy = self.d + 4 - 8 * up
        self.dd = self.dx + 4 - 8 * up
        self.odd = lax.rem(self.z, 2)
        z = self.z
        pick = lambda a, b, c, d: jnp.where(z < 2, jnp.where(z == 0, a, b), jnp.where(z == 2, c, d))
        self.order = [z, pick(1, 0, 3, 2), pick(2, 2, 1, 1), pick(3, 3, 0, 0)]

    def zt(self, step):
        return lax.rem(self.z + step, 4)

    def zf(self, step):
        return lax.rem(self.z + 4 - step, 4)

    def id(self, to):
        if to == "x":
            return (self.dx, self.z)
        if to == "y":
            return (self.dy, self.z)
        if to == "c":
            return (self.dc, self.z)
        if isinstance(to, tuple):
            return (to[1], self.z) if to[0] == "d" else (self.d, to[1])
        return (self.d, self.zt(to))


def enter(place, wide=False):
    barrier = pltpu.get_barrier_semaphore()
    sib = place.dc - place.d
    others = [("d", d + sib) for d in (place.dx, place.dy, place.dd)] + [("d", place.dd)] if wide else []
    partners = ["x", "y", "c", 1, 2, 3] + others
    for to in partners:
        pl.semaphore_signal(barrier, inc=1, device_id=place.id(to), device_id_type=MESH)
    pl.semaphore_wait(barrier, len(partners))


class Link:
    def __init__(self, place, send_sem, recv_sem):
        self.place, self.send_sem, self.recv_sem = place, send_sem, recv_sem
        self.count = 0
        self.copies = []

    def slot(self, many=1):
        self.count += many
        return self.count - many

    def copy(self, slot, source, target, to, land=None):
        return pltpu.make_async_remote_copy(
            src_ref=source, dst_ref=target, send_sem=self.send_sem.at[slot],
            recv_sem=self.recv_sem.at[slot if land is None else land], device_id=self.place.id(to),
            device_id_type=MESH)

    def send(self, slot, source, target, to, like, land=None, when=None):
        def start():
            self.copy(slot, source, target, to, land).start()

        if when is None:
            start()
        else:
            pl.when(when())(start)
        self.copies.append((slot, like, when))

    def got(self, slot, target):
        self.copy(slot, target, target, "x").wait_recv()

    def finish(self):
        for slot, like, when in self.copies:
            def done(slot=slot, like=like):
                view = like()
                self.copy(slot, view, view, "x").wait_send()

            if when is None:
                done()
            else:
                pl.when(when())(done)


class Gather:
    def __init__(self, link, place, block):
        p = place
        zr, zs = link.slot(4), link.slot(4)
        xs, ys, fx = link.slot(4), link.slot(4), link.slot(4)
        cs = link.slot(16)
        got = link.got
        send = functools.partial(link.send, like=lambda: block(0, 0))

        def z_step(a):
            def run():
                if a == 0:
                    own = block(p.z, p.d)
                    for k in (1, 2, 3):
                        send(zs + k, own, own, ("z", p.order[k]), land=zr + p.z)
                else:
                    got(zr + p.order[a], block(p.order[a], p.d))
            return run

        def x_step(a):
            def run():
                here = block(p.order[a], p.d)
                send(xs + a, here, here, "x")
                send(ys + a, here, here, "y")
                send(cs + a, here, here, "c")
            return run

        def turn(a):
            def run():
                b = p.order[a]
                bx, by = block(b, p.dx), block(b, p.dy)
                got(xs + a, bx)
                got(ys + a, by)
                if a in (0, 1):
                    send(fx + a, bx, bx, "y")
                else:
                    send(fx + a, by, by, "x")
                send(cs + 4 + a, bx, bx, "c")
                send(cs + 8 + a, by, by, "c")
            return run

        def corner(a):
            def run():
                bd = block(p.order[a], p.dd)
                got(fx + a, bd)
                send(cs + 12 + a, bd, bd, "c")
            return run

        def close():
            sib = p.dc - p.d
            for which, d in enumerate((p.d, p.dx, p.dy, p.dd)):
                for a in range(4):
                    got(cs + 4 * which + a, block(p.order[a], d + sib))

        self.z, self.x, self.t, self.q = ([make(a) for a in range(4)] for make in (z_step, x_step, turn, corner))
        self.close = close


def spread_z(link, place, ref):
    p = place
    zs, zr = link.slot(3), link.slot(4)

    def send():
        for k in (1, 2, 3):
            link.send(zs + k - 1, ref.at[p.z], ref.at[p.z], ("z", p.order[k]), lambda: ref.at[0], land=zr + p.z)

    def wait():
        for k in (1, 2, 3):
            b = p.order[k]
            link.got(zr + b, ref.at[b])

    return send, wait


def run(*events):
    def together():
        for event in events:
            event()
    return together


def window(value, odd, wide):
    rows, k = value.shape
    fill = jnp.zeros((rows, wide - k), F32)
    value = value.astype(F32)
    left = jnp.concatenate([value, fill], axis=1)
    right = jnp.concatenate([fill, value], axis=1)
    return jnp.where(odd == 0, left, right).astype(BF)


def merge_windows(blocks, full, tiles, rows_step):
    rows = full.shape[0]
    half = tiles // 2

    def body(i, _):
        r = pl.ds(mo(i * rows_step, rows_step), rows_step)
        for pair in range(2):
            even, odd = blocks.at[2 * pair], blocks.at[2 * pair + 1]
            base = pair * tiles * 128
            full[r, base:base + half * 128] = even[r, 0:half * 128]
            full[r, base + half * 128:base + (half + 1) * 128] = (
                even[r, half * 128:(half + 1) * 128] + odd[r, 0:128])
            full[r, base + (half + 1) * 128:base + tiles * 128] = odd[r, 128:(half + 1) * 128]
        return 0

    lax.fori_loop(0, rows // rows_step, body, 0)


def split3(value):
    high = value.astype(BF)
    rest = value - high.astype(F32)
    mid = rest.astype(BF)
    low = (rest - mid.astype(F32)).astype(BF)
    return high.astype(F32), mid.astype(F32), low.astype(F32)


def extend(head, pair, lane, one, two, three, four):
    base = 64 * (1 - head)
    extra = jnp.where(lane == base, one, jnp.where(lane == base + 1, two, jnp.where(
        lane == base + 2, three, jnp.where(lane == base + 3, four, 0.0))))
    keep = (lane < 64) if head == 0 else (lane >= 64)
    return jnp.where(keep, pair, extra).astype(BF)


def iota(shape, axis):
    return lax.broadcasted_iota(jnp.int32, shape, axis)


QB = 256


def first_kernel(length_ref, x_ref, wp_ref, wo_ref, we_ref, wc_ref, *refs):
    vec_refs, refs = refs[:8], refs[8:]
    first_body(length_ref, x_ref, wp_ref, wo_ref, we_ref, wc_ref, vec_refs, *refs)


def first_body(length_ref, x_ref, wp_ref, wo_ref, we_ref, wc_ref, vec_refs,
                 n1_out, proj_out, mixed_out, qa_out, wp_out, wo_out, we_out, c_out, v_out,
                 wp_blk, wo_blk, we, wp, wo, vb, n1, proj, mixed, qa, ka, va, vrow, cc,
                 send_sem, recv_sem, out_sem, pair_sem):
    p = Place()
    T, D = x_ref.shape
    R = wp_ref.shape[0]
    FF = we.shape[1]
    link = Link(p, send_sem, recv_sem)
    rows_of = lambda d: pl.ds(mo(d * R, 16), R)
    half = R // 2
    bpa = lambda z, d: wp_blk.at[z, pl.ds(mo(d * R, 16), half), :]
    bpb = lambda z, d: wp_blk.at[z, pl.ds(mo(d * R + half, 16), half), :]
    bo = lambda z, d: wo_blk.at[z, rows_of(d), :]
    be = lambda z, d: we.at[rows_of(d), pl.ds(mo(z * (FF // 4), 128), FF // 4)]
    g0, g1, go, ge = (Gather(link, p, b) for b in (bpa, bpb, bo, be))
    c_send, c_wait = spread_z(link, p, cc)
    vs = [link.slot() for _ in range(7)]

    wp_blk[p.z, rows_of(p.d), :] = window(wp_ref[...], p.odd, wp_blk.shape[2])
    wo_blk[p.z, rows_of(p.d), :] = window(wo_ref[...], p.odd, wo_blk.shape[2])
    we[rows_of(p.d), pl.ds(mo(p.z * (FF // 4), 128), FF // 4)] = we_ref[...]
    cc[p.z] = wc_ref[...]
    for i, ref in enumerate(vec_refs):
        vb[p.d, i:i + 1, 0:ref.shape[0]] = ref[...].astype(F32).reshape(1, ref.shape[0]).astype(BF)

    outs = []

    def out(source, target):
        made = pltpu.make_async_copy(source, target, out_sem.at[len(outs)])
        made.start()
        outs.append(made)

    enter(p)
    send_v = lambda slot, d, to: link.send(vs[slot], vb.at[d], vb.at[d], to, lambda: vb.at[0])
    for slot, to in ((0, "x"), (1, "y"), (3, "c")):
        send_v(slot, p.d, to)
    run(g0.z[0], g0.x[0], g1.z[0], g1.x[0])()
    link.got(vs[0], vb.at[p.dx])
    link.got(vs[1], vb.at[p.dy])
    send_v(2, p.dx, "y")
    send_v(4, p.dx, "c")
    send_v(5, p.dy, "c")
    run(g0.z[1], g0.x[1], g0.t[0], g1.t[0], g0.z[2], g0.x[2])()
    link.got(vs[2], vb.at[p.dd])
    send_v(6, p.dd, "c")
    sib = p.dc - p.d
    for slot, d in ((3, p.d), (4, p.dx), (5, p.dy), (6, p.dd)):
        link.got(vs[slot], vb.at[d + sib])
    got = vb[...].astype(F32)
    side = lambda row, wide: jnp.concatenate([got[i, row:row + 1, 0:wide] for i in range(8)], axis=1)
    bias = side(0, 2 * R)
    vrow[0:1, 0:D] = bias[:, 0:D]
    vrow[0:1, D:2 * D] = jnp.zeros((1, D), F32)
    vrow[0:1, 2 * D:3 * D] = bias[:, D:]
    vrow[1:2, :] = side(2, FF // 8)
    for row, at in ((2, 1), (3, 3), (4, 4), (5, 5), (6, 6), (7, 7)):
        vrow[row:row + 1, 0:D] = side(at, R)
    out(vrow, v_out)
    run(g0.t[1], g0.z[3], g0.x[3], g0.q[0], g1.z[1], g1.x[1], g1.q[0])()

    LR = 128
    gain, shift = vrow[4:5, 0:D], vrow[5:6, 0:D]

    def norm_body(i, _):
        r = pl.ds(mo(i * LR, LR), LR)
        value = x_ref[r, :].astype(F32)
        u = value - jnp.mean(value, axis=-1, keepdims=True)
        spread = jnp.mean(u * u, axis=-1, keepdims=True)
        n1[r, :] = (u * lax.rsqrt(spread + eps_norm) * gain + shift).astype(BF)
        return 0

    norm_part = lambda k: lax.fori_loop(k * (T // LR // 4), (k + 1) * (T // LR // 4), norm_body, 0)
    g0.t[2]()
    norm_part(0)
    run(g1.z[2], g1.x[2], g0.q[1])()
    norm_part(1)
    run(g1.z[3], g1.x[3], ge.z[0], go.z[0], g0.t[3])()
    norm_part(2)
    run(g0.q[2], g1.t[1])()
    norm_part(3)
    run(g1.t[2], g1.t[3], ge.x[0], g0.q[3], g1.q[1], g1.q[2], g1.q[3], go.x[0])()
    out(n1, n1_out)
    run(g0.close, g1.close)()
    merge_windows(wp_blk, wp, 9, 96)
    out(wp, wp_out)
    run(ge.z[1], ge.x[1])()

    def project_body(i, _):
        for at, event in ((2, run(ge.z[2], ge.x[2], ge.t[0])), (3, go.t[0])):
            pl.when(i == at)(event)
        r = pl.ds(mo(i * 256, 256), 256)
        left = n1[r, :]
        for j in range(3):
            cols = slice(j * D, (j + 1) * D)
            value = dot(left, wp[:, cols]) + vrow[0:1, cols]
            proj[r, cols] = value.astype(BF)
        return 0

    lax.fori_loop(0, T // 256, project_body, 0)
    out(proj, proj_out)

    length = length_ref[0]
    subs = T // QB

    def pair_outs(pair):
        heads = pl.ds(2 * pair, 2)
        cols = pl.ds(mo(pair * 128, 128), 128)
        return (pltpu.make_async_copy(qa.at[heads], qa_out.at[heads], pair_sem.at[pair, 0]),
                pltpu.make_async_copy(mixed.at[:, cols], mixed_out.at[:, cols], pair_sem.at[pair, 1]))

    def attend_steps(events):
        def body(pair, _):
            for at, event in events:
                pl.when(pair == at)(event)
            cols = lambda off: pl.ds(mo(off + pair * 128, 128), 128)
            lane, row = iota((T, 128), 1), iota((T, 128), 0)
            q = proj[:, cols(0)].astype(F32) * (HD ** -0.5)
            k = proj[:, cols(D)].astype(F32)
            v = proj[:, cols(2 * D)].astype(F32)
            dead = jnp.where(row < length, 0.0, neg_fill)
            for head in range(2):
                ka[head] = extend(head, k, lane, 1.0, 1.0, 1.0, dead)
                qa[pair * 2 + head] = extend(head, q, lane, 0.0, 0.0, 0.0, 1.0)
                keep = (lane < 64) if head == 0 else (lane >= 64)
                va[head] = jnp.where(keep, v, 1.0).astype(BF)
            sub_lane = iota((QB, 128), 1)
            items = [(head, pl.ds(i * QB, QB)) for i in range(subs) for head in range(2)]
            halves = {}

            def scores(n):
                head, r = items[n]
                return dot_nt(qa[pair * 2 + head, r, :], ka[head])

            def soften(value):
                top = jnp.max(value, axis=-1, keepdims=True)
                return top, jnp.exp(value - top).astype(BF)

            def finish(n, top, powers):
                head, r = items[n]
                value = dot(powers, va[head])
                total = value[:, 64:65] if head == 0 else value[:, 0:1]
                one, two, three = split3(-(top + jnp.log(total)))
                query = qa[pair * 2 + head, r, :].astype(F32)
                qa[pair * 2 + head, r, :] = extend(head, query, sub_lane, one, two, three, 1.0)
                halves[n] = value * (1.0 / total)
                if head == 1:
                    mixed[r, cols(0)] = jnp.where(sub_lane < 64, halves[n - 1], halves[n]).astype(BF)

            value, waiting = scores(0), None
            for n in range(len(items)):
                following = scores(n + 1) if n + 1 < len(items) else None
                soft = soften(value)
                if waiting is not None:
                    finish(n - 1, *waiting)
                value, waiting = following, soft
            finish(len(items) - 1, *waiting)
            for made in pair_outs(pair):
                made.start()
            return 0

        lax.fori_loop(0, H // 2, body, 0)

    attend_steps([(1, run(go.z[1], go.x[1], ge.z[3], ge.x[3], go.z[2], go.x[2], ge.t[1])),
                  (2, run(go.z[3], go.x[3], ge.t[2], c_send)), (3, run(ge.q[0], go.t[1], go.q[0])),
                  (4, run(ge.t[3], go.t[2])), (5, run(ge.q[1], ge.q[2], go.t[3]))])
    run(ge.q[3], go.q[1], go.q[2], go.q[3], go.close)()
    merge_windows(wo_blk, wo, 3, 96)
    out(wo, wo_out)
    ge.close()
    out(we, we_out)
    c_wait()
    out(cc, c_out)
    link.finish()
    for made in outs:
        made.wait()
    for pair in range(H // 2):
        for made in pair_outs(pair):
            made.wait()


def first_call(length, x, wp, wo, we, wc, vectors):
    T, D = x.shape
    FF = we.shape[1] * 4
    ANY = pl.BlockSpec(memory_space=pl.ANY)
    V = pl.BlockSpec(memory_space=pltpu.VMEM)
    S = pl.BlockSpec(memory_space=pltpu.SMEM)
    sds = jax.ShapeDtypeStruct
    n = 4 * 36 + 7 + 7
    return pl.pallas_call(
        first_kernel,
        in_specs=[S] + [V] * 13,
        out_specs=[ANY] * 9,
        out_shape=[sds((T, D), BF), sds((T, 3 * D), BF), sds((T, D), BF), sds((H, T, 128), BF),
                   sds((D, 3 * D), BF), sds((D, D), BF), sds((D, FF), BF), sds((4,) + wc.shape, BF), sds((8, FF), F32)],
        scratch_shapes=[
            pltpu.VMEM((4, D, 640), BF), pltpu.VMEM((4, D, 256), BF), pltpu.VMEM((D, FF), BF),
            pltpu.VMEM((D, 3 * D), BF), pltpu.VMEM((D, D), BF), pltpu.VMEM((8, 16, FF // 8), BF),
            pltpu.VMEM((T, D), BF), pltpu.VMEM((T, 3 * D), BF), pltpu.VMEM((T, D), BF),
            pltpu.VMEM((H, T, 128), BF), pltpu.VMEM((2, T, 128), BF), pltpu.VMEM((2, T, 128), BF),
            pltpu.VMEM((8, FF), F32), pltpu.VMEM((4,) + wc.shape, BF),
            pltpu.SemaphoreType.DMA((n,)), pltpu.SemaphoreType.DMA((n,)), pltpu.SemaphoreType.DMA((9,)), pltpu.SemaphoreType.DMA((H // 2, 2)),
        ],
        compiler_params=pltpu.CompilerParams(
            collective_id=0, has_side_effects=True, vmem_limit_bytes=60 << 20),
        name="first_part",
    )(length, x, wp, wo, we, wc, *vectors)


def layer_norm(values, gain_row, shift_row):
    centre = jnp.mean(values, axis=-1, keepdims=True)
    centred = values - centre
    spread = jnp.mean(centred * centred, axis=-1, keepdims=True)
    return centred * lax.rsqrt(spread + eps_norm) * gain_row + shift_row


def gelu_exact(values):
    return jax.nn.gelu(values, approximate=False)


def matmul(first, second):
    return jnp.dot(first, second, preferred_element_type=jnp.float32)


def over_rows(first, second):
    return lax.dot_general(
        first, second, (((0,), (0,)), ((), ())), preferred_element_type=jnp.float32
    )


def over_columns(first, second):
    return lax.dot_general(
        first, second, (((1,), (1,)), ((), ())), preferred_element_type=jnp.float32
    )


def fetch_forward(
    project_weight,
    output_weight,
    expand_weight,
    contract_weight,
    project_bias,
    output_bias,
    expand_bias,
    contract_bias,
    first_gain,
    first_shift,
    second_gain,
    second_shift,
):
    wide_project, wide_output, wide_expand, wide_contract = (
        lax.all_gather(project_weight, "fsdp", axis=1, tiled=True),
        lax.all_gather(output_weight, "fsdp", axis=1, tiled=True),
        lax.all_gather(expand_weight, "fsdp", axis=1, tiled=True),
        lax.all_gather(contract_weight, "fsdp", axis=1, tiled=True),
    )
    return (
        lax.all_gather(wide_project, "dp", axis=0, tiled=True),
        lax.all_gather(wide_output, "dp", axis=0, tiled=True),
        lax.all_gather(wide_expand, "dp", axis=0, tiled=True),
        lax.all_gather(wide_contract, "dp", axis=0, tiled=True),
        lax.all_gather(project_bias, "dp", axis=0, tiled=True),
        lax.all_gather(output_bias, "dp", axis=0, tiled=True),
        lax.all_gather(expand_bias, "dp", axis=0, tiled=True),
        lax.all_gather(contract_bias, "dp", axis=0, tiled=True),
        lax.all_gather(first_gain, "dp", axis=0, tiled=True),
        lax.all_gather(first_shift, "dp", axis=0, tiled=True),
        lax.all_gather(second_gain, "dp", axis=0, tiled=True),
        lax.all_gather(second_shift, "dp", axis=0, tiled=True),
    )


def fetch_backward(
    project_weight,
    output_weight,
    expand_weight,
    contract_weight,
    project_bias,
    output_bias,
    expand_bias,
    contract_bias,
    first_gain,
    first_shift,
    second_gain,
    second_shift,
):
    wide_project, wide_output, wide_expand, wide_contract = (
        lax.all_gather(project_weight, "fsdp", axis=1, tiled=True),
        lax.all_gather(output_weight, "fsdp", axis=1, tiled=True),
        lax.all_gather(expand_weight, "fsdp", axis=1, tiled=True),
        lax.all_gather(contract_weight, "fsdp", axis=1, tiled=True),
    )
    return (
        lax.all_gather(wide_project, "dp", axis=0, tiled=True),
        lax.all_gather(wide_output, "dp", axis=0, tiled=True),
        lax.all_gather(wide_expand, "dp", axis=0, tiled=True),
        lax.all_gather(wide_contract, "dp", axis=0, tiled=True),
        lax.all_gather(project_bias, "dp", axis=0, tiled=True),
        lax.all_gather(output_bias, "dp", axis=0, tiled=True),
        lax.all_gather(expand_bias, "dp", axis=0, tiled=True),
        lax.all_gather(contract_bias, "dp", axis=0, tiled=True),
        lax.all_gather(first_gain, "dp", axis=0, tiled=True),
        lax.all_gather(first_shift, "dp", axis=0, tiled=True),
        lax.all_gather(second_gain, "dp", axis=0, tiled=True),
        lax.all_gather(second_shift, "dp", axis=0, tiled=True),
    )


def split_heads(cell_rows, block_rows):
    slot_count = cell_rows.shape[0]
    width = cell_rows.shape[1] // 3
    query_blocks = cell_rows[:, :width].reshape(slot_count // block_rows, block_rows, H, HD)
    keys_all = cell_rows[:, width : 2 * width].reshape(slot_count, H, HD)
    values_all = cell_rows[:, 2 * width :].reshape(slot_count, H, HD)
    return (query_blocks, keys_all, values_all)


def block_scores(query_block, keys_all, key_live):
    scores = jnp.einsum(
        "qhe,khe->hqk", query_block, keys_all, preferred_element_type=jnp.float32
    ) * HD ** (-0.5)
    return jnp.where(key_live[None, None, :], scores, neg_fill)


def attend_forward(query_block, keys_all, values_all, key_live):
    scores = block_scores(query_block, keys_all, key_live)
    row_max = jnp.max(scores, axis=-1, keepdims=True)
    powers = jnp.exp(scores - row_max)
    row_total = jnp.sum(powers, axis=-1, keepdims=True)
    weights = (powers / row_total).astype(jnp.bfloat16)
    mixed_block = jnp.einsum(
        "hqk,khe->qhe", weights, values_all, preferred_element_type=jnp.float32
    )
    return (mixed_block, (row_max + jnp.log(row_total))[:, :, 0])


def attend_backward(query_block, grad_block, log_block, keys_all, values_all, key_live):
    scores = block_scores(query_block, keys_all, key_live)
    weights = jnp.exp(scores - log_block[:, :, None])
    grad_weights = jnp.einsum(
        "qhe,khe->hqk", grad_block, values_all, preferred_element_type=jnp.float32
    )
    row_inner = jnp.sum(grad_weights * weights, axis=-1, keepdims=True)
    grad_scores = (weights * (grad_weights - row_inner)).astype(jnp.bfloat16)
    grad_query = jnp.einsum(
        "hqk,khe->qhe", grad_scores, keys_all, preferred_element_type=jnp.float32
    ) * HD ** (-0.5)
    grad_key = jnp.einsum(
        "hqk,qhe->khe", grad_scores, query_block, preferred_element_type=jnp.float32
    ) * HD ** (-0.5)
    grad_value = jnp.einsum(
        "hqk,qhe->khe", weights.astype(jnp.bfloat16), grad_block, preferred_element_type=jnp.float32
    )
    return (grad_query, grad_key, grad_value)


def per_device(
    tokens,
    lengths,
    cotangent,
    project_weight,
    project_bias,
    output_weight,
    output_bias,
    expand_weight,
    expand_bias,
    contract_weight,
    contract_bias,
    first_gain,
    first_shift,
    second_gain,
    second_shift,
):
    fetched = fetch_forward(
        project_weight,
        output_weight,
        expand_weight,
        contract_weight,
        project_bias,
        output_bias,
        expand_bias,
        contract_bias,
        first_gain,
        first_shift,
        second_gain,
        second_shift,
    )
    full_project, full_output, full_expand, full_contract = (
        fetched[0],
        fetched[1],
        fetched[2],
        fetched[3],
    )
    vectors = [item.astype(jnp.float32) for item in fetched[4:]]
    bias_project, bias_output, bias_expand, bias_contract = (
        vectors[0],
        vectors[1],
        vectors[2],
        vectors[3],
    )
    gain_one, shift_one, gain_two, shift_two = (vectors[4], vectors[5], vectors[6], vectors[7])
    cell_count = lengths.shape[0]
    slot_count = tokens.shape[0] // cell_count
    width = tokens.shape[1]
    block_rows = min(512, slot_count)
    positions = jnp.arange(slot_count, dtype=jnp.int32)
    live_keys = positions[None, :] < lengths[:, None]
    live_rows = live_keys.reshape(-1)
    rows_in = tokens.astype(jnp.float32)
    normed_one = layer_norm(rows_in, gain_one, shift_one).astype(jnp.bfloat16)
    bias_full = jnp.concatenate(
        [bias_project[:width], jnp.zeros((width,), jnp.float32), bias_project[width:]]
    )
    projected = (matmul(normed_one, full_project) + bias_full).astype(jnp.bfloat16)
    cell_index = 0
    query_blocks, keys_all, values_all = split_heads(projected, block_rows)
    key_live = live_keys[cell_index]
    mixed_blocks, log_blocks = lax.map(
        lambda query_block: attend_forward(query_block, keys_all, values_all, key_live),
        query_blocks,
    )
    mixed_list = mixed_blocks.reshape(slot_count, width)
    log_list = [log_blocks]
    mixed_low = mixed_list.astype(jnp.bfloat16)
    middle = rows_in + (matmul(mixed_low, full_output) + bias_output)
    normed_two = layer_norm(middle, gain_two, shift_two).astype(jnp.bfloat16)
    hidden = matmul(normed_two, full_expand) + bias_expand
    active = gelu_exact(hidden).astype(jnp.bfloat16)
    result = middle + (matmul(active, full_contract) + bias_contract)
    block_out = jnp.where(live_rows[:, None], result, 0.0).astype(jnp.bfloat16)
    again = fetch_backward(
        project_weight,
        output_weight,
        expand_weight,
        contract_weight,
        project_bias,
        output_bias,
        expand_bias,
        contract_bias,
        first_gain,
        first_shift,
        second_gain,
        second_shift,
    )
    back_project, back_output, back_expand, back_contract = (again[0], again[1], again[2], again[3])
    grad_out = jnp.where(live_rows[:, None], cotangent.astype(jnp.float32), 0.0)
    grad_out_low = grad_out.astype(jnp.bfloat16)
    grad_contract = over_rows(active, grad_out_low)
    grad_contract_bias = jnp.sum(grad_out, axis=0)
    grad_active = over_columns(grad_out_low, back_contract)
    gelu_value, gelu_pull = jax.vjp(gelu_exact, hidden)
    grad_hidden = gelu_pull(grad_active)[0].astype(jnp.bfloat16)
    grad_expand = over_rows(normed_two, grad_hidden)
    grad_expand_bias = jnp.sum(grad_hidden.astype(jnp.float32), axis=0)
    grad_normed_two = over_columns(grad_hidden, back_expand)
    norm_value, second_pull = jax.vjp(layer_norm, middle, gain_two, shift_two)
    grad_middle, grad_gain_two, grad_shift_two = second_pull(grad_normed_two)
    grad_middle = grad_middle + grad_out
    grad_branch = grad_middle.astype(jnp.bfloat16)
    grad_output = over_rows(mixed_low, grad_branch)
    grad_output_bias = jnp.sum(grad_branch.astype(jnp.float32), axis=0)
    grad_mixed = over_columns(grad_branch, back_output).astype(jnp.bfloat16)
    cell_index = 0
    query_blocks, keys_all, values_all = split_heads(projected, block_rows)
    key_live = live_keys[cell_index]
    grad_blocks = grad_mixed.reshape(slot_count // block_rows, block_rows, H, HD)

    def visit_block(carried, inputs):
        query_block, grad_block, log_block = inputs
        grad_query, grad_key, grad_value = attend_backward(
            query_block, grad_block, log_block, keys_all, values_all, key_live
        )
        return ((carried[0] + grad_key, carried[1] + grad_value), grad_query)

    initial = (
        jnp.zeros((slot_count, H, HD), jnp.float32),
        jnp.zeros((slot_count, H, HD), jnp.float32),
    )
    (key_sums, value_sums), query_grads = lax.scan(
        visit_block, initial, (query_blocks, grad_blocks, log_list[cell_index])
    )
    grad_cells = jnp.concatenate(
        [
            query_grads.reshape(slot_count, width),
            key_sums.reshape(slot_count, width),
            value_sums.reshape(slot_count, width),
        ],
        axis=1,
    )
    grad_projected = grad_cells.astype(jnp.bfloat16)
    grad_project = over_rows(normed_one, grad_projected)
    column_sums = jnp.sum(grad_projected.astype(jnp.float32), axis=0)
    grad_project_bias = jnp.concatenate([column_sums[:width], column_sums[2 * width :]])
    grad_normed_one = over_columns(grad_projected, back_project)
    first_value, first_pull = jax.vjp(layer_norm, rows_in, gain_one, shift_one)
    grad_rows_in, grad_gain_one, grad_shift_one = first_pull(grad_normed_one)
    tokens_grad = (grad_rows_in + grad_middle).astype(jnp.bfloat16)
    reduced = (
        lax.psum_scatter(grad_project, "dp", scatter_dimension=0, tiled=True),
        lax.psum_scatter(grad_output, "dp", scatter_dimension=0, tiled=True),
        lax.psum_scatter(grad_expand, "dp", scatter_dimension=0, tiled=True),
        lax.psum_scatter(grad_contract, "dp", scatter_dimension=0, tiled=True),
        lax.psum_scatter(grad_project_bias, "dp", scatter_dimension=0, tiled=True),
        lax.psum_scatter(grad_output_bias, "dp", scatter_dimension=0, tiled=True),
        lax.psum_scatter(grad_expand_bias, "dp", scatter_dimension=0, tiled=True),
        lax.psum_scatter(grad_contract_bias, "dp", scatter_dimension=0, tiled=True),
        lax.psum_scatter(grad_gain_one, "dp", scatter_dimension=0, tiled=True),
        lax.psum_scatter(grad_shift_one, "dp", scatter_dimension=0, tiled=True),
        lax.psum_scatter(grad_gain_two, "dp", scatter_dimension=0, tiled=True),
        lax.psum_scatter(grad_shift_two, "dp", scatter_dimension=0, tiled=True),
    )
    shard_project, shard_output, shard_expand, shard_contract = (
        lax.psum_scatter(
            reduced[0].astype(jnp.bfloat16), "fsdp", scatter_dimension=1, tiled=True
        ).astype(jnp.float32),
        lax.psum_scatter(
            reduced[1].astype(jnp.bfloat16), "fsdp", scatter_dimension=1, tiled=True
        ).astype(jnp.float32),
        lax.psum_scatter(
            reduced[2].astype(jnp.bfloat16), "fsdp", scatter_dimension=1, tiled=True
        ).astype(jnp.float32),
        lax.psum_scatter(
            reduced[3].astype(jnp.bfloat16), "fsdp", scatter_dimension=1, tiled=True
        ).astype(jnp.float32),
    )
    summed = lax.psum(
        (
            reduced[4],
            reduced[5],
            reduced[6],
            reduced[7],
            reduced[8],
            reduced[9],
            reduced[10],
            reduced[11],
        ),
        "fsdp",
    )
    return (
        block_out,
        tokens_grad,
        shard_project,
        summed[0],
        shard_output,
        summed[1],
        shard_expand,
        summed[2],
        shard_contract,
        summed[3],
        summed[4],
        summed[5],
        summed[6],
        summed[7],
    )


def scatter_events(link, place, col, pair_of, lc, lxh, lyh, lx, ly):
    p = place
    family = (p.dc, p.dx + p.dc - p.d, p.dy + p.dc - p.d, p.dd + p.dc - p.d)
    cs = [link.slot() for _ in range(4)]
    hx, hy, fx, fy = (link.slot() for _ in range(4))
    got = link.got

    def add(target, *terms):
        flat = len(target.shape) == 2

        def body(i, _):
            at = (pl.ds(mo(i * 16, 16), 16), slice(None)) if flat else (i,)
            total = target[at].astype(F32)
            for term in terms:
                total = total + term[at].astype(F32)
            target[at] = total.astype(BF)
            return 0

        lax.fori_loop(0, target.shape[0] // 16 if flat else target.shape[0], body, 0)

    def to_sibling(which):
        link.send(cs[which], col(family[which]), lc.at[which], "c", lambda: col(0))

    def halves():
        got(cs[3], lc.at[3])
        add(col(p.dd), lc.at[3])
        link.send(hx, pair_of(col(p.dd), 0), lxh, "x", lambda: lxh)
        link.send(hy, pair_of(col(p.dd), 1), lyh, "y", lambda: lyh)

    def near():
        got(cs[1], lc.at[1])
        got(cs[2], lc.at[2])
        add(col(p.dx), lc.at[1])
        add(col(p.dy), lc.at[2])

    def pass_y():
        got(hx, lxh)
        add(pair_of(col(p.dy), 0), lxh)
        link.send(fy, col(p.dy), ly, "y", lambda: ly)

    def pass_x():
        got(hy, lyh)
        add(pair_of(col(p.dx), 1), lyh)
        link.send(fx, col(p.dx), lx, "x", lambda: lx)

    def own():
        got(cs[0], lc.at[0])

    def total():
        got(fx, lx)
        got(fy, ly)
        add(col(p.d), lc.at[0], lx, ly)

    return to_sibling, [halves, near, pass_y, pass_x, own, total]


def z_sum(link, place, block, lz, finish):
    p = place
    zs = link.slot(4)

    def send():
        for step in (1, 3, 2):
            link.send(zs + step, block(p.zt(step)), lz.at[step], step, lambda: lz.at[0])

    def last():
        total = block(p.z)[...].astype(F32)
        for step in (1, 3, 2):
            link.got(zs + step, lz.at[step])
            total = total + lz[step].astype(F32)
        finish(total)

    return send, last


def gelu_pair(value):
    lift = 0.5 * (1.0 + lax.erf(value * 0.7071067811865476))
    bell = jnp.exp(value * value * -0.5) * 0.3989422804014327
    return value * lift, lift + value * bell


def second_kernel(length_ref, x_hbm, cot_hbm, mixed_hbm, wo_hbm, we_hbm, c_hbm, v_ref,
                  block_out, dmixed_out, dmiddle_out, ge_out, go_out, gc_out, vg_out,
                  x_ref, cot_ref, mixed_ref, wo_ref, we, wct, act, slope, middle, n2t, dot_t, mixed_t, dbranch, dout, gc, go, dmixed, bout, vg,
                  lc, lxh, lyh, lx, ly, send_sem, recv_sem, out_sem):
    p = Place()
    T, D = x_ref.shape
    FF = we.shape[1]
    R = D // 8
    Q = FF // 4
    C8 = FF // 8
    link = Link(p, send_sem, recv_sem)
    bc = lambda z, d: wct.at[pl.ds(mo(z * (D // 4), 16), D // 4), pl.ds(mo(d * C8, 128), C8)]
    gather = Gather(link, p, bc)

    to_sibling, scatter = scatter_events(
        link, p, lambda d: gc.at[d], lambda ref, h: ref.at[pl.ds(2 * h, 2)], lc, lxh, lyh, lx, ly)
    load = pltpu.make_async_copy(we_hbm, we, out_sem.at[0])
    columns = [pltpu.make_async_copy(c_hbm.at[z], bc(z, p.d), out_sem.at[19 + z]) for z in range(4)]
    for made in columns:
        made.start()
    halves = [pl.ds(i * (T // 2), T // 2) for i in range(2)]
    early = [[pltpu.make_async_copy(wo_hbm, wo_ref, out_sem.at[12])], []]
    for i, r in enumerate(halves):
        for at, (a, b) in enumerate(((mixed_hbm, mixed_ref), (x_hbm, x_ref), (cot_hbm, cot_ref))):
            early[i].append(pltpu.make_async_copy(a.at[r], b.at[r], out_sem.at[13 + 3 * i + at]))
    for made in early[0] + early[1]:
        made.start()
    load.start()
    enter(p)
    for made in columns:
        made.wait()
    run(*gather.x)()
    for made in early[0] + early[1]:
        made.wait()
    length = length_ref[0]
    LR = 256
    rows = lambda i: pl.ds(mo(i * LR, LR), LR)
    vec = lambda i: v_ref[i:i + 1, 0:D]
    vg[...] = jnp.zeros_like(vg)

    def at(i, spots):
        for where, event in spots:
            pl.when(i == where)(event)

    def norm(value):
        u = value - jnp.mean(value, axis=-1, keepdims=True)
        r = lax.rsqrt(jnp.mean(u * u, axis=-1, keepdims=True) + eps_norm)
        return u * r, r

    def middle_body(i, _):
        r = rows(i)
        value = x_ref[r, :].astype(F32) + (dot(mixed_ref[r, :], wo_ref[...]) + vec(2))
        middle[r, :] = value
        xhat, _ = norm(value)
        n2 = (xhat * vec(6) + vec(7)).astype(BF)
        dmixed[r, :] = n2
        n2t[:, r] = n2.T
        live = iota((LR, D), 0) + i * LR < length
        grad = jnp.where(live, cot_ref[r, :].astype(F32), 0.0)
        vg[7:8, :] += jnp.sum(grad, axis=0, keepdims=True)
        dout[r, :] = grad.astype(BF)
        dot_t[:, r] = grad.astype(BF).T
        mixed_t[:, r] = mixed_ref[r, :].T
        return 0

    lax.fori_loop(0, T // LR, middle_body, 0)
    load.wait()

    def hidden_body(i, _):
        at(i, [(0, gather.t[0]), (1, gather.t[1]), (2, gather.t[2]), (3, gather.t[3])])
        r = rows(i)
        left = dmixed[r, :]
        for j in range(4):
            cols = slice(j * Q, (j + 1) * Q)
            first, second = gelu_pair(dot(left, we[:, cols]) + v_ref[1:2, cols])
            act[r, cols] = first.astype(BF)
            slope[r, cols] = second.astype(BF)
        return 0

    lax.fori_loop(0, T // LR, hidden_body, 0)

    def column(d):
        value = dot(dot_t[...], act[:, pl.ds(mo(d * C8, 128), C8)])
        gc[d] = value.reshape(4, D // 4, C8).astype(BF)

    sib = p.dc - p.d
    turns = (p.dd + sib, p.dd, p.dx + sib, p.dy + sib, p.dx, p.dy, p.d + sib, p.d)

    def column_body(i, _):
        d = turns[7]
        for k in range(7):
            d = jnp.where(i == k, turns[k], d)
        column(d)
        at(i, [(0, lambda: to_sibling(3)), (2, lambda: to_sibling(1)), (3, run(lambda: to_sibling(2), gather.q[0])),
               (5, run(gather.q[1], gather.q[2], scatter[0])), (6, lambda: to_sibling(0))])
        return 0

    lax.fori_loop(0, 8, column_body, 0)
    run(gather.q[3], scatter[1], gather.close)()

    def back_body(i, _):
        at(i, [(1, run(scatter[2], scatter[3], scatter[4]))])
        r = rows(i)
        grad_low = dout[r, :]
        result = middle[r, :] + vec(3)
        for j in range(4):
            cols = slice(j * Q, (j + 1) * Q)
            dh = dot(grad_low, wct[:, cols]) * slope[r, cols].astype(F32)
            low = dh.astype(BF)
            slope[r, cols] = low
            vg[3 + j:4 + j, :] += jnp.sum(low.astype(F32), axis=0, keepdims=True)
        result = result + dot_nt(act[r, :], wct[...])
        dn = dot_nt(slope[r, :], we[...])
        live = iota((LR, D), 0) + i * LR < length
        bout[r, :] = jnp.where(live, result, 0.0).astype(BF)
        xhat, spread = norm(middle[r, :])
        vg[10:11, :] += jnp.sum(dn * xhat, axis=0, keepdims=True)
        vg[11:12, :] += jnp.sum(dn, axis=0, keepdims=True)
        gx = dn * vec(6)
        back = spread * (gx - jnp.mean(gx, axis=-1, keepdims=True)
                         - xhat * jnp.mean(gx * xhat, axis=-1, keepdims=True))
        total = dout[r, :].astype(F32) + back
        middle[r, :] = total
        branch = total.astype(BF)
        dbranch[r, :] = branch
        vg[2:3, :] += jnp.sum(branch.astype(F32), axis=0, keepdims=True)
        dmixed[r, :] = dot_nt(branch, wo_ref[...]).astype(BF)
        return 0

    lax.fori_loop(0, T // LR, back_body, 0)
    outs = []

    def out(source, target):
        made = pltpu.make_async_copy(source, target, out_sem.at[1 + len(outs)])
        made.start()
        outs.append(made)

    out(bout, block_out)
    out(dmixed, dmixed_out)
    out(middle, dmiddle_out)
    for z in range(4):
        cols = slice(3 * z // 2 * 128, 3 * z // 2 * 128 + 256)
        go[:, z] = dot(mixed_t[...], dbranch[:, cols]).reshape(8, R, 256).astype(BF)
    out(go, go_out)
    for z in range(4):
        act[0:D, z * Q:(z + 1) * Q] = dot(n2t[...], slope[:, z * Q:(z + 1) * Q]).astype(BF)
        out(act.at[0:D, z * Q:(z + 1) * Q], ge_out.at[:, z * Q:(z + 1) * Q])
        if z == 2:
            scatter[5]()
            out(gc.at[p.d], gc_out)
    vg_out[...] = vg[...]
    link.finish()
    for made in outs:
        made.wait()


ANY = pl.BlockSpec(memory_space=pl.ANY)
VM = pl.BlockSpec(memory_space=pltpu.VMEM)
SM = pl.BlockSpec(memory_space=pltpu.SMEM)
sds = jax.ShapeDtypeStruct


def second_call(length, x, cot, mixed, wo, we, wc, v):
    T, D = x.shape
    FF = we.shape[1]
    n = 36 + 8
    R, C8, Z = D // 8, FF // 8, D // 4
    vm = pltpu.VMEM
    return pl.pallas_call(
        second_kernel,
        in_specs=[SM] + [ANY] * 6 + [VM],
        out_specs=[ANY] * 6 + [VM],
        out_shape=[sds((T, D), BF), sds((T, D), BF), sds((T, D), F32), sds((D, FF), BF), sds((8, 4, R, 256), BF),
                   sds((4, Z, C8), BF), sds((16, D), F32)],
        scratch_shapes=[
            vm((T, D), BF), vm((T, D), BF), vm((T, D), BF), vm((D, D), BF), vm((D, FF), BF), vm((D, FF), BF), vm((T, FF), BF), vm((T, FF), BF), vm((T, D), F32),
            vm((D, T), BF), vm((D, T), BF), vm((D, T), BF), vm((T, D), BF), vm((T, D), BF),
            vm((8, 4, Z, C8), BF), vm((8, 4, R, 256), BF), vm((T, D), BF), vm((T, D), BF), vm((16, D), F32),
            vm((4, 4, Z, C8), BF), vm((2, Z, C8), BF), vm((2, Z, C8), BF), vm((4, Z, C8), BF), vm((4, Z, C8), BF),
            pltpu.SemaphoreType.DMA((n,)), pltpu.SemaphoreType.DMA((n,)), pltpu.SemaphoreType.DMA((23,)),
        ],
        compiler_params=pltpu.CompilerParams(
            collective_id=1, has_side_effects=True, vmem_limit_bytes=62 << 20),
        name="second_part",
    )(length, x, cot, mixed, wo, we, wc, v)


def third_kernel(length_ref, proj_hbm, qa_hbm, mixed_hbm, dm_hbm, n1_hbm, wp_hbm, x_hbm, dmiddle_hbm, ge_hbm, go_hbm,
                 gc_hbm, vg_ref, v_ref,
                 tokens_out, gp_out, go_out, ge_out, gc_out, vec_out,
                 proj, qa, mixed, dm, n1, n1t, wpp, x, dmiddle, ge, go, dproj, tg, gp,
                 ka, da, dq, va, kt, vs, vo, vl, vz,
                 lce, lxhe, lyhe, lxe, lye, lze, lco, lxho, lyho, lxo, lyo, lzo,
                 lcp, lxhp, lyhp, lxp, lyp, lzp, gpw, gcol, lzc,
                 send_sem, recv_sem, load_sem):
    p = Place()
    T, D = x.shape
    FF = ge.shape[1]
    R = D // 8
    Q = FF // 4
    pairs = H // 2
    KB = 256
    parts = 2
    link = Link(p, send_sem, recv_sem)
    loads = []

    def load(source, target):
        made = pltpu.make_async_copy(source, target, load_sem.at[len(loads)])
        made.start()
        loads.append(made)
        return made

    first_loads = [load(a, b) for a, b in ((proj_hbm, proj), (qa_hbm, qa), (mixed_hbm, mixed), (dm_hbm, dm))]
    ge_load, gc_load, go_load, n1_load = load(ge_hbm, ge), load(gc_hbm, gcol), load(go_hbm, go), load(n1_hbm, n1)
    late = [load(x_hbm, x), load(dmiddle_hbm, dmiddle)]
    for i in range(pairs):
        for s in range(3):
            late.append(load(wp_hbm.at[:, pl.ds((s * pairs + i) * 128, 128)],
                             wpp.at[:, pl.ds((i * 3 + s) * 128, 128)]))

    def finish_e(total):
        ge_out[...] = total

    def finish_o(total):
        go_out[...] = jnp.where(p.odd == 0, total[:, 0:192], total[:, 64:256])

    rows_of = lambda d: pl.ds(mo(d * R, 16), R)
    def finish_c(total):
        gc_out[...] = total

    e_col, o_col = (lambda d: ge.at[rows_of(d), :]), (lambda d: go.at[d])
    e_sib, ev_e = scatter_events(
        link, p, e_col, lambda ref, h: ref.at[:, pl.ds(h * (FF // 2), FF // 2)], lce, lxhe, lyhe, lxe, lye)
    o_sib, ev_o = scatter_events(
        link, p, o_col, lambda ref, h: ref.at[pl.ds(2 * h, 2)], lco, lxho, lyho, lxo, lyo)
    e_send, e_last = z_sum(link, p, lambda z: e_col(p.d).at[:, pl.ds(mo(z * Q, 128), Q)], lze, finish_e)
    o_send, o_last = z_sum(link, p, lambda z: o_col(p.d).at[z], lzo, finish_o)
    c_send, c_last = z_sum(link, p, lambda z: gcol.at[z], lzc, finish_c)
    ended = []
    combos = []
    for i in range(pairs):
        for s in range(3):
            tile = s * pairs + i
            for owner in range(4):
                left = 9 * owner // 2
                if left <= tile < left + 5:
                    combos.append((i, s, owner, tile - left))
    assert len(combos) == 20
    z_slots = [[link.slot() for _ in range(3)] for _ in combos]

    def pair_scatter(i):
        column = lambda d: gp.at[i, d]
        sib, events = scatter_events(
            link, p, column, lambda ref, h: ref.at[pl.ds(h * (R // 2), R // 2)],
            lcp.at[i], lxhp.at[i], lyhp.at[i], lxp.at[i], lyp.at[i])
        mine = [(at, c) for at, c in enumerate(combos) if c[0] == i]

        def along(add_own):
            def run():
                add_own()
                for at, (_, s, owner, _) in mine:
                    @pl.when(p.z != owner)
                    def _():
                        step = lax.rem(owner - p.z + 4, 4)
                        part = column(p.d).at[:, pl.ds(s * 128, 128)]
                        link.copy(z_slots[at][0] + step - 1, part, lzp.at[at, step - 1], ("z", owner)).start()
            return run

        def last():
            for at, (_, s, owner, place) in mine:
                @pl.when(p.z == owner)
                def _():
                    total = gp[i, p.d, :, s * 128:(s + 1) * 128].astype(F32)
                    for step in range(1, 4):
                        link.got(z_slots[at][step - 1], lzp.at[at, step - 1])
                        total = total + lzp[at, step - 1].astype(F32)
                    gpw[:, place * 128:(place + 1) * 128] = total

        def ending():
            for at, (_, s, owner, _) in mine:
                @pl.when(p.z != owner)
                def _():
                    step = lax.rem(owner - p.z + 4, 4)
                    view = lzp.at[at, 0]
                    link.copy(z_slots[at][0] + step - 1, view, view, "x").wait_send()

        ended.append(ending)

        def start():
            for k in (3, 1, 2, 0):
                sib(k)

        return [start] + events[:5] + [along(events[5]), last]

    ev_p = [pair_scatter(i) for i in range(pairs)]

    enter(p, wide=True)
    for made in first_loads:
        made.wait()
    length = length_ref[0]

    def start_e():
        ge_load.wait()
        for k in (3, 1, 2, 0):
            e_sib(k)

    def start_o():
        go_load.wait()
        for k in (3, 1, 2, 0):
            o_sib(k)

    def turn_n1():
        n1_load.wait()
        for i in range(T // 256):
            n1t[:, i * 256:(i + 1) * 256] = n1[i * 256:(i + 1) * 256, :].T

    def start_c():
        gc_load.wait()
        c_send()

    e, o = ev_e, ev_o
    q = ev_p
    timeline = [
        (0, start_c), (0, start_e), (0, start_o), (0, turn_n1), (1, e[0]), (2, e[1]), (2, e[4]), (2, o[0]), (2, o[1]), (2, o[4]),
        (2, q[0][0]), (3, q[0][1]), (3, q[0][2]), (3, q[0][5]), (4, e[2]), (4, e[3]), (4, c_last), (4, o[2]), (4, o[3]),
        (4, q[0][3]), (4, q[0][4]), (4, q[1][0]), (5, q[1][1]), (5, q[1][2]), (5, q[1][5]), (6, q[2][0]),
        (7, q[2][1]), (7, q[2][2]), (7, q[2][5]), (8, e[5]), (8, e_send), (8, q[3][0]), (9, o[5]), (9, o_send),
        (9, q[3][1]), (9, q[3][2]), (9, q[3][5]), (10, q[0][6]), (10, q[1][3]), (10, q[1][4]), (10, q[2][3]), (10, q[2][4]),
        (10, q[3][3]), (10, q[3][4]), (10, q[4][0]), (11, q[4][1]), (11, q[4][2]), (11, q[4][5])]
    timeline.sort(key=lambda e: e[0])

    def body(step, _):
        for at, event in timeline:
            if at < pairs * parts:
                pl.when(step == at)(event)
        pair = lax.div(step, parts)
        part = lax.rem(step, parts)
        ps = lambda off: pl.ds(mo(off + pair * 128, 128), 128)
        own = lambda s: pl.ds(mo(pair * 384 + s * 128, 128), 128)

        @pl.when(part == 0)
        def _():
            lane, row = iota((T, 128), 1), iota((T, 128), 0)
            k = proj[:, ps(D)].astype(F32)
            v = proj[:, ps(2 * D)].astype(F32)
            do = dm[:, ps(0)].astype(F32)
            pr = do * mixed[:, ps(0)].astype(F32)
            dead = jnp.where(row < length, 0.0, neg_fill)
            for head in range(2):
                keep = (lane < 64) if head == 0 else (lane >= 64)
                delta = jnp.sum(jnp.where(keep, pr, 0.0), axis=-1, keepdims=True)
                one, two, three = split3(-delta)
                da[head] = extend(head, do, lane, one, two, three, 0.0)
                ka[head] = extend(head, k, lane, 1.0, 1.0, 1.0, dead)
                va[head] = extend(head, v, lane, 1.0, 1.0, 1.0, 0.0)
                kt[head] = jnp.where(keep, k, 0.0).astype(BF).T
            dq[...] = jnp.zeros_like(dq)

        lk = iota((KB, 128), 1)
        spans = [pl.ds(mo(part * (T // parts) + i * KB, KB), KB) for i in range(T // parts // KB)]
        items = [(head, r) for r in spans for head in range(2)]
        kept = {}

        def products(n):
            head, r = items[n]
            return dot_nt(ka[head, r, :], qa[pair * 2 + head]), dot_nt(va[head, r, :], da[head])

        def weigh(scores, grads):
            weights = jnp.exp(scores)
            return weights.astype(BF), (weights * grads).astype(BF)

        def finish(n, low, ds):
            head, r = items[n]
            kept[n] = dot(ds, qa[pair * 2 + head]), dot(low, da[head])
            dq[head] += dot(kt[head, :, r], ds)
            if head == 1:
                dproj[r, own(1)] = jnp.where(lk < 64, kept[n - 1][0], kept[n][0]).astype(BF)
                dproj[r, own(2)] = jnp.where(lk < 64, kept[n - 1][1], kept[n][1]).astype(BF)

        value, waiting = products(0), None
        for n in range(len(items)):
            following = products(n + 1) if n + 1 < len(items) else None
            done = weigh(*value)
            if waiting is not None:
                finish(n - 1, *waiting)
            value, waiting = following, done
        finish(len(items) - 1, *waiting)

        @pl.when(part == parts - 1)
        def _():
            dproj[:, own(0)] = ((dq[0] + dq[1]) * (HD ** -0.5)).T.astype(BF)
            value = dot(n1t[...], dproj[:, pl.ds(mo(pair * 384, 128), 384)])
            gp[pair] = value.reshape(8, R, 384).astype(BF)

        return 0

    lax.fori_loop(0, pairs * parts, body, 0)
    ev_p[pairs - 1][0]()
    for made in late:
        made.wait()
    vs[...] = vg_ref[...]
    LR = 256

    def norm_body(i, _):
        def spot(where, events):
            @pl.when(i == where)
            def _():
                for event in events:
                    event()

        spot(0, [e_last, q[1][6], q[2][6], q[3][6], q[4][3], q[4][4]])
        spot(1, q[5][1:3] + q[5][5:6])
        spot(2, [o_last, q[0][7], q[1][7], q[4][6], q[2][7]])
        spot(3, q[5][3:5] + q[3][7:8])
        r = pl.ds(mo(i * LR, LR), LR)
        left = dproj[r, :]
        dn = dot_nt(left, wpp[...])
        sums = jnp.sum(left.astype(F32), axis=0, keepdims=True)
        for j in range(pairs):
            vs[0:1, j * 128:(j + 1) * 128] += sums[:, j * 384:j * 384 + 128]
            vs[1:2, j * 128:(j + 1) * 128] += sums[:, j * 384 + 256:j * 384 + 384]
        value = x[r, :].astype(F32)
        u = value - jnp.mean(value, axis=-1, keepdims=True)
        spread = lax.rsqrt(jnp.mean(u * u, axis=-1, keepdims=True) + eps_norm)
        xhat = u * spread
        vs[8:9, :] += jnp.sum(dn * xhat, axis=0, keepdims=True)
        vs[9:10, :] += jnp.sum(dn, axis=0, keepdims=True)
        gx = dn * v_ref[4:5, 0:D]
        back = spread * (gx - jnp.mean(gx, axis=-1, keepdims=True)
                         - xhat * jnp.mean(gx * xhat, axis=-1, keepdims=True))
        tg[r, :] = (back + dmiddle[r, :]).astype(BF)
        return 0

    lax.fori_loop(0, T // LR, norm_body, 0)
    out = load(tg, tokens_out)
    v_slots = link.slot(16)
    for d in range(8):
        line = lambda row, at, n: jnp.concatenate(
            [vs[row:row + 1, at:at + n], jnp.zeros((1, 384 - n), F32)], axis=1) if n < 384 else vs[row:row + 1, at:at + n]
        vo[d] = jnp.concatenate(
            [line(d // 4, d % 4 * 2 * R, 2 * R), line(2, d * R, R), line(3 + d // 2, d % 2 * 4 * R, 4 * R)]
            + [line(row, d * R, R) for row in (7, 8, 9, 10, 11)], axis=0)
    for d in range(8):
        @pl.when(p.d != d)
        def _():
            link.copy(v_slots + d, vo.at[d], vl.at[p.d], ("d", d), land=v_slots + p.d).start()
    for event in (q[4][7], q[5][6]):
        event()
    vl[p.d] = vo[p.d]
    for d in range(8):
        @pl.when(p.d != d)
        def _():
            link.got(v_slots + d, vl.at[d])
    own = vl[0]
    for d in range(1, 8):
        own = own + vl[d]
    vz[p.z] = own
    for k in (1, 2, 3):
        link.send(v_slots + 8 + k, vz.at[p.z], vz.at[p.z], ("z", p.order[k]), lambda: vz.at[0], land=v_slots + 12 + p.z)
    q[5][7]()
    gp_out[...] = jnp.where(p.odd == 0, gpw[:, 0:576], gpw[:, 64:640])
    for k in (1, 2, 3):
        link.got(v_slots + 12 + p.order[k], vz.at[p.order[k]])
    vec_out[...] = vz[0] + vz[1] + vz[2] + vz[3]
    for d in range(8):
        @pl.when(p.d != d)
        def _():
            link.copy(v_slots + d, vo.at[d], vo.at[d], "x").wait_send()
    link.finish()
    for ending in ended:
        ending()
    out.wait()


def third_call(length, proj, qa, mixed, dm, n1, wp, x, dmiddle, ge, go, gc, vg, v):
    T, D = x.shape
    FF = ge.shape[1]
    R, Q, pairs = D // 8, FF // 4, H // 2
    vm = pltpu.VMEM
    n = 8 * 8 + 12 + 60 + 16
    return pl.pallas_call(
        third_kernel,
        in_specs=[SM] + [ANY] * 11 + [VM] * 2,
        out_specs=[ANY] + [VM] * 5,
        out_shape=[sds((T, D), BF), sds((R, 3 * D // 4), F32), sds((R, D // 4), F32), sds((R, Q), F32), sds((D // 4, FF // 8), F32),
                   sds((8, 384), F32)],
        scratch_shapes=[
            vm((T, 3 * D), BF), vm((H, T, 128), BF), vm((T, D), BF), vm((T, D), BF), vm((T, D), BF), vm((D, T), BF),
            vm((D, 3 * D), BF), vm((T, D), BF), vm((T, D), F32), vm((D, FF), BF), vm((8, 4, R, 256), BF),
            vm((T, 3 * D), BF), vm((T, D), BF), vm((pairs, 8, R, 384), BF),
            vm((2, T, 128), BF), vm((2, T, 128), BF), vm((2, 128, T), F32), vm((2, T, 128), BF), vm((2, 128, T), BF),
            vm((16, D), F32), vm((8, 8, 384), F32), vm((8, 8, 384), F32), vm((4, 8, 384), F32),
            vm((4, R, FF), BF), vm((R, FF // 2), BF), vm((R, FF // 2), BF), vm((R, FF), BF), vm((R, FF), BF), vm((4, R, Q), BF),
            vm((4, 4, R, 256), BF), vm((2, R, 256), BF), vm((2, R, 256), BF), vm((4, R, 256), BF), vm((4, R, 256), BF),
            vm((4, R, 256), BF),
            vm((pairs, 4, R, 384), BF), vm((pairs, R // 2, 384), BF), vm((pairs, R // 2, 384), BF),
            vm((pairs, R, 384), BF), vm((pairs, R, 384), BF), vm((20, 3, R, 128), BF), vm((R, 640), F32),
            vm((4, D // 4, FF // 8), BF), vm((4, D // 4, FF // 8), BF),
            pltpu.SemaphoreType.DMA((n,)), pltpu.SemaphoreType.DMA((n,)), pltpu.SemaphoreType.DMA((29,)),
        ],
        compiler_params=pltpu.CompilerParams(
            collective_id=2, has_side_effects=True, vmem_limit_bytes=63 << 20),
        name="third_part",
    )(length, proj, qa, mixed, dm, n1, wp, x, dmiddle, ge, go, gc, vg, v)


def last_kernel(block_in, tokens_in, p_in, o_in, e_in, c_in, vec_in,
                block_out, tokens_out, p_out, o_out, e_out, c_out, *rest):
    vectors, held, vec, sem = rest[:8], rest[8:14], rest[14], rest[15]
    parts = 2
    rows = block_in.shape[0] // parts
    whole = lambda ref: ref
    legs = []
    for i in range(parts):
        part = lambda ref, i=i: ref.at[pl.ds(i * rows, rows)]
        legs += [(part, block_in, held[0], block_out), (part, tokens_in, held[1], tokens_out)]
    legs += [(whole, a, b, c) for a, b, c in zip((p_in, o_in, e_in, c_in), held[2:], (p_out, o_out, e_out, c_out))]
    first = pltpu.make_async_copy(vec_in, vec, sem.at[2 * len(legs)])
    first.start()
    ins = [pltpu.make_async_copy(part(a), part(b), sem.at[k]) for k, (part, a, b, _) in enumerate(legs)]
    outs = [pltpu.make_async_copy(part(b), part(c), sem.at[len(legs) + k]) for k, (part, _, b, c) in enumerate(legs)]
    for made in ins:
        made.start()
    for came, goes in zip(ins, outs):
        came.wait()
        goes.start()
    first.wait()
    for at, target in enumerate(vectors):
        n = target.shape[0]
        target[...] = vec[at:at + 1, 0:n].reshape(n)
    for goes in outs:
        goes.wait()


def last_call(sizes, *arrays):
    return pl.pallas_call(
        last_kernel,
        in_specs=[ANY] * 7,
        out_specs=[ANY] * 6 + [VM] * 8,
        out_shape=[sds(item.shape, item.dtype) for item in arrays[:6]] + [sds((n,), F32) for n in sizes],
        scratch_shapes=[pltpu.VMEM(item.shape, item.dtype) for item in arrays] + [pltpu.SemaphoreType.DMA((17,))],
        compiler_params=pltpu.CompilerParams(vmem_limit_bytes=63 << 20),
        name="last_part",
    )(*arrays)


def per_device_fast(tokens, lengths, cotangent, project_weight, project_bias, output_weight, output_bias,
                    expand_weight, expand_bias, contract_weight, contract_bias, first_gain, first_shift,
                    second_gain, second_shift):
    vectors = (project_bias, output_bias, expand_bias, contract_bias, first_gain, first_shift, second_gain, second_shift)
    normed_one, projected, mixed, qa, full_project, full_output, full_expand, cc, v = first_call(
        lengths, tokens, project_weight, output_weight, expand_weight, contract_weight.T, vectors)
    block_out, grad_mixed, grad_middle, ge, go, gc, vg = second_call(
        lengths, tokens, cotangent, mixed, full_output, full_expand, cc, v)
    third = third_call(
        lengths, projected, qa, mixed, grad_mixed, normed_one, full_project, tokens, grad_middle, ge, go, gc, vg, v)
    out = last_call([item.shape[0] for item in vectors], block_out, *third)
    return (out[0], out[1], out[2], out[6], out[3], out[7], out[4], out[8], out[5].T, *out[9:])


def solution(mesh):
    both, rows, grid = P(("dp", "fsdp"), None), P("dp"), P("dp", "fsdp")
    weights = (grid, rows, grid, rows, grid, rows, grid, rows)
    fast = mesh.shape["dp"] == 8 and mesh.shape["fsdp"] == 4
    return jax.shard_map(
        per_device_fast if fast else per_device,
        mesh=mesh,
        in_specs=(both, P(("dp", "fsdp")), both) + weights + (rows,) * 4,
        out_specs=(both, both) + weights + (rows,) * 4,
        check_vma=False,
    )
```

```python
import functools
import jax
import jax.numpy as jnp
from jax import lax
from jax.experimental import pallas as pl
from jax.experimental.pallas import tpu as pltpu
from jax.sharding import PartitionSpec as P

H = 12
HD = 64
F32 = jnp.float32
BF = jnp.bfloat16
MESH = pl.DeviceIdType.MESH
eps_norm = 1e-05
neg_fill = -1000000000.0


def dot(first, second):
    return jnp.dot(first, second, preferred_element_type=F32)


def dot_nt(first, second):
    return lax.dot_general(first, second, (((1,), (1,)), ((), ())), preferred_element_type=F32)


def dot_tn(first, second):
    return lax.dot_general(first, second, (((0,), (0,)), ((), ())), preferred_element_type=F32)


def mo(value, multiple):
    return pl.multiple_of(value, multiple)


class Place:
    def __init__(self):
        self.d = lax.axis_index("dp")
        self.z = lax.axis_index("fsdp")
        core = lax.rem(self.d, 2)
        across = lax.rem(lax.div(self.d, 2), 2)
        up = lax.div(self.d, 4)
        self.dc = self.d + 1 - 2 * core
        self.dx = self.d + 2 - 4 * across
        self.dy = self.d + 4 - 8 * up
        self.dd = self.dx + 4 - 8 * up
        self.odd = lax.rem(self.z, 2)
        z = self.z
        pick = lambda a, b, c, d: jnp.where(z < 2, jnp.where(z == 0, a, b), jnp.where(z == 2, c, d))
        self.order = [z, pick(1, 0, 3, 2), pick(2, 2, 1, 1), pick(3, 3, 0, 0)]

    def zt(self, step):
        return lax.rem(self.z + step, 4)

    def zf(self, step):
        return lax.rem(self.z + 4 - step, 4)

    def id(self, to):
        if to == "x":
            return (self.dx, self.z)
        if to == "y":
            return (self.dy, self.z)
        if to == "c":
            return (self.dc, self.z)
        if isinstance(to, tuple):
            return (to[1], self.z) if to[0] == "d" else (self.d, to[1])
        return (self.d, self.zt(to))


def enter(place, wide=False):
    barrier = pltpu.get_barrier_semaphore()
    sib = place.dc - place.d
    others = [("d", d + sib) for d in (place.dx, place.dy, place.dd)] + [("d", place.dd)] if wide else []
    partners = ["x", "y", "c", 1, 2, 3] + others
    for to in partners:
        pl.semaphore_signal(barrier, inc=1, device_id=place.id(to), device_id_type=MESH)
    pl.semaphore_wait(barrier, len(partners))


class Link:
    def __init__(self, place, send_sem, recv_sem):
        self.place, self.send_sem, self.recv_sem = place, send_sem, recv_sem
        self.count = 0
        self.copies = []

    def slot(self, many=1):
        self.count += many
        return self.count - many

    def copy(self, slot, source, target, to, land=None):
        return pltpu.make_async_remote_copy(
            src_ref=source, dst_ref=target, send_sem=self.send_sem.at[slot],
            recv_sem=self.recv_sem.at[slot if land is None else land], device_id=self.place.id(to),
            device_id_type=MESH)

    def send(self, slot, source, target, to, like, land=None, when=None):
        def start():
            self.copy(slot, source, target, to, land).start()

        if when is None:
            start()
        else:
            pl.when(when())(start)
        self.copies.append((slot, like, when))

    def got(self, slot, target):
        self.copy(slot, target, target, "x").wait_recv()

    def finish(self):
        for slot, like, when in self.copies:
            def done(slot=slot, like=like):
                view = like()
                self.copy(slot, view, view, "x").wait_send()

            if when is None:
                done()
            else:
                pl.when(when())(done)


class Gather:
    def __init__(self, link, place, block):
        p = place
        zr, zs = link.slot(4), link.slot(4)
        xs, ys, fx = link.slot(4), link.slot(4), link.slot(4)
        cs = link.slot(16)
        got = link.got
        send = functools.partial(link.send, like=lambda: block(0, 0))

        def z_step(a):
            def run():
                if a == 0:
                    own = block(p.z, p.d)
                    for k in (1, 2, 3):
                        send(zs + k, own, own, ("z", p.order[k]), land=zr + p.z)
                else:
                    got(zr + p.order[a], block(p.order[a], p.d))
            return run

        def x_step(a):
            def run():
                here = block(p.order[a], p.d)
                send(xs + a, here, here, "x")
                send(ys + a, here, here, "y")
                send(cs + a, here, here, "c")
            return run

        def turn(a):
            def run():
                b = p.order[a]
                bx, by = block(b, p.dx), block(b, p.dy)
                got(xs + a, bx)
                got(ys + a, by)
                if a in (0, 1):
                    send(fx + a, bx, bx, "y")
                else:
                    send(fx + a, by, by, "x")
                send(cs + 4 + a, bx, bx, "c")
                send(cs + 8 + a, by, by, "c")
            return run

        def corner(a):
            def run():
                bd = block(p.order[a], p.dd)
                got(fx + a, bd)
                send(cs + 12 + a, bd, bd, "c")
            return run

        def close():
            sib = p.dc - p.d
            for which, d in enumerate((p.d, p.dx, p.dy, p.dd)):
                for a in range(4):
                    got(cs + 4 * which + a, block(p.order[a], d + sib))

        self.z, self.x, self.t, self.q = ([make(a) for a in range(4)] for make in (z_step, x_step, turn, corner))
        self.close = close


def spread_z(link, place, ref):
    p = place
    zs, zr = link.slot(3), link.slot(4)

    def send():
        for k in (1, 2, 3):
            link.send(zs + k - 1, ref.at[p.z], ref.at[p.z], ("z", p.order[k]), lambda: ref.at[0], land=zr + p.z)

    def wait():
        for k in (1, 2, 3):
            b = p.order[k]
            link.got(zr + b, ref.at[b])

    return send, wait


def run(*events):
    def together():
        for event in events:
            event()
    return together


def window(value, odd, wide):
    rows, k = value.shape
    fill = jnp.zeros((rows, wide - k), F32)
    value = value.astype(F32)
    left = jnp.concatenate([value, fill], axis=1)
    right = jnp.concatenate([fill, value], axis=1)
    return jnp.where(odd == 0, left, right).astype(BF)


def merge_windows(blocks, full, tiles, rows_step):
    rows = full.shape[0]
    half = tiles // 2

    def body(i, _):
        r = pl.ds(mo(i * rows_step, rows_step), rows_step)
        for pair in range(2):
            even, odd = blocks.at[2 * pair], blocks.at[2 * pair + 1]
            base = pair * tiles * 128
            full[r, base:base + half * 128] = even[r, 0:half * 128]
            full[r, base + half * 128:base + (half + 1) * 128] = (
                even[r, half * 128:(half + 1) * 128] + odd[r, 0:128])
            full[r, base + (half + 1) * 128:base + tiles * 128] = odd[r, 128:(half + 1) * 128]
        return 0

    lax.fori_loop(0, rows // rows_step, body, 0)


def split3(value):
    high = value.astype(BF)
    rest = value - high.astype(F32)
    mid = rest.astype(BF)
    low = (rest - mid.astype(F32)).astype(BF)
    return high.astype(F32), mid.astype(F32), low.astype(F32)


def extend(head, pair, lane, one, two, three, four):
    base = 64 * (1 - head)
    extra = jnp.where(lane == base, one, jnp.where(lane == base + 1, two, jnp.where(
        lane == base + 2, three, jnp.where(lane == base + 3, four, 0.0))))
    keep = (lane < 64) if head == 0 else (lane >= 64)
    return jnp.where(keep, pair, extra).astype(BF)


def iota(shape, axis):
    return lax.broadcasted_iota(jnp.int32, shape, axis)


QB = 256


def first_kernel(length_ref, x_ref, wp_ref, wo_ref, we_ref, wc_ref, *refs):
    vec_refs, refs = refs[:8], refs[8:]
    first_body(length_ref, x_ref, wp_ref, wo_ref, we_ref, wc_ref, vec_refs, *refs)


def first_body(length_ref, x_ref, wp_ref, wo_ref, we_ref, wc_ref, vec_refs,
                 n1_out, proj_out, mixed_out, qa_out, wp_out, wo_out, we_out, c_out, v_out,
                 wp_blk, wo_blk, we, wp, wo, vb, n1, proj, mixed, qa, ka, va, vrow, cc,
                 send_sem, recv_sem, out_sem, pair_sem):
    p = Place()
    T, D = x_ref.shape
    R = wp_ref.shape[0]
    FF = we.shape[1]
    link = Link(p, send_sem, recv_sem)
    rows_of = lambda d: pl.ds(mo(d * R, 16), R)
    half = R // 2
    bpa = lambda z, d: wp_blk.at[z, pl.ds(mo(d * R, 16), half), :]
    bpb = lambda z, d: wp_blk.at[z, pl.ds(mo(d * R + half, 16), half), :]
    bo = lambda z, d: wo_blk.at[z, rows_of(d), :]
    be = lambda z, d: we.at[rows_of(d), pl.ds(mo(z * (FF // 4), 128), FF // 4)]
    g0, g1, go, ge = (Gather(link, p, b) for b in (bpa, bpb, bo, be))
    c_send, c_wait = spread_z(link, p, cc)
    vs = [link.slot() for _ in range(7)]

    wp_blk[p.z, rows_of(p.d), :] = window(wp_ref[...], p.odd, wp_blk.shape[2])
    wo_blk[p.z, rows_of(p.d), :] = window(wo_ref[...], p.odd, wo_blk.shape[2])
    we[rows_of(p.d), pl.ds(mo(p.z * (FF // 4), 128), FF // 4)] = we_ref[...]
    cc[p.z] = wc_ref[...]
    for i, ref in enumerate(vec_refs):
        vb[p.d, i:i + 1, 0:ref.shape[0]] = ref[...].astype(F32).reshape(1, ref.shape[0]).astype(BF)

    outs = []

    def out(source, target):
        made = pltpu.make_async_copy(source, target, out_sem.at[len(outs)])
        made.start()
        outs.append(made)

    enter(p)
    send_v = lambda slot, d, to: link.send(vs[slot], vb.at[d], vb.at[d], to, lambda: vb.at[0])
    for slot, to in ((0, "x"), (1, "y"), (3, "c")):
        send_v(slot, p.d, to)
    run(g0.z[0], g0.x[0], g1.z[0], g1.x[0])()
    link.got(vs[0], vb.at[p.dx])
    link.got(vs[1], vb.at[p.dy])
    send_v(2, p.dx, "y")
    send_v(4, p.dx, "c")
    send_v(5, p.dy, "c")
    run(g0.z[1], g0.x[1], g0.t[0], g1.t[0], g0.z[2], g0.x[2])()
    link.got(vs[2], vb.at[p.dd])
    send_v(6, p.dd, "c")
    sib = p.dc - p.d
    for slot, d in ((3, p.d), (4, p.dx), (5, p.dy), (6, p.dd)):
        link.got(vs[slot], vb.at[d + sib])
    got = vb[...].astype(F32)
    side = lambda row, wide: jnp.concatenate([got[i, row:row + 1, 0:wide] for i in range(8)], axis=1)
    bias = side(0, 2 * R)
    vrow[0:1, 0:D] = bias[:, 0:D]
    vrow[0:1, D:2 * D] = jnp.zeros((1, D), F32)
    vrow[0:1, 2 * D:3 * D] = bias[:, D:]
    vrow[1:2, :] = side(2, FF // 8)
    for row, at in ((2, 1), (3, 3), (4, 4), (5, 5), (6, 6), (7, 7)):
        vrow[row:row + 1, 0:D] = side(at, R)
    out(vrow, v_out)
    run(g0.t[1], g0.z[3], g0.x[3], g0.q[0], g1.z[1], g1.x[1], g1.q[0])()

    LR = 128
    gain, shift = vrow[4:5, 0:D], vrow[5:6, 0:D]

    def norm_body(i, _):
        r = pl.ds(mo(i * LR, LR), LR)
        value = x_ref[r, :].astype(F32)
        u = value - jnp.mean(value, axis=-1, keepdims=True)
        spread = jnp.mean(u * u, axis=-1, keepdims=True)
        n1[r, :] = (u * lax.rsqrt(spread + eps_norm) * gain + shift).astype(BF)
        return 0

    norm_part = lambda k: lax.fori_loop(k * (T // LR // 4), (k + 1) * (T // LR // 4), norm_body, 0)
    g0.t[2]()
    norm_part(0)
    run(g1.z[2], g1.x[2], g0.q[1])()
    norm_part(1)
    run(g1.z[3], g1.x[3], ge.z[0], go.z[0], g0.t[3])()
    norm_part(2)
    run(g0.q[2], g1.t[1])()
    norm_part(3)
    run(g1.t[2], g1.t[3], ge.x[0], g0.q[3], g1.q[1], g1.q[2], g1.q[3], go.x[0])()
    out(n1, n1_out)
    run(g0.close, g1.close)()
    merge_windows(wp_blk, wp, 9, 96)
    out(wp, wp_out)
    run(ge.z[1], ge.x[1])()

    def project_body(i, _):
        for at, event in ((2, run(ge.z[2], ge.x[2], ge.t[0])), (3, go.t[0])):
            pl.when(i == at)(event)
        r = pl.ds(mo(i * 256, 256), 256)
        left = n1[r, :]
        for j in range(3):
            cols = slice(j * D, (j + 1) * D)
            value = dot(left, wp[:, cols]) + vrow[0:1, cols]
            proj[r, cols] = value.astype(BF)
        return 0

    lax.fori_loop(0, T // 256, project_body, 0)
    out(proj, proj_out)

    length = length_ref[0]
    subs = T // QB

    def pair_outs(pair):
        heads = pl.ds(2 * pair, 2)
        cols = pl.ds(mo(pair * 128, 128), 128)
        return (pltpu.make_async_copy(qa.at[heads], qa_out.at[heads], pair_sem.at[pair, 0]),
                pltpu.make_async_copy(mixed.at[:, cols], mixed_out.at[:, cols], pair_sem.at[pair, 1]))

    def attend_steps(events):
        def body(pair, _):
            for at, event in events:
                pl.when(pair == at)(event)
            cols = lambda off: pl.ds(mo(off + pair * 128, 128), 128)
            lane, row = iota((T, 128), 1), iota((T, 128), 0)
            q = proj[:, cols(0)].astype(F32) * (HD ** -0.5)
            k = proj[:, cols(D)].astype(F32)
            v = proj[:, cols(2 * D)].astype(F32)
            dead = jnp.where(row < length, 0.0, neg_fill)
            for head in range(2):
                ka[head] = extend(head, k, lane, 1.0, 1.0, 1.0, dead)
                qa[pair * 2 + head] = extend(head, q, lane, 0.0, 0.0, 0.0, 1.0)
                keep = (lane < 64) if head == 0 else (lane >= 64)
                va[head] = jnp.where(keep, v, 1.0).astype(BF)
            sub_lane = iota((QB, 128), 1)
            items = [(head, pl.ds(i * QB, QB)) for i in range(subs) for head in range(2)]
            halves = {}

            def scores(n):
                head, r = items[n]
                return dot_nt(qa[pair * 2 + head, r, :], ka[head])

            def soften(value):
                top = jnp.max(value, axis=-1, keepdims=True)
                return top, jnp.exp(value - top).astype(BF)

            def finish(n, top, powers):
                head, r = items[n]
                value = dot(powers, va[head])
                total = value[:, 64:65] if head == 0 else value[:, 0:1]
                one, two, three = split3(-(top + jnp.log(total)))
                query = qa[pair * 2 + head, r, :].astype(F32)
                qa[pair * 2 + head, r, :] = extend(head, query, sub_lane, one, two, three, 1.0)
                halves[n] = value * (1.0 / total)
                if head == 1:
                    mixed[r, cols(0)] = jnp.where(sub_lane < 64, halves[n - 1], halves[n]).astype(BF)

            value, waiting = scores(0), None
            for n in range(len(items)):
                following = scores(n + 1) if n + 1 < len(items) else None
                soft = soften(value)
                if waiting is not None:
                    finish(n - 1, *waiting)
                value, waiting = following, soft
            finish(len(items) - 1, *waiting)
            for made in pair_outs(pair):
                made.start()
            return 0

        lax.fori_loop(0, H // 2, body, 0)

    attend_steps([(1, run(go.z[1], go.x[1], ge.z[3], ge.x[3], go.z[2], go.x[2], ge.t[1])),
                  (2, run(go.z[3], go.x[3], ge.t[2], c_send)), (3, run(ge.q[0], go.t[1], go.q[0])),
                  (4, run(ge.t[3], go.t[2])), (5, run(ge.q[1], ge.q[2], go.t[3]))])
    run(ge.q[3], go.q[1], go.q[2], go.q[3], go.close)()
    merge_windows(wo_blk, wo, 3, 96)
    out(wo, wo_out)
    ge.close()
    out(we, we_out)
    c_wait()
    out(cc, c_out)
    link.finish()
    for made in outs:
        made.wait()
    for pair in range(H // 2):
        for made in pair_outs(pair):
            made.wait()


def first_call(length, x, wp, wo, we, wc, vectors):
    T, D = x.shape
    FF = we.shape[1] * 4
    ANY = pl.BlockSpec(memory_space=pl.ANY)
    V = pl.BlockSpec(memory_space=pltpu.VMEM)
    S = pl.BlockSpec(memory_space=pltpu.SMEM)
    sds = jax.ShapeDtypeStruct
    n = 4 * 36 + 7 + 7
    return pl.pallas_call(
        first_kernel,
        in_specs=[S] + [V] * 13,
        out_specs=[ANY] * 9,
        out_shape=[sds((T, D), BF), sds((T, 3 * D), BF), sds((T, D), BF), sds((H, T, 128), BF),
                   sds((D, 3 * D), BF), sds((D, D), BF), sds((D, FF), BF), sds((4,) + wc.shape, BF), sds((8, FF), F32)],
        scratch_shapes=[
            pltpu.VMEM((4, D, 640), BF), pltpu.VMEM((4, D, 256), BF), pltpu.VMEM((D, FF), BF),
            pltpu.VMEM((D, 3 * D), BF), pltpu.VMEM((D, D), BF), pltpu.VMEM((8, 16, FF // 8), BF),
            pltpu.VMEM((T, D), BF), pltpu.VMEM((T, 3 * D), BF), pltpu.VMEM((T, D), BF),
            pltpu.VMEM((H, T, 128), BF), pltpu.VMEM((2, T, 128), BF), pltpu.VMEM((2, T, 128), BF),
            pltpu.VMEM((8, FF), F32), pltpu.VMEM((4,) + wc.shape, BF),
            pltpu.SemaphoreType.DMA((n,)), pltpu.SemaphoreType.DMA((n,)), pltpu.SemaphoreType.DMA((9,)), pltpu.SemaphoreType.DMA((H // 2, 2)),
        ],
        compiler_params=pltpu.CompilerParams(
            collective_id=0, has_side_effects=True, vmem_limit_bytes=60 << 20),
        name="first_part",
    )(length, x, wp, wo, we, wc, *vectors)


def layer_norm(values, gain_row, shift_row):
    centre = jnp.mean(values, axis=-1, keepdims=True)
    centred = values - centre
    spread = jnp.mean(centred * centred, axis=-1, keepdims=True)
    return centred * lax.rsqrt(spread + eps_norm) * gain_row + shift_row


def gelu_exact(values):
    return jax.nn.gelu(values, approximate=False)


def matmul(first, second):
    return jnp.dot(first, second, preferred_element_type=jnp.float32)


def over_rows(first, second):
    return lax.dot_general(
        first, second, (((0,), (0,)), ((), ())), preferred_element_type=jnp.float32
    )


def over_columns(first, second):
    return lax.dot_general(
        first, second, (((1,), (1,)), ((), ())), preferred_element_type=jnp.float32
    )


def fetch_forward(
    project_weight,
    output_weight,
    expand_weight,
    contract_weight,
    project_bias,
    output_bias,
    expand_bias,
    contract_bias,
    first_gain,
    first_shift,
    second_gain,
    second_shift,
):
    wide_project, wide_output, wide_expand, wide_contract = (
        lax.all_gather(project_weight, "fsdp", axis=1, tiled=True),
        lax.all_gather(output_weight, "fsdp", axis=1, tiled=True),
        lax.all_gather(expand_weight, "fsdp", axis=1, tiled=True),
        lax.all_gather(contract_weight, "fsdp", axis=1, tiled=True),
    )
    return (
        lax.all_gather(wide_project, "dp", axis=0, tiled=True),
        lax.all_gather(wide_output, "dp", axis=0, tiled=True),
        lax.all_gather(wide_expand, "dp", axis=0, tiled=True),
        lax.all_gather(wide_contract, "dp", axis=0, tiled=True),
        lax.all_gather(project_bias, "dp", axis=0, tiled=True),
        lax.all_gather(output_bias, "dp", axis=0, tiled=True),
        lax.all_gather(expand_bias, "dp", axis=0, tiled=True),
        lax.all_gather(contract_bias, "dp", axis=0, tiled=True),
        lax.all_gather(first_gain, "dp", axis=0, tiled=True),
        lax.all_gather(first_shift, "dp", axis=0, tiled=True),
        lax.all_gather(second_gain, "dp", axis=0, tiled=True),
        lax.all_gather(second_shift, "dp", axis=0, tiled=True),
    )


def fetch_backward(
    project_weight,
    output_weight,
    expand_weight,
    contract_weight,
    project_bias,
    output_bias,
    expand_bias,
    contract_bias,
    first_gain,
    first_shift,
    second_gain,
    second_shift,
):
    wide_project, wide_output, wide_expand, wide_contract = (
        lax.all_gather(project_weight, "fsdp", axis=1, tiled=True),
        lax.all_gather(output_weight, "fsdp", axis=1, tiled=True),
        lax.all_gather(expand_weight, "fsdp", axis=1, tiled=True),
        lax.all_gather(contract_weight, "fsdp", axis=1, tiled=True),
    )
    return (
        lax.all_gather(wide_project, "dp", axis=0, tiled=True),
        lax.all_gather(wide_output, "dp", axis=0, tiled=True),
        lax.all_gather(wide_expand, "dp", axis=0, tiled=True),
        lax.all_gather(wide_contract, "dp", axis=0, tiled=True),
        lax.all_gather(project_bias, "dp", axis=0, tiled=True),
        lax.all_gather(output_bias, "dp", axis=0, tiled=True),
        lax.all_gather(expand_bias, "dp", axis=0, tiled=True),
        lax.all_gather(contract_bias, "dp", axis=0, tiled=True),
        lax.all_gather(first_gain, "dp", axis=0, tiled=True),
        lax.all_gather(first_shift, "dp", axis=0, tiled=True),
        lax.all_gather(second_gain, "dp", axis=0, tiled=True),
        lax.all_gather(second_shift, "dp", axis=0, tiled=True),
    )


def split_heads(cell_rows, block_rows):
    slot_count = cell_rows.shape[0]
    width = cell_rows.shape[1] // 3
    query_blocks = cell_rows[:, :width].reshape(slot_count // block_rows, block_rows, H, HD)
    keys_all = cell_rows[:, width : 2 * width].reshape(slot_count, H, HD)
    values_all = cell_rows[:, 2 * width :].reshape(slot_count, H, HD)
    return (query_blocks, keys_all, values_all)


def block_scores(query_block, keys_all, key_live):
    scores = jnp.einsum(
        "qhe,khe->hqk", query_block, keys_all, preferred_element_type=jnp.float32
    ) * HD ** (-0.5)
    return jnp.where(key_live[None, None, :], scores, neg_fill)


def attend_forward(query_block, keys_all, values_all, key_live):
    scores = block_scores(query_block, keys_all, key_live)
    row_max = jnp.max(scores, axis=-1, keepdims=True)
    powers = jnp.exp(scores - row_max)
    row_total = jnp.sum(powers, axis=-1, keepdims=True)
    weights = (powers / row_total).astype(jnp.bfloat16)
    mixed_block = jnp.einsum(
        "hqk,khe->qhe", weights, values_all, preferred_element_type=jnp.float32
    )
    return (mixed_block, (row_max + jnp.log(row_total))[:, :, 0])


def attend_backward(query_block, grad_block, log_block, keys_all, values_all, key_live):
    scores = block_scores(query_block, keys_all, key_live)
    weights = jnp.exp(scores - log_block[:, :, None])
    grad_weights = jnp.einsum(
        "qhe,khe->hqk", grad_block, values_all, preferred_element_type=jnp.float32
    )
    row_inner = jnp.sum(grad_weights * weights, axis=-1, keepdims=True)
    grad_scores = (weights * (grad_weights - row_inner)).astype(jnp.bfloat16)
    grad_query = jnp.einsum(
        "hqk,khe->qhe", grad_scores, keys_all, preferred_element_type=jnp.float32
    ) * HD ** (-0.5)
    grad_key = jnp.einsum(
        "hqk,qhe->khe", grad_scores, query_block, preferred_element_type=jnp.float32
    ) * HD ** (-0.5)
    grad_value = jnp.einsum(
        "hqk,qhe->khe", weights.astype(jnp.bfloat16), grad_block, preferred_element_type=jnp.float32
    )
    return (grad_query, grad_key, grad_value)


def per_device(
    tokens,
    lengths,
    cotangent,
    project_weight,
    project_bias,
    output_weight,
    output_bias,
    expand_weight,
    expand_bias,
    contract_weight,
    contract_bias,
    first_gain,
    first_shift,
    second_gain,
    second_shift,
):
    fetched = fetch_forward(
        project_weight,
        output_weight,
        expand_weight,
        contract_weight,
        project_bias,
        output_bias,
        expand_bias,
        contract_bias,
        first_gain,
        first_shift,
        second_gain,
        second_shift,
    )
    full_project, full_output, full_expand, full_contract = (
        fetched[0],
        fetched[1],
        fetched[2],
        fetched[3],
    )
    vectors = [item.astype(jnp.float32) for item in fetched[4:]]
    bias_project, bias_output, bias_expand, bias_contract = (
        vectors[0],
        vectors[1],
        vectors[2],
        vectors[3],
    )
    gain_one, shift_one, gain_two, shift_two = (vectors[4], vectors[5], vectors[6], vectors[7])
    cell_count = lengths.shape[0]
    slot_count = tokens.shape[0] // cell_count
    width = tokens.shape[1]
    block_rows = min(512, slot_count)
    positions = jnp.arange(slot_count, dtype=jnp.int32)
    live_keys = positions[None, :] < lengths[:, None]
    live_rows = live_keys.reshape(-1)
    rows_in = tokens.astype(jnp.float32)
    normed_one = layer_norm(rows_in, gain_one, shift_one).astype(jnp.bfloat16)
    bias_full = jnp.concatenate(
        [bias_project[:width], jnp.zeros((width,), jnp.float32), bias_project[width:]]
    )
    projected = (matmul(normed_one, full_project) + bias_full).astype(jnp.bfloat16)
    cell_index = 0
    query_blocks, keys_all, values_all = split_heads(projected, block_rows)
    key_live = live_keys[cell_index]
    mixed_blocks, log_blocks = lax.map(
        lambda query_block: attend_forward(query_block, keys_all, values_all, key_live),
        query_blocks,
    )
    mixed_list = mixed_blocks.reshape(slot_count, width)
    log_list = [log_blocks]
    mixed_low = mixed_list.astype(jnp.bfloat16)
    middle = rows_in + (matmul(mixed_low, full_output) + bias_output)
    normed_two = layer_norm(middle, gain_two, shift_two).astype(jnp.bfloat16)
    hidden = matmul(normed_two, full_expand) + bias_expand
    active = gelu_exact(hidden).astype(jnp.bfloat16)
    result = middle + (matmul(active, full_contract) + bias_contract)
    block_out = jnp.where(live_rows[:, None], result, 0.0).astype(jnp.bfloat16)
    again = fetch_backward(
        project_weight,
        output_weight,
        expand_weight,
        contract_weight,
        project_bias,
        output_bias,
        expand_bias,
        contract_bias,
        first_gain,
        first_shift,
        second_gain,
        second_shift,
    )
    back_project, back_output, back_expand, back_contract = (again[0], again[1], again[2], again[3])
    grad_out = jnp.where(live_rows[:, None], cotangent.astype(jnp.float32), 0.0)
    grad_out_low = grad_out.astype(jnp.bfloat16)
    grad_contract = over_rows(active, grad_out_low)
    grad_contract_bias = jnp.sum(grad_out, axis=0)
    grad_active = over_columns(grad_out_low, back_contract)
    gelu_value, gelu_pull = jax.vjp(gelu_exact, hidden)
    grad_hidden = gelu_pull(grad_active)[0].astype(jnp.bfloat16)
    grad_expand = over_rows(normed_two, grad_hidden)
    grad_expand_bias = jnp.sum(grad_hidden.astype(jnp.float32), axis=0)
    grad_normed_two = over_columns(grad_hidden, back_expand)
    norm_value, second_pull = jax.vjp(layer_norm, middle, gain_two, shift_two)
    grad_middle, grad_gain_two, grad_shift_two = second_pull(grad_normed_two)
    grad_middle = grad_middle + grad_out
    grad_branch = grad_middle.astype(jnp.bfloat16)
    grad_output = over_rows(mixed_low, grad_branch)
    grad_output_bias = jnp.sum(grad_branch.astype(jnp.float32), axis=0)
    grad_mixed = over_columns(grad_branch, back_output).astype(jnp.bfloat16)
    cell_index = 0
    query_blocks, keys_all, values_all = split_heads(projected, block_rows)
    key_live = live_keys[cell_index]
    grad_blocks = grad_mixed.reshape(slot_count // block_rows, block_rows, H, HD)

    def visit_block(carried, inputs):
        query_block, grad_block, log_block = inputs
        grad_query, grad_key, grad_value = attend_backward(
            query_block, grad_block, log_block, keys_all, values_all, key_live
        )
        return ((carried[0] + grad_key, carried[1] + grad_value), grad_query)

    initial = (
        jnp.zeros((slot_count, H, HD), jnp.float32),
        jnp.zeros((slot_count, H, HD), jnp.float32),
    )
    (key_sums, value_sums), query_grads = lax.scan(
        visit_block, initial, (query_blocks, grad_blocks, log_list[cell_index])
    )
    grad_cells = jnp.concatenate(
        [
            query_grads.reshape(slot_count, width),
            key_sums.reshape(slot_count, width),
            value_sums.reshape(slot_count, width),
        ],
        axis=1,
    )
    grad_projected = grad_cells.astype(jnp.bfloat16)
    grad_project = over_rows(normed_one, grad_projected)
    column_sums = jnp.sum(grad_projected.astype(jnp.float32), axis=0)
    grad_project_bias = jnp.concatenate([column_sums[:width], column_sums[2 * width :]])
    grad_normed_one = over_columns(grad_projected, back_project)
    first_value, first_pull = jax.vjp(layer_norm, rows_in, gain_one, shift_one)
    grad_rows_in, grad_gain_one, grad_shift_one = first_pull(grad_normed_one)
    tokens_grad = (grad_rows_in + grad_middle).astype(jnp.bfloat16)
    reduced = (
        lax.psum_scatter(grad_project, "dp", scatter_dimension=0, tiled=True),
        lax.psum_scatter(grad_output, "dp", scatter_dimension=0, tiled=True),
        lax.psum_scatter(grad_expand, "dp", scatter_dimension=0, tiled=True),
        lax.psum_scatter(grad_contract, "dp", scatter_dimension=0, tiled=True),
        lax.psum_scatter(grad_project_bias, "dp", scatter_dimension=0, tiled=True),
        lax.psum_scatter(grad_output_bias, "dp", scatter_dimension=0, tiled=True),
        lax.psum_scatter(grad_expand_bias, "dp", scatter_dimension=0, tiled=True),
        lax.psum_scatter(grad_contract_bias, "dp", scatter_dimension=0, tiled=True),
        lax.psum_scatter(grad_gain_one, "dp", scatter_dimension=0, tiled=True),
        lax.psum_scatter(grad_shift_one, "dp", scatter_dimension=0, tiled=True),
        lax.psum_scatter(grad_gain_two, "dp", scatter_dimension=0, tiled=True),
        lax.psum_scatter(grad_shift_two, "dp", scatter_dimension=0, tiled=True),
    )
    shard_project, shard_output, shard_expand, shard_contract = (
        lax.psum_scatter(
            reduced[0].astype(jnp.bfloat16), "fsdp", scatter_dimension=1, tiled=True
        ).astype(jnp.float32),
        lax.psum_scatter(
            reduced[1].astype(jnp.bfloat16), "fsdp", scatter_dimension=1, tiled=True
        ).astype(jnp.float32),
        lax.psum_scatter(
            reduced[2].astype(jnp.bfloat16), "fsdp", scatter_dimension=1, tiled=True
        ).astype(jnp.float32),
        lax.psum_scatter(
            reduced[3].astype(jnp.bfloat16), "fsdp", scatter_dimension=1, tiled=True
        ).astype(jnp.float32),
    )
    summed = lax.psum(
        (
            reduced[4],
            reduced[5],
            reduced[6],
            reduced[7],
            reduced[8],
            reduced[9],
            reduced[10],
            reduced[11],
        ),
        "fsdp",
    )
    return (
        block_out,
        tokens_grad,
        shard_project,
        summed[0],
        shard_output,
        summed[1],
        shard_expand,
        summed[2],
        shard_contract,
        summed[3],
        summed[4],
        summed[5],
        summed[6],
        summed[7],
    )


def scatter_events(link, place, col, pair_of, lc, lxh, lyh, lx, ly):
    p = place
    family = (p.dc, p.dx + p.dc - p.d, p.dy + p.dc - p.d, p.dd + p.dc - p.d)
    cs = [link.slot() for _ in range(4)]
    hx, hy, fx, fy = (link.slot() for _ in range(4))
    got = link.got

    def add(target, *terms):
        flat = len(target.shape) == 2

        def body(i, _):
            at = (pl.ds(mo(i * 16, 16), 16), slice(None)) if flat else (i,)
            total = target[at].astype(F32)
            for term in terms:
                total = total + term[at].astype(F32)
            target[at] = total.astype(BF)
            return 0

        lax.fori_loop(0, target.shape[0] // 16 if flat else target.shape[0], body, 0)

    def to_sibling(which):
        link.send(cs[which], col(family[which]), lc.at[which], "c", lambda: col(0))

    def halves():
        got(cs[3], lc.at[3])
        add(col(p.dd), lc.at[3])
        link.send(hx, pair_of(col(p.dd), 0), lxh, "x", lambda: lxh)
        link.send(hy, pair_of(col(p.dd), 1), lyh, "y", lambda: lyh)

    def near():
        got(cs[1], lc.at[1])
        got(cs[2], lc.at[2])
        add(col(p.dx), lc.at[1])
        add(col(p.dy), lc.at[2])

    def pass_y():
        got(hx, lxh)
        add(pair_of(col(p.dy), 0), lxh)
        link.send(fy, col(p.dy), ly, "y", lambda: ly)

    def pass_x():
        got(hy, lyh)
        add(pair_of(col(p.dx), 1), lyh)
        link.send(fx, col(p.dx), lx, "x", lambda: lx)

    def own():
        got(cs[0], lc.at[0])

    def total():
        got(fx, lx)
        got(fy, ly)
        add(col(p.d), lc.at[0], lx, ly)

    return to_sibling, [halves, near, pass_y, pass_x, own, total]


def z_sum(link, place, block, lz, finish):
    p = place
    zs = link.slot(4)

    def send():
        for step in (1, 3, 2):
            link.send(zs + step, block(p.zt(step)), lz.at[step], step, lambda: lz.at[0])

    def last():
        total = block(p.z)[...].astype(F32)
        for step in (1, 3, 2):
            link.got(zs + step, lz.at[step])
            total = total + lz[step].astype(F32)
        finish(total)

    return send, last


def gelu_pair(value):
    lift = 0.5 * (1.0 + lax.erf(value * 0.7071067811865476))
    bell = jnp.exp(value * value * -0.5) * 0.3989422804014327
    return value * lift, lift + value * bell


def second_kernel(length_ref, x_hbm, cot_hbm, mixed_hbm, wo_hbm, we_hbm, c_hbm, v_ref,
                  block_out, dmixed_out, dmiddle_out, ge_out, go_out, gc_out, vg_out,
                  x_ref, cot_ref, mixed_ref, wo_ref, we, wct, act, slope, middle, n2t, dot_t, mixed_t, dbranch, dout, gc, go, dmixed, bout, vg,
                  lc, lxh, lyh, lx, ly, send_sem, recv_sem, out_sem):
    p = Place()
    T, D = x_ref.shape
    FF = we.shape[1]
    R = D // 8
    Q = FF // 4
    C8 = FF // 8
    link = Link(p, send_sem, recv_sem)
    bc = lambda z, d: wct.at[pl.ds(mo(z * (D // 4), 16), D // 4), pl.ds(mo(d * C8, 128), C8)]
    gather = Gather(link, p, bc)

    to_sibling, scatter = scatter_events(
        link, p, lambda d: gc.at[d], lambda ref, h: ref.at[pl.ds(2 * h, 2)], lc, lxh, lyh, lx, ly)
    load = pltpu.make_async_copy(we_hbm, we, out_sem.at[0])
    columns = [pltpu.make_async_copy(c_hbm.at[z], bc(z, p.d), out_sem.at[19 + z]) for z in range(4)]
    for made in columns:
        made.start()
    halves = [pl.ds(i * (T // 2), T // 2) for i in range(2)]
    early = [[pltpu.make_async_copy(wo_hbm, wo_ref, out_sem.at[12])], []]
    for i, r in enumerate(halves):
        for at, (a, b) in enumerate(((mixed_hbm, mixed_ref), (x_hbm, x_ref), (cot_hbm, cot_ref))):
            early[i].append(pltpu.make_async_copy(a.at[r], b.at[r], out_sem.at[13 + 3 * i + at]))
    for made in early[0] + early[1]:
        made.start()
    enter(p)
    for made in columns:
        made.wait()
    run(*gather.x)()
    for made in early[0] + early[1]:
        made.wait()
    load.start()
    length = length_ref[0]
    LR = 256
    rows = lambda i: pl.ds(mo(i * LR, LR), LR)
    vec = lambda i: v_ref[i:i + 1, 0:D]
    vg[...] = jnp.zeros_like(vg)

    def at(i, spots):
        for where, event in spots:
            pl.when(i == where)(event)

    def norm(value):
        u = value - jnp.mean(value, axis=-1, keepdims=True)
        r = lax.rsqrt(jnp.mean(u * u, axis=-1, keepdims=True) + eps_norm)
        return u * r, r

    def middle_body(i, _):
        r = rows(i)
        value = x_ref[r, :].astype(F32) + (dot(mixed_ref[r, :], wo_ref[...]) + vec(2))
        middle[r, :] = value
        xhat, _ = norm(value)
        n2 = (xhat * vec(6) + vec(7)).astype(BF)
        dmixed[r, :] = n2
        n2t[:, r] = n2.T
        live = iota((LR, D), 0) + i * LR < length
        grad = jnp.where(live, cot_ref[r, :].astype(F32), 0.0)
        vg[7:8, :] += jnp.sum(grad, axis=0, keepdims=True)
        dout[r, :] = grad.astype(BF)
        dot_t[:, r] = grad.astype(BF).T
        mixed_t[:, r] = mixed_ref[r, :].T
        return 0

    lax.fori_loop(0, T // LR, middle_body, 0)
    load.wait()

    def hidden_body(i, _):
        at(i, [(0, gather.t[0]), (1, gather.t[1]), (2, gather.t[2]), (3, gather.t[3])])
        r = rows(i)
        left = dmixed[r, :]
        for j in range(4):
            cols = slice(j * Q, (j + 1) * Q)
            first, second = gelu_pair(dot(left, we[:, cols]) + v_ref[1:2, cols])
            act[r, cols] = first.astype(BF)
            slope[r, cols] = second.astype(BF)
        return 0

    lax.fori_loop(0, T // LR, hidden_body, 0)

    def column(d):
        value = dot(dot_t[...], act[:, pl.ds(mo(d * C8, 128), C8)])
        gc[d] = value.reshape(4, D // 4, C8).astype(BF)

    sib = p.dc - p.d
    turns = (p.dd + sib, p.dd, p.dx + sib, p.dy + sib, p.dx, p.dy, p.d + sib, p.d)

    def column_body(i, _):
        d = turns[7]
        for k in range(7):
            d = jnp.where(i == k, turns[k], d)
        column(d)
        at(i, [(0, lambda: to_sibling(3)), (2, lambda: to_sibling(1)), (3, run(lambda: to_sibling(2), gather.q[0])),
               (5, run(gather.q[1], gather.q[2], scatter[0])), (6, lambda: to_sibling(0))])
        return 0

    lax.fori_loop(0, 8, column_body, 0)
    run(gather.q[3], scatter[1], gather.close)()

    def back_body(i, _):
        at(i, [(1, run(scatter[2], scatter[3], scatter[4]))])
        r = rows(i)
        grad_low = dout[r, :]
        result = middle[r, :] + vec(3)
        for j in range(4):
            cols = slice(j * Q, (j + 1) * Q)
            dh = dot(grad_low, wct[:, cols]) * slope[r, cols].astype(F32)
            low = dh.astype(BF)
            slope[r, cols] = low
            vg[3 + j:4 + j, :] += jnp.sum(low.astype(F32), axis=0, keepdims=True)
        result = result + dot_nt(act[r, :], wct[...])
        dn = dot_nt(slope[r, :], we[...])
        live = iota((LR, D), 0) + i * LR < length
        bout[r, :] = jnp.where(live, result, 0.0).astype(BF)
        xhat, spread = norm(middle[r, :])
        vg[10:11, :] += jnp.sum(dn * xhat, axis=0, keepdims=True)
        vg[11:12, :] += jnp.sum(dn, axis=0, keepdims=True)
        gx = dn * vec(6)
        back = spread * (gx - jnp.mean(gx, axis=-1, keepdims=True)
                         - xhat * jnp.mean(gx * xhat, axis=-1, keepdims=True))
        total = dout[r, :].astype(F32) + back
        middle[r, :] = total
        branch = total.astype(BF)
        dbranch[r, :] = branch
        vg[2:3, :] += jnp.sum(branch.astype(F32), axis=0, keepdims=True)
        dmixed[r, :] = dot_nt(branch, wo_ref[...]).astype(BF)
        return 0

    lax.fori_loop(0, T // LR, back_body, 0)
    outs = []

    def out(source, target):
        made = pltpu.make_async_copy(source, target, out_sem.at[1 + len(outs)])
        made.start()
        outs.append(made)

    out(bout, block_out)
    out(dmixed, dmixed_out)
    out(middle, dmiddle_out)
    for z in range(4):
        cols = slice(3 * z // 2 * 128, 3 * z // 2 * 128 + 256)
        go[:, z] = dot(mixed_t[...], dbranch[:, cols]).reshape(8, R, 256).astype(BF)
    out(go, go_out)
    for z in range(4):
        act[0:D, z * Q:(z + 1) * Q] = dot(n2t[...], slope[:, z * Q:(z + 1) * Q]).astype(BF)
        out(act.at[0:D, z * Q:(z + 1) * Q], ge_out.at[:, z * Q:(z + 1) * Q])
        if z == 2:
            scatter[5]()
            out(gc.at[p.d], gc_out)
    vg_out[...] = vg[...]
    link.finish()
    for made in outs:
        made.wait()


ANY = pl.BlockSpec(memory_space=pl.ANY)
VM = pl.BlockSpec(memory_space=pltpu.VMEM)
SM = pl.BlockSpec(memory_space=pltpu.SMEM)
sds = jax.ShapeDtypeStruct


def second_call(length, x, cot, mixed, wo, we, wc, v):
    T, D = x.shape
    FF = we.shape[1]
    n = 36 + 8
    R, C8, Z = D // 8, FF // 8, D // 4
    vm = pltpu.VMEM
    return pl.pallas_call(
        second_kernel,
        in_specs=[SM] + [ANY] * 6 + [VM],
        out_specs=[ANY] * 6 + [VM],
        out_shape=[sds((T, D), BF), sds((T, D), BF), sds((T, D), F32), sds((D, FF), BF), sds((8, 4, R, 256), BF),
                   sds((4, Z, C8), BF), sds((16, D), F32)],
        scratch_shapes=[
            vm((T, D), BF), vm((T, D), BF), vm((T, D), BF), vm((D, D), BF), vm((D, FF), BF), vm((D, FF), BF), vm((T, FF), BF), vm((T, FF), BF), vm((T, D), F32),
            vm((D, T), BF), vm((D, T), BF), vm((D, T), BF), vm((T, D), BF), vm((T, D), BF),
            vm((8, 4, Z, C8), BF), vm((8, 4, R, 256), BF), vm((T, D), BF), vm((T, D), BF), vm((16, D), F32),
            vm((4, 4, Z, C8), BF), vm((2, Z, C8), BF), vm((2, Z, C8), BF), vm((4, Z, C8), BF), vm((4, Z, C8), BF),
            pltpu.SemaphoreType.DMA((n,)), pltpu.SemaphoreType.DMA((n,)), pltpu.SemaphoreType.DMA((23,)),
        ],
        compiler_params=pltpu.CompilerParams(
            collective_id=1, has_side_effects=True, vmem_limit_bytes=62 << 20),
        name="second_part",
    )(length, x, cot, mixed, wo, we, wc, v)


def third_kernel(length_ref, proj_hbm, qa_hbm, mixed_hbm, dm_hbm, n1_hbm, wp_hbm, x_hbm, dmiddle_hbm, ge_hbm, go_hbm,
                 gc_hbm, vg_ref, v_ref,
                 tokens_out, gp_out, go_out, ge_out, gc_out, vec_out,
                 proj, qa, mixed, dm, n1, n1t, wpp, x, dmiddle, ge, go, dproj, tg, gp,
                 ka, da, dq, va, kt, vs, vo, vl, vz,
                 lce, lxhe, lyhe, lxe, lye, lze, lco, lxho, lyho, lxo, lyo, lzo,
                 lcp, lxhp, lyhp, lxp, lyp, lzp, gpw, gcol, lzc,
                 send_sem, recv_sem, load_sem):
    p = Place()
    T, D = x.shape
    FF = ge.shape[1]
    R = D // 8
    Q = FF // 4
    pairs = H // 2
    KB = 256
    parts = 2
    link = Link(p, send_sem, recv_sem)
    loads = []

    def load(source, target, now=True):
        made = pltpu.make_async_copy(source, target, load_sem.at[len(loads)])
        if now:
            made.start()
        loads.append(made)
        return made

    first_loads = [load(a, b) for a, b in ((proj_hbm, proj), (qa_hbm, qa), (mixed_hbm, mixed), (dm_hbm, dm))]
    ge_load, gc_load, go_load, n1_load = load(ge_hbm, ge), load(gc_hbm, gcol), load(go_hbm, go), load(n1_hbm, n1, False)
    late = [load(x_hbm, x, False), load(dmiddle_hbm, dmiddle, False)]
    for i in range(pairs):
        for s in range(3):
            late.append(load(wp_hbm.at[:, pl.ds((s * pairs + i) * 128, 128)],
                             wpp.at[:, pl.ds((i * 3 + s) * 128, 128)], False))

    def finish_e(total):
        ge_out[...] = total

    def finish_o(total):
        go_out[...] = jnp.where(p.odd == 0, total[:, 0:192], total[:, 64:256])

    rows_of = lambda d: pl.ds(mo(d * R, 16), R)
    def finish_c(total):
        gc_out[...] = total

    e_col, o_col = (lambda d: ge.at[rows_of(d), :]), (lambda d: go.at[d])
    e_sib, ev_e = scatter_events(
        link, p, e_col, lambda ref, h: ref.at[:, pl.ds(h * (FF // 2), FF // 2)], lce, lxhe, lyhe, lxe, lye)
    o_sib, ev_o = scatter_events(
        link, p, o_col, lambda ref, h: ref.at[pl.ds(2 * h, 2)], lco, lxho, lyho, lxo, lyo)
    e_send, e_last = z_sum(link, p, lambda z: e_col(p.d).at[:, pl.ds(mo(z * Q, 128), Q)], lze, finish_e)
    o_send, o_last = z_sum(link, p, lambda z: o_col(p.d).at[z], lzo, finish_o)
    c_send, c_last = z_sum(link, p, lambda z: gcol.at[z], lzc, finish_c)
    ended = []
    combos = []
    for i in range(pairs):
        for s in range(3):
            tile = s * pairs + i
            for owner in range(4):
                left = 9 * owner // 2
                if left <= tile < left + 5:
                    combos.append((i, s, owner, tile - left))
    assert len(combos) == 20
    z_slots = [[link.slot() for _ in range(3)] for _ in combos]

    def pair_scatter(i):
        column = lambda d: gp.at[i, d]
        sib, events = scatter_events(
            link, p, column, lambda ref, h: ref.at[pl.ds(h * (R // 2), R // 2)],
            lcp.at[i], lxhp.at[i], lyhp.at[i], lxp.at[i], lyp.at[i])
        mine = [(at, c) for at, c in enumerate(combos) if c[0] == i]

        def along(add_own):
            def run():
                add_own()
                for at, (_, s, owner, _) in mine:
                    @pl.when(p.z != owner)
                    def _():
                        step = lax.rem(owner - p.z + 4, 4)
                        part = column(p.d).at[:, pl.ds(s * 128, 128)]
                        link.copy(z_slots[at][0] + step - 1, part, lzp.at[at, step - 1], ("z", owner)).start()
            return run

        def last():
            for at, (_, s, owner, place) in mine:
                @pl.when(p.z == owner)
                def _():
                    total = gp[i, p.d, :, s * 128:(s + 1) * 128].astype(F32)
                    for step in range(1, 4):
                        link.got(z_slots[at][step - 1], lzp.at[at, step - 1])
                        total = total + lzp[at, step - 1].astype(F32)
                    gpw[:, place * 128:(place + 1) * 128] = total

        def ending():
            for at, (_, s, owner, _) in mine:
                @pl.when(p.z != owner)
                def _():
                    step = lax.rem(owner - p.z + 4, 4)
                    view = lzp.at[at, 0]
                    link.copy(z_slots[at][0] + step - 1, view, view, "x").wait_send()

        ended.append(ending)

        def start():
            for k in (3, 1, 2, 0):
                sib(k)

        return [start] + events[:5] + [along(events[5]), last]

    ev_p = [pair_scatter(i) for i in range(pairs)]

    enter(p, wide=True)
    for made in first_loads:
        made.wait()
    n1_load.start()
    length = length_ref[0]

    def start_e():
        ge_load.wait()
        for k in (3, 1, 2, 0):
            e_sib(k)

    def start_o():
        go_load.wait()
        for k in (3, 1, 2, 0):
            o_sib(k)

    def start_late():
        for made in late:
            made.start()

    def turn_n1():
        n1_load.wait()
        for i in range(T // 256):
            n1t[:, i * 256:(i + 1) * 256] = n1[i * 256:(i + 1) * 256, :].T

    def start_c():
        gc_load.wait()
        c_send()

    e, o = ev_e, ev_o
    q = ev_p
    timeline = [
        (0, start_c), (0, start_e), (0, start_o), (1, turn_n1), (1, e[0]), (2, start_late), (2, e[1]), (2, e[4]), (2, o[0]), (2, o[1]), (2, o[4]),
        (2, q[0][0]), (3, q[0][1]), (3, q[0][2]), (3, q[0][5]), (4, e[2]), (4, e[3]), (4, c_last), (4, o[2]), (4, o[3]),
        (4, q[0][3]), (4, q[0][4]), (4, q[1][0]), (5, q[1][1]), (5, q[1][2]), (5, q[1][5]), (6, q[2][0]),
        (7, q[2][1]), (7, q[2][2]), (7, q[2][5]), (8, e[5]), (8, e_send), (8, q[3][0]), (9, o[5]), (9, o_send),
        (9, q[3][1]), (9, q[3][2]), (9, q[3][5]), (10, q[0][6]), (10, q[1][3]), (10, q[1][4]), (10, q[2][3]), (10, q[2][4]),
        (10, q[3][3]), (10, q[3][4]), (10, q[4][0]), (11, q[4][1]), (11, q[4][2]), (11, q[4][5])]
    timeline.sort(key=lambda e: e[0])

    def body(step, _):
        for at, event in timeline:
            if at < pairs * parts:
                pl.when(step == at)(event)
        pair = lax.div(step, parts)
        part = lax.rem(step, parts)
        ps = lambda off: pl.ds(mo(off + pair * 128, 128), 128)
        own = lambda s: pl.ds(mo(pair * 384 + s * 128, 128), 128)

        @pl.when(part == 0)
        def _():
            lane, row = iota((T, 128), 1), iota((T, 128), 0)
            k = proj[:, ps(D)].astype(F32)
            v = proj[:, ps(2 * D)].astype(F32)
            do = dm[:, ps(0)].astype(F32)
            pr = do * mixed[:, ps(0)].astype(F32)
            dead = jnp.where(row < length, 0.0, neg_fill)
            for head in range(2):
                keep = (lane < 64) if head == 0 else (lane >= 64)
                delta = jnp.sum(jnp.where(keep, pr, 0.0), axis=-1, keepdims=True)
                one, two, three = split3(-delta)
                da[head] = extend(head, do, lane, one, two, three, 0.0)
                ka[head] = extend(head, k, lane, 1.0, 1.0, 1.0, dead)
                va[head] = extend(head, v, lane, 1.0, 1.0, 1.0, 0.0)
                kt[head] = jnp.where(keep, k, 0.0).astype(BF).T
            dq[...] = jnp.zeros_like(dq)

        lk = iota((KB, 128), 1)
        spans = [pl.ds(mo(part * (T // parts) + i * KB, KB), KB) for i in range(T // parts // KB)]
        items = [(head, r) for r in spans for head in range(2)]
        kept = {}

        def products(n):
            head, r = items[n]
            return dot_nt(ka[head, r, :], qa[pair * 2 + head]), dot_nt(va[head, r, :], da[head])

        def weigh(scores, grads):
            weights = jnp.exp(scores)
            return weights.astype(BF), (weights * grads).astype(BF)

        def finish(n, low, ds):
            head, r = items[n]
            kept[n] = dot(ds, qa[pair * 2 + head]), dot(low, da[head])
            dq[head] += dot(kt[head, :, r], ds)
            if head == 1:
                dproj[r, own(1)] = jnp.where(lk < 64, kept[n - 1][0], kept[n][0]).astype(BF)
                dproj[r, own(2)] = jnp.where(lk < 64, kept[n - 1][1], kept[n][1]).astype(BF)

        value, waiting = products(0), None
        for n in range(len(items)):
            following = products(n + 1) if n + 1 < len(items) else None
            done = weigh(*value)
            if waiting is not None:
                finish(n - 1, *waiting)
            value, waiting = following, done
        finish(len(items) - 1, *waiting)

        @pl.when(part == parts - 1)
        def _():
            dproj[:, own(0)] = ((dq[0] + dq[1]) * (HD ** -0.5)).T.astype(BF)
            value = dot(n1t[...], dproj[:, pl.ds(mo(pair * 384, 128), 384)])
            gp[pair] = value.reshape(8, R, 384).astype(BF)

        return 0

    lax.fori_loop(0, pairs * parts, body, 0)
    ev_p[pairs - 1][0]()
    for made in late:
        made.wait()
    vs[...] = vg_ref[...]
    LR = 256

    def norm_body(i, _):
        def spot(where, events):
            @pl.when(i == where)
            def _():
                for event in events:
                    event()

        spot(0, [e_last, q[1][6], q[2][6], q[3][6], q[4][3], q[4][4]])
        spot(1, q[5][1:3] + q[5][5:6])
        spot(2, [o_last, q[0][7], q[1][7], q[4][6], q[2][7]])
        spot(3, q[5][3:5] + q[3][7:8])
        r = pl.ds(mo(i * LR, LR), LR)
        left = dproj[r, :]
        dn = dot_nt(left, wpp[...])
        sums = jnp.sum(left.astype(F32), axis=0, keepdims=True)
        for j in range(pairs):
            vs[0:1, j * 128:(j + 1) * 128] += sums[:, j * 384:j * 384 + 128]
            vs[1:2, j * 128:(j + 1) * 128] += sums[:, j * 384 + 256:j * 384 + 384]
        value = x[r, :].astype(F32)
        u = value - jnp.mean(value, axis=-1, keepdims=True)
        spread = lax.rsqrt(jnp.mean(u * u, axis=-1, keepdims=True) + eps_norm)
        xhat = u * spread
        vs[8:9, :] += jnp.sum(dn * xhat, axis=0, keepdims=True)
        vs[9:10, :] += jnp.sum(dn, axis=0, keepdims=True)
        gx = dn * v_ref[4:5, 0:D]
        back = spread * (gx - jnp.mean(gx, axis=-1, keepdims=True)
                         - xhat * jnp.mean(gx * xhat, axis=-1, keepdims=True))
        tg[r, :] = (back + dmiddle[r, :]).astype(BF)
        return 0

    lax.fori_loop(0, T // LR, norm_body, 0)
    out = load(tg, tokens_out)
    v_slots = link.slot(16)
    for d in range(8):
        line = lambda row, at, n: jnp.concatenate(
            [vs[row:row + 1, at:at + n], jnp.zeros((1, 384 - n), F32)], axis=1) if n < 384 else vs[row:row + 1, at:at + n]
        vo[d] = jnp.concatenate(
            [line(d // 4, d % 4 * 2 * R, 2 * R), line(2, d * R, R), line(3 + d // 2, d % 2 * 4 * R, 4 * R)]
            + [line(row, d * R, R) for row in (7, 8, 9, 10, 11)], axis=0)
    for d in range(8):
        @pl.when(p.d != d)
        def _():
            link.copy(v_slots + d, vo.at[d], vl.at[p.d], ("d", d), land=v_slots + p.d).start()
    for event in (q[4][7], q[5][6]):
        event()
    vl[p.d] = vo[p.d]
    for d in range(8):
        @pl.when(p.d != d)
        def _():
            link.got(v_slots + d, vl.at[d])
    own = vl[0]
    for d in range(1, 8):
        own = own + vl[d]
    vz[p.z] = own
    for k in (1, 2, 3):
        link.send(v_slots + 8 + k, vz.at[p.z], vz.at[p.z], ("z", p.order[k]), lambda: vz.at[0], land=v_slots + 12 + p.z)
    q[5][7]()
    gp_out[...] = jnp.where(p.odd == 0, gpw[:, 0:576], gpw[:, 64:640])
    for k in (1, 2, 3):
        link.got(v_slots + 12 + p.order[k], vz.at[p.order[k]])
    vec_out[...] = vz[0] + vz[1] + vz[2] + vz[3]
    for d in range(8):
        @pl.when(p.d != d)
        def _():
            link.copy(v_slots + d, vo.at[d], vo.at[d], "x").wait_send()
    link.finish()
    for ending in ended:
        ending()
    out.wait()


def third_call(length, proj, qa, mixed, dm, n1, wp, x, dmiddle, ge, go, gc, vg, v):
    T, D = x.shape
    FF = ge.shape[1]
    R, Q, pairs = D // 8, FF // 4, H // 2
    vm = pltpu.VMEM
    n = 8 * 8 + 12 + 60 + 16
    return pl.pallas_call(
        third_kernel,
        in_specs=[SM] + [ANY] * 11 + [VM] * 2,
        out_specs=[ANY] + [VM] * 5,
        out_shape=[sds((T, D), BF), sds((R, 3 * D // 4), F32), sds((R, D // 4), F32), sds((R, Q), F32), sds((D // 4, FF // 8), F32),
                   sds((8, 384), F32)],
        scratch_shapes=[
            vm((T, 3 * D), BF), vm((H, T, 128), BF), vm((T, D), BF), vm((T, D), BF), vm((T, D), BF), vm((D, T), BF),
            vm((D, 3 * D), BF), vm((T, D), BF), vm((T, D), F32), vm((D, FF), BF), vm((8, 4, R, 256), BF),
            vm((T, 3 * D), BF), vm((T, D), BF), vm((pairs, 8, R, 384), BF),
            vm((2, T, 128), BF), vm((2, T, 128), BF), vm((2, 128, T), F32), vm((2, T, 128), BF), vm((2, 128, T), BF),
            vm((16, D), F32), vm((8, 8, 384), F32), vm((8, 8, 384), F32), vm((4, 8, 384), F32),
            vm((4, R, FF), BF), vm((R, FF // 2), BF), vm((R, FF // 2), BF), vm((R, FF), BF), vm((R, FF), BF), vm((4, R, Q), BF),
            vm((4, 4, R, 256), BF), vm((2, R, 256), BF), vm((2, R, 256), BF), vm((4, R, 256), BF), vm((4, R, 256), BF),
            vm((4, R, 256), BF),
            vm((pairs, 4, R, 384), BF), vm((pairs, R // 2, 384), BF), vm((pairs, R // 2, 384), BF),
            vm((pairs, R, 384), BF), vm((pairs, R, 384), BF), vm((20, 3, R, 128), BF), vm((R, 640), F32),
            vm((4, D // 4, FF // 8), BF), vm((4, D // 4, FF // 8), BF),
            pltpu.SemaphoreType.DMA((n,)), pltpu.SemaphoreType.DMA((n,)), pltpu.SemaphoreType.DMA((29,)),
        ],
        compiler_params=pltpu.CompilerParams(
            collective_id=2, has_side_effects=True, vmem_limit_bytes=63 << 20),
        name="third_part",
    )(length, proj, qa, mixed, dm, n1, wp, x, dmiddle, ge, go, gc, vg, v)


def last_kernel(block_in, tokens_in, p_in, o_in, e_in, c_in, vec_in,
                block_out, tokens_out, p_out, o_out, e_out, c_out, *rest):
    vectors, held, vec, sem = rest[:8], rest[8:14], rest[14], rest[15]
    parts = 2
    rows = block_in.shape[0] // parts
    whole = lambda ref: ref
    legs = []
    for i in range(parts):
        part = lambda ref, i=i: ref.at[pl.ds(i * rows, rows)]
        legs += [(part, block_in, held[0], block_out), (part, tokens_in, held[1], tokens_out)]
    legs += [(whole, a, b, c) for a, b, c in zip((p_in, o_in, e_in, c_in), held[2:], (p_out, o_out, e_out, c_out))]
    first = pltpu.make_async_copy(vec_in, vec, sem.at[2 * len(legs)])
    first.start()
    ins = [pltpu.make_async_copy(part(a), part(b), sem.at[k]) for k, (part, a, b, _) in enumerate(legs)]
    outs = [pltpu.make_async_copy(part(b), part(c), sem.at[len(legs) + k]) for k, (part, _, b, c) in enumerate(legs)]
    for made in ins:
        made.start()
    for came, goes in zip(ins, outs):
        came.wait()
        goes.start()
    first.wait()
    for at, target in enumerate(vectors):
        n = target.shape[0]
        target[...] = vec[at:at + 1, 0:n].reshape(n)
    for goes in outs:
        goes.wait()


def last_call(sizes, *arrays):
    return pl.pallas_call(
        last_kernel,
        in_specs=[ANY] * 7,
        out_specs=[ANY] * 6 + [VM] * 8,
        out_shape=[sds(item.shape, item.dtype) for item in arrays[:6]] + [sds((n,), F32) for n in sizes],
        scratch_shapes=[pltpu.VMEM(item.shape, item.dtype) for item in arrays] + [pltpu.SemaphoreType.DMA((17,))],
        compiler_params=pltpu.CompilerParams(vmem_limit_bytes=63 << 20),
        name="last_part",
    )(*arrays)


def per_device_fast(tokens, lengths, cotangent, project_weight, project_bias, output_weight, output_bias,
                    expand_weight, expand_bias, contract_weight, contract_bias, first_gain, first_shift,
                    second_gain, second_shift):
    vectors = (project_bias, output_bias, expand_bias, contract_bias, first_gain, first_shift, second_gain, second_shift)
    normed_one, projected, mixed, qa, full_project, full_output, full_expand, cc, v = first_call(
        lengths, tokens, project_weight, output_weight, expand_weight, contract_weight.T, vectors)
    block_out, grad_mixed, grad_middle, ge, go, gc, vg = second_call(
        lengths, tokens, cotangent, mixed, full_output, full_expand, cc, v)
    third = third_call(
        lengths, projected, qa, mixed, grad_mixed, normed_one, full_project, tokens, grad_middle, ge, go, gc, vg, v)
    out = last_call([item.shape[0] for item in vectors], block_out, *third)
    return (out[0], out[1], out[2], out[6], out[3], out[7], out[4], out[8], out[5].T, *out[9:])


def solution(mesh):
    both, rows, grid = P(("dp", "fsdp"), None), P("dp"), P("dp", "fsdp")
    weights = (grid, rows, grid, rows, grid, rows, grid, rows)
    fast = mesh.shape["dp"] == 8 and mesh.shape["fsdp"] == 4
    return jax.shard_map(
        per_device_fast if fast else per_device,
        mesh=mesh,
        in_specs=(both, P(("dp", "fsdp")), both) + weights + (rows,) * 4,
        out_specs=(both, both) + weights + (rows,) * 4,
        check_vma=False,
    )
```

```python
import functools
import jax
import jax.numpy as jnp
from jax import lax
from jax.experimental import pallas as pl
from jax.experimental.pallas import tpu as pltpu
from jax.sharding import PartitionSpec as P

H = 12
HD = 64
F32 = jnp.float32
BF = jnp.bfloat16
MESH = pl.DeviceIdType.MESH
eps_norm = 1e-05
neg_fill = -1000000000.0


def dot(first, second):
    return jnp.dot(first, second, preferred_element_type=F32)


def dot_nt(first, second):
    return lax.dot_general(first, second, (((1,), (1,)), ((), ())), preferred_element_type=F32)


def dot_tn(first, second):
    return lax.dot_general(first, second, (((0,), (0,)), ((), ())), preferred_element_type=F32)


def mo(value, multiple):
    return pl.multiple_of(value, multiple)


class Place:
    def __init__(self):
        self.d = lax.axis_index("dp")
        self.z = lax.axis_index("fsdp")
        core = lax.rem(self.d, 2)
        across = lax.rem(lax.div(self.d, 2), 2)
        up = lax.div(self.d, 4)
        self.dc = self.d + 1 - 2 * core
        self.dx = self.d + 2 - 4 * across
        self.dy = self.d + 4 - 8 * up
        self.dd = self.dx + 4 - 8 * up
        self.odd = lax.rem(self.z, 2)
        z = self.z
        pick = lambda a, b, c, d: jnp.where(z < 2, jnp.where(z == 0, a, b), jnp.where(z == 2, c, d))
        self.order = [z, pick(1, 0, 3, 2), pick(2, 2, 1, 1), pick(3, 3, 0, 0)]

    def zt(self, step):
        return lax.rem(self.z + step, 4)

    def zf(self, step):
        return lax.rem(self.z + 4 - step, 4)

    def id(self, to):
        if to == "x":
            return (self.dx, self.z)
        if to == "y":
            return (self.dy, self.z)
        if to == "c":
            return (self.dc, self.z)
        if isinstance(to, tuple):
            return (to[1], self.z) if to[0] == "d" else (self.d, to[1])
        return (self.d, self.zt(to))


def enter(place, wide=False):
    barrier = pltpu.get_barrier_semaphore()
    sib = place.dc - place.d
    others = [("d", d + sib) for d in (place.dx, place.dy, place.dd)] + [("d", place.dd)] if wide else []
    partners = ["x", "y", "c", 1, 2, 3] + others
    for to in partners:
        pl.semaphore_signal(barrier, inc=1, device_id=place.id(to), device_id_type=MESH)
    pl.semaphore_wait(barrier, len(partners))


class Link:
    def __init__(self, place, send_sem, recv_sem):
        self.place, self.send_sem, self.recv_sem = place, send_sem, recv_sem
        self.count = 0
        self.copies = []

    def slot(self, many=1):
        self.count += many
        return self.count - many

    def copy(self, slot, source, target, to, land=None):
        return pltpu.make_async_remote_copy(
            src_ref=source, dst_ref=target, send_sem=self.send_sem.at[slot],
            recv_sem=self.recv_sem.at[slot if land is None else land], device_id=self.place.id(to),
            device_id_type=MESH)

    def send(self, slot, source, target, to, like, land=None, when=None):
        def start():
            self.copy(slot, source, target, to, land).start()

        if when is None:
            start()
        else:
            pl.when(when())(start)
        self.copies.append((slot, like, when))

    def got(self, slot, target):
        self.copy(slot, target, target, "x").wait_recv()

    def finish(self):
        for slot, like, when in self.copies:
            def done(slot=slot, like=like):
                view = like()
                self.copy(slot, view, view, "x").wait_send()

            if when is None:
                done()
            else:
                pl.when(when())(done)


class Gather:
    def __init__(self, link, place, block):
        p = place
        zr, zs = link.slot(4), link.slot(4)
        xs, ys, fx = link.slot(4), link.slot(4), link.slot(4)
        cs = link.slot(16)
        got = link.got
        send = functools.partial(link.send, like=lambda: block(0, 0))

        def z_step(a):
            def run():
                if a == 0:
                    own = block(p.z, p.d)
                    for k in (1, 2, 3):
                        send(zs + k, own, own, ("z", p.order[k]), land=zr + p.z)
                else:
                    got(zr + p.order[a], block(p.order[a], p.d))
            return run

        def x_step(a):
            def run():
                here = block(p.order[a], p.d)
                send(xs + a, here, here, "x")
                send(ys + a, here, here, "y")
                send(cs + a, here, here, "c")
            return run

        def turn(a):
            def run():
                b = p.order[a]
                bx, by = block(b, p.dx), block(b, p.dy)
                got(xs + a, bx)
                got(ys + a, by)
                if a in (0, 1):
                    send(fx + a, bx, bx, "y")
                else:
                    send(fx + a, by, by, "x")
                send(cs + 4 + a, bx, bx, "c")
                send(cs + 8 + a, by, by, "c")
            return run

        def corner(a):
            def run():
                bd = block(p.order[a], p.dd)
                got(fx + a, bd)
                send(cs + 12 + a, bd, bd, "c")
            return run

        def close():
            sib = p.dc - p.d
            for which, d in enumerate((p.d, p.dx, p.dy, p.dd)):
                for a in range(4):
                    got(cs + 4 * which + a, block(p.order[a], d + sib))

        self.z, self.x, self.t, self.q = ([make(a) for a in range(4)] for make in (z_step, x_step, turn, corner))
        self.close = close


def spread_z(link, place, ref):
    p = place
    zs, zr = link.slot(3), link.slot(4)

    def send():
        for k in (1, 2, 3):
            link.send(zs + k - 1, ref.at[p.z], ref.at[p.z], ("z", p.order[k]), lambda: ref.at[0], land=zr + p.z)

    def wait():
        for k in (1, 2, 3):
            b = p.order[k]
            link.got(zr + b, ref.at[b])

    return send, wait


def run(*events):
    def together():
        for event in events:
            event()
    return together


def window(value, odd, wide):
    rows, k = value.shape
    fill = jnp.zeros((rows, wide - k), F32)
    value = value.astype(F32)
    left = jnp.concatenate([value, fill], axis=1)
    right = jnp.concatenate([fill, value], axis=1)
    return jnp.where(odd == 0, left, right).astype(BF)


def merge_windows(blocks, full, tiles, rows_step):
    rows = full.shape[0]
    half = tiles // 2

    def body(i, _):
        r = pl.ds(mo(i * rows_step, rows_step), rows_step)
        for pair in range(2):
            even, odd = blocks.at[2 * pair], blocks.at[2 * pair + 1]
            base = pair * tiles * 128
            full[r, base:base + half * 128] = even[r, 0:half * 128]
            full[r, base + half * 128:base + (half + 1) * 128] = (
                even[r, half * 128:(half + 1) * 128] + odd[r, 0:128])
            full[r, base + (half + 1) * 128:base + tiles * 128] = odd[r, 128:(half + 1) * 128]
        return 0

    lax.fori_loop(0, rows // rows_step, body, 0)


def split3(value):
    high = value.astype(BF)
    rest = value - high.astype(F32)
    mid = rest.astype(BF)
    low = (rest - mid.astype(F32)).astype(BF)
    return high.astype(F32), mid.astype(F32), low.astype(F32)


def extend(head, pair, lane, one, two, three, four):
    base = 64 * (1 - head)
    extra = jnp.where(lane == base, one, jnp.where(lane == base + 1, two, jnp.where(
        lane == base + 2, three, jnp.where(lane == base + 3, four, 0.0))))
    keep = (lane < 64) if head == 0 else (lane >= 64)
    return jnp.where(keep, pair, extra).astype(BF)


def iota(shape, axis):
    return lax.broadcasted_iota(jnp.int32, shape, axis)


QB = 256


def first_kernel(length_ref, x_ref, wp_ref, wo_ref, we_ref, wc_ref, *refs):
    vec_refs, refs = refs[:8], refs[8:]
    first_body(length_ref, x_ref, wp_ref, wo_ref, we_ref, wc_ref, vec_refs, *refs)


def first_body(length_ref, x_hbm, wp_ref, wo_ref, we_ref, wc_ref, vec_refs,
                 n1_out, proj_out, mixed_out, qa_out, wp_out, wo_out, we_out, c_out, v_out,
                 wp_blk, wo_blk, we, wp, wo, vb, n1, proj, mixed, qa, ka, va, vrow, cc, x_ref,
                 send_sem, recv_sem, out_sem, pair_sem):
    p = Place()
    T, D = x_ref.shape
    R = wp_ref.shape[0]
    FF = we.shape[1]
    link = Link(p, send_sem, recv_sem)
    rows_of = lambda d: pl.ds(mo(d * R, 16), R)
    half = R // 2
    bpa = lambda z, d: wp_blk.at[z, pl.ds(mo(d * R, 16), half), :]
    bpb = lambda z, d: wp_blk.at[z, pl.ds(mo(d * R + half, 16), half), :]
    bo = lambda z, d: wo_blk.at[z, rows_of(d), :]
    be = lambda z, d: we.at[rows_of(d), pl.ds(mo(z * (FF // 4), 128), FF // 4)]
    g0, g1, go, ge = (Gather(link, p, b) for b in (bpa, bpb, bo, be))
    c_send, c_wait = spread_z(link, p, cc)
    vs = [link.slot() for _ in range(7)]

    wp_blk[p.z, rows_of(p.d), :] = window(wp_ref[...], p.odd, wp_blk.shape[2])
    wo_blk[p.z, rows_of(p.d), :] = window(wo_ref[...], p.odd, wo_blk.shape[2])
    we[rows_of(p.d), pl.ds(mo(p.z * (FF // 4), 128), FF // 4)] = we_ref[...]
    x_load = pltpu.make_async_copy(x_hbm, x_ref, out_sem.at[9])
    x_load.start()
    cc[p.z] = wc_ref[...]
    for i, ref in enumerate(vec_refs):
        vb[p.d, i:i + 1, 0:ref.shape[0]] = ref[...].astype(F32).reshape(1, ref.shape[0]).astype(BF)

    outs = []

    def out(source, target):
        made = pltpu.make_async_copy(source, target, out_sem.at[len(outs)])
        made.start()
        outs.append(made)

    enter(p)
    send_v = lambda slot, d, to: link.send(vs[slot], vb.at[d], vb.at[d], to, lambda: vb.at[0])
    for slot, to in ((0, "x"), (1, "y"), (3, "c")):
        send_v(slot, p.d, to)
    run(g0.z[0], g0.x[0], g1.z[0], g1.x[0])()
    link.got(vs[0], vb.at[p.dx])
    link.got(vs[1], vb.at[p.dy])
    send_v(2, p.dx, "y")
    send_v(4, p.dx, "c")
    send_v(5, p.dy, "c")
    run(g0.z[1], g0.x[1], g0.t[0], g1.t[0], g0.z[2], g0.x[2])()
    link.got(vs[2], vb.at[p.dd])
    send_v(6, p.dd, "c")
    sib = p.dc - p.d
    for slot, d in ((3, p.d), (4, p.dx), (5, p.dy), (6, p.dd)):
        link.got(vs[slot], vb.at[d + sib])
    got = vb[...].astype(F32)
    side = lambda row, wide: jnp.concatenate([got[i, row:row + 1, 0:wide] for i in range(8)], axis=1)
    bias = side(0, 2 * R)
    vrow[0:1, 0:D] = bias[:, 0:D]
    vrow[0:1, D:2 * D] = jnp.zeros((1, D), F32)
    vrow[0:1, 2 * D:3 * D] = bias[:, D:]
    vrow[1:2, :] = side(2, FF // 8)
    for row, at in ((2, 1), (3, 3), (4, 4), (5, 5), (6, 6), (7, 7)):
        vrow[row:row + 1, 0:D] = side(at, R)
    out(vrow, v_out)
    run(g0.t[1], g0.z[3], g0.x[3], g0.q[0], g1.z[1], g1.x[1], g1.q[0])()

    LR = 128
    gain, shift = vrow[4:5, 0:D], vrow[5:6, 0:D]

    def norm_body(i, _):
        r = pl.ds(mo(i * LR, LR), LR)
        value = x_ref[r, :].astype(F32)
        u = value - jnp.mean(value, axis=-1, keepdims=True)
        spread = jnp.mean(u * u, axis=-1, keepdims=True)
        n1[r, :] = (u * lax.rsqrt(spread + eps_norm) * gain + shift).astype(BF)
        return 0

    norm_part = lambda k: lax.fori_loop(k * (T // LR // 4), (k + 1) * (T // LR // 4), norm_body, 0)
    g0.t[2]()
    x_load.wait()
    norm_part(0)
    run(g1.z[2], g1.x[2], g0.q[1])()
    norm_part(1)
    run(g1.z[3], g1.x[3], ge.z[0], go.z[0], g0.t[3])()
    norm_part(2)
    run(g0.q[2], g1.t[1])()
    norm_part(3)
    run(g1.t[2], g1.t[3], ge.x[0], g0.q[3], g1.q[1], g1.q[2], g1.q[3], go.x[0])()
    out(n1, n1_out)
    run(g0.close, g1.close)()
    merge_windows(wp_blk, wp, 9, 96)
    out(wp, wp_out)
    run(ge.z[1], ge.x[1])()

    def project_body(i, _):
        for at, event in ((2, run(ge.z[2], ge.x[2], ge.t[0])), (3, go.t[0])):
            pl.when(i == at)(event)
        r = pl.ds(mo(i * 256, 256), 256)
        left = n1[r, :]
        for j in range(3):
            cols = slice(j * D, (j + 1) * D)
            value = dot(left, wp[:, cols]) + vrow[0:1, cols]
            proj[r, cols] = value.astype(BF)
        return 0

    lax.fori_loop(0, T // 256, project_body, 0)
    out(proj, proj_out)

    length = length_ref[0]
    subs = T // QB

    def pair_outs(pair):
        heads = pl.ds(2 * pair, 2)
        cols = pl.ds(mo(pair * 128, 128), 128)
        return (pltpu.make_async_copy(qa.at[heads], qa_out.at[heads], pair_sem.at[pair, 0]),
                pltpu.make_async_copy(mixed.at[:, cols], mixed_out.at[:, cols], pair_sem.at[pair, 1]))

    def attend_steps(events):
        def body(pair, _):
            for at, event in events:
                pl.when(pair == at)(event)
            cols = lambda off: pl.ds(mo(off + pair * 128, 128), 128)
            lane, row = iota((T, 128), 1), iota((T, 128), 0)
            q = proj[:, cols(0)].astype(F32) * (HD ** -0.5)
            k = proj[:, cols(D)].astype(F32)
            v = proj[:, cols(2 * D)].astype(F32)
            dead = jnp.where(row < length, 0.0, neg_fill)
            for head in range(2):
                ka[head] = extend(head, k, lane, 1.0, 1.0, 1.0, dead)
                qa[pair * 2 + head] = extend(head, q, lane, 0.0, 0.0, 0.0, 1.0)
                keep = (lane < 64) if head == 0 else (lane >= 64)
                va[head] = jnp.where(keep, v, 1.0).astype(BF)
            sub_lane = iota((QB, 128), 1)
            items = [(head, pl.ds(i * QB, QB)) for i in range(subs) for head in range(2)]
            halves = {}

            def scores(n):
                head, r = items[n]
                return dot_nt(qa[pair * 2 + head, r, :], ka[head])

            def soften(value):
                top = jnp.max(value, axis=-1, keepdims=True)
                return top, jnp.exp(value - top).astype(BF)

            def finish(n, top, powers):
                head, r = items[n]
                value = dot(powers, va[head])
                total = value[:, 64:65] if head == 0 else value[:, 0:1]
                one, two, three = split3(-(top + jnp.log(total)))
                query = qa[pair * 2 + head, r, :].astype(F32)
                qa[pair * 2 + head, r, :] = extend(head, query, sub_lane, one, two, three, 1.0)
                halves[n] = value * (1.0 / total)
                if head == 1:
                    mixed[r, cols(0)] = jnp.where(sub_lane < 64, halves[n - 1], halves[n]).astype(BF)

            value, waiting = scores(0), None
            for n in range(len(items)):
                following = scores(n + 1) if n + 1 < len(items) else None
                soft = soften(value)
                if waiting is not None:
                    finish(n - 1, *waiting)
                value, waiting = following, soft
            finish(len(items) - 1, *waiting)
            for made in pair_outs(pair):
                made.start()
            return 0

        lax.fori_loop(0, H // 2, body, 0)

    attend_steps([(1, run(go.z[1], go.x[1], ge.z[3], ge.x[3], go.z[2], go.x[2], ge.t[1])),
                  (2, run(go.z[3], go.x[3], ge.t[2], c_send)), (3, run(ge.q[0], go.t[1], go.q[0])),
                  (4, run(ge.t[3], go.t[2])), (5, run(ge.q[1], ge.q[2], go.t[3]))])
    run(ge.q[3], go.q[1], go.q[2], go.q[3], go.close)()
    merge_windows(wo_blk, wo, 3, 96)
    out(wo, wo_out)
    ge.close()
    out(we, we_out)
    c_wait()
    out(cc, c_out)
    link.finish()
    for made in outs:
        made.wait()
    for pair in range(H // 2):
        for made in pair_outs(pair):
            made.wait()


def first_call(length, x, wp, wo, we, wc, vectors):
    T, D = x.shape
    FF = we.shape[1] * 4
    ANY = pl.BlockSpec(memory_space=pl.ANY)
    V = pl.BlockSpec(memory_space=pltpu.VMEM)
    S = pl.BlockSpec(memory_space=pltpu.SMEM)
    sds = jax.ShapeDtypeStruct
    n = 4 * 36 + 7 + 7
    return pl.pallas_call(
        first_kernel,
        in_specs=[S, ANY] + [V] * 12,
        out_specs=[ANY] * 9,
        out_shape=[sds((T, D), BF), sds((T, 3 * D), BF), sds((T, D), BF), sds((H, T, 128), BF),
                   sds((D, 3 * D), BF), sds((D, D), BF), sds((D, FF), BF), sds((4,) + wc.shape, BF), sds((8, FF), F32)],
        scratch_shapes=[
            pltpu.VMEM((4, D, 640), BF), pltpu.VMEM((4, D, 256), BF), pltpu.VMEM((D, FF), BF),
            pltpu.VMEM((D, 3 * D), BF), pltpu.VMEM((D, D), BF), pltpu.VMEM((8, 16, FF // 8), BF),
            pltpu.VMEM((T, D), BF), pltpu.VMEM((T, 3 * D), BF), pltpu.VMEM((T, D), BF),
            pltpu.VMEM((H, T, 128), BF), pltpu.VMEM((2, T, 128), BF), pltpu.VMEM((2, T, 128), BF),
            pltpu.VMEM((8, FF), F32), pltpu.VMEM((4,) + wc.shape, BF),
            pltpu.VMEM((T, D), BF),
            pltpu.SemaphoreType.DMA((n,)), pltpu.SemaphoreType.DMA((n,)), pltpu.SemaphoreType.DMA((10,)), pltpu.SemaphoreType.DMA((H // 2, 2)),
        ],
        compiler_params=pltpu.CompilerParams(
            collective_id=0, has_side_effects=True, vmem_limit_bytes=60 << 20),
        name="first_part",
    )(length, x, wp, wo, we, wc, *vectors)


def layer_norm(values, gain_row, shift_row):
    centre = jnp.mean(values, axis=-1, keepdims=True)
    centred = values - centre
    spread = jnp.mean(centred * centred, axis=-1, keepdims=True)
    return centred * lax.rsqrt(spread + eps_norm) * gain_row + shift_row


def gelu_exact(values):
    return jax.nn.gelu(values, approximate=False)


def matmul(first, second):
    return jnp.dot(first, second, preferred_element_type=jnp.float32)


def over_rows(first, second):
    return lax.dot_general(
        first, second, (((0,), (0,)), ((), ())), preferred_element_type=jnp.float32
    )


def over_columns(first, second):
    return lax.dot_general(
        first, second, (((1,), (1,)), ((), ())), preferred_element_type=jnp.float32
    )


def fetch_forward(
    project_weight,
    output_weight,
    expand_weight,
    contract_weight,
    project_bias,
    output_bias,
    expand_bias,
    contract_bias,
    first_gain,
    first_shift,
    second_gain,
    second_shift,
):
    wide_project, wide_output, wide_expand, wide_contract = (
        lax.all_gather(project_weight, "fsdp", axis=1, tiled=True),
        lax.all_gather(output_weight, "fsdp", axis=1, tiled=True),
        lax.all_gather(expand_weight, "fsdp", axis=1, tiled=True),
        lax.all_gather(contract_weight, "fsdp", axis=1, tiled=True),
    )
    return (
        lax.all_gather(wide_project, "dp", axis=0, tiled=True),
        lax.all_gather(wide_output, "dp", axis=0, tiled=True),
        lax.all_gather(wide_expand, "dp", axis=0, tiled=True),
        lax.all_gather(wide_contract, "dp", axis=0, tiled=True),
        lax.all_gather(project_bias, "dp", axis=0, tiled=True),
        lax.all_gather(output_bias, "dp", axis=0, tiled=True),
        lax.all_gather(expand_bias, "dp", axis=0, tiled=True),
        lax.all_gather(contract_bias, "dp", axis=0, tiled=True),
        lax.all_gather(first_gain, "dp", axis=0, tiled=True),
        lax.all_gather(first_shift, "dp", axis=0, tiled=True),
        lax.all_gather(second_gain, "dp", axis=0, tiled=True),
        lax.all_gather(second_shift, "dp", axis=0, tiled=True),
    )


def fetch_backward(
    project_weight,
    output_weight,
    expand_weight,
    contract_weight,
    project_bias,
    output_bias,
    expand_bias,
    contract_bias,
    first_gain,
    first_shift,
    second_gain,
    second_shift,
):
    wide_project, wide_output, wide_expand, wide_contract = (
        lax.all_gather(project_weight, "fsdp", axis=1, tiled=True),
        lax.all_gather(output_weight, "fsdp", axis=1, tiled=True),
        lax.all_gather(expand_weight, "fsdp", axis=1, tiled=True),
        lax.all_gather(contract_weight, "fsdp", axis=1, tiled=True),
    )
    return (
        lax.all_gather(wide_project, "dp", axis=0, tiled=True),
        lax.all_gather(wide_output, "dp", axis=0, tiled=True),
        lax.all_gather(wide_expand, "dp", axis=0, tiled=True),
        lax.all_gather(wide_contract, "dp", axis=0, tiled=True),
        lax.all_gather(project_bias, "dp", axis=0, tiled=True),
        lax.all_gather(output_bias, "dp", axis=0, tiled=True),
        lax.all_gather(expand_bias, "dp", axis=0, tiled=True),
        lax.all_gather(contract_bias, "dp", axis=0, tiled=True),
        lax.all_gather(first_gain, "dp", axis=0, tiled=True),
        lax.all_gather(first_shift, "dp", axis=0, tiled=True),
        lax.all_gather(second_gain, "dp", axis=0, tiled=True),
        lax.all_gather(second_shift, "dp", axis=0, tiled=True),
    )


def split_heads(cell_rows, block_rows):
    slot_count = cell_rows.shape[0]
    width = cell_rows.shape[1] // 3
    query_blocks = cell_rows[:, :width].reshape(slot_count // block_rows, block_rows, H, HD)
    keys_all = cell_rows[:, width : 2 * width].reshape(slot_count, H, HD)
    values_all = cell_rows[:, 2 * width :].reshape(slot_count, H, HD)
    return (query_blocks, keys_all, values_all)


def block_scores(query_block, keys_all, key_live):
    scores = jnp.einsum(
        "qhe,khe->hqk", query_block, keys_all, preferred_element_type=jnp.float32
    ) * HD ** (-0.5)
    return jnp.where(key_live[None, None, :], scores, neg_fill)


def attend_forward(query_block, keys_all, values_all, key_live):
    scores = block_scores(query_block, keys_all, key_live)
    row_max = jnp.max(scores, axis=-1, keepdims=True)
    powers = jnp.exp(scores - row_max)
    row_total = jnp.sum(powers, axis=-1, keepdims=True)
    weights = (powers / row_total).astype(jnp.bfloat16)
    mixed_block = jnp.einsum(
        "hqk,khe->qhe", weights, values_all, preferred_element_type=jnp.float32
    )
    return (mixed_block, (row_max + jnp.log(row_total))[:, :, 0])


def attend_backward(query_block, grad_block, log_block, keys_all, values_all, key_live):
    scores = block_scores(query_block, keys_all, key_live)
    weights = jnp.exp(scores - log_block[:, :, None])
    grad_weights = jnp.einsum(
        "qhe,khe->hqk", grad_block, values_all, preferred_element_type=jnp.float32
    )
    row_inner = jnp.sum(grad_weights * weights, axis=-1, keepdims=True)
    grad_scores = (weights * (grad_weights - row_inner)).astype(jnp.bfloat16)
    grad_query = jnp.einsum(
        "hqk,khe->qhe", grad_scores, keys_all, preferred_element_type=jnp.float32
    ) * HD ** (-0.5)
    grad_key = jnp.einsum(
        "hqk,qhe->khe", grad_scores, query_block, preferred_element_type=jnp.float32
    ) * HD ** (-0.5)
    grad_value = jnp.einsum(
        "hqk,qhe->khe", weights.astype(jnp.bfloat16), grad_block, preferred_element_type=jnp.float32
    )
    return (grad_query, grad_key, grad_value)


def per_device(
    tokens,
    lengths,
    cotangent,
    project_weight,
    project_bias,
    output_weight,
    output_bias,
    expand_weight,
    expand_bias,
    contract_weight,
    contract_bias,
    first_gain,
    first_shift,
    second_gain,
    second_shift,
):
    fetched = fetch_forward(
        project_weight,
        output_weight,
        expand_weight,
        contract_weight,
        project_bias,
        output_bias,
        expand_bias,
        contract_bias,
        first_gain,
        first_shift,
        second_gain,
        second_shift,
    )
    full_project, full_output, full_expand, full_contract = (
        fetched[0],
        fetched[1],
        fetched[2],
        fetched[3],
    )
    vectors = [item.astype(jnp.float32) for item in fetched[4:]]
    bias_project, bias_output, bias_expand, bias_contract = (
        vectors[0],
        vectors[1],
        vectors[2],
        vectors[3],
    )
    gain_one, shift_one, gain_two, shift_two = (vectors[4], vectors[5], vectors[6], vectors[7])
    cell_count = lengths.shape[0]
    slot_count = tokens.shape[0] // cell_count
    width = tokens.shape[1]
    block_rows = min(512, slot_count)
    positions = jnp.arange(slot_count, dtype=jnp.int32)
    live_keys = positions[None, :] < lengths[:, None]
    live_rows = live_keys.reshape(-1)
    rows_in = tokens.astype(jnp.float32)
    normed_one = layer_norm(rows_in, gain_one, shift_one).astype(jnp.bfloat16)
    bias_full = jnp.concatenate(
        [bias_project[:width], jnp.zeros((width,), jnp.float32), bias_project[width:]]
    )
    projected = (matmul(normed_one, full_project) + bias_full).astype(jnp.bfloat16)
    cell_index = 0
    query_blocks, keys_all, values_all = split_heads(projected, block_rows)
    key_live = live_keys[cell_index]
    mixed_blocks, log_blocks = lax.map(
        lambda query_block: attend_forward(query_block, keys_all, values_all, key_live),
        query_blocks,
    )
    mixed_list = mixed_blocks.reshape(slot_count, width)
    log_list = [log_blocks]
    mixed_low = mixed_list.astype(jnp.bfloat16)
    middle = rows_in + (matmul(mixed_low, full_output) + bias_output)
    normed_two = layer_norm(middle, gain_two, shift_two).astype(jnp.bfloat16)
    hidden = matmul(normed_two, full_expand) + bias_expand
    active = gelu_exact(hidden).astype(jnp.bfloat16)
    result = middle + (matmul(active, full_contract) + bias_contract)
    block_out = jnp.where(live_rows[:, None], result, 0.0).astype(jnp.bfloat16)
    again = fetch_backward(
        project_weight,
        output_weight,
        expand_weight,
        contract_weight,
        project_bias,
        output_bias,
        expand_bias,
        contract_bias,
        first_gain,
        first_shift,
        second_gain,
        second_shift,
    )
    back_project, back_output, back_expand, back_contract = (again[0], again[1], again[2], again[3])
    grad_out = jnp.where(live_rows[:, None], cotangent.astype(jnp.float32), 0.0)
    grad_out_low = grad_out.astype(jnp.bfloat16)
    grad_contract = over_rows(active, grad_out_low)
    grad_contract_bias = jnp.sum(grad_out, axis=0)
    grad_active = over_columns(grad_out_low, back_contract)
    gelu_value, gelu_pull = jax.vjp(gelu_exact, hidden)
    grad_hidden = gelu_pull(grad_active)[0].astype(jnp.bfloat16)
    grad_expand = over_rows(normed_two, grad_hidden)
    grad_expand_bias = jnp.sum(grad_hidden.astype(jnp.float32), axis=0)
    grad_normed_two = over_columns(grad_hidden, back_expand)
    norm_value, second_pull = jax.vjp(layer_norm, middle, gain_two, shift_two)
    grad_middle, grad_gain_two, grad_shift_two = second_pull(grad_normed_two)
    grad_middle = grad_middle + grad_out
    grad_branch = grad_middle.astype(jnp.bfloat16)
    grad_output = over_rows(mixed_low, grad_branch)
    grad_output_bias = jnp.sum(grad_branch.astype(jnp.float32), axis=0)
    grad_mixed = over_columns(grad_branch, back_output).astype(jnp.bfloat16)
    cell_index = 0
    query_blocks, keys_all, values_all = split_heads(projected, block_rows)
    key_live = live_keys[cell_index]
    grad_blocks = grad_mixed.reshape(slot_count // block_rows, block_rows, H, HD)

    def visit_block(carried, inputs):
        query_block, grad_block, log_block = inputs
        grad_query, grad_key, grad_value = attend_backward(
            query_block, grad_block, log_block, keys_all, values_all, key_live
        )
        return ((carried[0] + grad_key, carried[1] + grad_value), grad_query)

    initial = (
        jnp.zeros((slot_count, H, HD), jnp.float32),
        jnp.zeros((slot_count, H, HD), jnp.float32),
    )
    (key_sums, value_sums), query_grads = lax.scan(
        visit_block, initial, (query_blocks, grad_blocks, log_list[cell_index])
    )
    grad_cells = jnp.concatenate(
        [
            query_grads.reshape(slot_count, width),
            key_sums.reshape(slot_count, width),
            value_sums.reshape(slot_count, width),
        ],
        axis=1,
    )
    grad_projected = grad_cells.astype(jnp.bfloat16)
    grad_project = over_rows(normed_one, grad_projected)
    column_sums = jnp.sum(grad_projected.astype(jnp.float32), axis=0)
    grad_project_bias = jnp.concatenate([column_sums[:width], column_sums[2 * width :]])
    grad_normed_one = over_columns(grad_projected, back_project)
    first_value, first_pull = jax.vjp(layer_norm, rows_in, gain_one, shift_one)
    grad_rows_in, grad_gain_one, grad_shift_one = first_pull(grad_normed_one)
    tokens_grad = (grad_rows_in + grad_middle).astype(jnp.bfloat16)
    reduced = (
        lax.psum_scatter(grad_project, "dp", scatter_dimension=0, tiled=True),
        lax.psum_scatter(grad_output, "dp", scatter_dimension=0, tiled=True),
        lax.psum_scatter(grad_expand, "dp", scatter_dimension=0, tiled=True),
        lax.psum_scatter(grad_contract, "dp", scatter_dimension=0, tiled=True),
        lax.psum_scatter(grad_project_bias, "dp", scatter_dimension=0, tiled=True),
        lax.psum_scatter(grad_output_bias, "dp", scatter_dimension=0, tiled=True),
        lax.psum_scatter(grad_expand_bias, "dp", scatter_dimension=0, tiled=True),
        lax.psum_scatter(grad_contract_bias, "dp", scatter_dimension=0, tiled=True),
        lax.psum_scatter(grad_gain_one, "dp", scatter_dimension=0, tiled=True),
        lax.psum_scatter(grad_shift_one, "dp", scatter_dimension=0, tiled=True),
        lax.psum_scatter(grad_gain_two, "dp", scatter_dimension=0, tiled=True),
        lax.psum_scatter(grad_shift_two, "dp", scatter_dimension=0, tiled=True),
    )
    shard_project, shard_output, shard_expand, shard_contract = (
        lax.psum_scatter(
            reduced[0].astype(jnp.bfloat16), "fsdp", scatter_dimension=1, tiled=True
        ).astype(jnp.float32),
        lax.psum_scatter(
            reduced[1].astype(jnp.bfloat16), "fsdp", scatter_dimension=1, tiled=True
        ).astype(jnp.float32),
        lax.psum_scatter(
            reduced[2].astype(jnp.bfloat16), "fsdp", scatter_dimension=1, tiled=True
        ).astype(jnp.float32),
        lax.psum_scatter(
            reduced[3].astype(jnp.bfloat16), "fsdp", scatter_dimension=1, tiled=True
        ).astype(jnp.float32),
    )
    summed = lax.psum(
        (
            reduced[4],
            reduced[5],
            reduced[6],
            reduced[7],
            reduced[8],
            reduced[9],
            reduced[10],
            reduced[11],
        ),
        "fsdp",
    )
    return (
        block_out,
        tokens_grad,
        shard_project,
        summed[0],
        shard_output,
        summed[1],
        shard_expand,
        summed[2],
        shard_contract,
        summed[3],
        summed[4],
        summed[5],
        summed[6],
        summed[7],
    )


def scatter_events(link, place, col, pair_of, lc, lxh, lyh, lx, ly):
    p = place
    family = (p.dc, p.dx + p.dc - p.d, p.dy + p.dc - p.d, p.dd + p.dc - p.d)
    cs = [link.slot() for _ in range(4)]
    hx, hy, fx, fy = (link.slot() for _ in range(4))
    got = link.got

    def add(target, *terms):
        flat = len(target.shape) == 2

        def body(i, _):
            at = (pl.ds(mo(i * 16, 16), 16), slice(None)) if flat else (i,)
            total = target[at].astype(F32)
            for term in terms:
                total = total + term[at].astype(F32)
            target[at] = total.astype(BF)
            return 0

        lax.fori_loop(0, target.shape[0] // 16 if flat else target.shape[0], body, 0)

    def to_sibling(which):
        link.send(cs[which], col(family[which]), lc.at[which], "c", lambda: col(0))

    def halves():
        got(cs[3], lc.at[3])
        add(col(p.dd), lc.at[3])
        link.send(hx, pair_of(col(p.dd), 0), lxh, "x", lambda: lxh)
        link.send(hy, pair_of(col(p.dd), 1), lyh, "y", lambda: lyh)

    def near():
        got(cs[1], lc.at[1])
        got(cs[2], lc.at[2])
        add(col(p.dx), lc.at[1])
        add(col(p.dy), lc.at[2])

    def pass_y():
        got(hx, lxh)
        add(pair_of(col(p.dy), 0), lxh)
        link.send(fy, col(p.dy), ly, "y", lambda: ly)

    def pass_x():
        got(hy, lyh)
        add(pair_of(col(p.dx), 1), lyh)
        link.send(fx, col(p.dx), lx, "x", lambda: lx)

    def own():
        got(cs[0], lc.at[0])

    def total():
        got(fx, lx)
        got(fy, ly)
        add(col(p.d), lc.at[0], lx, ly)

    return to_sibling, [halves, near, pass_y, pass_x, own, total]


def z_sum(link, place, block, lz, finish):
    p = place
    zs = link.slot(4)

    def send():
        for step in (1, 3, 2):
            link.send(zs + step, block(p.zt(step)), lz.at[step], step, lambda: lz.at[0])

    def last():
        total = block(p.z)[...].astype(F32)
        for step in (1, 3, 2):
            link.got(zs + step, lz.at[step])
            total = total + lz[step].astype(F32)
        finish(total)

    return send, last


def gelu_pair(value):
    lift = 0.5 * (1.0 + lax.erf(value * 0.7071067811865476))
    bell = jnp.exp(value * value * -0.5) * 0.3989422804014327
    return value * lift, lift + value * bell


def second_kernel(length_ref, x_hbm, cot_hbm, mixed_hbm, wo_hbm, we_hbm, c_hbm, v_ref,
                  block_out, dmixed_out, dmiddle_out, ge_out, go_out, gc_out, vg_out,
                  x_ref, cot_ref, mixed_ref, wo_ref, we, wct, act, slope, middle, n2t, dot_t, mixed_t, dbranch, dout, gc, go, dmixed, bout, vg,
                  lc, lxh, lyh, lx, ly, send_sem, recv_sem, out_sem):
    p = Place()
    T, D = x_ref.shape
    FF = we.shape[1]
    R = D // 8
    Q = FF // 4
    C8 = FF // 8
    link = Link(p, send_sem, recv_sem)
    bc = lambda z, d: wct.at[pl.ds(mo(z * (D // 4), 16), D // 4), pl.ds(mo(d * C8, 128), C8)]
    gather = Gather(link, p, bc)

    to_sibling, scatter = scatter_events(
        link, p, lambda d: gc.at[d], lambda ref, h: ref.at[pl.ds(2 * h, 2)], lc, lxh, lyh, lx, ly)
    load = pltpu.make_async_copy(we_hbm, we, out_sem.at[0])
    columns = [pltpu.make_async_copy(c_hbm.at[z], bc(z, p.d), out_sem.at[19 + z]) for z in range(4)]
    for made in columns:
        made.start()
    halves = [pl.ds(i * (T // 2), T // 2) for i in range(2)]
    early = [[pltpu.make_async_copy(wo_hbm, wo_ref, out_sem.at[12])], []]
    for i, r in enumerate(halves):
        for at, (a, b) in enumerate(((mixed_hbm, mixed_ref), (x_hbm, x_ref), (cot_hbm, cot_ref))):
            early[i].append(pltpu.make_async_copy(a.at[r], b.at[r], out_sem.at[13 + 3 * i + at]))
    for made in early[0] + early[1]:
        made.start()
    enter(p)
    for made in columns:
        made.wait()
    run(*gather.x)()
    for made in early[0] + early[1]:
        made.wait()
    load.start()
    length = length_ref[0]
    LR = 256
    rows = lambda i: pl.ds(mo(i * LR, LR), LR)
    vec = lambda i: v_ref[i:i + 1, 0:D]
    vg[...] = jnp.zeros_like(vg)

    def at(i, spots):
        for where, event in spots:
            pl.when(i == where)(event)

    def norm(value):
        u = value - jnp.mean(value, axis=-1, keepdims=True)
        r = lax.rsqrt(jnp.mean(u * u, axis=-1, keepdims=True) + eps_norm)
        return u * r, r

    def middle_body(i, _):
        r = rows(i)
        value = x_ref[r, :].astype(F32) + (dot(mixed_ref[r, :], wo_ref[...]) + vec(2))
        middle[r, :] = value
        xhat, _ = norm(value)
        n2 = (xhat * vec(6) + vec(7)).astype(BF)
        dmixed[r, :] = n2
        n2t[:, r] = n2.T
        live = iota((LR, D), 0) + i * LR < length
        grad = jnp.where(live, cot_ref[r, :].astype(F32), 0.0)
        vg[7:8, :] += jnp.sum(grad, axis=0, keepdims=True)
        dout[r, :] = grad.astype(BF)
        dot_t[:, r] = grad.astype(BF).T
        mixed_t[:, r] = mixed_ref[r, :].T
        return 0

    lax.fori_loop(0, T // LR, middle_body, 0)
    load.wait()

    def hidden_body(i, _):
        at(i, [(0, gather.t[0]), (1, gather.t[1]), (2, gather.t[2]), (3, gather.t[3])])
        r = rows(i)
        left = dmixed[r, :]
        for j in range(4):
            cols = slice(j * Q, (j + 1) * Q)
            first, second = gelu_pair(dot(left, we[:, cols]) + v_ref[1:2, cols])
            act[r, cols] = first.astype(BF)
            slope[r, cols] = second.astype(BF)
        return 0

    lax.fori_loop(0, T // LR, hidden_body, 0)

    def column(d):
        value = dot(dot_t[...], act[:, pl.ds(mo(d * C8, 128), C8)])
        gc[d] = value.reshape(4, D // 4, C8).astype(BF)

    sib = p.dc - p.d
    turns = (p.dd + sib, p.dd, p.dx + sib, p.dy + sib, p.dx, p.dy, p.d + sib, p.d)

    def column_body(i, _):
        d = turns[7]
        for k in range(7):
            d = jnp.where(i == k, turns[k], d)
        column(d)
        at(i, [(0, lambda: to_sibling(3)), (2, lambda: to_sibling(1)), (3, run(lambda: to_sibling(2), gather.q[0])),
               (5, run(gather.q[1], gather.q[2], scatter[0])), (6, lambda: to_sibling(0))])
        return 0

    lax.fori_loop(0, 8, column_body, 0)
    run(gather.q[3], scatter[1], gather.close)()

    def back_body(i, _):
        at(i, [(1, run(scatter[2], scatter[3], scatter[4]))])
        r = rows(i)
        grad_low = dout[r, :]
        result = middle[r, :] + vec(3)
        for j in range(4):
            cols = slice(j * Q, (j + 1) * Q)
            dh = dot(grad_low, wct[:, cols]) * slope[r, cols].astype(F32)
            low = dh.astype(BF)
            slope[r, cols] = low
            vg[3 + j:4 + j, :] += jnp.sum(low.astype(F32), axis=0, keepdims=True)
        result = result + dot_nt(act[r, :], wct[...])
        dn = dot_nt(slope[r, :], we[...])
        live = iota((LR, D), 0) + i * LR < length
        bout[r, :] = jnp.where(live, result, 0.0).astype(BF)
        xhat, spread = norm(middle[r, :])
        vg[10:11, :] += jnp.sum(dn * xhat, axis=0, keepdims=True)
        vg[11:12, :] += jnp.sum(dn, axis=0, keepdims=True)
        gx = dn * vec(6)
        back = spread * (gx - jnp.mean(gx, axis=-1, keepdims=True)
                         - xhat * jnp.mean(gx * xhat, axis=-1, keepdims=True))
        total = dout[r, :].astype(F32) + back
        middle[r, :] = total
        branch = total.astype(BF)
        dbranch[r, :] = branch
        vg[2:3, :] += jnp.sum(branch.astype(F32), axis=0, keepdims=True)
        dmixed[r, :] = dot_nt(branch, wo_ref[...]).astype(BF)
        return 0

    lax.fori_loop(0, T // LR, back_body, 0)
    outs = []

    def out(source, target):
        made = pltpu.make_async_copy(source, target, out_sem.at[1 + len(outs)])
        made.start()
        outs.append(made)

    out(bout, block_out)
    out(dmixed, dmixed_out)
    out(middle, dmiddle_out)
    for z in range(4):
        cols = slice(3 * z // 2 * 128, 3 * z // 2 * 128 + 256)
        go[:, z] = dot(mixed_t[...], dbranch[:, cols]).reshape(8, R, 256).astype(BF)
    out(go, go_out)
    for z in range(4):
        act[0:D, z * Q:(z + 1) * Q] = dot(n2t[...], slope[:, z * Q:(z + 1) * Q]).astype(BF)
        out(act.at[0:D, z * Q:(z + 1) * Q], ge_out.at[:, z * Q:(z + 1) * Q])
        if z == 2:
            scatter[5]()
            out(gc.at[p.d], gc_out)
    vg_out[...] = vg[...]
    link.finish()
    for made in outs:
        made.wait()


ANY = pl.BlockSpec(memory_space=pl.ANY)
VM = pl.BlockSpec(memory_space=pltpu.VMEM)
SM = pl.BlockSpec(memory_space=pltpu.SMEM)
sds = jax.ShapeDtypeStruct


def second_call(length, x, cot, mixed, wo, we, wc, v):
    T, D = x.shape
    FF = we.shape[1]
    n = 36 + 8
    R, C8, Z = D // 8, FF // 8, D // 4
    vm = pltpu.VMEM
    return pl.pallas_call(
        second_kernel,
        in_specs=[SM] + [ANY] * 6 + [VM],
        out_specs=[ANY] * 6 + [VM],
        out_shape=[sds((T, D), BF), sds((T, D), BF), sds((T, D), F32), sds((D, FF), BF), sds((8, 4, R, 256), BF),
                   sds((4, Z, C8), BF), sds((16, D), F32)],
        scratch_shapes=[
            vm((T, D), BF), vm((T, D), BF), vm((T, D), BF), vm((D, D), BF), vm((D, FF), BF), vm((D, FF), BF), vm((T, FF), BF), vm((T, FF), BF), vm((T, D), F32),
            vm((D, T), BF), vm((D, T), BF), vm((D, T), BF), vm((T, D), BF), vm((T, D), BF),
            vm((8, 4, Z, C8), BF), vm((8, 4, R, 256), BF), vm((T, D), BF), vm((T, D), BF), vm((16, D), F32),
            vm((4, 4, Z, C8), BF), vm((2, Z, C8), BF), vm((2, Z, C8), BF), vm((4, Z, C8), BF), vm((4, Z, C8), BF),
            pltpu.SemaphoreType.DMA((n,)), pltpu.SemaphoreType.DMA((n,)), pltpu.SemaphoreType.DMA((23,)),
        ],
        compiler_params=pltpu.CompilerParams(
            collective_id=1, has_side_effects=True, vmem_limit_bytes=62 << 20),
        name="second_part",
    )(length, x, cot, mixed, wo, we, wc, v)


def third_kernel(length_ref, proj_hbm, qa_hbm, mixed_hbm, dm_hbm, n1_hbm, wp_hbm, x_hbm, dmiddle_hbm, ge_hbm, go_hbm,
                 gc_hbm, vg_ref, v_ref,
                 tokens_out, gp_out, go_out, ge_out, gc_out, vec_out,
                 proj, qa, mixed, dm, n1, n1t, wpp, x, dmiddle, ge, go, dproj, tg, gp,
                 ka, da, dq, va, kt, vs, vo, vl, vz,
                 lce, lxhe, lyhe, lxe, lye, lze, lco, lxho, lyho, lxo, lyo, lzo,
                 lcp, lxhp, lyhp, lxp, lyp, lzp, gpw, gcol, lzc,
                 send_sem, recv_sem, load_sem):
    p = Place()
    T, D = x.shape
    FF = ge.shape[1]
    R = D // 8
    Q = FF // 4
    pairs = H // 2
    KB = 256
    parts = 2
    link = Link(p, send_sem, recv_sem)
    loads = []

    def load(source, target, now=True):
        made = pltpu.make_async_copy(source, target, load_sem.at[len(loads)])
        if now:
            made.start()
        loads.append(made)
        return made

    first_loads = [load(a, b) for a, b in ((proj_hbm, proj), (qa_hbm, qa), (mixed_hbm, mixed), (dm_hbm, dm))]
    ge_load, gc_load, go_load, n1_load = load(ge_hbm, ge), load(gc_hbm, gcol), load(go_hbm, go), load(n1_hbm, n1, False)
    late = [load(x_hbm, x, False), load(dmiddle_hbm, dmiddle, False)]
    for i in range(pairs):
        for s in range(3):
            late.append(load(wp_hbm.at[:, pl.ds((s * pairs + i) * 128, 128)],
                             wpp.at[:, pl.ds((i * 3 + s) * 128, 128)], False))

    def finish_e(total):
        ge_out[...] = total

    def finish_o(total):
        go_out[...] = jnp.where(p.odd == 0, total[:, 0:192], total[:, 64:256])

    rows_of = lambda d: pl.ds(mo(d * R, 16), R)
    def finish_c(total):
        gc_out[...] = total

    e_col, o_col = (lambda d: ge.at[rows_of(d), :]), (lambda d: go.at[d])
    e_sib, ev_e = scatter_events(
        link, p, e_col, lambda ref, h: ref.at[:, pl.ds(h * (FF // 2), FF // 2)], lce, lxhe, lyhe, lxe, lye)
    o_sib, ev_o = scatter_events(
        link, p, o_col, lambda ref, h: ref.at[pl.ds(2 * h, 2)], lco, lxho, lyho, lxo, lyo)
    e_send, e_last = z_sum(link, p, lambda z: e_col(p.d).at[:, pl.ds(mo(z * Q, 128), Q)], lze, finish_e)
    o_send, o_last = z_sum(link, p, lambda z: o_col(p.d).at[z], lzo, finish_o)
    c_send, c_last = z_sum(link, p, lambda z: gcol.at[z], lzc, finish_c)
    ended = []
    combos = []
    for i in range(pairs):
        for s in range(3):
            tile = s * pairs + i
            for owner in range(4):
                left = 9 * owner // 2
                if left <= tile < left + 5:
                    combos.append((i, s, owner, tile - left))
    assert len(combos) == 20
    z_slots = [[link.slot() for _ in range(3)] for _ in combos]

    def pair_scatter(i):
        column = lambda d: gp.at[i, d]
        sib, events = scatter_events(
            link, p, column, lambda ref, h: ref.at[pl.ds(h * (R // 2), R // 2)],
            lcp.at[i], lxhp.at[i], lyhp.at[i], lxp.at[i], lyp.at[i])
        mine = [(at, c) for at, c in enumerate(combos) if c[0] == i]

        def along(add_own):
            def run():
                add_own()
                for at, (_, s, owner, _) in mine:
                    @pl.when(p.z != owner)
                    def _():
                        step = lax.rem(owner - p.z + 4, 4)
                        part = column(p.d).at[:, pl.ds(s * 128, 128)]
                        link.copy(z_slots[at][0] + step - 1, part, lzp.at[at, step - 1], ("z", owner)).start()
            return run

        def last():
            for at, (_, s, owner, place) in mine:
                @pl.when(p.z == owner)
                def _():
                    total = gp[i, p.d, :, s * 128:(s + 1) * 128].astype(F32)
                    for step in range(1, 4):
                        link.got(z_slots[at][step - 1], lzp.at[at, step - 1])
                        total = total + lzp[at, step - 1].astype(F32)
                    gpw[:, place * 128:(place + 1) * 128] = total

        def ending():
            for at, (_, s, owner, _) in mine:
                @pl.when(p.z != owner)
                def _():
                    step = lax.rem(owner - p.z + 4, 4)
                    view = lzp.at[at, 0]
                    link.copy(z_slots[at][0] + step - 1, view, view, "x").wait_send()

        ended.append(ending)

        def start():
            for k in (3, 1, 2, 0):
                sib(k)

        return [start] + events[:5] + [along(events[5]), last]

    ev_p = [pair_scatter(i) for i in range(pairs)]

    enter(p, wide=True)
    for made in first_loads:
        made.wait()
    n1_load.start()
    length = length_ref[0]

    def start_e():
        ge_load.wait()
        for k in (3, 1, 2, 0):
            e_sib(k)

    def start_o():
        go_load.wait()
        for k in (3, 1, 2, 0):
            o_sib(k)

    def start_late():
        for made in late:
            made.start()

    def turn_n1():
        n1_load.wait()
        for i in range(T // 256):
            n1t[:, i * 256:(i + 1) * 256] = n1[i * 256:(i + 1) * 256, :].T

    def start_c():
        gc_load.wait()
        c_send()

    e, o = ev_e, ev_o
    q = ev_p
    timeline = [
        (0, start_c), (0, start_e), (0, start_o), (1, turn_n1), (1, e[0]), (2, start_late), (2, e[1]), (2, e[4]), (2, o[0]), (2, o[1]), (2, o[4]),
        (2, q[0][0]), (3, q[0][1]), (3, q[0][2]), (3, q[0][5]), (4, e[2]), (4, e[3]), (4, c_last), (4, o[2]), (4, o[3]),
        (4, q[0][3]), (4, q[0][4]), (4, q[1][0]), (5, q[1][1]), (5, q[1][2]), (5, q[1][5]), (6, q[2][0]),
        (7, q[2][1]), (7, q[2][2]), (7, q[2][5]), (8, e[5]), (8, e_send), (8, q[3][0]), (9, o[5]), (9, o_send),
        (9, q[3][1]), (9, q[3][2]), (9, q[3][5]), (10, q[0][6]), (10, q[1][3]), (10, q[1][4]), (10, q[2][3]), (10, q[2][4]),
        (10, q[3][3]), (10, q[3][4]), (10, q[4][0]), (11, q[4][1]), (11, q[4][2]), (11, q[4][5])]
    timeline.sort(key=lambda e: e[0])

    def body(step, _):
        for at, event in timeline:
            if at < pairs * parts:
                pl.when(step == at)(event)
        pair = lax.div(step, parts)
        part = lax.rem(step, parts)
        ps = lambda off: pl.ds(mo(off + pair * 128, 128), 128)
        own = lambda s: pl.ds(mo(pair * 384 + s * 128, 128), 128)

        @pl.when(part == 0)
        def _():
            lane, row = iota((T, 128), 1), iota((T, 128), 0)
            k = proj[:, ps(D)].astype(F32)
            v = proj[:, ps(2 * D)].astype(F32)
            do = dm[:, ps(0)].astype(F32)
            pr = do * mixed[:, ps(0)].astype(F32)
            dead = jnp.where(row < length, 0.0, neg_fill)
            for head in range(2):
                keep = (lane < 64) if head == 0 else (lane >= 64)
                delta = jnp.sum(jnp.where(keep, pr, 0.0), axis=-1, keepdims=True)
                one, two, three = split3(-delta)
                da[head] = extend(head, do, lane, one, two, three, 0.0)
                ka[head] = extend(head, k, lane, 1.0, 1.0, 1.0, dead)
                va[head] = extend(head, v, lane, 1.0, 1.0, 1.0, 0.0)
                kt[head] = jnp.where(keep, k, 0.0).astype(BF).T
            dq[...] = jnp.zeros_like(dq)

        lk = iota((KB, 128), 1)
        spans = [pl.ds(mo(part * (T // parts) + i * KB, KB), KB) for i in range(T // parts // KB)]
        items = [(head, r) for r in spans for head in range(2)]
        kept = {}

        def products(n):
            head, r = items[n]
            return dot_nt(ka[head, r, :], qa[pair * 2 + head]), dot_nt(va[head, r, :], da[head])

        def weigh(scores, grads):
            weights = jnp.exp(scores)
            return weights.astype(BF), (weights * grads).astype(BF)

        def finish(n, low, ds):
            head, r = items[n]
            kept[n] = dot(ds, qa[pair * 2 + head]), dot(low, da[head])
            dq[head] += dot(kt[head, :, r], ds)
            if head == 1:
                dproj[r, own(1)] = jnp.where(lk < 64, kept[n - 1][0], kept[n][0]).astype(BF)
                dproj[r, own(2)] = jnp.where(lk < 64, kept[n - 1][1], kept[n][1]).astype(BF)

        value, waiting = products(0), None
        for n in range(len(items)):
            following = products(n + 1) if n + 1 < len(items) else None
            done = weigh(*value)
            if waiting is not None:
                finish(n - 1, *waiting)
            value, waiting = following, done
        finish(len(items) - 1, *waiting)

        @pl.when(part == parts - 1)
        def _():
            dproj[:, own(0)] = ((dq[0] + dq[1]) * (HD ** -0.5)).T.astype(BF)
            value = dot(n1t[...], dproj[:, pl.ds(mo(pair * 384, 128), 384)])
            gp[pair] = value.reshape(8, R, 384).astype(BF)

        return 0

    lax.fori_loop(0, pairs * parts, body, 0)
    ev_p[pairs - 1][0]()
    for made in late:
        made.wait()
    vs[...] = vg_ref[...]
    LR = 256

    def norm_body(i, _):
        def spot(where, events):
            @pl.when(i == where)
            def _():
                for event in events:
                    event()

        spot(0, [e_last, q[1][6], q[2][6], q[3][6], q[4][3], q[4][4]])
        spot(1, q[5][1:3] + q[5][5:6])
        spot(2, [o_last, q[0][7], q[1][7], q[4][6], q[2][7]])
        spot(3, q[5][3:5] + q[3][7:8])
        r = pl.ds(mo(i * LR, LR), LR)
        left = dproj[r, :]
        dn = dot_nt(left, wpp[...])
        sums = jnp.sum(left.astype(F32), axis=0, keepdims=True)
        for j in range(pairs):
            vs[0:1, j * 128:(j + 1) * 128] += sums[:, j * 384:j * 384 + 128]
            vs[1:2, j * 128:(j + 1) * 128] += sums[:, j * 384 + 256:j * 384 + 384]
        value = x[r, :].astype(F32)
        u = value - jnp.mean(value, axis=-1, keepdims=True)
        spread = lax.rsqrt(jnp.mean(u * u, axis=-1, keepdims=True) + eps_norm)
        xhat = u * spread
        vs[8:9, :] += jnp.sum(dn * xhat, axis=0, keepdims=True)
        vs[9:10, :] += jnp.sum(dn, axis=0, keepdims=True)
        gx = dn * v_ref[4:5, 0:D]
        back = spread * (gx - jnp.mean(gx, axis=-1, keepdims=True)
                         - xhat * jnp.mean(gx * xhat, axis=-1, keepdims=True))
        tg[r, :] = (back + dmiddle[r, :]).astype(BF)
        return 0

    lax.fori_loop(0, T // LR, norm_body, 0)
    out = load(tg, tokens_out)
    v_slots = link.slot(16)
    for d in range(8):
        line = lambda row, at, n: jnp.concatenate(
            [vs[row:row + 1, at:at + n], jnp.zeros((1, 384 - n), F32)], axis=1) if n < 384 else vs[row:row + 1, at:at + n]
        vo[d] = jnp.concatenate(
            [line(d // 4, d % 4 * 2 * R, 2 * R), line(2, d * R, R), line(3 + d // 2, d % 2 * 4 * R, 4 * R)]
            + [line(row, d * R, R) for row in (7, 8, 9, 10, 11)], axis=0)
    for d in range(8):
        @pl.when(p.d != d)
        def _():
            link.copy(v_slots + d, vo.at[d], vl.at[p.d], ("d", d), land=v_slots + p.d).start()
    for event in (q[4][7], q[5][6]):
        event()
    vl[p.d] = vo[p.d]
    for d in range(8):
        @pl.when(p.d != d)
        def _():
            link.got(v_slots + d, vl.at[d])
    own = vl[0]
    for d in range(1, 8):
        own = own + vl[d]
    vz[p.z] = own
    for k in (1, 2, 3):
        link.send(v_slots + 8 + k, vz.at[p.z], vz.at[p.z], ("z", p.order[k]), lambda: vz.at[0], land=v_slots + 12 + p.z)
    q[5][7]()
    gp_out[...] = jnp.where(p.odd == 0, gpw[:, 0:576], gpw[:, 64:640])
    for k in (1, 2, 3):
        link.got(v_slots + 12 + p.order[k], vz.at[p.order[k]])
    vec_out[...] = vz[0] + vz[1] + vz[2] + vz[3]
    for d in range(8):
        @pl.when(p.d != d)
        def _():
            link.copy(v_slots + d, vo.at[d], vo.at[d], "x").wait_send()
    link.finish()
    for ending in ended:
        ending()
    out.wait()


def third_call(length, proj, qa, mixed, dm, n1, wp, x, dmiddle, ge, go, gc, vg, v):
    T, D = x.shape
    FF = ge.shape[1]
    R, Q, pairs = D // 8, FF // 4, H // 2
    vm = pltpu.VMEM
    n = 8 * 8 + 12 + 60 + 16
    return pl.pallas_call(
        third_kernel,
        in_specs=[SM] + [ANY] * 11 + [VM] * 2,
        out_specs=[ANY] + [VM] * 5,
        out_shape=[sds((T, D), BF), sds((R, 3 * D // 4), F32), sds((R, D // 4), F32), sds((R, Q), F32), sds((D // 4, FF // 8), F32),
                   sds((8, 384), F32)],
        scratch_shapes=[
            vm((T, 3 * D), BF), vm((H, T, 128), BF), vm((T, D), BF), vm((T, D), BF), vm((T, D), BF), vm((D, T), BF),
            vm((D, 3 * D), BF), vm((T, D), BF), vm((T, D), F32), vm((D, FF), BF), vm((8, 4, R, 256), BF),
            vm((T, 3 * D), BF), vm((T, D), BF), vm((pairs, 8, R, 384), BF),
            vm((2, T, 128), BF), vm((2, T, 128), BF), vm((2, 128, T), F32), vm((2, T, 128), BF), vm((2, 128, T), BF),
            vm((16, D), F32), vm((8, 8, 384), F32), vm((8, 8, 384), F32), vm((4, 8, 384), F32),
            vm((4, R, FF), BF), vm((R, FF // 2), BF), vm((R, FF // 2), BF), vm((R, FF), BF), vm((R, FF), BF), vm((4, R, Q), BF),
            vm((4, 4, R, 256), BF), vm((2, R, 256), BF), vm((2, R, 256), BF), vm((4, R, 256), BF), vm((4, R, 256), BF),
            vm((4, R, 256), BF),
            vm((pairs, 4, R, 384), BF), vm((pairs, R // 2, 384), BF), vm((pairs, R // 2, 384), BF),
            vm((pairs, R, 384), BF), vm((pairs, R, 384), BF), vm((20, 3, R, 128), BF), vm((R, 640), F32),
            vm((4, D // 4, FF // 8), BF), vm((4, D // 4, FF // 8), BF),
            pltpu.SemaphoreType.DMA((n,)), pltpu.SemaphoreType.DMA((n,)), pltpu.SemaphoreType.DMA((29,)),
        ],
        compiler_params=pltpu.CompilerParams(
            collective_id=2, has_side_effects=True, vmem_limit_bytes=63 << 20),
        name="third_part",
    )(length, proj, qa, mixed, dm, n1, wp, x, dmiddle, ge, go, gc, vg, v)


def last_kernel(block_in, tokens_in, p_in, o_in, e_in, c_in, vec_in,
                block_out, tokens_out, p_out, o_out, e_out, c_out, *rest):
    vectors, held, vec, sem = rest[:8], rest[8:14], rest[14], rest[15]
    parts = 2
    rows = block_in.shape[0] // parts
    whole = lambda ref: ref
    legs = []
    for i in range(parts):
        part = lambda ref, i=i: ref.at[pl.ds(i * rows, rows)]
        legs += [(part, block_in, held[0], block_out), (part, tokens_in, held[1], tokens_out)]
    legs += [(whole, a, b, c) for a, b, c in zip((p_in, o_in, e_in, c_in), held[2:], (p_out, o_out, e_out, c_out))]
    first = pltpu.make_async_copy(vec_in, vec, sem.at[2 * len(legs)])
    first.start()
    ins = [pltpu.make_async_copy(part(a), part(b), sem.at[k]) for k, (part, a, b, _) in enumerate(legs)]
    outs = [pltpu.make_async_copy(part(b), part(c), sem.at[len(legs) + k]) for k, (part, _, b, c) in enumerate(legs)]
    for made in ins:
        made.start()
    for came, goes in zip(ins, outs):
        came.wait()
        goes.start()
    first.wait()
    for at, target in enumerate(vectors):
        n = target.shape[0]
        target[...] = vec[at:at + 1, 0:n].reshape(n)
    for goes in outs:
        goes.wait()


def last_call(sizes, *arrays):
    return pl.pallas_call(
        last_kernel,
        in_specs=[ANY] * 7,
        out_specs=[ANY] * 6 + [VM] * 8,
        out_shape=[sds(item.shape, item.dtype) for item in arrays[:6]] + [sds((n,), F32) for n in sizes],
        scratch_shapes=[pltpu.VMEM(item.shape, item.dtype) for item in arrays] + [pltpu.SemaphoreType.DMA((17,))],
        compiler_params=pltpu.CompilerParams(vmem_limit_bytes=63 << 20),
        name="last_part",
    )(*arrays)


def per_device_fast(tokens, lengths, cotangent, project_weight, project_bias, output_weight, output_bias,
                    expand_weight, expand_bias, contract_weight, contract_bias, first_gain, first_shift,
                    second_gain, second_shift):
    vectors = (project_bias, output_bias, expand_bias, contract_bias, first_gain, first_shift, second_gain, second_shift)
    normed_one, projected, mixed, qa, full_project, full_output, full_expand, cc, v = first_call(
        lengths, tokens, project_weight, output_weight, expand_weight, contract_weight.T, vectors)
    block_out, grad_mixed, grad_middle, ge, go, gc, vg = second_call(
        lengths, tokens, cotangent, mixed, full_output, full_expand, cc, v)
    third = third_call(
        lengths, projected, qa, mixed, grad_mixed, normed_one, full_project, tokens, grad_middle, ge, go, gc, vg, v)
    out = last_call([item.shape[0] for item in vectors], block_out, *third)
    return (out[0], out[1], out[2], out[6], out[3], out[7], out[4], out[8], out[5].T, *out[9:])


def solution(mesh):
    both, rows, grid = P(("dp", "fsdp"), None), P("dp"), P("dp", "fsdp")
    weights = (grid, rows, grid, rows, grid, rows, grid, rows)
    fast = mesh.shape["dp"] == 8 and mesh.shape["fsdp"] == 4
    return jax.shard_map(
        per_device_fast if fast else per_device,
        mesh=mesh,
        in_specs=(both, P(("dp", "fsdp")), both) + weights + (rows,) * 4,
        out_specs=(both, both) + weights + (rows,) * 4,
        check_vma=False,
    )
```
